32 devices in a mesh: ctx: 8 (over y, x, core), fsdp: 4 (over z).
Axes of the slice: x: 2, y: 2, z: 4, core: 2. Of those that a mesh axis runs over, the one named last changes fastest.
Arguments:
- hidden_in: bfloat16 [4, 2048, 1024], P('fsdp', 'ctx'), may hold values from -6 to 6
- seq_lengths: int32 [4, 4], P('fsdp'), may hold values from 1 to 1024, 1984 in all within a row
- in_gain: bfloat16 [1024], P(('ctx', 'fsdp')), may hold values from 0.5 to 1.5
- w_query: bfloat16 [1024, 2048], P(('ctx', 'fsdp')), may hold values from -0.1875 to 0.1875
- w_key: bfloat16 [1024, 1024], P(('ctx', 'fsdp')), may hold values from -0.1875 to 0.1875
- w_value: bfloat16 [1024, 1024], P(('ctx', 'fsdp')), may hold values from -0.1875 to 0.1875
- q_gain: bfloat16 [128], P(('ctx', 'fsdp')), may hold values from 0.5 to 1.5
- k_gain: bfloat16 [128], P(('ctx', 'fsdp')), may hold values from 0.5 to 1.5
- w_out: bfloat16 [2048, 1024], P(('ctx', 'fsdp')), may hold values from -1.5 to 1.5
- post_gain: bfloat16 [1024], P(('ctx', 'fsdp')), may hold values from 0.5 to 1.5
- w_gate: bfloat16 [1024, 3072], P(('ctx', 'fsdp')), may hold values from -0.1875 to 0.1875
- w_up: bfloat16 [1024, 3072], P(('ctx', 'fsdp')), may hold values from -0.1875 to 0.1875
- w_down: bfloat16 [3072, 1024], P(('ctx', 'fsdp')), may hold values from -0.109375 to 0.109375
- d_out: bfloat16 [4, 2048, 1024], P('fsdp', 'ctx'), may hold values from -6 to 6
Outputs:
- block_out: bfloat16 [4, 2048, 1024], P('fsdp', 'ctx')
- d_hidden: float32 [4, 2048, 1024], P('fsdp', 'ctx')
- grad_in_gain: float32 [1024], P(('ctx', 'fsdp'))
- grad_w_query: float32 [1024, 2048], P(('ctx', 'fsdp'))
- grad_w_key: float32 [1024, 1024], P(('ctx', 'fsdp'))
- grad_w_value: float32 [1024, 1024], P(('ctx', 'fsdp'))
- grad_q_gain: float32 [128], P(('ctx', 'fsdp'))
- grad_k_gain: float32 [128], P(('ctx', 'fsdp'))
- grad_w_out: float32 [2048, 1024], P(('ctx', 'fsdp'))
- grad_post_gain: float32 [1024], P(('ctx', 'fsdp'))
- grad_w_gate: float32 [1024, 3072], P(('ctx', 'fsdp'))
- grad_w_up: float32 [1024, 3072], P(('ctx', 'fsdp'))
- grad_w_down: float32 [3072, 1024], P(('ctx', 'fsdp'))
The draws below stay inside these ranges and needn't reach their ends.
Inputs may be any that keep to these rules, and one draw needn't show every extreme that they name: `seq_lengths`: in every group the 4 lengths sum to 1984, and the longest is exactly 1024.
All inputs are finite; a program needn't handle non-finite values.
Results may differ from the reference program's by a relative error of at most 0.019.
Values may be sent and summed in bfloat16 or wider, within the bound.
A program may use at most 320 MiB of HBM per device.

```python
import math
import jax
import jax.numpy as jnp
import numpy as np
from jax import lax

D = 1024
QUERY_HEADS = 16
KEY_VALUE_HEADS = 8
HEAD_SIZE = 128
FF = 3072
DEVICE_TOKENS = 256
SEQS = 4
QW = 2048
KW = 1024
GROUP = 2048
FILLED = 1984
MOST = 1024
N_CTX = 8
N_FSDP = 4


def levels(key, shape, shards, low, largest):
    factor_of, own = 1.0, jax.random.fold_in(key, 6)
    for dim, blocks in shards:
        heights = jnp.exp(jax.random.uniform(jax.random.fold_in(own, dim), (blocks,), jnp.float32, low / len(shards), largest / len(shards)))
        factor_of = factor_of * jnp.repeat(heights, shape[dim] // blocks).reshape([-1 if axis == dim else 1 for axis in range(len(shape))])
    return factor_of


def length_profile(amount, total, bound, slope):
    weights = [(1 << 20) // math.isqrt(grade ** slope) + 1 for grade in range(2, amount + 1)]
    rest, counts = total - bound - (amount - 1), [1] * (amount - 1)
    while rest > 0:
        free = [i for i in range(amount - 1) if counts[i] < bound]
        whole, budget = sum([weights[i] for i in free]), rest
        for i in free:
            more = min(bound - counts[i], max(1, budget * weights[i] // whole), rest)
            counts[i] = counts[i] + more
            rest = rest - more
    return np.array([bound] + counts)


def ragged(stream_key, count, total, most, lean):
    if count == 2:
        one = jax.random.randint(stream_key, (), max(1, total - most), min(most, total - 1) + 1)
        return jnp.stack([one, total - one])
    sizes = jnp.asarray(length_profile(count, total, most, lean), jnp.int32)
    pairs = (count - 1) // 2
    donor, receiver = sizes[1:1 + 2 * pairs:2], sizes[2:2 + 2 * pairs:2]
    room = jnp.minimum(donor - 1, most - receiver)
    shifted = jax.random.randint(jax.random.fold_in(stream_key, 1), (pairs,), 0, 1 << 20) % (room + 1)
    sizes = sizes.at[1:1 + 2 * pairs:2].set(donor - shifted).at[2:2 + 2 * pairs:2].set(receiver + shifted)
    return sizes[jax.random.permutation(jax.random.fold_in(stream_key, 2), count)]


def bell_draw(rng, dims, width, bound, split=(), held_as=jnp.bfloat16):
    drawn = jax.random.normal(rng, dims, jnp.float32) * width
    if len(split) > 0:
        drawn = levels(rng, dims, split, -0.22, 0.18) * drawn
    return jnp.clip(drawn, min=-bound, max=bound).astype(held_as)


def setup_inputs(seed: int = 0) -> dict:
    arg_keys = jax.random.split(jax.random.key(seed), 15)
    hidden_in = bell_draw(arg_keys[0], (N_FSDP, GROUP, D), 1.0, 6.0, ((0, 4), (1, 8)))
    seq_lengths = jax.vmap(lambda own: ragged(own, SEQS, FILLED, MOST, 2))(jax.random.split(arg_keys[1], N_FSDP)).reshape((N_FSDP, SEQS)).astype(jnp.int32)
    in_gain = jnp.clip(1.0 + 0.1 * jax.random.normal(arg_keys[2], (D,), jnp.float32), 0.5, 1.5).astype(jnp.bfloat16)
    w_query = bell_draw(arg_keys[3], (D, QW), D ** -0.5, 0.1875, ((0, 32),))
    w_key = bell_draw(arg_keys[4], (D, KW), D ** -0.5, 0.1875, ((0, 32),))
    w_value = bell_draw(arg_keys[5], (D, KW), D ** -0.5, 0.1875, ((0, 32),))
    q_gain = jnp.clip(1.0 + 0.1 * jax.random.normal(arg_keys[6], (HEAD_SIZE,), jnp.float32), 0.5, 1.5).astype(jnp.bfloat16)
    k_gain = jnp.clip(1.0 + 0.1 * jax.random.normal(arg_keys[7], (HEAD_SIZE,), jnp.float32), 0.5, 1.5).astype(jnp.bfloat16)
    w_out = bell_draw(arg_keys[8], (QW, D), (QW // 128) ** -0.5, 1.5, ((0, 32),))
    post_gain = jnp.clip(1.0 + 0.1 * jax.random.normal(arg_keys[9], (D,), jnp.float32), 0.5, 1.5).astype(jnp.bfloat16)
    w_gate = bell_draw(arg_keys[10], (D, FF), D ** -0.5, 0.1875, ((0, 32),))
    w_up = bell_draw(arg_keys[11], (D, FF), D ** -0.5, 0.1875, ((0, 32),))
    w_down = bell_draw(arg_keys[12], (FF, D), FF ** -0.5, 0.109375, ((0, 32),))
    d_out = bell_draw(arg_keys[13], (N_FSDP, GROUP, D), 1.0, 6.0, ((0, 4), (1, 8)))
    return dict(hidden_in=hidden_in, seq_lengths=seq_lengths, in_gain=in_gain, w_query=w_query, w_key=w_key, w_value=w_value, q_gain=q_gain, k_gain=k_gain, w_out=w_out, post_gain=post_gain, w_gate=w_gate, w_up=w_up, w_down=w_down, d_out=d_out)


@jax.custom_vjp
def narrow_type(v):
    return lax.optimization_barrier(v.astype(jnp.bfloat16)).astype(jnp.float32)

@jax.custom_vjp
def low_back(v):
    return v

def low_keep(v):
    return (narrow_type(v), None)

def low_pass(kept, grad):
    return (grad,)

def back_keep(v):
    return (v, None)

def back_low(kept, grad):
    return (narrow_type(grad),)
narrow_type.defvjp(low_keep, low_pass)
low_back.defvjp(back_keep, back_low)
epsilon = 1e-06
rope_base = 1000000.0
negative = -1e+30

def row_info(lengths, row_ids, tok_dev, n_ctx):
    half_len = tok_dev // 2
    device = row_ids // tok_dev
    local_row = row_ids % tok_dev
    block_id = jnp.where(local_row < half_len, device, 2 * n_ctx - 1 - device)
    packed = (block_id * half_len + local_row % half_len).astype(jnp.int32)
    seq_ends = jnp.cumsum(lengths).astype(jnp.int32)
    seq_starts = (seq_ends - lengths).astype(jnp.int32)
    member = (packed[:, None] >= seq_starts[None, :]) & (packed[:, None] < seq_ends[None, :])
    row_valid = jnp.any(member, axis=1)
    numbers = jnp.arange(lengths.shape[0], dtype=jnp.int32)
    seq_id = lax.optimization_barrier(jnp.sum(jnp.where(member, numbers[None, :], 0), axis=1)).astype(jnp.int32)
    offset = lax.optimization_barrier(jnp.sum(jnp.where(member, seq_starts[None, :], 0), axis=1)).astype(jnp.int32)
    segment = jnp.where(row_valid, seq_id, -1 - packed).astype(jnp.int32)
    position = jnp.where(row_valid, packed - offset, 0).astype(jnp.int32)
    return (segment, position, row_valid)

def norm_gain(values_in, gain_vec):
    row_scale = lax.rsqrt(lax.optimization_barrier(jnp.mean(values_in * values_in, axis=-1, keepdims=True)) + epsilon)
    return values_in * row_scale * gain_vec

def rotary(position, head_dim):
    half_len = head_dim // 2
    inv_freq = jnp.power(rope_base, -jnp.arange(half_len, dtype=jnp.float32) * (2.0 / head_dim))
    angles = position.astype(jnp.float32)[:, None] * inv_freq[None, :]
    angles = jnp.concatenate([angles, angles], axis=1)
    return (jnp.cos(angles), jnp.sin(angles))

def rotate(heads, cos_table, sin_table):
    half_len = heads.shape[-1] // 2
    turned = jnp.concatenate([-heads[..., half_len:], heads[..., :half_len]], axis=-1)
    return heads * cos_table[:, None, :] + turned * sin_table[:, None, :]

def head_post(q_in, k_in, q_scale, k_scale, cos_table, sin_table):
    head_dim = q_scale.shape[0]
    row_count = q_in.shape[0]
    q_heads = norm_gain(q_in.reshape(row_count, -1, head_dim), q_scale)
    k_heads = norm_gain(k_in.reshape(row_count, -1, head_dim), k_scale)
    query_rotated = rotate(q_heads, cos_table, sin_table).reshape(row_count, -1)
    key_rotated = rotate(k_heads, cos_table, sin_table).reshape(row_count, -1)
    return (query_rotated, key_rotated)

def matmul(left, right):
    return jnp.dot(left, right, precision=lax.Precision.HIGHEST, preferred_element_type=jnp.float32)

def group_forward(x_group, lengths, weights):
    g_in, w_q, w_k, w_v, g_q, g_k, w_o, g_post, w_g, w_u, w_d = weights
    rows_per_group = x_group.shape[0]
    group_count = QUERY_HEADS // KEY_VALUE_HEADS
    score_scale = HEAD_SIZE ** (-0.5)
    row_ids = jnp.arange(rows_per_group, dtype=jnp.int32)
    segment, position, row_valid = row_info(lengths, row_ids, DEVICE_TOKENS, N_CTX)
    x_norm = narrow_type(norm_gain(x_group, g_in))
    q_pre = low_back(matmul(x_norm, w_q))
    k_pre = low_back(matmul(x_norm, w_k))
    value_projected = low_back(matmul(x_norm, w_v))
    cos_table, sin_table = rotary(position, HEAD_SIZE)
    query_rotated, key_rotated = head_post(q_pre, k_pre, g_q, g_k, cos_table, sin_table)
    query_narrow = narrow_type(query_rotated).reshape(N_CTX, DEVICE_TOKENS, KEY_VALUE_HEADS, group_count, HEAD_SIZE)
    key_narrow = narrow_type(key_rotated).reshape(rows_per_group, KEY_VALUE_HEADS, HEAD_SIZE)
    value_narrow = narrow_type(value_projected).reshape(rows_per_group, KEY_VALUE_HEADS, HEAD_SIZE)
    seg_blocks = segment.reshape(N_CTX, DEVICE_TOKENS)
    pos_blocks = position.reshape(N_CTX, DEVICE_TOKENS)

    def attend(item):
        q_part, seg_part, pos_part = item
        score = low_back(jnp.einsum('qhgd,khd->hgqk', q_part, key_narrow, precision=lax.Precision.HIGHEST) * score_scale)
        allowed = ((seg_part[:, None] == segment[None, :]) & (position[None, :] <= pos_part[:, None]))[None, None]
        row_max = lax.optimization_barrier(jnp.max(jnp.where(allowed, score, negative), axis=-1, keepdims=True))
        expo = jnp.where(allowed, jnp.exp(score - row_max), 0.0)
        totals = lax.optimization_barrier(jnp.sum(expo, axis=-1))
        weighted = jnp.einsum('hgqk,khd->hgqd', narrow_type(expo), value_narrow, precision=lax.Precision.HIGHEST) / totals[..., None]
        return jnp.transpose(weighted, (2, 0, 1, 3)).reshape(q_part.shape[0], -1)
    attn = lax.map(jax.checkpoint(attend), (query_narrow, seg_blocks, pos_blocks)).reshape(rows_per_group, -1)
    attn_low = narrow_type(low_back(attn))
    h_mid = x_group + low_back(matmul(attn_low, w_o))
    h_norm = narrow_type(norm_gain(h_mid, g_post))
    gate_out = low_back(matmul(h_norm, w_g))
    up_out = low_back(matmul(h_norm, w_u))
    act_low = narrow_type(jax.nn.silu(gate_out) * up_out)
    mlp_out = low_back(matmul(act_low, w_d))
    return row_valid.astype(jnp.float32)[:, None] * (h_mid + mlp_out)

def reference(hidden_in, seq_lengths, in_gain, w_query, w_key, w_value, q_gain, k_gain, w_out, post_gain, w_gate, w_up, w_down, d_out):
    params = (in_gain.astype(jnp.float32), w_query.astype(jnp.float32), w_key.astype(jnp.float32), w_value.astype(jnp.float32), q_gain.astype(jnp.float32), k_gain.astype(jnp.float32), w_out.astype(jnp.float32), post_gain.astype(jnp.float32), w_gate.astype(jnp.float32), w_up.astype(jnp.float32), w_down.astype(jnp.float32))

    def forward(x_all, weights):

        def one_group(pair):
            return group_forward(pair[0], pair[1], weights)
        return lax.map(jax.checkpoint(one_group), (x_all, seq_lengths))
    block_out, pull_back = jax.vjp(forward, hidden_in.astype(jnp.float32), params)
    d_hidden, grads = pull_back(d_out.astype(jnp.float32))
    return (block_out.astype(jnp.bfloat16), d_hidden, grads[0], grads[1], grads[2], grads[3], grads[4], grads[5], grads[6], grads[7], grads[8], grads[9], grads[10])
```

```python
import functools
import math

import jax
import jax.numpy as jnp
from jax import lax
from jax.experimental import pallas as pl
from jax.experimental.pallas import tpu as pltpu
from jax.sharding import PartitionSpec as P

BF = jnp.bfloat16
F32 = jnp.float32
MESH = pl.DeviceIdType.MESH
VMEM = pl.BlockSpec(memory_space=pltpu.VMEM)
GAIN_ROWS = 24
LANES = 128
TILE = 256
LIMIT = 60 * 2**20


def dot(a, b):
    return jnp.dot(a, b, preferred_element_type=F32)


def dot_rt(a, b):
    return lax.dot_general(a, b, (((1,), (1,)), ((), ())), preferred_element_type=F32)


def dot_lt(a, b):
    return lax.dot_general(a, b, (((0,), (0,)), ((), ())), preferred_element_type=F32)


def flip(place, mask, size):
    out, bit = 0, 1
    while bit < size:
        out = out + bit * lax.rem(lax.div(place, bit) + (mask // bit) % 2, 2)
        bit *= 2
    return out


class Net:
    def __init__(self, n, nz, send, recv):
        self.n, self.nz, self.send, self.recv = n, nz, send, recv
        self.c = lax.axis_index("ctx")
        self.z = lax.axis_index("fsdp")

    def at(self, mask):
        return flip(self.c, mask, self.n)

    def zat(self, mask):
        return flip(self.z, mask, self.nz)

    def peer(self, mask):
        return (self.at(mask), self.z)

    def zpeer(self, mask):
        return (self.c, self.zat(mask))

    def barrier(self):
        bar = pltpu.get_barrier_semaphore()
        for mask in range(1, self.n):
            pl.semaphore_signal(bar, inc=1, device_id=self.peer(mask), device_id_type=MESH)
        for mask in range(1, self.nz):
            pl.semaphore_signal(bar, inc=1, device_id=self.zpeer(mask), device_id_type=MESH)
        pl.semaphore_wait(bar, self.n + self.nz - 2)

    def copy(self, src, dst, slot, device):
        return pltpu.make_async_remote_copy(
            src_ref=src,
            dst_ref=dst,
            send_sem=self.send.at[slot],
            recv_sem=self.recv.at[slot],
            device_id=device,
            device_id_type=MESH,
        )


class Gather:
    def __init__(self, net, src, buf, base):
        self.net, self.buf, self.base = net, buf, base
        self.copies = {}
        evens = list(range(2, net.n, 2))
        for mask in [1] + evens[::-1]:
            cp = net.copy(src, buf.at[net.c], base + mask, net.peer(mask))
            cp.start()
            self.copies[mask] = cp

    def arrive(self, mask):
        net = self.net
        self.copies[mask].wait_recv()
        if mask % 2 == 0:
            d = net.at(mask)
            cp = net.copy(self.buf.at[d], self.buf.at[d], self.base + mask + 1, net.peer(1))
            cp.start()
            self.copies[mask + 1] = cp

    def finish(self):
        for cp in self.copies.values():
            cp.wait_send()


class PlaneSum:
    def __init__(self, net, sib_out, sib_in, out, inn, keep, base):
        self.net, self.base = net, base
        self.sib_out, self.sib_in, self.out, self.inn, self.keep = sib_out, sib_in, out, inn, keep
        self.copies = []
        self.pending = {}

    def give_sibling(self, mask, value):
        i = mask // 2
        self.sib_out[i] = value.astype(BF)
        cp = self.net.copy(self.sib_out.at[i], self.sib_in.at[i], self.base + mask + 1, self.net.peer(1))
        cp.start()
        self.copies.append(cp)
        self.pending[mask] = cp

    def give(self, mask, value):
        i = mask // 2
        self.pending[mask].wait_recv()
        both = value + self.sib_in[i].astype(F32)
        if mask == 0:
            self.keep[...] = both
            return
        self.out[i - 1] = both.astype(BF)
        cp = self.net.copy(self.out.at[i - 1], self.inn.at[i - 1], self.base + mask, self.net.peer(mask))
        cp.start()
        self.copies.append(cp)
        self.pending[mask] = cp

    def total(self):
        for mask in range(2, self.net.n, 2):
            self.pending[mask].wait_recv()
        value = self.keep[...]
        for i in range(self.net.n // 2 - 1):
            value = value + self.inn[i].astype(F32)
        return value

    def finish(self):
        for cp in self.copies:
            cp.wait_send()


def plane_sum_scratch(n, rows, width):
    half = n // 2
    return [
        pltpu.VMEM((half, rows, width), BF),
        pltpu.VMEM((half, rows, width), BF),
        pltpu.VMEM((half - 1, rows, width), BF),
        pltpu.VMEM((half - 1, rows, width), BF),
        pltpu.VMEM((rows, width), F32),
    ]


def row_of(g, first, count):
    return jnp.concatenate([g[first + j : first + j + 1, :] for j in range(count)], axis=1)


def half_places(net, d, half):
    per = TILE // half
    blocks = (d, 2 * net.n - 1 - d)
    return [(lax.div(b, per), pl.multiple_of(lax.rem(b, per) * half, half)) for b in blocks]


def gather_qkv(cfg, x_ref, wqkv_ref, gu_ref, wo_ref, gains_ref, cos_ref, sin_ref,
               xn_ref, q_ref, k_ref, v_ref, pre_ref, gu_out, wo_out, w_ref, gains_out,
               xg, gbuf, gz, send, recv):
    n, nz, ql, kvl, hd = cfg["n"], cfg["nz"], cfg["ql"], cfg["kvl"], cfg["hd"]
    t, dm = x_ref.shape
    net = Net(n, nz, send, recv)
    c, z = net.c, net.z
    net.barrier()
    slot = 0
    plane = []
    for mask in range(1, n):
        cp = net.copy(gains_ref, gbuf.at[c], slot + mask, net.peer(mask))
        cp.start()
        plane.append(cp)
    slot += n
    for mask in range(1, n):
        cp = net.copy(wqkv_ref.at[net.at(mask)], w_ref.at[c, z], slot + mask, net.peer(mask))
        cp.start()
        plane.append(cp)
    slot += n
    line = []
    for mask in range(1, nz):
        cp = net.copy(wo_ref, wo_out.at[z], slot + mask, net.zpeer(mask))
        cp.start()
        line.append(cp)
    slot += nz
    gath = Gather(net, x_ref, xg, slot)
    slot += n
    late = []
    for mask in range(1, n):
        cp = net.copy(gu_ref.at[net.at(mask)], gu_out.at[c], slot + mask, net.peer(mask))
        cp.start()
        late.append(cp)
    slot += n
    gbuf[c] = gains_ref[...]
    w_ref[c, z] = wqkv_ref[c]
    gu_out[c] = gu_ref[c]
    wo_out[z] = wo_ref[...]
    xg[c] = x_ref[...]
    for cp in plane[: n - 1]:
        cp.wait_recv()
    gz[z] = jnp.sum(gbuf[...], axis=0)
    gains_line = []
    for mask in range(1, nz):
        cp = net.copy(gz.at[z], gz.at[z], slot + mask, net.zpeer(mask))
        cp.start()
        gains_line.append(cp)
    slot += nz
    for cp in plane[n - 1 :]:
        cp.wait_recv()
    for mask in range(1, nz):
        cp = net.copy(w_ref.at[:, z], w_ref.at[:, z], slot + mask, net.zpeer(mask))
        cp.start()
        line.append(cp)
    slot += nz
    for cp in gains_line:
        cp.wait_recv()
    gains = jnp.sum(gz[...], axis=0)
    gains_out[...] = gains
    g_in = row_of(gains, 0, dm // LANES)
    g_q = gains[16:17, :]
    g_k = gains[17:18, :]
    step = 32

    def normalise(d):
        def rows(i, carry):
            at = pl.ds(pl.multiple_of(i * step, step), step)
            x = xg[d, at, :].astype(F32)
            r = lax.rsqrt(jnp.mean(x * x, axis=-1, keepdims=True) + cfg["eps"])
            xn_ref[d, at, :] = (x * r * g_in).astype(BF)
            return carry

        lax.fori_loop(0, t // step, rows, 0)

    order = [0, 1] + [m for e in range(2, n, 2) for m in (e,)] + [m for e in range(2, n, 2) for m in (e + 1,)]
    for mask in order:
        if mask:
            gath.arrive(mask)
        normalise(net.at(mask))
    for cp in line:
        cp.wait_recv()
    w = w_ref[...].reshape(dm, -1)

    def head_block(d, carry):
        qkv = dot(xn_ref[d], w)
        width = (ql + kvl) * hd
        pre_ref[d] = qkv[:, :width]
        cos, sin = cos_ref[d], sin_ref[d]
        places = half_places(net, d, t // 2)
        for h in range(ql + kvl):
            v = qkv[:, h * hd : (h + 1) * hd]
            r = lax.rsqrt(jnp.mean(v * v, axis=-1, keepdims=True) + cfg["eps"])
            hat = v * r * (g_q if h < ql else g_k)
            low = (hat * cos + pltpu.roll(hat, hd // 2, 1) * sin).astype(BF)
            for s, (tile, row) in enumerate(places):
                part = low[s * (t // 2) : (s + 1) * (t // 2)]
                if h < ql:
                    q_ref[tile, h, pl.ds(row, t // 2), :] = part
                else:
                    k_ref[tile, h - ql, pl.ds(row, t // 2), :] = part
        for h in range(kvl):
            low = qkv[:, width + h * hd : width + (h + 1) * hd].astype(BF)
            for s, (tile, row) in enumerate(places):
                v_ref[tile, h, pl.ds(row, t // 2), :] = low[s * (t // 2) : (s + 1) * (t // 2)]
        return carry

    lax.fori_loop(0, n, head_block, 0)
    for cp in late:
        cp.wait_recv()
    gath.finish()
    for cp in plane + line + gains_line + late:
        cp.wait_send()


def attend(cfg, q_ref, k_ref, v_ref, start_ref, db_ref, gu_ref,
           attn_ref, qx_ref, dblk_ref, gu_out,
           vx, acc, send, recv):
    n, nz, ql, hd = cfg["n"], cfg["nz"], cfg["ql"], cfg["hd"]
    tiles = q_ref.shape[0]
    net = Net(n, nz, send, recv)
    c, z = net.c, net.z
    net.barrier()
    line = []
    for mask in range(1, nz):
        cp = net.copy(gu_ref, gu_out.at[:, z], mask, net.zpeer(mask))
        cp.start()
        line.append(cp)
    gath = Gather(net, db_ref, dblk_ref, nz)
    gu_out[:, z] = gu_ref[...]
    dblk_ref[c] = db_ref[...]
    rows = ql * TILE
    factor = math.log2(math.e) / math.sqrt(hd)
    vx[:, :, :hd] = v_ref[:, 0]
    vx[:, :, hd:] = jnp.ones((tiles, TILE, hd), BF)
    lane = lax.broadcasted_iota(jnp.int32, (rows, hd), 1)

    def q_tile(i, carry):
        q = q_ref[i].reshape(rows, hd)
        start = start_ref[pl.ds(pl.multiple_of(i * TILE, TILE), TILE), :]
        q_at = i * TILE + lax.broadcasted_iota(jnp.int32, (TILE, TILE), 0)
        acc[...] = jnp.zeros_like(acc)

        def k_tile(j, carry):
            s = dot_rt(q, k_ref[j, 0])
            k_at = j * TILE + lax.broadcasted_iota(jnp.int32, (TILE, TILE), 1)
            allowed = (k_at <= q_at) & (k_at >= start)
            e = jnp.where(allowed[None], jnp.exp2(s * factor).reshape(ql, TILE, TILE), 0.0)
            acc[...] += dot(e.astype(BF).reshape(rows, TILE), vx[j])
            return carry

        lax.fori_loop(jnp.maximum(i - cfg["window"], 0), i + 1, k_tile, 0)
        total = acc[:, hd:]
        attn = acc[:, :hd] / total
        for h in range(ql):
            attn_ref[pl.ds(pl.multiple_of(i * TILE, TILE), TILE), h * hd : (h + 1) * hd] = attn[
                h * TILE : (h + 1) * TILE
            ].astype(BF)
        extra = jnp.log(total) * math.sqrt(hd)
        qx_ref[i, :, :, :hd] = q_ref[i]
        qx_ref[i, :, :, hd:] = split_three(extra, lane).reshape(ql, TILE, hd)
        return carry

    lax.fori_loop(0, tiles, q_tile, 0)
    for mask in list(range(2, n, 2)) + [1] + list(range(3, n, 2)):
        gath.arrive(mask)
    for cp in line:
        cp.wait_recv()
    gath.finish()
    for cp in line:
        cp.wait_send()


def split_three(value, lane):
    first = value.astype(BF).astype(F32)
    rest = value - first
    second = rest.astype(BF).astype(F32)
    third = rest - second
    out = jnp.where(lane == 0, first, jnp.where(lane == 1, second, jnp.where(lane == 2, third, 0.0)))
    return out.astype(BF)


def feed(cfg, attn_ref, x_ref, dblk_ref, wo_ref, gu_ref, wd_ref, gains_ref,
         mo_ref, dax_ref, hmid_ref, dhmid_ref, gwo_ref, gwd_ref, ggu_ref, gpost_ref,
         wd_all, hn, act, dgu, dres, gwd_buf, ggu_buf, gwd_in, ggu_in, *rest):
    n, nz, ql, hd, ff = cfg["n"], cfg["nz"], cfg["ql"], cfg["hd"], cfg["ff"]
    first, second, (hres, send, recv) = rest[:5], rest[5:10], rest[10:]
    t, dm = x_ref.shape
    half = t // 2
    net = Net(n, nz, send, recv)
    c, z = net.c, net.z
    net.barrier()
    slot = 0
    line = []
    for mask in range(1, nz):
        cp = net.copy(wd_ref, wd_all.at[z], slot + mask, net.zpeer(mask))
        cp.start()
        line.append(cp)
    slot += nz
    wd_all[z] = wd_ref[...]
    wo = wo_ref[...].reshape(-1, dm)

    def attn_rows(d):
        return jnp.concatenate(
            [attn_ref[pl.ds(pl.multiple_of(b * half, half), half), :] for b in (d, 2 * n - 1 - d)], axis=0
        )

    sum1 = PlaneSum(net, *first, slot)
    slot += n
    for mask in list(range(2, n, 2))[::-1] + [0]:
        sum1.give_sibling(mask, dot(attn_rows(net.at(mask + 1)), wo))
        sum1.give(mask, dot(attn_rows(net.at(mask)), wo))
    g_post = row_of(gains_ref[...], 8, dm // LANES)
    h_mid = x_ref[...].astype(F32) + sum1.total()
    hmid_ref[...] = h_mid
    r_mid = lax.rsqrt(jnp.mean(h_mid * h_mid, axis=-1, keepdims=True) + cfg["eps"])
    hres[...] = (h_mid * r_mid * g_post).astype(BF)
    gath1 = Gather(net, hres, hn, slot)
    slot += n
    hn[c] = hres[...]
    for cp in line:
        cp.wait_recv()
    wgu = gu_ref[...].reshape(dm, -1)
    wd = wd_all[...].reshape(-1, dm)

    def block(d):
        gu = dot(hn[d], wgu)
        gate, up = gu[:, :ff], gu[:, ff:]
        sig = 1.0 / (1.0 + jnp.exp(-gate))
        silu = gate * sig
        low = (silu * up).astype(BF)
        act[d] = low
        mo_ref[d] = dot(low, wd).astype(BF)
        d_act = dot_rt(dblk_ref[d], wd)
        d_gate = (d_act * up * sig * (1.0 + gate * (1.0 - sig))).astype(BF)
        d_up = (d_act * silu).astype(BF)
        dgu[d, :, :ff] = d_gate
        dgu[d, :, ff:] = d_up
        return dot_rt(dgu[d], wgu)

    sum2 = PlaneSum(net, *second, slot)
    slot += n
    for mask in range(0, n, 2):
        if mask:
            gath1.arrive(mask)
            gath1.arrive(mask + 1)
        else:
            gath1.arrive(1)
        sum2.give_sibling(mask, block(net.at(mask + 1)))
        sum2.give(mask, block(net.at(mask)))
    rows = n * t
    dgu_all = dgu[...].reshape(rows, 2 * ff)
    gwd_buf[...] = dot_lt(act[...].reshape(rows, ff), dblk_ref[...].reshape(rows, dm)).astype(BF).reshape(gwd_buf.shape)
    gline = []
    for mask in range(1, nz):
        cp = net.copy(gwd_buf.at[net.zat(mask)], gwd_in.at[mask - 1], slot + mask, net.zpeer(mask))
        cp.start()
        gline.append(cp)
    slot += nz
    per = dm // n
    cols = 2
    wide = dm // cols
    for j in range(cols):
        part = dot_lt(hn[:, :, j * wide : (j + 1) * wide].reshape(rows, wide), dgu_all)
        ggu_buf[j * (n // cols) : (j + 1) * (n // cols)] = part.astype(BF).reshape(n // cols, nz, per // nz, 2 * ff)
    for mask in range(1, nz):
        cp = net.copy(ggu_buf.at[:, net.zat(mask)], ggu_in.at[mask - 1], slot + mask, net.zpeer(mask))
        cp.start()
        gline.append(cp)
    slot += nz
    d_hn = sum2.total()
    v = hmid_ref[...]
    r = lax.rsqrt(jnp.mean(v * v, axis=-1, keepdims=True) + cfg["eps"])
    gpost_ref[...] = jnp.sum(d_hn * v * r, axis=0, keepdims=True)
    gdy = g_post * d_hn
    d_hmid = dblk_ref[c].astype(F32) + r * gdy - v * (r * r * r) * jnp.mean(gdy * v, axis=-1, keepdims=True)
    dhmid_ref[...] = d_hmid
    gath1.finish()
    hres[...] = d_hmid.astype(BF)
    gath2 = Gather(net, hres, dres, slot)
    slot += n
    dres[c] = hres[...]
    lane = lax.broadcasted_iota(jnp.int32, (half, hd), 1)

    def back(d):
        d_attn = dot_rt(dres[d], wo)
        for s, (tile, row) in enumerate(half_places(net, d, half)):
            b = (d, 2 * n - 1 - d)[s]
            attn = attn_ref[pl.ds(pl.multiple_of(b * half, half), half), :].astype(F32)
            low = d_attn[s * half : (s + 1) * half].astype(BF)
            prod = low.astype(F32) * attn
            for h in range(ql):
                delta = jnp.sum(prod[:, h * hd : (h + 1) * hd], axis=-1, keepdims=True)
                dax_ref[tile, h, pl.ds(row, half), :hd] = low[:, h * hd : (h + 1) * hd]
                dax_ref[tile, h, pl.ds(row, half), hd:] = split_three(jnp.broadcast_to(delta, (half, hd)), lane)

    back(c)
    for mask in [1] + list(range(2, n, 2)) + list(range(3, n, 2)):
        gath2.arrive(mask)
        back(net.at(mask))
    total = None
    for s in range(2):
        blocks = attn_ref[s * (rows // 2) : (s + 1) * (rows // 2), :]
        if s:
            blocks = jnp.concatenate([blocks[(n - 1 - i) * half : (n - i) * half] for i in range(n)], axis=0)
        part = dot_lt(blocks, dres[:, s * half : (s + 1) * half, :].reshape(n * half, dm))
        total = part if total is None else total + part
    gwo_ref[...] = total.astype(BF).reshape(gwo_ref.shape)
    for cp in gline:
        cp.wait_recv()
    gwd = gwd_buf[z].astype(F32)
    ggu = ggu_buf[:, z].astype(F32)
    for i in range(nz - 1):
        gwd = gwd + gwd_in[i].astype(F32)
        ggu = ggu + ggu_in[i].astype(F32)
    gwd_ref[...] = gwd
    ggu_ref[...] = ggu.astype(BF)
    for part in (sum1, sum2, gath2):
        part.finish()
    for cp in line + gline:
        cp.wait_send()


def attend_back(cfg, qx_ref, k_ref, v_ref, dax_ref, start_ref, mo_ref, hmid_ref, valid_ref, gwo_ref, ggu_ref,
                dq_ref, dk_ref, dv_ref, block_ref, gwo_out, ggate_ref, gup_ref,
                kx, vx, dk_acc, dv_acc, gwo_in, ggu_in, *rest):
    n, nz, ql, hd, ff = cfg["n"], cfg["nz"], cfg["ql"], cfg["hd"], cfg["ff"]
    sums, (send, recv) = rest[:5], rest[5:]
    tiles = qx_ref.shape[0]
    net = Net(n, nz, send, recv)
    c, z = net.c, net.z
    net.barrier()
    slot = 0
    sum1 = PlaneSum(net, *sums, slot)
    slot += n
    for mask in list(range(2, n, 2))[::-1] + [0]:
        sum1.give_sibling(mask, mo_ref[net.at(mask + 1)])
    for mask in list(range(2, n, 2))[::-1] + [0]:
        sum1.give(mask, mo_ref[net.at(mask)].astype(F32))
    line = []
    for mask in range(1, nz):
        cp = net.copy(gwo_ref.at[net.zat(mask)], gwo_in.at[mask - 1], slot + mask, net.zpeer(mask))
        cp.start()
        line.append(cp)
    slot += nz
    for mask in range(1, n):
        cp = net.copy(ggu_ref.at[net.at(mask)], ggu_in.at[c], slot + mask, net.peer(mask))
        cp.start()
        line.append(cp)
    slot += n
    ggu_in[c] = ggu_ref[c]
    rows = ql * TILE
    factor = math.log2(math.e) / math.sqrt(hd)
    scale = 1.0 / math.sqrt(hd)
    lane = lax.broadcasted_iota(jnp.int32, (tiles, TILE, hd), 2)
    minus = jnp.where(lane < 3, -1.0, 0.0).astype(BF)
    kx[:, :, :hd] = k_ref[:, 0]
    kx[:, :, hd:] = minus
    vx[:, :, :hd] = v_ref[:, 0]
    vx[:, :, hd:] = minus
    dq_ref[...] = jnp.zeros_like(dq_ref)

    def k_tile(j, carry):
        k_at = j * TILE + lax.broadcasted_iota(jnp.int32, (TILE, TILE), 0)
        dk_acc[...] = jnp.zeros_like(dk_acc)
        dv_acc[...] = jnp.zeros_like(dv_acc)

        def q_tile(i, carry):
            qx = qx_ref[i].reshape(rows, 2 * hd)
            dax = dax_ref[i].reshape(rows, 2 * hd)
            start = start_ref[:, pl.ds(pl.multiple_of(i * TILE, TILE), TILE)]
            q_at = i * TILE + lax.broadcasted_iota(jnp.int32, (TILE, TILE), 1)
            allowed = (k_at <= q_at) & (k_at >= start)
            allowed = jnp.concatenate([allowed] * ql, axis=1)
            s = dot_rt(kx[j], qx)
            p = jnp.where(allowed, jnp.exp2(s * factor), 0.0)
            ds = (p * dot_rt(vx[j], dax)).astype(BF)
            dv_acc[...] += dot(p.astype(BF), dax[:, :hd])
            dk_acc[...] += dot(ds, qx[:, :hd])
            dq_ref[i] += dot_lt(ds, k_ref[j, 0])
            return carry

        lax.fori_loop(j, jnp.minimum(j + cfg["window"], tiles - 1) + 1, q_tile, 0)
        dk_ref[j] = dk_acc[...] * scale
        dv_ref[j] = dv_acc[...]
        return carry

    lax.fori_loop(0, tiles, k_tile, 0)
    dq_ref[...] = dq_ref[...] * scale
    for cp in line:
        cp.wait_recv()
    gwo = gwo_ref[z].astype(F32)
    for i in range(nz - 1):
        gwo = gwo + gwo_in[i].astype(F32)
    gwo_out[...] = gwo
    for d in range(n):
        both = ggu_in[d].astype(F32)
        ggate_ref[:, d * ff : (d + 1) * ff] = both[:, :ff]
        gup_ref[:, d * ff : (d + 1) * ff] = both[:, ff:]
    block_ref[...] = (valid_ref[...] * (hmid_ref[...] + sum1.total())).astype(BF)
    sum1.finish()
    for cp in line:
        cp.wait_send()


def head_back(cfg, pre_ref, dq_ref, dk_ref, dv_ref, cos_ref, sin_ref, gains_ref, xn_ref, w_ref, x_ref, dhmid_ref,
              gpost_ref,
              dx_ref, gq_ref, gk_ref, gv_ref, gains_out,
              dqkv, gbuf, g_in_line, gsum, g_in, part, gplane, gz, *rest):
    n, nz, ql, kvl, hd = cfg["n"], cfg["nz"], cfg["ql"], cfg["kvl"], cfg["hd"]
    sums, (send, recv) = rest[:5], rest[5:]
    t, dm = x_ref.shape
    half = t // 2
    net = Net(n, nz, send, recv)
    c, z = net.c, net.z
    net.barrier()
    gains = gains_ref[...]
    w = w_ref[...].reshape(dm, -1)

    def head_block(d, carry):
        pre = pre_ref[d]
        cos, sin = cos_ref[d], sin_ref[d]
        places = half_places(net, d, half)
        new = []
        for h in range(ql + kvl):
            if h < ql:
                dy = jnp.concatenate([dq_ref[tile, pl.ds(h * TILE + row, half), :] for tile, row in places], axis=0)
            else:
                dy = jnp.concatenate([dk_ref[tile, pl.ds(row, half), :] for tile, row in places], axis=0)
            g = gains[16:17, :] if h < ql else gains[17:18, :]
            v = pre[:, h * hd : (h + 1) * hd]
            r = lax.rsqrt(jnp.mean(v * v, axis=-1, keepdims=True) + cfg["eps"])
            dy = dy * cos - pltpu.roll(dy, hd // 2, 1) * sin
            new.append(jnp.sum(dy * v * r, axis=0, keepdims=True))
            gdy = g * dy
            dv = r * gdy - v * (r * r * r) * jnp.mean(gdy * v, axis=-1, keepdims=True)
            dqkv[d, :, h * hd : (h + 1) * hd] = dv.astype(BF)
        dv = jnp.concatenate([dv_ref[tile, pl.ds(row, half), :] for tile, row in places], axis=0)
        dqkv[d, :, (ql + kvl) * hd :] = dv.astype(BF)
        q_sum = sum(new[1:ql], new[0])
        k_sum = sum(new[ql + 1 :], new[ql])
        return (carry[0] + q_sum, carry[1] + k_sum)

    zero = jnp.zeros((1, hd), F32)
    gq, gk = lax.fori_loop(0, n, head_block, (zero, zero))
    rows = n * t
    per = dm // n
    cols = 2
    wide = dm // cols
    d_all = dqkv[...].reshape(rows, -1)
    for j in range(cols):
        grad = dot_lt(xn_ref[:, :, j * wide : (j + 1) * wide].reshape(rows, wide), d_all)
        gbuf[j * (n // cols) : (j + 1) * (n // cols)] = grad.astype(BF).reshape(n // cols, nz, per // nz, -1)
    slot = 0
    line = []
    for mask in range(1, nz):
        cp = net.copy(gbuf.at[:, net.zat(mask)], g_in_line.at[mask - 1], slot + mask, net.zpeer(mask))
        cp.start()
        line.append(cp)
    slot += nz
    sum1 = PlaneSum(net, *sums, slot)
    slot += n
    for mask in list(range(2, n, 2))[::-1] + [0]:
        sum1.give_sibling(mask, dot_rt(dqkv[net.at(mask + 1)], w))
        sum1.give(mask, dot_rt(dqkv[net.at(mask)], w))
    for cp in line:
        cp.wait_recv()
    total = gbuf[:, z].astype(F32)
    for i in range(nz - 1):
        total = total + g_in_line[i].astype(F32)
    gsum[...] = total.astype(BF)
    plane = []
    for mask in range(1, n):
        cp = net.copy(gsum.at[net.at(mask)], g_in.at[c], slot + mask, net.peer(mask))
        cp.start()
        plane.append(cp)
    slot += n
    g_in[c] = gsum[c]
    d_xn = sum1.total()
    x = x_ref[...].astype(F32)
    g = row_of(gains, 0, dm // LANES)
    r = lax.rsqrt(jnp.mean(x * x, axis=-1, keepdims=True) + cfg["eps"])
    grad_in = jnp.sum(d_xn * x * r, axis=0, keepdims=True)
    gdy = g * d_xn
    dx_ref[...] = dhmid_ref[...] + r * gdy - x * (r * r * r) * jnp.mean(gdy * x, axis=-1, keepdims=True)
    part[...] = jnp.zeros_like(part)
    for j in range(dm // LANES):
        part[j : j + 1, :] = grad_in[:, j * LANES : (j + 1) * LANES]
        part[8 + j : 9 + j, :] = gpost_ref[:, j * LANES : (j + 1) * LANES]
    part[16:17, :] = gq
    part[17:18, :] = gk
    small = []
    for mask in range(1, n):
        cp = net.copy(part, gplane.at[c], slot + mask, net.peer(mask))
        cp.start()
        small.append(cp)
    slot += n
    gplane[c] = part[...]
    for cp in small:
        cp.wait_recv()
    gz[z] = jnp.sum(gplane[...], axis=0)
    last = []
    for mask in range(1, nz):
        cp = net.copy(gz.at[z], gz.at[z], slot + mask, net.zpeer(mask))
        cp.start()
        last.append(cp)
    for cp in plane:
        cp.wait_recv()
    qw, kw = ql * hd, kvl * hd
    for d in range(n):
        both = g_in[d].astype(F32)
        gq_ref[:, d * qw : (d + 1) * qw] = both[:, :qw]
        gk_ref[:, d * kw : (d + 1) * kw] = both[:, qw : qw + kw]
        gv_ref[:, d * kw : (d + 1) * kw] = both[:, qw + kw :]
    for cp in last:
        cp.wait_recv()
    gains_out[...] = jnp.sum(gz[...], axis=0)
    sum1.finish()
    for cp in line + plane + small + last:
        cp.wait_send()


def call(body, cfg, outs, scratch, cid, *args):
    slots = cfg["slots"]
    return pl.pallas_call(
        functools.partial(body, cfg),
        out_shape=[jax.ShapeDtypeStruct(shape, dtype) for shape, dtype in outs],
        in_specs=[VMEM] * len(args),
        out_specs=[VMEM] * len(outs),
        scratch_shapes=scratch + [pltpu.SemaphoreType.DMA((slots,)), pltpu.SemaphoreType.DMA((slots,))],
        compiler_params=pltpu.CompilerParams(collective_id=cid, has_side_effects=True, vmem_limit_bytes=LIMIT),
        name=body.__name__,
    )(*args)


def rope_base_tables(pos, hd):
    half = hd // 2
    inv = jnp.power(1000000.0, -jnp.arange(half, dtype=F32) * (2.0 / hd))
    angles = pos.astype(F32)[:, None] * inv[None, :]
    cos, sin = jnp.cos(angles), jnp.sin(angles)
    return jnp.concatenate([cos, cos], axis=1), jnp.concatenate([-sin, sin], axis=1)


def on_plane(hidden_in, seq_lengths, in_gain, w_query, w_key, w_value, q_gain, k_gain, w_out, post_gain,
             w_gate, w_up, w_down, d_out):
    n, nz = lax.axis_size("ctx"), lax.axis_size("fsdp")
    c, z = lax.axis_index("ctx"), lax.axis_index("fsdp")
    t, dm = hidden_in.shape[1:]
    half = t // 2
    rows = n * t
    hd = q_gain.shape[0] * n * nz
    ql = w_query.shape[1] // hd // n
    kvl = w_key.shape[1] // hd // n
    ff = w_gate.shape[1] // n
    r_in, r_out, r_down = w_query.shape[0], w_out.shape[0], w_down.shape[0]
    qkv = (ql + 2 * kvl) * hd
    tiles = rows // TILE
    cfg = dict(n=n, nz=nz, ql=ql, kvl=kvl, hd=hd, ff=ff, eps=1e-6, window=rows // 2 // TILE, slots=6 * n + 6 * nz)

    lengths = seq_lengths[0]
    ends = jnp.cumsum(lengths)
    begins = ends - lengths
    packed = jnp.arange(rows, dtype=jnp.int32)
    inside = packed[:, None] >= begins[None, :]
    start = jnp.max(jnp.where(inside, begins[None, :], 0), axis=1)
    start = jnp.where(packed < ends[-1], start, packed).astype(jnp.int32)
    pos = packed - start
    by_block = pos.reshape(2 * n, half)
    pos_dev = jnp.concatenate([by_block[:n, None], by_block[n:][::-1][:, None]], axis=1).reshape(rows)
    cos, sin = rope_base_tables(pos_dev, hd)
    cos, sin = cos.reshape(n, t, hd), sin.reshape(n, t, hd)
    own = jnp.concatenate([c * half + jnp.arange(half), (2 * n - 1 - c) * half + jnp.arange(half)])
    valid = (own < ends[-1]).astype(F32)[:, None]
    db = d_out[0] * valid.astype(BF)
    x = hidden_in[0]

    def place(gain, width):
        wide = jnp.zeros((width,), F32)
        return lax.dynamic_update_slice(wide, gain.astype(F32), ((c * nz + z) * gain.shape[0],)).reshape(-1, LANES)

    gains = jnp.concatenate([place(in_gain, dm), place(post_gain, dm), place(q_gain, hd), place(k_gain, hd),
                             jnp.zeros((GAIN_ROWS - 18, LANES), F32)], axis=0)

    def by_device(w):
        return jnp.transpose(w.reshape(w.shape[0], n, -1), (1, 0, 2))

    wqkv = jnp.concatenate([by_device(w_query), by_device(w_key), by_device(w_value)], axis=2)
    wgu = jnp.concatenate([by_device(w_gate), by_device(w_up)], axis=2)

    xn, q, k, v, pre, gu_plane, wo, w, gains = call(
        gather_qkv, cfg,
        [((n, t, dm), BF), ((tiles, ql, TILE, hd), BF), ((tiles, kvl, TILE, hd), BF), ((tiles, kvl, TILE, hd), BF),
         ((n, t, (ql + kvl) * hd), F32), ((n, r_in, 2 * ff), BF), ((nz, r_out, dm), BF), ((n, nz, r_in, qkv), BF),
         ((GAIN_ROWS, LANES), F32)],
        [pltpu.VMEM((n, t, dm), BF), pltpu.VMEM((n, GAIN_ROWS, LANES), F32), pltpu.VMEM((nz, GAIN_ROWS, LANES), F32)],
        1, x, wqkv, wgu, w_out, gains, cos, sin)

    attn, qx, dblk, gu = call(
        attend, cfg,
        [((rows, ql * hd), BF), ((tiles, ql, TILE, 2 * hd), BF), ((n, t, dm), BF), ((n, nz, r_in, 2 * ff), BF)],
        [pltpu.VMEM((tiles, TILE, 2 * hd), BF), pltpu.VMEM((ql * TILE, 2 * hd), F32)],
        2, q, k, v, start[:, None], db, gu_plane)

    mo, dax, h_mid, d_hmid, gwo, gwd, ggu, gpost = call(
        feed, cfg,
        [((n, t, dm), BF), ((tiles, ql, TILE, 2 * hd), BF), ((t, dm), F32), ((t, dm), F32), ((nz, r_out, dm), BF),
         ((r_down, dm), F32), ((n, r_in, 2 * ff), BF), ((1, dm), F32)],
        [pltpu.VMEM((nz, r_down, dm), BF), pltpu.VMEM((n, t, dm), BF), pltpu.VMEM((n, t, ff), BF),
         pltpu.VMEM((n, t, 2 * ff), BF), pltpu.VMEM((n, t, dm), BF),
         pltpu.VMEM((nz, r_down, dm), BF), pltpu.VMEM((n, nz, r_in, 2 * ff), BF),
         pltpu.VMEM((nz - 1, r_down, dm), BF), pltpu.VMEM((nz - 1, n, r_in, 2 * ff), BF)]
        + plane_sum_scratch(n, t, dm) + plane_sum_scratch(n, t, dm) + [pltpu.VMEM((t, dm), BF)],
        3, attn, x, dblk, wo, gu, w_down, gains)

    dq, dk, dv, block_out, grad_wo, grad_gate, grad_up = call(
        attend_back, cfg,
        [((tiles, ql * TILE, hd), F32), ((tiles, TILE, hd), F32), ((tiles, TILE, hd), F32), ((t, dm), BF),
         ((r_out, dm), F32), ((r_in, n * ff), F32), ((r_in, n * ff), F32)],
        [pltpu.VMEM((tiles, TILE, 2 * hd), BF), pltpu.VMEM((tiles, TILE, 2 * hd), BF),
         pltpu.VMEM((TILE, hd), F32), pltpu.VMEM((TILE, hd), F32),
         pltpu.VMEM((nz - 1, r_out, dm), BF), pltpu.VMEM((n, r_in, 2 * ff), BF)]
        + plane_sum_scratch(n, t, dm),
        4, qx, k, v, dax, start[None, :], mo, h_mid, valid, gwo, ggu)

    dx, grad_q, grad_k, grad_v, small = call(
        head_back, cfg,
        [((t, dm), F32), ((r_in, n * ql * hd), F32), ((r_in, n * kvl * hd), F32), ((r_in, n * kvl * hd), F32),
         ((GAIN_ROWS, LANES), F32)],
        [pltpu.VMEM((n, t, qkv), BF), pltpu.VMEM((n, nz, r_in, qkv), BF), pltpu.VMEM((nz - 1, n, r_in, qkv), BF),
         pltpu.VMEM((n, r_in, qkv), BF), pltpu.VMEM((n, r_in, qkv), BF),
         pltpu.VMEM((GAIN_ROWS, LANES), F32), pltpu.VMEM((n, GAIN_ROWS, LANES), F32),
         pltpu.VMEM((nz, GAIN_ROWS, LANES), F32)]
        + plane_sum_scratch(n, t, dm),
        5, pre, dq, dk, dv, cos, sin, gains, xn, w, x, d_hmid, gpost)

    def mine(first, width, share):
        flat = small[first : first + width // LANES].reshape(width)
        return lax.dynamic_slice(flat, ((c * nz + z) * share,), (share,))

    return (block_out[None], dx[None], mine(0, dm, in_gain.shape[0]), grad_q, grad_k, grad_v,
            mine(16, hd, q_gain.shape[0]), mine(17, hd, k_gain.shape[0]), grad_wo,
            mine(8, dm, post_gain.shape[0]), grad_gate, grad_up, gwd)


epsilon = 1e-06
rope_base = 1000000.0
negative = -1e30


def row_info(lengths, row_ids, tok_dev, n_ctx):
    half_len = tok_dev // 2
    device = row_ids // tok_dev
    local_row = row_ids % tok_dev
    block_id = jnp.where(local_row < half_len, device, 2 * n_ctx - 1 - device)
    packed = block_id * half_len + local_row % half_len
    seq_ends = jnp.cumsum(lengths)
    seq_starts = seq_ends - lengths
    member = (packed[:, None] >= seq_starts[None, :]) & (packed[:, None] < seq_ends[None, :])
    row_valid = jnp.any(member, axis=1)
    numbers = jnp.arange(lengths.shape[0], dtype=jnp.int32)
    seq_id = jnp.sum(jnp.where(member, numbers[None, :], 0), axis=1)
    offset = jnp.sum(jnp.where(member, seq_starts[None, :], 0), axis=1)
    segment = jnp.where(row_valid, seq_id, -1 - packed)
    position = jnp.where(row_valid, packed - offset, 0)
    return (segment, position, row_valid)


def norm_gain(values_in, gain_vec):
    row_scale = lax.rsqrt(jnp.mean(values_in * values_in, axis=-1, keepdims=True) + epsilon)
    return values_in * row_scale * gain_vec


def rotary(position, head_dim):
    half_len = head_dim // 2
    inv_freq = jnp.power(rope_base, -jnp.arange(half_len, dtype=jnp.float32) * (2.0 / head_dim))
    angles = position.astype(jnp.float32)[:, None] * inv_freq[None, :]
    angles = jnp.concatenate([angles, angles], axis=1)
    return (jnp.cos(angles), jnp.sin(angles))


def rotate(heads, cos_table, sin_table):
    half_len = heads.shape[-1] // 2
    turned = jnp.concatenate([-heads[..., half_len:], heads[..., :half_len]], axis=-1)
    return heads * cos_table[:, None, :] + turned * sin_table[:, None, :]


def head_post(q_in, k_in, q_scale, k_scale, cos_table, sin_table):
    head_dim = q_scale.shape[0]
    row_count = q_in.shape[0]
    q_heads = norm_gain(q_in.reshape(row_count, -1, head_dim), q_scale)
    k_heads = norm_gain(k_in.reshape(row_count, -1, head_dim), k_scale)
    query_rotated = rotate(q_heads, cos_table, sin_table).reshape(row_count, -1)
    key_rotated = rotate(k_heads, cos_table, sin_table).reshape(row_count, -1)
    return (query_rotated, key_rotated)


def swiglu(gate_in, up_in):
    return jax.nn.silu(gate_in) * up_in


def matmul(left, right):
    return jnp.dot(left, right, preferred_element_type=jnp.float32)


def inner(left, right):
    return lax.dot_general(
        left, right, (((0,), (0,)), ((), ())), preferred_element_type=jnp.float32
    )


def backdot(left, right):
    return lax.dot_general(
        left, right, (((1,), (1,)), ((), ())), preferred_element_type=jnp.float32
    )


def pick_step(key_count):
    for candidate in (512, 384, 256):
        return candidate
    return key_count


def on_rows(
    hidden_in,
    seq_lengths,
    in_gain,
    w_query,
    w_key,
    w_value,
    q_gain,
    k_gain,
    w_out,
    post_gain,
    w_gate,
    w_up,
    w_down,
    d_out,
):
    n_ctx = lax.axis_size("ctx")
    row_count = hidden_in.shape[1]
    lengths = seq_lengths[0]
    own_rows = lax.axis_index("ctx") * row_count + jnp.arange(row_count, dtype=jnp.int32)
    seg_q, pos_q, row_valid = row_info(lengths, own_rows, row_count, n_ctx)
    shards = (
        in_gain,
        w_query,
        w_key,
        w_value,
        q_gain,
        k_gain,
        w_out,
        post_gain,
        w_gate,
        w_up,
        w_down,
    )
    gathered = (
        lax.all_gather(shards[0], ("ctx", "fsdp"), axis=0, tiled=True),
        lax.all_gather(shards[1], ("ctx", "fsdp"), axis=0, tiled=True),
        lax.all_gather(shards[2], ("ctx", "fsdp"), axis=0, tiled=True),
        lax.all_gather(shards[3], ("ctx", "fsdp"), axis=0, tiled=True),
        lax.all_gather(shards[4], ("ctx", "fsdp"), axis=0, tiled=True),
        lax.all_gather(shards[5], ("ctx", "fsdp"), axis=0, tiled=True),
        lax.all_gather(shards[6], ("ctx", "fsdp"), axis=0, tiled=True),
        lax.all_gather(shards[7], ("ctx", "fsdp"), axis=0, tiled=True),
        lax.all_gather(shards[8], ("ctx", "fsdp"), axis=0, tiled=True),
        lax.all_gather(shards[9], ("ctx", "fsdp"), axis=0, tiled=True),
        lax.all_gather(shards[10], ("ctx", "fsdp"), axis=0, tiled=True),
    )
    g_in = gathered[0].astype(jnp.float32)
    g_query = gathered[4].astype(jnp.float32)
    g_key = gathered[5].astype(jnp.float32)
    g_post = gathered[7].astype(jnp.float32)
    head_dim = gathered[4].shape[0]
    kv_width = gathered[2].shape[1]
    kv_heads = kv_width // head_dim
    group_count = gathered[1].shape[1] // kv_width
    score_scale = head_dim ** (-0.5)
    rows_per_group = row_count * n_ctx
    x_float = hidden_in[0].astype(jnp.float32)
    x_normf, in_back = jax.vjp(norm_gain, x_float, g_in)
    x_norm = x_normf.astype(jnp.bfloat16)
    q_pre = matmul(x_norm, gathered[1])
    k_pre = matmul(x_norm, gathered[2])
    value_projected = matmul(x_norm, gathered[3])
    cos_table, sin_table = rotary(pos_q, head_dim)

    def post_local(q_in, k_in, q_scale, k_scale):
        return head_post(q_in, k_in, q_scale, k_scale, cos_table, sin_table)

    rotated, post_back = jax.vjp(post_local, q_pre, k_pre, g_query, g_key)
    q_low4 = rotated[0].astype(jnp.bfloat16).reshape(row_count, kv_heads, group_count, head_dim)
    key_narrow = rotated[1].astype(jnp.bfloat16)
    value_narrow = value_projected.astype(jnp.bfloat16)

    def sweep_keys(carry, k_piece, v_piece, block_fn):
        key_count = k_piece.shape[0]
        key_step = pick_step(key_count)

        def one_turn(state, turn_index):
            offset = turn_index * key_step
            k_block = lax.dynamic_slice_in_dim(k_piece, offset, key_step, 0)
            v_block = lax.dynamic_slice_in_dim(v_piece, offset, key_step, 0)
            key_rows = offset + jnp.arange(key_step, dtype=jnp.int32)
            seg_k, pos_k, unused = row_info(lengths, key_rows, row_count, n_ctx)
            allowed = (seg_q[:, None] == seg_k[None, :]) & (pos_k[None, :] <= pos_q[:, None])
            state = block_fn(state, k_block, v_block, allowed, offset)
            return (state, None)

        carry, unused = lax.scan(
            one_turn, carry, jnp.arange(key_count // key_step, dtype=jnp.int32)
        )
        return carry

    def forward_block(carry, k_block, v_block, allowed, first_key):
        row_max, totals, weighted = carry
        k_heads = k_block.reshape(-1, kv_heads, head_dim)
        v_heads = v_block.reshape(-1, kv_heads, head_dim)
        mask_four = allowed[None, None]
        score = (
            jnp.einsum("qhgd,khd->hgqk", q_low4, k_heads, preferred_element_type=jnp.float32)
            * score_scale
        )
        block_max = jnp.max(jnp.where(mask_four, score, negative), axis=-1)
        new_max = jnp.maximum(row_max, block_max)
        expo = jnp.where(mask_four, jnp.exp(score - new_max[..., None]), 0.0)
        factor = jnp.exp(row_max - new_max)
        totals = totals * factor + jnp.sum(expo, axis=-1)
        weighted = weighted * factor[..., None] + jnp.einsum(
            "hgqk,khd->hgqd", expo.astype(jnp.bfloat16), v_heads, preferred_element_type=jnp.float32
        )
        return (new_max, totals, weighted)

    start_state = (
        jnp.full((kv_heads, group_count, row_count), negative, jnp.float32),
        jnp.zeros((kv_heads, group_count, row_count), jnp.float32),
        jnp.zeros((kv_heads, group_count, row_count, head_dim), jnp.float32),
    )
    pieces = (
        lax.all_gather(key_narrow, "ctx", axis=0, tiled=True),
        lax.all_gather(value_narrow, "ctx", axis=0, tiled=True),
    )
    fold_state = sweep_keys(start_state, pieces[0], pieces[1], forward_block)
    row_max, totals, weighted = fold_state
    attn_four = weighted / totals[..., None]
    log_total = row_max + jnp.log(totals)
    attn = jnp.transpose(attn_four, (2, 0, 1, 3)).reshape(row_count, -1)
    attn_low = attn.astype(jnp.bfloat16)
    h_mid = x_float + matmul(attn_low, gathered[6])
    h_normf, post_norm_back = jax.vjp(norm_gain, h_mid, g_post)
    h_norm = h_normf.astype(jnp.bfloat16)
    gate_out = matmul(h_norm, gathered[8])
    up_out = matmul(h_norm, gathered[9])
    act_float, swiglu_back = jax.vjp(swiglu, gate_out, up_out)
    act_low = act_float.astype(jnp.bfloat16)
    row_mask = row_valid.astype(jnp.float32)[:, None]
    block_out = (row_mask * (h_mid + matmul(act_low, gathered[10]))).astype(jnp.bfloat16)
    again = (
        lax.all_gather(shards[0], ("ctx", "fsdp"), axis=0, tiled=True),
        lax.all_gather(shards[1], ("ctx", "fsdp"), axis=0, tiled=True),
        lax.all_gather(shards[2], ("ctx", "fsdp"), axis=0, tiled=True),
        lax.all_gather(shards[3], ("ctx", "fsdp"), axis=0, tiled=True),
        lax.all_gather(shards[4], ("ctx", "fsdp"), axis=0, tiled=True),
        lax.all_gather(shards[5], ("ctx", "fsdp"), axis=0, tiled=True),
        lax.all_gather(shards[6], ("ctx", "fsdp"), axis=0, tiled=True),
        lax.all_gather(shards[7], ("ctx", "fsdp"), axis=0, tiled=True),
        lax.all_gather(shards[8], ("ctx", "fsdp"), axis=0, tiled=True),
        lax.all_gather(shards[9], ("ctx", "fsdp"), axis=0, tiled=True),
        lax.all_gather(shards[10], ("ctx", "fsdp"), axis=0, tiled=True),
    )
    d_block = d_out[0].astype(jnp.float32) * row_mask
    dm_low = d_block.astype(jnp.bfloat16)
    grad_down = inner(act_low, dm_low)
    d_act = backdot(dm_low, again[10])
    d_gate, d_up = swiglu_back(d_act)
    dg_low = d_gate.astype(jnp.bfloat16)
    du_low = d_up.astype(jnp.bfloat16)
    grad_gate = inner(h_norm, dg_low)
    grad_up = inner(h_norm, du_low)
    d_hnorm = backdot(dg_low, again[8]) + backdot(du_low, again[9])
    d_hpart, grad_post = post_norm_back(d_hnorm)
    d_hmid = d_block + d_hpart
    d_res = d_hmid.astype(jnp.bfloat16)
    grad_wout = inner(attn_low, d_res)
    d_attn = backdot(d_res, again[6]).astype(jnp.bfloat16)
    d_attn4 = d_attn.reshape(row_count, kv_heads, group_count, head_dim)
    delta = jnp.einsum("qhgd,hgqd->hgq", d_attn4.astype(jnp.float32), attn_four)

    def backward_block(carry, k_block, v_block, allowed, first_key):
        d_query, d_kv = carry
        key_count = k_block.shape[0]
        k_heads = k_block.reshape(-1, kv_heads, head_dim)
        v_heads = v_block.reshape(-1, kv_heads, head_dim)
        mask_four = allowed[None, None]
        score = (
            jnp.einsum("qhgd,khd->hgqk", q_low4, k_heads, preferred_element_type=jnp.float32)
            * score_scale
        )
        prob = jnp.where(mask_four, jnp.exp(score - log_total[..., None]), 0.0)
        prob_low = prob.astype(jnp.bfloat16)
        d_prob = jnp.einsum("qhgd,khd->hgqk", d_attn4, v_heads, preferred_element_type=jnp.float32)
        d_score = (prob * (d_prob - delta[..., None])).astype(jnp.bfloat16)
        d_query = d_query + jnp.einsum(
            "hgqk,khd->qhgd", d_score, k_heads, preferred_element_type=jnp.float32
        )
        d_key = (
            jnp.einsum("hgqk,qhgd->khd", d_score, q_low4, preferred_element_type=jnp.float32)
            * score_scale
        )
        d_value = jnp.einsum(
            "hgqk,qhgd->khd", prob_low, d_attn4, preferred_element_type=jnp.float32
        )
        joined = jnp.concatenate(
            [d_key.reshape(key_count, -1), d_value.reshape(key_count, -1)], axis=1
        )
        before = lax.dynamic_slice_in_dim(d_kv, first_key, key_count, 0)
        d_kv = lax.dynamic_update_slice_in_dim(d_kv, before + joined, first_key, 0)
        return (d_query, d_kv)

    back_start = (
        jnp.zeros((row_count, kv_heads, group_count, head_dim), jnp.float32),
        jnp.zeros((rows_per_group, 2 * kv_width), jnp.float32),
    )
    pieces = (
        lax.all_gather(key_narrow, "ctx", axis=0, tiled=True),
        lax.all_gather(value_narrow, "ctx", axis=0, tiled=True),
    )
    back_state = sweep_keys(back_start, pieces[0], pieces[1], backward_block)
    d_qrot = back_state[0].reshape(row_count, -1) * score_scale
    d_kv_own = lax.psum_scatter(
        back_state[1].astype(jnp.bfloat16), "ctx", scatter_dimension=0, tiled=True
    ).astype(jnp.float32)
    d_krot = d_kv_own[:, :kv_width]
    d_vpre = d_kv_own[:, kv_width:]
    d_qpre, d_kpre, grad_qgain, grad_kgain = post_back((d_qrot, d_krot))
    dq_low = d_qpre.astype(jnp.bfloat16)
    dk_low = d_kpre.astype(jnp.bfloat16)
    dv_low = d_vpre.astype(jnp.bfloat16)
    grad_query = inner(x_norm, dq_low)
    grad_key = inner(x_norm, dk_low)
    grad_value = inner(x_norm, dv_low)
    d_xnorm = backdot(dq_low, again[1]) + backdot(dk_low, again[2]) + backdot(dv_low, again[3])
    d_xpart, grad_ingain = in_back(d_xnorm)
    d_hidden = d_hmid + d_xpart
    owned = (
        lax.psum_scatter(grad_ingain, ("ctx", "fsdp"), scatter_dimension=0, tiled=True),
        lax.psum_scatter(grad_query, ("ctx", "fsdp"), scatter_dimension=0, tiled=True),
        lax.psum_scatter(grad_key, ("ctx", "fsdp"), scatter_dimension=0, tiled=True),
        lax.psum_scatter(grad_value, ("ctx", "fsdp"), scatter_dimension=0, tiled=True),
        lax.psum_scatter(grad_qgain, ("ctx", "fsdp"), scatter_dimension=0, tiled=True),
        lax.psum_scatter(grad_kgain, ("ctx", "fsdp"), scatter_dimension=0, tiled=True),
        lax.psum_scatter(grad_wout, ("ctx", "fsdp"), scatter_dimension=0, tiled=True),
        lax.psum_scatter(grad_post, ("ctx", "fsdp"), scatter_dimension=0, tiled=True),
        lax.psum_scatter(grad_gate, ("ctx", "fsdp"), scatter_dimension=0, tiled=True),
        lax.psum_scatter(grad_up, ("ctx", "fsdp"), scatter_dimension=0, tiled=True),
        lax.psum_scatter(grad_down, ("ctx", "fsdp"), scatter_dimension=0, tiled=True),
    )
    return (
        block_out[None],
        d_hidden[None],
        owned[0],
        owned[1],
        owned[2],
        owned[3],
        owned[4],
        owned[5],
        owned[6],
        owned[7],
        owned[8],
        owned[9],
        owned[10],
    )


def on_device(*args):
    n = lax.axis_size("ctx")
    hidden_in, w_key, w_out, w_gate, q_gain = args[0], args[4], args[8], args[10], args[6]
    hd = q_gain.shape[0] * n * lax.axis_size("fsdp")
    heads, ff = w_key.shape[1] // hd, w_gate.shape[1] // n
    even = heads % n == 0 and ff % LANES == 0 and w_key.shape[0] % 16 == 0 and w_out.shape[0] % 16 == 0
    if even and heads == n and (hidden_in.shape[1] * n) % (2 * TILE) == 0:
        return on_plane(*args)
    return on_rows(*args)


def solution(mesh):
    in_specs = (
        P("fsdp", "ctx", None),
        P("fsdp", None),
        P(("ctx", "fsdp")),
        P(("ctx", "fsdp"), None),
        P(("ctx", "fsdp"), None),
        P(("ctx", "fsdp"), None),
        P(("ctx", "fsdp")),
        P(("ctx", "fsdp")),
        P(("ctx", "fsdp"), None),
        P(("ctx", "fsdp")),
        P(("ctx", "fsdp"), None),
        P(("ctx", "fsdp"), None),
        P(("ctx", "fsdp"), None),
        P("fsdp", "ctx", None),
    )
    out_specs = (
        P("fsdp", "ctx", None),
        P("fsdp", "ctx", None),
        P(("ctx", "fsdp")),
        P(("ctx", "fsdp"), None),
        P(("ctx", "fsdp"), None),
        P(("ctx", "fsdp"), None),
        P(("ctx", "fsdp")),
        P(("ctx", "fsdp")),
        P(("ctx", "fsdp"), None),
        P(("ctx", "fsdp")),
        P(("ctx", "fsdp"), None),
        P(("ctx", "fsdp"), None),
        P(("ctx", "fsdp"), None),
    )
    return jax.shard_map(
        on_device, mesh=mesh, in_specs=in_specs, out_specs=out_specs, check_vma=False
    )
```

```python
import functools
import math

import jax
import jax.numpy as jnp
import numpy as np
from jax import lax
from jax.experimental import pallas as pl
from jax.experimental.pallas import tpu as pltpu
from jax.sharding import PartitionSpec as P

BF = jnp.bfloat16
F32 = jnp.float32
MESH = pl.DeviceIdType.MESH
VMEM = pl.BlockSpec(memory_space=pltpu.VMEM)
GAIN_ROWS = 24
LANES = 128
TILE = 256
LIMIT = 60 * 2**20


def dot(a, b):
    return jnp.dot(a, b, preferred_element_type=F32)


def dot_rt(a, b):
    return lax.dot_general(a, b, (((1,), (1,)), ((), ())), preferred_element_type=F32)


def dot_lt(a, b):
    return lax.dot_general(a, b, (((0,), (0,)), ((), ())), preferred_element_type=F32)


def flip(place, mask, size):
    out, bit = 0, 1
    while bit < size:
        out = out + bit * lax.rem(lax.div(place, bit) + (mask // bit) % 2, 2)
        bit *= 2
    return out


class Net:
    def __init__(self, n, nz, send, recv):
        self.n, self.nz, self.send, self.recv = n, nz, send, recv
        self.c = lax.axis_index("ctx")
        self.z = lax.axis_index("fsdp")

    def at(self, mask):
        return flip(self.c, mask, self.n)

    def zat(self, mask):
        return flip(self.z, mask, self.nz)

    def peer(self, mask):
        return (self.at(mask), self.z)

    def zpeer(self, mask):
        return (self.c, self.zat(mask))

    def barrier(self):
        bar = pltpu.get_barrier_semaphore()
        for mask in range(1, self.n):
            pl.semaphore_signal(bar, inc=1, device_id=self.peer(mask), device_id_type=MESH)
        for mask in range(1, self.nz):
            pl.semaphore_signal(bar, inc=1, device_id=self.zpeer(mask), device_id_type=MESH)
        pl.semaphore_wait(bar, self.n + self.nz - 2)

    def copy(self, src, dst, slot, device):
        return pltpu.make_async_remote_copy(
            src_ref=src,
            dst_ref=dst,
            send_sem=self.send.at[slot],
            recv_sem=self.recv.at[slot],
            device_id=device,
            device_id_type=MESH,
        )


class Gather:
    def __init__(self, net, src, buf, base):
        self.net, self.buf, self.base = net, buf, base
        self.copies = {}
        evens = list(range(2, net.n, 2))
        for mask in [1] + evens[::-1]:
            cp = net.copy(src, buf.at[net.c], base + mask, net.peer(mask))
            cp.start()
            self.copies[mask] = cp

    def arrive(self, mask):
        net = self.net
        self.copies[mask].wait_recv()
        if mask % 2 == 0:
            d = net.at(mask)
            cp = net.copy(self.buf.at[d], self.buf.at[d], self.base + mask + 1, net.peer(1))
            cp.start()
            self.copies[mask + 1] = cp

    def finish(self):
        for cp in self.copies.values():
            cp.wait_send()


class PlaneSum:
    def __init__(self, net, sib_out, sib_in, out, inn, keep, base):
        self.net, self.base = net, base
        self.sib_out, self.sib_in, self.out, self.inn, self.keep = sib_out, sib_in, out, inn, keep
        self.copies = []
        self.pending = {}

    def give_sibling(self, mask, value):
        i = mask // 2
        self.sib_out[i] = value.astype(BF)
        cp = self.net.copy(self.sib_out.at[i], self.sib_in.at[i], self.base + mask + 1, self.net.peer(1))
        cp.start()
        self.copies.append(cp)
        self.pending[mask] = cp

    def give(self, mask, value):
        i = mask // 2
        self.pending[mask].wait_recv()
        both = value + self.sib_in[i].astype(F32)
        if mask == 0:
            self.keep[...] = both
            return
        self.out[i - 1] = both.astype(BF)
        cp = self.net.copy(self.out.at[i - 1], self.inn.at[i - 1], self.base + mask, self.net.peer(mask))
        cp.start()
        self.copies.append(cp)
        self.pending[mask] = cp

    def total(self):
        for mask in range(2, self.net.n, 2):
            self.pending[mask].wait_recv()
        value = self.keep[...]
        for i in range(self.net.n // 2 - 1):
            value = value + self.inn[i].astype(F32)
        return value

    def finish(self):
        for cp in self.copies:
            cp.wait_send()


def plane_sum_scratch(n, rows, width):
    half = n // 2
    return [
        pltpu.VMEM((half, rows, width), BF),
        pltpu.VMEM((half, rows, width), BF),
        pltpu.VMEM((half - 1, rows, width), BF),
        pltpu.VMEM((half - 1, rows, width), BF),
        pltpu.VMEM((rows, width), F32),
    ]


def row_of(g, first, count):
    return jnp.concatenate([g[first + j : first + j + 1, :] for j in range(count)], axis=1)


def half_places(net, d, half):
    per = TILE // half
    blocks = (d, 2 * net.n - 1 - d)
    return [(lax.div(b, per), pl.multiple_of(lax.rem(b, per) * half, half)) for b in blocks]


def split_three(value, lane):
    first = value.astype(BF).astype(F32)
    rest = value - first
    second = rest.astype(BF).astype(F32)
    third = rest - second
    out = jnp.where(lane == 0, first, jnp.where(lane == 1, second, jnp.where(lane == 2, third, 0.0)))
    return out.astype(BF)


def first_keys(lengths_ref, at):
    count = lengths_ref.shape[1]
    start = jnp.zeros_like(at)
    begin = 0
    for s in range(count):
        start = jnp.where(at >= begin, begin, start)
        begin = begin + lengths_ref[0, s]
    padding = at >= begin
    return jnp.where(padding, at, start), padding


def front(cfg, lengths_ref, x_ref, do_ref, wq_ref, wk_ref, wv_ref, wo_ref, wg_ref, wu_ref, wd_ref, gpack_ref,
          table_ref, begin_ref,
          qx_out, kx_out, vx_out, dax_out, mo_out, pre_out, cs_out, xn_out, w_out, gwo_out, gwd_out, ggu_out,
          hmid_out, dhmid_out, gains_out, gpost_out,
          wsend, gsend, w, wo_all, gu_in, gu, wd_all, gpart, gbuf, gz, xg, xn, dob, pre, cs, qx, kx, vx, acc, attn,
          dblk, act, dgu, mo, sib_out, sib_in, out, inn, keep, hres, hmid, dhmid, dax, gwo, gwd_buf, gwd_in, ggu_buf,
          ggu_in, gwd, ggu, gpost, local, send, recv):
    n, nz, ql, kvl, hd, ff = cfg["n"], cfg["nz"], cfg["ql"], cfg["kvl"], cfg["hd"], cfg["ff"]
    t, dm = x_ref.shape
    half = t // 2
    tiles = qx.shape[0]
    rows = n * t
    net = Net(n, nz, send, recv)
    c, z = net.c, net.z
    evens, odds = list(range(2, n, 2)), list(range(3, n, 2))
    stores = []

    def store(src, dst):
        cp = pltpu.make_async_copy(src, dst, local.at[len(stores)])
        cp.start()
        stores.append(cp)
        return cp

    qw, kw = ql * hd, kvl * hd
    for j in range(n):
        wsend[j, :, :qw] = wq_ref[:, j * qw : (j + 1) * qw]
        wsend[j, :, qw : qw + kw] = wk_ref[:, j * kw : (j + 1) * kw]
        wsend[j, :, qw + kw :] = wv_ref[:, j * kw : (j + 1) * kw]
        gsend[j, :, :ff] = wg_ref[:, j * ff : (j + 1) * ff]
        gsend[j, :, ff:] = wu_ref[:, j * ff : (j + 1) * ff]
    place = c * nz + z
    share = dm // (n * nz)
    at = lax.broadcasted_iota(jnp.int32, (8, LANES), 0) * LANES + lax.broadcasted_iota(jnp.int32, (8, LANES), 1)
    here = (at >= place * share) & (at < (place + 1) * share)
    gpart[0:8, :] = jnp.where(here, gpack_ref[0:1, :], 0.0)
    gpart[8:16, :] = jnp.where(here, gpack_ref[1:2, :], 0.0)
    share = hd // (n * nz)
    here = (at >= place * share) & (at < (place + 1) * share)
    gpart[16:24, :] = jnp.where(here, gpack_ref[2:3, :], 0.0) + jnp.where(
        (at >= LANES + place * share) & (at < LANES + (place + 1) * share), gpack_ref[3:4, :], 0.0
    )
    net.barrier()
    slot = 0
    plane = []
    for mask in range(1, n):
        cp = net.copy(gpart, gbuf.at[c], slot + mask, net.peer(mask))
        cp.start()
        plane.append(cp)
    slot += n
    for mask in range(1, n):
        cp = net.copy(wsend.at[net.at(mask)], w.at[c, z], slot + mask, net.peer(mask))
        cp.start()
        plane.append(cp)
    slot += n
    line_wo = []
    for mask in range(1, nz):
        cp = net.copy(wo_ref, wo_all.at[z], slot + mask, net.zpeer(mask))
        cp.start()
        line_wo.append(cp)
    slot += nz
    gath = Gather(net, x_ref, xg, slot)
    slot += n
    late = []
    for mask in range(1, n):
        cp = net.copy(gsend.at[net.at(mask)], gu.at[c, z], slot + mask, net.peer(mask))
        cp.start()
        late.append(cp)
    slot += n
    gbuf[c] = gpart[...]
    w[c, z] = wsend[c]
    gu[c, z] = gsend[c]
    wo_all[z] = wo_ref[...]
    wd_all[z] = wd_ref[...]
    xg[c] = x_ref[...]
    for cp in plane[: n - 1]:
        cp.wait_recv()
    gz[z] = jnp.sum(gbuf[...], axis=0)
    gains_line = []
    for mask in range(1, nz):
        cp = net.copy(gz.at[z], gz.at[z], slot + mask, net.zpeer(mask))
        cp.start()
        gains_line.append(cp)
    slot += nz
    for cp in plane[n - 1 :]:
        cp.wait_recv()
    line_w = []
    for mask in range(1, nz):
        cp = net.copy(w.at[:, z], w.at[:, z], slot + mask, net.zpeer(mask))
        cp.start()
        line_w.append(cp)
    slot += nz

    lane = lax.broadcasted_iota(jnp.int32, (t, hd), 1)
    for d in range(n):
        u = lax.broadcasted_iota(jnp.int32, (t, hd), 0)
        packed = jnp.where(u < half, d * half + u, (2 * n - 1 - d) * half + u - half)
        mine = jnp.concatenate(
            [table_ref[d * half : (d + 1) * half], table_ref[(2 * n - 1 - d) * half : (2 * n - d) * half]], axis=0
        )
        first = jnp.broadcast_to(begin_ref[0:1, :], (t, hd))
        begin = 0
        for s in range(lengths_ref.shape[1]):
            if s:
                first = jnp.where(packed >= begin, begin_ref[s : s + 1, :], first)
            begin = begin + lengths_ref[0, s]
        first = jnp.where(packed >= begin, mine, first)
        mine_other, first_other = pltpu.roll(mine, hd // 2, 1), pltpu.roll(first, hd // 2, 1)
        cs[d] = jnp.where(
            lane < hd // 2, mine * first + mine_other * first_other, mine * first_other - mine_other * first
        )

    for cp in gains_line:
        cp.wait_recv()
    gains = jnp.sum(gz[...], axis=0)
    g_in = row_of(gains, 0, dm // LANES)
    g_post = row_of(gains, 8, dm // LANES)
    g_q = gains[16:17, :]
    g_k = gains[17:18, :]
    step = 32

    def normalise(d):
        def some(i, carry):
            here = pl.ds(pl.multiple_of(i * step, step), step)
            v = xg[d, here, :].astype(F32)
            r = lax.rsqrt(jnp.mean(v * v, axis=-1, keepdims=True) + cfg["eps"])
            xn[d, here, :] = (v * r * g_in).astype(BF)
            return carry

        lax.fori_loop(0, t // step, some, 0)

    for mask in [0, 1] + evens:
        if mask:
            gath.arrive(mask)
        normalise(net.at(mask))
    for cp in late:
        cp.wait_recv()
    line_gu = []
    for mask in range(1, nz):
        cp = net.copy(gu.at[:, z], gu.at[:, z], slot + mask, net.zpeer(mask))
        cp.start()
        line_gu.append(cp)
    slot += nz
    for mask in range(1, nz):
        cp = net.copy(wd_ref, wd_all.at[z], slot + mask, net.zpeer(mask))
        cp.start()
        line_gu.append(cp)
    slot += nz
    u = lax.broadcasted_iota(jnp.int32, (t, 1), 0)
    packed = jnp.where(u < half, c * half + u, (2 * n - 1 - c) * half + u - half)
    padding = first_keys(lengths_ref, packed)[1]
    dob[...] = jnp.where(padding, 0.0, do_ref[...].astype(F32)).astype(BF)
    dblk[c] = dob[...]
    gath_d = Gather(net, dob, dblk, slot)
    slot += n
    for mask in odds:
        gath.arrive(mask)
        normalise(net.at(mask))
    for cp in line_w:
        cp.wait_recv()
    wqkv = w[...].reshape(dm, -1)
    lane_b = lax.broadcasted_iota(jnp.int32, (half, hd), 1)
    minus = jnp.where(lane_b < 3, -1.0, 0.0).astype(BF)

    def head_block(d, carry):
        qkv = dot(xn[d], wqkv)
        width = (ql + kvl) * hd
        pre[d] = qkv[:, :width]
        both = cs[d]
        other = pltpu.roll(both, hd // 2, 1)
        cos = jnp.where(lane < hd // 2, both, other)
        sin = jnp.where(lane < hd // 2, -other, both)
        places = half_places(net, d, half)
        for h in range(ql + kvl):
            v = qkv[:, h * hd : (h + 1) * hd]
            r = lax.rsqrt(jnp.mean(v * v, axis=-1, keepdims=True) + cfg["eps"])
            hat = v * r * (g_q if h < ql else g_k)
            low = (hat * cos + pltpu.roll(hat, hd // 2, 1) * sin).astype(BF)
            for s, (tile, row) in enumerate(places):
                part = low[s * half : (s + 1) * half]
                if h < ql:
                    qx[tile, h, pl.ds(row, half), :hd] = part
                else:
                    kx[tile, pl.ds(row, half), :hd] = part
        low = qkv[:, width:].astype(BF)
        for s, (tile, row) in enumerate(places):
            vx[tile, pl.ds(row, half), :hd] = low[s * half : (s + 1) * half]
            kx[tile, pl.ds(row, half), hd:] = minus
            vx[tile, pl.ds(row, half), hd:] = minus
        return carry

    lax.fori_loop(0, n, head_block, 0)
    xn_stored = store(xn, xn_out)
    store(pre, pre_out)
    store(cs, cs_out)
    store(kx, kx_out)
    store(vx, vx_out)
    store(w, w_out)

    wide = ql * TILE
    factor = math.log2(math.e) / math.sqrt(hd)
    lane_q = lax.broadcasted_iota(jnp.int32, (wide, hd), 1)

    def q_tile(i, carry):
        q = qx[i, :, :, :hd].reshape(wide, hd)
        start = first_keys(lengths_ref, i * TILE + lax.broadcasted_iota(jnp.int32, (TILE, 1), 0))[0]
        q_at = i * TILE + lax.broadcasted_iota(jnp.int32, (TILE, TILE), 0)
        acc[...] = jnp.zeros_like(acc)

        def k_tile(j, carry):
            s = dot_rt(q, kx[j, :, :hd])
            k_at = j * TILE + lax.broadcasted_iota(jnp.int32, (TILE, TILE), 1)
            allowed = (k_at <= q_at) & (k_at >= start)
            e = jnp.where(allowed[None], jnp.exp2(s * factor).reshape(ql, TILE, TILE), 0.0)
            acc[...] += dot(e.astype(BF).reshape(wide, TILE), vx[j])
            return carry

        lax.fori_loop(jnp.maximum(i - cfg["window"], 0), i + 1, k_tile, 0)
        total = -acc[:, hd : hd + 1]
        low = (acc[:, :hd] / total).astype(BF)
        for h in range(ql):
            attn[pl.ds(pl.multiple_of(i * TILE, TILE), TILE), h * hd : (h + 1) * hd] = low[h * TILE : (h + 1) * TILE]
        extra = jnp.broadcast_to(jnp.log(total) * math.sqrt(hd), (wide, hd))
        qx[i, :, :, hd:] = split_three(extra, lane_q).reshape(ql, TILE, hd)
        return carry

    lax.fori_loop(0, tiles // 2, q_tile, 0)
    for mask in evens:
        gath_d.arrive(mask)
    lax.fori_loop(tiles // 2, tiles, q_tile, 0)
    store(qx, qx_out)
    for cp in line_wo:
        cp.wait_recv()
    wout = wo_all[...].reshape(-1, dm)

    def attn_rows(d):
        return jnp.concatenate(
            [attn[pl.ds(pl.multiple_of(b * half, half), half), :] for b in (d, 2 * n - 1 - d)], axis=0
        )

    xn_stored.wait()
    hn, dres = xn, xg
    gath.finish()
    sum1 = PlaneSum(net, sib_out, sib_in, out, inn, keep, slot)
    slot += n
    for mask in evens[::-1] + [0]:
        sum1.give_sibling(mask, dot(attn_rows(net.at(mask + 1)), wout))
        sum1.give(mask, dot(attn_rows(net.at(mask)), wout))
    for mask in [1] + odds:
        gath_d.arrive(mask)
    for cp in line_gu:
        cp.wait_recv()
    h_mid = x_ref[...].astype(F32) + sum1.total()
    hmid[...] = h_mid
    r_mid = lax.rsqrt(jnp.mean(h_mid * h_mid, axis=-1, keepdims=True) + cfg["eps"])
    hres[...] = (h_mid * r_mid * g_post).astype(BF)
    gath1 = Gather(net, hres, hn, slot)
    slot += n
    hn[c] = hres[...]
    store(hmid, hmid_out)
    sum1.finish()
    wgu = gu[...].reshape(dm, -1)
    wd = wd_all[...].reshape(-1, dm)

    mo_stores = []

    def block(d):
        both = dot(hn[d], wgu)
        gate, up = both[:, :ff], both[:, ff:]
        sig = 1.0 / (1.0 + jnp.exp(-gate))
        silu = gate * sig
        low = (silu * up).astype(BF)
        act[d] = low
        if len(mo_stores) > 1:
            mo_stores[-2].wait()
        place = len(mo_stores) % 2
        mo[place] = dot(low, wd).astype(BF)
        mo_stores.append(store(mo.at[place], mo_out.at[d]))
        d_act = dot_rt(dblk[d], wd)
        dgu[d, :, :ff] = (d_act * up * sig * (1.0 + gate * (1.0 - sig))).astype(BF)
        dgu[d, :, ff:] = (d_act * silu).astype(BF)
        return dot_rt(dgu[d], wgu)

    sum2 = PlaneSum(net, sib_out, sib_in, out, inn, keep, slot)
    slot += n
    for mask in range(0, n, 2):
        if mask:
            gath1.arrive(mask)
        gath1.arrive(mask + 1)
        sum2.give_sibling(mask, block(net.at(mask + 1)))
        sum2.give(mask, block(net.at(mask)))
    dgu_all = dgu[...].reshape(rows, 2 * ff)
    gwd_buf[...] = dot_lt(act[...].reshape(rows, ff), dblk[...].reshape(rows, dm)).astype(BF).reshape(gwd_buf.shape)
    gline = []
    for mask in range(1, nz):
        cp = net.copy(gwd_buf.at[net.zat(mask)], gwd_in.at[mask - 1], slot + mask, net.zpeer(mask))
        cp.start()
        gline.append(cp)
    slot += nz
    per = dm // n
    cols = 2
    part_w = dm // cols
    for j in range(cols):
        part = dot_lt(hn[:, :, j * part_w : (j + 1) * part_w].reshape(rows, part_w), dgu_all)
        ggu_buf[j * (n // cols) : (j + 1) * (n // cols)] = part.astype(BF).reshape(n // cols, nz, per // nz, 2 * ff)
    for mask in range(1, nz):
        cp = net.copy(ggu_buf.at[:, net.zat(mask)], ggu_in.at[mask - 1], slot + mask, net.zpeer(mask))
        cp.start()
        gline.append(cp)
    slot += nz
    d_hn = sum2.total()
    v = hmid[...]
    r = lax.rsqrt(jnp.mean(v * v, axis=-1, keepdims=True) + cfg["eps"])
    gpost[...] = jnp.sum(d_hn * v * r, axis=0, keepdims=True)
    gdy = g_post * d_hn
    d_hmid = dblk[c].astype(F32) + r * gdy - v * (r * r * r) * jnp.mean(gdy * v, axis=-1, keepdims=True)
    dhmid[...] = d_hmid
    gath1.finish()
    hres[...] = d_hmid.astype(BF)
    gath2 = Gather(net, hres, dres, slot)
    slot += n
    dres[c] = hres[...]
    store(dhmid, dhmid_out)

    def back(d):
        d_attn = dot_rt(dres[d], wout)
        for s, (tile, row) in enumerate(half_places(net, d, half)):
            b = (d, 2 * n - 1 - d)[s]
            rows_b = attn[pl.ds(pl.multiple_of(b * half, half), half), :].astype(F32)
            low = d_attn[s * half : (s + 1) * half].astype(BF)
            prod = low.astype(F32) * rows_b
            for h in range(ql):
                delta = jnp.sum(prod[:, h * hd : (h + 1) * hd], axis=-1, keepdims=True)
                dax[tile, h, pl.ds(row, half), :hd] = low[:, h * hd : (h + 1) * hd]
                dax[tile, h, pl.ds(row, half), hd:] = split_three(jnp.broadcast_to(delta, (half, hd)), lane_b)

    back(c)
    for mask in [1] + evens + odds:
        gath2.arrive(mask)
        back(net.at(mask))
    store(dax, dax_out)
    total = None
    for s in range(2):
        blocks = attn[s * (rows // 2) : (s + 1) * (rows // 2), :]
        if s:
            blocks = jnp.concatenate([blocks[(n - 1 - i) * half : (n - i) * half] for i in range(n)], axis=0)
        part = dot_lt(blocks, dres[:, s * half : (s + 1) * half, :].reshape(n * half, dm))
        total = part if total is None else total + part
    gwo[...] = total.astype(BF).reshape(gwo.shape)
    store(gwo, gwo_out)
    for cp in gline:
        cp.wait_recv()
    gwd_sum = gwd_buf[z].astype(F32)
    ggu_sum = ggu_buf[:, z].astype(F32)
    for i in range(nz - 1):
        gwd_sum = gwd_sum + gwd_in[i].astype(F32)
        ggu_sum = ggu_sum + ggu_in[i].astype(F32)
    gwd[...] = gwd_sum
    ggu[...] = ggu_sum.astype(BF)
    store(gwd, gwd_out)
    store(ggu, ggu_out)
    gains_out[...] = gains
    gpost_out[...] = gpost[...]
    for part in (gath_d, sum2, gath2):
        part.finish()
    for cp in plane + line_wo + late + gains_line + line_w + line_gu + gline:
        cp.wait_send()
    for cp in stores:
        if not any(cp is other for other in [xn_stored] + mo_stores[:-2]):
            cp.wait()


def back(cfg, lengths_ref, qx_ref, kx_ref, vx_ref, dax_ref, mo_ref, pre_ref, cs_ref, xn_ref, w_ref, gwo_ref, ggu_ref,
         hmid_ref, dhmid_ref, gains_ref, gpost_ref, x_ref,
         block_out, dx_out, gwo_out, ggu_out, gqkv_out, gains_out,
         mo_own, mo_in, mo_send, mo_recv, pre, cs, xn, w, hmid, dhmid, dq, dk, dv, dk_acc, dv_acc, gwo_in,
         ggu_in, dqkv, gbuf, g_line, gsum, g_in, part, gplane, gz, sib_out, sib_in, out, inn, keep, local, send, recv):
    n, nz, ql, kvl, hd, ff = cfg["n"], cfg["nz"], cfg["ql"], cfg["kvl"], cfg["hd"], cfg["ff"]
    t, dm = x_ref.shape
    half = t // 2
    rows = n * t
    tiles = qx_ref.shape[0]
    net = Net(n, nz, send, recv)
    c, z = net.c, net.z
    evens = list(range(2, n, 2))
    loads = []

    def load(src, dst):
        cp = pltpu.make_async_copy(src, dst, local.at[len(loads)])
        cp.start()
        loads.append(cp)
        return cp

    own = [load(mo_ref.at[net.at(mask)], mo_own.at[mask // 2]) for mask in range(0, n, 2)]
    net.barrier()
    slot = 0
    plane = []
    for mask in evens[::-1] + [0]:
        cp = net.copy(mo_ref.at[net.at(mask + 1)], mo_in.at[mask // 2], slot + mask + 1, net.peer(1))
        cp.start()
        plane.append(cp)
    first_sums = dict(zip(evens[::-1] + [0], plane))
    line = []
    sum_slot = slot
    slot += n
    for mask in range(1, nz):
        cp = net.copy(gwo_ref.at[net.zat(mask)], gwo_in.at[mask - 1], slot + mask, net.zpeer(mask))
        cp.start()
        line.append(cp)
    slot += nz
    more = [load(a, b) for a, b in ((pre_ref, pre), (cs_ref, cs), (xn_ref, xn), (w_ref, w), (hmid_ref, hmid), (dhmid_ref, dhmid))]
    wide = ql * TILE
    factor = math.log2(math.e) / math.sqrt(hd)
    scale = 1.0 / math.sqrt(hd)
    dq[...] = jnp.zeros_like(dq)

    def k_tile(j, carry):
        k_at = j * TILE + lax.broadcasted_iota(jnp.int32, (TILE, TILE), 0)
        dk_acc[...] = jnp.zeros_like(dk_acc)
        dv_acc[...] = jnp.zeros_like(dv_acc)

        def q_tile(i, carry):
            qx = qx_ref[i].reshape(wide, 2 * hd)
            dax = dax_ref[i].reshape(wide, 2 * hd)
            start = first_keys(lengths_ref, i * TILE + lax.broadcasted_iota(jnp.int32, (1, TILE), 1))[0]
            q_at = i * TILE + lax.broadcasted_iota(jnp.int32, (TILE, TILE), 1)
            allowed = (k_at <= q_at) & (k_at >= start)
            allowed = jnp.concatenate([allowed] * ql, axis=1)
            s = dot_rt(kx_ref[j], qx)
            p = jnp.where(allowed, jnp.exp2(s * factor), 0.0)
            ds = (p * dot_rt(vx_ref[j], dax)).astype(BF)
            dv_acc[...] += dot(p.astype(BF), dax[:, :hd])
            dk_acc[...] += dot(ds, qx[:, :hd])
            dq[i] += dot_lt(ds, kx_ref[j, :, :hd])
            return carry

        lax.fori_loop(j, jnp.minimum(j + cfg["window"], tiles - 1) + 1, q_tile, 0)
        dk[j] = dk_acc[...] * scale
        dv[j] = dv_acc[...]
        return carry

    lax.fori_loop(0, tiles // 4, k_tile, 0)
    second = {}
    for mask in evens[::-1]:
        i = mask // 2
        own[i].wait()
        first_sums[mask].wait_recv()
        mo_send[i - 1] = (mo_own[i].astype(F32) + mo_in[i].astype(F32)).astype(BF)
        cp = net.copy(mo_send.at[i - 1], mo_recv.at[i - 1], sum_slot + mask, net.peer(mask))
        cp.start()
        plane.append(cp)
        second[mask] = cp
    for mask in range(1, n):
        cp = net.copy(ggu_ref.at[net.at(mask)], ggu_in.at[c], slot + mask, net.peer(mask))
        cp.start()
        line.append(cp)
    slot += n
    ggu_in[c] = ggu_ref[c]
    lax.fori_loop(tiles // 4, tiles, k_tile, 0)
    for cp in more:
        cp.wait()
    gains = gains_ref[...]
    lane = lax.broadcasted_iota(jnp.int32, (t, hd), 1)

    def head_block(d, carry):
        before = pre[d]
        both = cs[d]
        other = pltpu.roll(both, hd // 2, 1)
        cos = jnp.where(lane < hd // 2, both, other)
        sin = jnp.where(lane < hd // 2, -other, both)
        places = half_places(net, d, half)
        new = []
        for h in range(ql + kvl):
            if h < ql:
                dy = jnp.concatenate([dq[tile, pl.ds(h * TILE + row, half), :] for tile, row in places], axis=0) * scale
            else:
                dy = jnp.concatenate([dk[tile, pl.ds(row, half), :] for tile, row in places], axis=0)
            g = gains[16:17, :] if h < ql else gains[17:18, :]
            v = before[:, h * hd : (h + 1) * hd]
            r = lax.rsqrt(jnp.mean(v * v, axis=-1, keepdims=True) + cfg["eps"])
            dy = dy * cos - pltpu.roll(dy, hd // 2, 1) * sin
            new.append(jnp.sum(dy * v * r, axis=0, keepdims=True))
            gdy = g * dy
            dpre = r * gdy - v * (r * r * r) * jnp.mean(gdy * v, axis=-1, keepdims=True)
            dqkv[d, :, h * hd : (h + 1) * hd] = dpre.astype(BF)
        dval = jnp.concatenate([dv[tile, pl.ds(row, half), :] for tile, row in places], axis=0)
        dqkv[d, :, (ql + kvl) * hd :] = dval.astype(BF)
        q_sum = sum(new[1:ql], new[0])
        k_sum = sum(new[ql + 1 :], new[ql])
        return (carry[0] + q_sum, carry[1] + k_sum)

    zero = jnp.zeros((1, hd), F32)
    gq, gk = lax.fori_loop(0, n, head_block, (zero, zero))
    wqkv = w[...].reshape(dm, -1)
    sum1 = PlaneSum(net, sib_out, sib_in, out, inn, keep, slot)
    slot += n
    for mask in evens[::-1] + [0]:
        sum1.give_sibling(mask, dot_rt(dqkv[net.at(mask + 1)], wqkv))
        sum1.give(mask, dot_rt(dqkv[net.at(mask)], wqkv))
    per = dm // n
    cols = 2
    part_w = dm // cols
    d_all = dqkv[...].reshape(rows, -1)
    for j in range(cols):
        grad = dot_lt(xn[:, :, j * part_w : (j + 1) * part_w].reshape(rows, part_w), d_all)
        gbuf[j * (n // cols) : (j + 1) * (n // cols)] = grad.astype(BF).reshape(n // cols, nz, per // nz, -1)
    gline = []
    for mask in range(1, nz):
        cp = net.copy(gbuf.at[:, net.zat(mask)], g_line.at[mask - 1], slot + mask, net.zpeer(mask))
        cp.start()
        gline.append(cp)
    slot += nz
    own[0].wait()
    total = hmid[...] + mo_own[0].astype(F32)
    first_sums[0].wait_recv()
    total = total + mo_in[0].astype(F32)
    for mask in evens:
        second[mask].wait_recv()
        total = total + mo_recv[mask // 2 - 1].astype(F32)
    u = lax.broadcasted_iota(jnp.int32, (t, 1), 0)
    packed = jnp.where(u < half, c * half + u, (2 * n - 1 - c) * half + u - half)
    padding = first_keys(lengths_ref, packed)[1]
    block_out[...] = jnp.where(padding, 0.0, total).astype(BF)
    for cp in line:
        cp.wait_recv()
    gwo_sum = gwo_ref[z].astype(F32)
    for i in range(nz - 1):
        gwo_sum = gwo_sum + gwo_in[i].astype(F32)
    gwo_out[...] = gwo_sum
    ggu_out[...] = ggu_in[...]
    d_xn = sum1.total()
    x = x_ref[...].astype(F32)
    g = row_of(gains, 0, dm // LANES)
    r = lax.rsqrt(jnp.mean(x * x, axis=-1, keepdims=True) + cfg["eps"])
    grad_in = jnp.sum(d_xn * x * r, axis=0, keepdims=True)
    gdy = g * d_xn
    dx_out[...] = dhmid[...] + r * gdy - x * (r * r * r) * jnp.mean(gdy * x, axis=-1, keepdims=True)
    part[...] = jnp.zeros_like(part)
    for j in range(dm // LANES):
        part[j : j + 1, :] = grad_in[:, j * LANES : (j + 1) * LANES]
        part[8 + j : 9 + j, :] = gpost_ref[:, j * LANES : (j + 1) * LANES]
    part[16:17, :] = gq
    part[17:18, :] = gk
    small = []
    for mask in range(1, n):
        cp = net.copy(part, gplane.at[c], slot + mask, net.peer(mask))
        cp.start()
        small.append(cp)
    slot += n
    gplane[c] = part[...]
    for cp in gline:
        cp.wait_recv()
    qkv_sum = gbuf[:, z].astype(F32)
    for i in range(nz - 1):
        qkv_sum = qkv_sum + g_line[i].astype(F32)
    gsum[...] = qkv_sum.astype(BF)
    for mask in range(1, n):
        cp = net.copy(gsum.at[net.at(mask)], g_in.at[c], slot + mask, net.peer(mask))
        cp.start()
        gline.append(cp)
    slot += n
    g_in[c] = gsum[c]
    for cp in small:
        cp.wait_recv()
    gz[z] = jnp.sum(gplane[...], axis=0)
    for mask in range(1, nz):
        cp = net.copy(gz.at[z], gz.at[z], slot + mask, net.zpeer(mask))
        cp.start()
        small.append(cp)
    for cp in gline[nz - 1 :]:
        cp.wait_recv()
    gqkv_out[...] = g_in[...]
    for cp in small[n - 1 :]:
        cp.wait_recv()
    gains_out[...] = jnp.sum(gz[...], axis=0)
    sum1.finish()
    for cp in line + plane + small + gline:
        cp.wait_send()


def finish(cfg, block_ref, dx_ref, gwo_ref, gwd_ref, ggu_ref, gqkv_ref, gains_ref,
           block_out, dx_out, gin_out, gq_out, gk_out, gv_out, gqg_out, gkg_out, gwo_out, gpost_out, ggate_out, gup_out,
           gwd_out):
    n, nz, ql, kvl, hd, ff = cfg["n"], cfg["nz"], cfg["ql"], cfg["kvl"], cfg["hd"], cfg["ff"]
    block_out[...] = block_ref[...]
    dx_out[...] = dx_ref[...]
    gwo_out[...] = gwo_ref[...]
    gwd_out[...] = gwd_ref[...]
    qw, kw = ql * hd, kvl * hd
    for d in range(n):
        both = gqkv_ref[d].astype(F32)
        gq_out[:, d * qw : (d + 1) * qw] = both[:, :qw]
        gk_out[:, d * kw : (d + 1) * kw] = both[:, qw : qw + kw]
        gv_out[:, d * kw : (d + 1) * kw] = both[:, qw + kw :]
        both = ggu_ref[d].astype(F32)
        ggate_out[:, d * ff : (d + 1) * ff] = both[:, :ff]
        gup_out[:, d * ff : (d + 1) * ff] = both[:, ff:]
    place = lax.axis_index("ctx") * nz + lax.axis_index("fsdp")
    for first, ref in ((0, gin_out), (8, gpost_out), (16, gqg_out), (17, gkg_out)):
        width = ref.shape[1]
        at = place * width
        row = gains_ref[pl.ds(first + lax.div(at, LANES), 1), :]
        ref[...] = pltpu.roll(row, lax.rem(LANES - lax.rem(at, LANES), LANES), 1)[:, :width]


def call(body, cfg, ins, outs, scratch, cid, *args):
    remote = cid is not None
    params = dict(collective_id=cid, has_side_effects=True) if remote else {}
    if remote:
        sems = pltpu.SemaphoreType.DMA((cfg["slots"],))
        scratch = scratch + [pltpu.SemaphoreType.DMA((32,)), sems, sems]
    return pl.pallas_call(
        functools.partial(body, cfg),
        out_shape=[jax.ShapeDtypeStruct(shape, dtype) for shape, dtype, *_ in outs],
        in_specs=ins,
        out_specs=[o[2] if len(o) > 2 else VMEM for o in outs],
        scratch_shapes=scratch,
        compiler_params=pltpu.CompilerParams(vmem_limit_bytes=LIMIT, **params),
        name=body.__name__,
    )(*args)


def on_plane(hidden_in, seq_lengths, in_gain, w_query, w_key, w_value, q_gain, k_gain, w_out, post_gain,
             w_gate, w_up, w_down, d_out):
    n, nz = lax.axis_size("ctx"), lax.axis_size("fsdp")
    t, dm = hidden_in.shape[1:]
    rows = n * t
    hd = q_gain.shape[0] * n * nz
    ql = w_query.shape[1] // hd // n
    kvl = w_key.shape[1] // hd // n
    ff = w_gate.shape[1] // n
    r_in, r_out, r_down = w_query.shape[0], w_out.shape[0], w_down.shape[0]
    qkv = (ql + 2 * kvl) * hd
    tiles = rows // TILE
    cfg = dict(n=n, nz=nz, ql=ql, kvl=kvl, hd=hd, ff=ff, eps=1e-6, window=rows // 2 // TILE, slots=10 * n + 8 * nz)

    inv = 1000000.0 ** (-np.arange(hd // 2) * (2.0 / hd))
    angles = np.arange(rows)[:, None] * inv[None, :]
    table = jnp.asarray(np.concatenate([np.cos(angles), np.sin(angles)], axis=1), F32)
    begins = jnp.cumsum(seq_lengths[0]) - seq_lengths[0]
    begin_rows = jnp.take(table, begins, axis=0, mode="clip")

    def tiled(gain):
        return jnp.tile(gain, LANES // gain.shape[0])[None]

    gpack = jnp.concatenate([tiled(in_gain), tiled(post_gain), tiled(q_gain), tiled(k_gain)], axis=0).astype(F32)
    x = hidden_in[0]
    smem = pl.BlockSpec(memory_space=pltpu.SMEM)
    anywhere = pl.BlockSpec(memory_space=pl.ANY)

    def hbm(shape, dtype):
        return (shape, dtype, anywhere)

    big, low, wide = (n, t, dm), (tiles, TILE, 2 * hd), (tiles, ql, TILE, 2 * hd)
    pre_w = (ql + kvl) * hd
    sums = [pltpu.VMEM((n // 2, t, dm), BF)] * 2 + [pltpu.VMEM((n // 2 - 1, t, dm), BF)] * 2 + [pltpu.VMEM((t, dm), F32)]
    gains_s = [pltpu.VMEM((GAIN_ROWS, LANES), F32), pltpu.VMEM((n, GAIN_ROWS, LANES), F32),
               pltpu.VMEM((nz, GAIN_ROWS, LANES), F32)]
    (qx, kx, vx, dax, mo, pre, cs, xn, w, gwo, grad_down, ggu, h_mid, d_hmid, gains, gpost) = call(
        front, cfg, [smem] + [VMEM] * 12,
        [hbm(wide, BF), hbm(low, BF), hbm(low, BF), hbm(wide, BF), hbm(big, BF), hbm((n, t, pre_w), F32),
         hbm((n, t, hd), F32), hbm(big, BF), hbm((n, nz, r_in, qkv), BF), hbm((nz, r_out, dm), BF),
         hbm((r_down, dm), F32), hbm((n, r_in, 2 * ff), BF), hbm((t, dm), F32), hbm((t, dm), F32),
         ((GAIN_ROWS, LANES), F32), ((1, dm), F32)],
        [pltpu.VMEM((n, r_in, qkv), BF), pltpu.VMEM((n, r_in, 2 * ff), BF), pltpu.VMEM((n, nz, r_in, qkv), BF),
         pltpu.VMEM((nz, r_out, dm), BF), pltpu.VMEM((8, LANES), BF), pltpu.VMEM((n, nz, r_in, 2 * ff), BF),
         pltpu.VMEM((nz, r_down, dm), BF)] + gains_s
        + [pltpu.VMEM(big, BF), pltpu.VMEM(big, BF), pltpu.VMEM((t, dm), BF), pltpu.VMEM((n, t, pre_w), F32),
           pltpu.VMEM((n, t, hd), F32), pltpu.VMEM(wide, BF), pltpu.VMEM(low, BF), pltpu.VMEM(low, BF),
           pltpu.VMEM((ql * TILE, 2 * hd), F32), pltpu.VMEM((rows, ql * hd), BF),
           pltpu.VMEM(big, BF), pltpu.VMEM((n, t, ff), BF), pltpu.VMEM((n, t, 2 * ff), BF), pltpu.VMEM((2, t, dm), BF)]
        + sums
        + [pltpu.VMEM((t, dm), BF), pltpu.VMEM((t, dm), F32), pltpu.VMEM((t, dm), F32), pltpu.VMEM(wide, BF),
           pltpu.VMEM((nz, r_out, dm), BF), pltpu.VMEM((nz, r_down, dm), BF), pltpu.VMEM((nz - 1, r_down, dm), BF),
           pltpu.VMEM((n, nz, r_in, 2 * ff), BF), pltpu.VMEM((nz - 1, n, r_in, 2 * ff), BF),
           pltpu.VMEM((r_down, dm), F32), pltpu.VMEM((n, r_in, 2 * ff), BF), pltpu.VMEM((1, dm), F32)],
        1, seq_lengths, x, d_out[0], w_query, w_key, w_value, w_out, w_gate, w_up, w_down, gpack, table, begin_rows)

    block, dx, gwo, ggu, gqkv, small = call(
        back, cfg, [smem] + [VMEM] * 4 + [anywhere] * 5 + [VMEM] * 2 + [anywhere] * 2 + [VMEM] * 3,
        [((t, dm), BF), ((t, dm), F32), ((r_out, dm), F32), ((n, r_in, 2 * ff), BF), ((n, r_in, qkv), BF),
         ((GAIN_ROWS, LANES), F32)],
        sums[:4]
        + [pltpu.VMEM((n, t, pre_w), F32), pltpu.VMEM((n, t, hd), F32), pltpu.VMEM(big, BF),
           pltpu.VMEM((n, nz, r_in, qkv), BF), pltpu.VMEM((t, dm), F32), pltpu.VMEM((t, dm), F32),
           pltpu.VMEM((tiles, ql * TILE, hd), F32), pltpu.VMEM((tiles, TILE, hd), F32),
           pltpu.VMEM((tiles, TILE, hd), F32), pltpu.VMEM((TILE, hd), F32), pltpu.VMEM((TILE, hd), F32),
           pltpu.VMEM((nz - 1, r_out, dm), BF), pltpu.VMEM((n, r_in, 2 * ff), BF),
           pltpu.VMEM((n, t, qkv), BF), pltpu.VMEM((n, nz, r_in, qkv), BF), pltpu.VMEM((nz - 1, n, r_in, qkv), BF),
           pltpu.VMEM((n, r_in, qkv), BF), pltpu.VMEM((n, r_in, qkv), BF)]
        + gains_s + sums,
        2, seq_lengths, qx, kx, vx, dax, mo, pre, cs, xn, w, gwo, ggu, h_mid, d_hmid, gains, gpost, x)

    grads = call(
        finish, cfg, [VMEM] * 7,
        [((t, dm), BF), ((t, dm), F32), ((1, in_gain.shape[0]), F32), ((r_in, n * ql * hd), F32),
         ((r_in, n * kvl * hd), F32), ((r_in, n * kvl * hd), F32), ((1, q_gain.shape[0]), F32),
         ((1, k_gain.shape[0]), F32), ((r_out, dm), F32), ((1, post_gain.shape[0]), F32), ((r_in, n * ff), F32),
         ((r_in, n * ff), F32), ((r_down, dm), F32)],
        [], None, block, dx, gwo, grad_down, ggu, gqkv, small)
    (block, dx, g_in, g_q, g_k, g_v, g_qg, g_kg, g_o, g_post, g_gate, g_up, g_down) = grads
    return (block[None], dx[None], g_in[0], g_q, g_k, g_v, g_qg[0], g_kg[0], g_o, g_post[0], g_gate, g_up, g_down)


epsilon = 1e-06
rope_base = 1000000.0
negative = -1e30


def row_info(lengths, row_ids, tok_dev, n_ctx):
    half_len = tok_dev // 2
    device = row_ids // tok_dev
    local_row = row_ids % tok_dev
    block_id = jnp.where(local_row < half_len, device, 2 * n_ctx - 1 - device)
    packed = block_id * half_len + local_row % half_len
    seq_ends = jnp.cumsum(lengths)
    seq_starts = seq_ends - lengths
    member = (packed[:, None] >= seq_starts[None, :]) & (packed[:, None] < seq_ends[None, :])
    row_valid = jnp.any(member, axis=1)
    numbers = jnp.arange(lengths.shape[0], dtype=jnp.int32)
    seq_id = jnp.sum(jnp.where(member, numbers[None, :], 0), axis=1)
    offset = jnp.sum(jnp.where(member, seq_starts[None, :], 0), axis=1)
    segment = jnp.where(row_valid, seq_id, -1 - packed)
    position = jnp.where(row_valid, packed - offset, 0)
    return (segment, position, row_valid)


def norm_gain(values_in, gain_vec):
    row_scale = lax.rsqrt(jnp.mean(values_in * values_in, axis=-1, keepdims=True) + epsilon)
    return values_in * row_scale * gain_vec


def rotary(position, head_dim):
    half_len = head_dim // 2
    inv_freq = jnp.power(rope_base, -jnp.arange(half_len, dtype=jnp.float32) * (2.0 / head_dim))
    angles = position.astype(jnp.float32)[:, None] * inv_freq[None, :]
    angles = jnp.concatenate([angles, angles], axis=1)
    return (jnp.cos(angles), jnp.sin(angles))


def rotate(heads, cos_table, sin_table):
    half_len = heads.shape[-1] // 2
    turned = jnp.concatenate([-heads[..., half_len:], heads[..., :half_len]], axis=-1)
    return heads * cos_table[:, None, :] + turned * sin_table[:, None, :]


def head_post(q_in, k_in, q_scale, k_scale, cos_table, sin_table):
    head_dim = q_scale.shape[0]
    row_count = q_in.shape[0]
    q_heads = norm_gain(q_in.reshape(row_count, -1, head_dim), q_scale)
    k_heads = norm_gain(k_in.reshape(row_count, -1, head_dim), k_scale)
    query_rotated = rotate(q_heads, cos_table, sin_table).reshape(row_count, -1)
    key_rotated = rotate(k_heads, cos_table, sin_table).reshape(row_count, -1)
    return (query_rotated, key_rotated)


def swiglu(gate_in, up_in):
    return jax.nn.silu(gate_in) * up_in


def matmul(left, right):
    return jnp.dot(left, right, preferred_element_type=jnp.float32)


def inner(left, right):
    return lax.dot_general(
        left, right, (((0,), (0,)), ((), ())), preferred_element_type=jnp.float32
    )


def backdot(left, right):
    return lax.dot_general(
        left, right, (((1,), (1,)), ((), ())), preferred_element_type=jnp.float32
    )


def pick_step(key_count):
    for candidate in (512, 384, 256):
        return candidate
    return key_count


def on_rows(
    hidden_in,
    seq_lengths,
    in_gain,
    w_query,
    w_key,
    w_value,
    q_gain,
    k_gain,
    w_out,
    post_gain,
    w_gate,
    w_up,
    w_down,
    d_out,
):
    n_ctx = lax.axis_size("ctx")
    row_count = hidden_in.shape[1]
    lengths = seq_lengths[0]
    own_rows = lax.axis_index("ctx") * row_count + jnp.arange(row_count, dtype=jnp.int32)
    seg_q, pos_q, row_valid = row_info(lengths, own_rows, row_count, n_ctx)
    shards = (
        in_gain,
        w_query,
        w_key,
        w_value,
        q_gain,
        k_gain,
        w_out,
        post_gain,
        w_gate,
        w_up,
        w_down,
    )
    gathered = (
        lax.all_gather(shards[0], ("ctx", "fsdp"), axis=0, tiled=True),
        lax.all_gather(shards[1], ("ctx", "fsdp"), axis=0, tiled=True),
        lax.all_gather(shards[2], ("ctx", "fsdp"), axis=0, tiled=True),
        lax.all_gather(shards[3], ("ctx", "fsdp"), axis=0, tiled=True),
        lax.all_gather(shards[4], ("ctx", "fsdp"), axis=0, tiled=True),
        lax.all_gather(shards[5], ("ctx", "fsdp"), axis=0, tiled=True),
        lax.all_gather(shards[6], ("ctx", "fsdp"), axis=0, tiled=True),
        lax.all_gather(shards[7], ("ctx", "fsdp"), axis=0, tiled=True),
        lax.all_gather(shards[8], ("ctx", "fsdp"), axis=0, tiled=True),
        lax.all_gather(shards[9], ("ctx", "fsdp"), axis=0, tiled=True),
        lax.all_gather(shards[10], ("ctx", "fsdp"), axis=0, tiled=True),
    )
    g_in = gathered[0].astype(jnp.float32)
    g_query = gathered[4].astype(jnp.float32)
    g_key = gathered[5].astype(jnp.float32)
    g_post = gathered[7].astype(jnp.float32)
    head_dim = gathered[4].shape[0]
    kv_width = gathered[2].shape[1]
    kv_heads = kv_width // head_dim
    group_count = gathered[1].shape[1] // kv_width
    score_scale = head_dim ** (-0.5)
    rows_per_group = row_count * n_ctx
    x_float = hidden_in[0].astype(jnp.float32)
    x_normf, in_back = jax.vjp(norm_gain, x_float, g_in)
    x_norm = x_normf.astype(jnp.bfloat16)
    q_pre = matmul(x_norm, gathered[1])
    k_pre = matmul(x_norm, gathered[2])
    value_projected = matmul(x_norm, gathered[3])
    cos_table, sin_table = rotary(pos_q, head_dim)

    def post_local(q_in, k_in, q_scale, k_scale):
        return head_post(q_in, k_in, q_scale, k_scale, cos_table, sin_table)

    rotated, post_back = jax.vjp(post_local, q_pre, k_pre, g_query, g_key)
    q_low4 = rotated[0].astype(jnp.bfloat16).reshape(row_count, kv_heads, group_count, head_dim)
    key_narrow = rotated[1].astype(jnp.bfloat16)
    value_narrow = value_projected.astype(jnp.bfloat16)

    def sweep_keys(carry, k_piece, v_piece, block_fn):
        key_count = k_piece.shape[0]
        key_step = pick_step(key_count)

        def one_turn(state, turn_index):
            offset = turn_index * key_step
            k_block = lax.dynamic_slice_in_dim(k_piece, offset, key_step, 0)
            v_block = lax.dynamic_slice_in_dim(v_piece, offset, key_step, 0)
            key_rows = offset + jnp.arange(key_step, dtype=jnp.int32)
            seg_k, pos_k, unused = row_info(lengths, key_rows, row_count, n_ctx)
            allowed = (seg_q[:, None] == seg_k[None, :]) & (pos_k[None, :] <= pos_q[:, None])
            state = block_fn(state, k_block, v_block, allowed, offset)
            return (state, None)

        carry, unused = lax.scan(
            one_turn, carry, jnp.arange(key_count // key_step, dtype=jnp.int32)
        )
        return carry

    def forward_block(carry, k_block, v_block, allowed, first_key):
        row_max, totals, weighted = carry
        k_heads = k_block.reshape(-1, kv_heads, head_dim)
        v_heads = v_block.reshape(-1, kv_heads, head_dim)
        mask_four = allowed[None, None]
        score = (
            jnp.einsum("qhgd,khd->hgqk", q_low4, k_heads, preferred_element_type=jnp.float32)
            * score_scale
        )
        block_max = jnp.max(jnp.where(mask_four, score, negative), axis=-1)
        new_max = jnp.maximum(row_max, block_max)
        expo = jnp.where(mask_four, jnp.exp(score - new_max[..., None]), 0.0)
        factor = jnp.exp(row_max - new_max)
        totals = totals * factor + jnp.sum(expo, axis=-1)
        weighted = weighted * factor[..., None] + jnp.einsum(
            "hgqk,khd->hgqd", expo.astype(jnp.bfloat16), v_heads, preferred_element_type=jnp.float32
        )
        return (new_max, totals, weighted)

    start_state = (
        jnp.full((kv_heads, group_count, row_count), negative, jnp.float32),
        jnp.zeros((kv_heads, group_count, row_count), jnp.float32),
        jnp.zeros((kv_heads, group_count, row_count, head_dim), jnp.float32),
    )
    pieces = (
        lax.all_gather(key_narrow, "ctx", axis=0, tiled=True),
        lax.all_gather(value_narrow, "ctx", axis=0, tiled=True),
    )
    fold_state = sweep_keys(start_state, pieces[0], pieces[1], forward_block)
    row_max, totals, weighted = fold_state
    attn_four = weighted / totals[..., None]
    log_total = row_max + jnp.log(totals)
    attn = jnp.transpose(attn_four, (2, 0, 1, 3)).reshape(row_count, -1)
    attn_low = attn.astype(jnp.bfloat16)
    h_mid = x_float + matmul(attn_low, gathered[6])
    h_normf, post_norm_back = jax.vjp(norm_gain, h_mid, g_post)
    h_norm = h_normf.astype(jnp.bfloat16)
    gate_out = matmul(h_norm, gathered[8])
    up_out = matmul(h_norm, gathered[9])
    act_float, swiglu_back = jax.vjp(swiglu, gate_out, up_out)
    act_low = act_float.astype(jnp.bfloat16)
    row_mask = row_valid.astype(jnp.float32)[:, None]
    block_out = (row_mask * (h_mid + matmul(act_low, gathered[10]))).astype(jnp.bfloat16)
    again = (
        lax.all_gather(shards[0], ("ctx", "fsdp"), axis=0, tiled=True),
        lax.all_gather(shards[1], ("ctx", "fsdp"), axis=0, tiled=True),
        lax.all_gather(shards[2], ("ctx", "fsdp"), axis=0, tiled=True),
        lax.all_gather(shards[3], ("ctx", "fsdp"), axis=0, tiled=True),
        lax.all_gather(shards[4], ("ctx", "fsdp"), axis=0, tiled=True),
        lax.all_gather(shards[5], ("ctx", "fsdp"), axis=0, tiled=True),
        lax.all_gather(shards[6], ("ctx", "fsdp"), axis=0, tiled=True),
        lax.all_gather(shards[7], ("ctx", "fsdp"), axis=0, tiled=True),
        lax.all_gather(shards[8], ("ctx", "fsdp"), axis=0, tiled=True),
        lax.all_gather(shards[9], ("ctx", "fsdp"), axis=0, tiled=True),
        lax.all_gather(shards[10], ("ctx", "fsdp"), axis=0, tiled=True),
    )
    d_block = d_out[0].astype(jnp.float32) * row_mask
    dm_low = d_block.astype(jnp.bfloat16)
    grad_down = inner(act_low, dm_low)
    d_act = backdot(dm_low, again[10])
    d_gate, d_up = swiglu_back(d_act)
    dg_low = d_gate.astype(jnp.bfloat16)
    du_low = d_up.astype(jnp.bfloat16)
    grad_gate = inner(h_norm, dg_low)
    grad_up = inner(h_norm, du_low)
    d_hnorm = backdot(dg_low, again[8]) + backdot(du_low, again[9])
    d_hpart, grad_post = post_norm_back(d_hnorm)
    d_hmid = d_block + d_hpart
    d_res = d_hmid.astype(jnp.bfloat16)
    grad_wout = inner(attn_low, d_res)
    d_attn = backdot(d_res, again[6]).astype(jnp.bfloat16)
    d_attn4 = d_attn.reshape(row_count, kv_heads, group_count, head_dim)
    delta = jnp.einsum("qhgd,hgqd->hgq", d_attn4.astype(jnp.float32), attn_four)

    def backward_block(carry, k_block, v_block, allowed, first_key):
        d_query, d_kv = carry
        key_count = k_block.shape[0]
        k_heads = k_block.reshape(-1, kv_heads, head_dim)
        v_heads = v_block.reshape(-1, kv_heads, head_dim)
        mask_four = allowed[None, None]
        score = (
            jnp.einsum("qhgd,khd->hgqk", q_low4, k_heads, preferred_element_type=jnp.float32)
            * score_scale
        )
        prob = jnp.where(mask_four, jnp.exp(score - log_total[..., None]), 0.0)
        prob_low = prob.astype(jnp.bfloat16)
        d_prob = jnp.einsum("qhgd,khd->hgqk", d_attn4, v_heads, preferred_element_type=jnp.float32)
        d_score = (prob * (d_prob - delta[..., None])).astype(jnp.bfloat16)
        d_query = d_query + jnp.einsum(
            "hgqk,khd->qhgd", d_score, k_heads, preferred_element_type=jnp.float32
        )
        d_key = (
            jnp.einsum("hgqk,qhgd->khd", d_score, q_low4, preferred_element_type=jnp.float32)
            * score_scale
        )
        d_value = jnp.einsum(
            "hgqk,qhgd->khd", prob_low, d_attn4, preferred_element_type=jnp.float32
        )
        joined = jnp.concatenate(
            [d_key.reshape(key_count, -1), d_value.reshape(key_count, -1)], axis=1
        )
        before = lax.dynamic_slice_in_dim(d_kv, first_key, key_count, 0)
        d_kv = lax.dynamic_update_slice_in_dim(d_kv, before + joined, first_key, 0)
        return (d_query, d_kv)

    back_start = (
        jnp.zeros((row_count, kv_heads, group_count, head_dim), jnp.float32),
        jnp.zeros((rows_per_group, 2 * kv_width), jnp.float32),
    )
    pieces = (
        lax.all_gather(key_narrow, "ctx", axis=0, tiled=True),
        lax.all_gather(value_narrow, "ctx", axis=0, tiled=True),
    )
    back_state = sweep_keys(back_start, pieces[0], pieces[1], backward_block)
    d_qrot = back_state[0].reshape(row_count, -1) * score_scale
    d_kv_own = lax.psum_scatter(
        back_state[1].astype(jnp.bfloat16), "ctx", scatter_dimension=0, tiled=True
    ).astype(jnp.float32)
    d_krot = d_kv_own[:, :kv_width]
    d_vpre = d_kv_own[:, kv_width:]
    d_qpre, d_kpre, grad_qgain, grad_kgain = post_back((d_qrot, d_krot))
    dq_low = d_qpre.astype(jnp.bfloat16)
    dk_low = d_kpre.astype(jnp.bfloat16)
    dv_low = d_vpre.astype(jnp.bfloat16)
    grad_query = inner(x_norm, dq_low)
    grad_key = inner(x_norm, dk_low)
    grad_value = inner(x_norm, dv_low)
    d_xnorm = backdot(dq_low, again[1]) + backdot(dk_low, again[2]) + backdot(dv_low, again[3])
    d_xpart, grad_ingain = in_back(d_xnorm)
    d_hidden = d_hmid + d_xpart
    owned = (
        lax.psum_scatter(grad_ingain, ("ctx", "fsdp"), scatter_dimension=0, tiled=True),
        lax.psum_scatter(grad_query, ("ctx", "fsdp"), scatter_dimension=0, tiled=True),
        lax.psum_scatter(grad_key, ("ctx", "fsdp"), scatter_dimension=0, tiled=True),
        lax.psum_scatter(grad_value, ("ctx", "fsdp"), scatter_dimension=0, tiled=True),
        lax.psum_scatter(grad_qgain, ("ctx", "fsdp"), scatter_dimension=0, tiled=True),
        lax.psum_scatter(grad_kgain, ("ctx", "fsdp"), scatter_dimension=0, tiled=True),
        lax.psum_scatter(grad_wout, ("ctx", "fsdp"), scatter_dimension=0, tiled=True),
        lax.psum_scatter(grad_post, ("ctx", "fsdp"), scatter_dimension=0, tiled=True),
        lax.psum_scatter(grad_gate, ("ctx", "fsdp"), scatter_dimension=0, tiled=True),
        lax.psum_scatter(grad_up, ("ctx", "fsdp"), scatter_dimension=0, tiled=True),
        lax.psum_scatter(grad_down, ("ctx", "fsdp"), scatter_dimension=0, tiled=True),
    )
    return (
        block_out[None],
        d_hidden[None],
        owned[0],
        owned[1],
        owned[2],
        owned[3],
        owned[4],
        owned[5],
        owned[6],
        owned[7],
        owned[8],
        owned[9],
        owned[10],
    )


def on_device(*args):
    n = lax.axis_size("ctx")
    hidden_in, w_key, w_out, w_gate, q_gain = args[0], args[4], args[8], args[10], args[6]
    hd = q_gain.shape[0] * n * lax.axis_size("fsdp")
    heads, ff = w_key.shape[1] // hd, w_gate.shape[1] // n
    even = heads % n == 0 and ff % LANES == 0 and w_key.shape[0] % 16 == 0 and w_out.shape[0] % 16 == 0
    if even and heads == n and (hidden_in.shape[1] * n) % (2 * TILE) == 0:
        return on_plane(*args)
    return on_rows(*args)


def solution(mesh):
    in_specs = (
        P("fsdp", "ctx", None),
        P("fsdp", None),
        P(("ctx", "fsdp")),
        P(("ctx", "fsdp"), None),
        P(("ctx", "fsdp"), None),
        P(("ctx", "fsdp"), None),
        P(("ctx", "fsdp")),
        P(("ctx", "fsdp")),
        P(("ctx", "fsdp"), None),
        P(("ctx", "fsdp")),
        P(("ctx", "fsdp"), None),
        P(("ctx", "fsdp"), None),
        P(("ctx", "fsdp"), None),
        P("fsdp", "ctx", None),
    )
    out_specs = (
        P("fsdp", "ctx", None),
        P("fsdp", "ctx", None),
        P(("ctx", "fsdp")),
        P(("ctx", "fsdp"), None),
        P(("ctx", "fsdp"), None),
        P(("ctx", "fsdp"), None),
        P(("ctx", "fsdp")),
        P(("ctx", "fsdp")),
        P(("ctx", "fsdp"), None),
        P(("ctx", "fsdp")),
        P(("ctx", "fsdp"), None),
        P(("ctx", "fsdp"), None),
        P(("ctx", "fsdp"), None),
    )
    return jax.shard_map(
        on_device, mesh=mesh, in_specs=in_specs, out_specs=out_specs, check_vma=False
    )
```

```python
import functools
import math

import jax
import jax.numpy as jnp
import numpy as np
from jax import lax
from jax.experimental import pallas as pl
from jax.experimental.pallas import tpu as pltpu
from jax.sharding import PartitionSpec as P

BF = jnp.bfloat16
F32 = jnp.float32
MESH = pl.DeviceIdType.MESH
VMEM = pl.BlockSpec(memory_space=pltpu.VMEM)
GAIN_ROWS = 24
LANES = 128
TILE = 256
LIMIT = 61 * 2**20
CORE, ALONG_X, ALONG_Y, ACROSS = 1, 2, 4, 6
CHIPS = (ALONG_X, ALONG_Y, ACROSS)
NEXT = (ALONG_X, ALONG_Y)


def dot(a, b):
    return jnp.dot(a, b, preferred_element_type=F32)


def dot_rt(a, b):
    return lax.dot_general(a, b, (((1,), (1,)), ((), ())), preferred_element_type=F32)


def dot_lt(a, b):
    return lax.dot_general(a, b, (((0,), (0,)), ((), ())), preferred_element_type=F32)


def flip(place, mask, size):
    out, bit = 0, 1
    while bit < size:
        out = out + bit * lax.rem(lax.div(place, bit) + (mask // bit) % 2, 2)
        bit *= 2
    return out


class Net:
    def __init__(self, n, nz, tiles, send, recv):
        self.n, self.nz, self.tiles, self.send, self.recv = n, nz, tiles, send, recv
        self.c = lax.axis_index("ctx")
        self.z = lax.axis_index("fsdp")
        self.core = lax.rem(self.c, 2)
        self.slot = 0

    def slots(self, count):
        first = self.slot
        self.slot += count
        return first

    def at(self, mask):
        return flip(self.c, mask, self.n)

    def zat(self, mask):
        return flip(self.z, mask, self.nz)

    def peer(self, mask):
        return (self.at(mask), self.z)

    def zpeer(self, mask):
        return (self.c, self.zat(mask))

    def tile(self, mask, s):
        chip = lax.div(self.at(mask), 2)
        return chip if s == 0 else self.tiles - 1 - chip

    def view(self, buf, mask, s):
        half = TILE // 2
        core = lax.rem(self.at(mask), 2)
        first = core if s == 0 else 1 - core
        return buf.at[self.tile(mask, s), pl.ds(pl.multiple_of(first * half, half), half), :]

    def barrier(self):
        bar = pltpu.get_barrier_semaphore()
        for mask in range(1, self.n):
            pl.semaphore_signal(bar, inc=1, device_id=self.peer(mask), device_id_type=MESH)
        for mask in range(1, self.nz):
            pl.semaphore_signal(bar, inc=1, device_id=self.zpeer(mask), device_id_type=MESH)
        pl.semaphore_wait(bar, self.n + self.nz - 2)

    def copy(self, src, dst, slot, device, send_slot=None):
        return pltpu.make_async_remote_copy(
            src_ref=src,
            dst_ref=dst,
            send_sem=self.send.at[slot if send_slot is None else send_slot],
            recv_sem=self.recv.at[slot],
            device_id=device,
            device_id_type=MESH,
        )

    def to_plane(self, src, dst):
        base = self.slots(self.n)
        out = []
        for mask in range(1, self.n):
            cp = self.copy(src(mask), dst, base + mask, self.peer(mask))
            cp.start()
            out.append(cp)
        return out

    def to_line(self, src, dst):
        base = self.slots(self.nz)
        out = []
        for mask in range(1, self.nz):
            cp = self.copy(src(mask), dst(mask), base + mask, self.zpeer(mask))
            cp.start()
            out.append(cp)
        return out


class Line:
    def __init__(self, net, view):
        self.net, self.view = net, view
        self.base = net.slots(net.nz)
        self.middle = (net.z == 1) | (net.z == 2)
        self.relayed = net.nz == 4
        own = view(net.z)
        self.direct = [m for m in range(1, net.nz) if not (self.relayed and m == 3)]
        self.copies = {m: net.copy(own, own, self.base + m, net.zpeer(m)) for m in range(1, net.nz)}
        for m in self.direct[::-1]:
            self.copies[m].start()
        if self.relayed:
            far = view(net.zat(2))
            self.passed = net.copy(far, far, self.base + 3, net.zpeer(1), send_slot=self.base)

    def relay(self):
        if self.relayed:
            self.copies[2].wait_recv()

            @pl.when(self.middle)
            def _():
                self.passed.start()
                self.copies[3].start()

    def arrive(self):
        for m, cp in self.copies.items():
            if not (self.relayed and m == 2):
                cp.wait_recv()

    def finish(self):
        for m in self.direct:
            self.copies[m].wait_send()
        if self.relayed:

            @pl.when(self.middle)
            def _():
                self.copies[3].wait_send()
                self.passed.wait_send()


class LineSum:
    def __init__(self, net, piece, inn, passing, both):
        self.net, self.piece, self.inn, self.passing, self.both = net, piece, inn, passing, both
        self.base = net.slots(net.nz)
        self.middle = (net.z == 1) | (net.z == 2)
        self.relayed = net.nz == 4
        if not self.relayed:
            for m in range(1, net.nz):
                self.to(m).start()
            return

        @pl.when(jnp.logical_not(self.middle))
        def _():
            self.far().start()
            self.to(2).start()
            self.to(1).start()

        @pl.when(self.middle)
        def _():
            self.to(3).start()
            self.to(1).start()

    def to(self, m):
        return self.net.copy(self.piece(self.net.zat(m)), self.inn.at[m - 1], self.base + m, self.net.zpeer(m))

    def far(self):
        return self.net.copy(
            self.piece(self.net.zat(3)), self.passing, self.base, self.net.zpeer(1), send_slot=self.base + 3
        )

    def joined(self):
        return self.net.copy(self.both, self.inn.at[1], self.base + 2, self.net.zpeer(2))

    def relay(self):
        if self.relayed:

            @pl.when(self.middle)
            def _():
                self.far().wait_recv()
                own = self.piece(self.net.zat(2))[...].astype(F32)
                self.both[...] = (own + self.passing[...].astype(F32)).astype(BF)
                self.joined().start()

    def total(self, write):
        def some(masks):
            value = self.piece(self.net.z)[...].astype(F32)
            for m in masks:
                self.to(m).wait_recv()
                value = value + self.inn[m - 1].astype(F32)
            write(value)

        if not self.relayed:
            some(range(1, self.net.nz))
            return

        @pl.when(self.middle)
        def _():
            some((1, 2, 3))

        @pl.when(jnp.logical_not(self.middle))
        def _():
            some((1, 2))

    def finish(self):
        if not self.relayed:
            for m in range(1, self.net.nz):
                self.to(m).wait_send()
            return
        self.to(1).wait_send()
        self.to(2).wait_send()
        self.to(3).wait_send()


class Gather:
    def __init__(self, net, buf):
        self.net, self.buf = net, buf
        self.base = net.slots(2 * net.n)
        self.sent = []

    def send(self, mask, s, to, arrives_as):
        view = self.net.view(self.buf, mask, s)
        slot = self.base + 2 * arrives_as + s
        cp = self.net.copy(view, view, slot, self.net.peer(to))
        cp.start()
        self.sent.append(cp)

    def start(self, s):
        for mask in (CORE, ALONG_X, ALONG_Y):
            self.send(0, s, mask, mask)

    def arrive(self, mask, s):
        view = self.net.view(self.buf, mask, s)
        self.net.copy(view, view, self.base + 2 * mask + s, self.net.peer(mask)).wait_recv()
        if mask % 2 == 0:
            if mask == (ALONG_X, ALONG_Y)[s]:
                self.send(mask, s, (ALONG_Y, ALONG_X)[s], ACROSS)
            self.send(mask, s, CORE, mask + 1)

    def finish(self):
        for cp in self.sent:
            cp.wait_send()


class PlaneSum:
    def __init__(self, net, sib_out, sib_in, out, inn, mine, keep):
        self.net = net
        self.sib_out, self.sib_in, self.out, self.inn, self.mine, self.keep = sib_out, sib_in, out, inn, mine, keep
        self.base = net.slots(2 * net.n)
        self.sent, self.queue, self.given = [], [], 0

    def sibling(self, mask, s):
        return self.net.copy(
            self.sib_out.at[mask + s], self.sib_in.at[mask + s], self.base + 2 * (mask + 1) + s, self.net.peer(CORE)
        )

    def chip(self, mask, s):
        i = mask - 2 + s
        to = NEXT[s] if mask == ACROSS else mask
        return self.net.copy(self.out.at[i], self.inn.at[i], self.base + 2 * mask + s, self.net.peer(to))

    def give(self, mask, s, value):
        half = TILE // 2
        place = self.given % 2
        self.given += 1
        self.mine[place] = value
        mine = lax.rem(self.net.core + s, 2) * half
        own = pl.ds(pl.multiple_of(mine, half), half)
        other = pl.ds(pl.multiple_of(half - mine, half), half)
        self.sib_out[mask + s] = self.mine[place, other, :].astype(BF)
        cp = self.sibling(mask, s)
        cp.start()
        self.sent.append(cp)
        self.queue.append((mask, s, place, own))
        if len(self.queue) > 1:
            self.combine()

    def combine(self):
        mask, s, place, own = self.queue.pop(0)
        self.sibling(mask, s).wait_recv()
        both = self.mine[place, own, :] + self.sib_in[mask + s].astype(F32)
        if mask == 0:
            self.keep[s] = both
            return
        if mask == NEXT[1 - s]:
            self.chip(ACROSS, s).wait_recv()
            both = both + self.inn[ACROSS - 2 + s].astype(F32)
        self.out[mask - 2 + s] = both.astype(BF)
        cp = self.chip(mask, s)
        cp.start()
        self.sent.append(cp)

    def flush(self):
        while self.queue:
            self.combine()

    def total(self, s):
        value = self.keep[s]
        for mask in NEXT:
            self.chip(mask, s).wait_recv()
            value = value + self.inn[mask - 2 + s].astype(F32)
        return value

    def finish(self):
        for cp in self.sent:
            cp.wait_send()


SEND_ORDER = ((ACROSS, 0), (ALONG_X, 0), (0, 0), (ALONG_Y, 0), (ACROSS, 1), (ALONG_Y, 1), (0, 1), (ALONG_X, 1))
ARRIVE_ORDER = ((0, 0), (0, 1), (ALONG_X, 0), (ALONG_Y, 0), (ALONG_X, 1), (ALONG_Y, 1), (ACROSS, 0), (ACROSS, 1))


def arrive_for(gath, mask, s):
    if mask == ALONG_X:
        gath.arrive(ALONG_X, s)
        gath.arrive(ALONG_Y, s)
    elif mask == ACROSS:
        gath.arrive(ACROSS, s)
    gath.arrive(mask + 1, s)


def row_of(g, first, count):
    return jnp.concatenate([g[first + j : first + j + 1, :] for j in range(count)], axis=1)


def split_three(value, lane):
    first = value.astype(BF).astype(F32)
    rest = value - first
    second = rest.astype(BF).astype(F32)
    third = rest - second
    out = jnp.where(lane == 0, first, jnp.where(lane == 1, second, jnp.where(lane == 2, third, 0.0)))
    return out.astype(BF)


def first_keys(lengths_ref, at):
    start = jnp.zeros_like(at)
    begin = 0
    for s in range(lengths_ref.shape[1]):
        start = jnp.where(at >= begin, begin, start)
        begin = begin + lengths_ref[0, s]
    padding = at >= begin
    return jnp.where(padding, at, start), padding


def halves(a, hd):
    lane = lax.broadcasted_iota(jnp.int32, a.shape, 1)
    other = pltpu.roll(a, hd // 2, 1)
    return jnp.where(lane < hd // 2, a, other), jnp.where(lane < hd // 2, -other, a)


def angle_sum(a, b, hd):
    lane = lax.broadcasted_iota(jnp.int32, jnp.broadcast_shapes(a.shape, b.shape), 1)
    a2, b2 = pltpu.roll(a, hd // 2, 1), pltpu.roll(b, hd // 2, 1)
    return jnp.where(lane < hd // 2, a * b - a2 * b2, a * b2 + a2 * b)


def minus_angle(a, hd):
    lane = lax.broadcasted_iota(jnp.int32, a.shape, 1)
    return jnp.where(lane < hd // 2, a, -a)


def norm_back(v, gain, dy, eps):
    r = lax.rsqrt(jnp.mean(v * v, axis=-1, keepdims=True) + eps)
    gdy = gain * dy
    dv = r * gdy - v * (r * r * r) * jnp.mean(gdy * v, axis=-1, keepdims=True)
    return jnp.sum(dy * v * r, axis=0, keepdims=True), dv


def front(cfg, lengths_ref, x_ref, do_ref, wq_ref, wk_ref, wv_ref, wo_ref, wg_ref, wu_ref, wd_ref, gshare_ref, table_ref,
          qx_out, kx_out, vx_out, attn_out, mo_out, pre_out, cs_out, xn_out, w_out, wo_out, gwd_out, ggu_out,
          hmid_out, dhmid_out, dres_out, gains_out, gpost_out,
          wsend, gsend, w, wo_all, gu, wd_all, grow, gpart, gbuf, gz, xg, xn, pre, cs, qx, kx, vx, acc, attn,
          dblk, act, dgu, mo, sib_out, sib_in, out, inn, mine, keep, hmid, dhmid, dres, gwd_buf, ggu_buf,
          local, send, recv):
    n, nz, ql, kvl, hd, ff = cfg["n"], cfg["nz"], cfg["ql"], cfg["kvl"], cfg["hd"], cfg["ff"]
    eps = cfg["eps"]
    t, dm = x_ref.shape
    half = TILE // 2
    tiles = qx.shape[0]
    rows = n * t
    net = Net(n, nz, tiles, send, recv)
    c, z = net.c, net.z
    stores = []

    def store(src, dst):
        cp = pltpu.make_async_copy(src, dst, local.at[len(stores)])
        cp.start()
        stores.append(cp)
        return cp

    qw, kw = ql * hd, kvl * hd
    for j in range(n):
        wsend[j, :, :qw] = wq_ref[:, j * qw : (j + 1) * qw]
        wsend[j, :, qw : qw + kw] = wk_ref[:, j * kw : (j + 1) * kw]
        wsend[j, :, qw + kw :] = wv_ref[:, j * kw : (j + 1) * kw]
        gsend[j, :, :ff] = wg_ref[:, j * ff : (j + 1) * ff]
        gsend[j, :, ff:] = wu_ref[:, j * ff : (j + 1) * ff]
    grow[...] = jnp.zeros_like(grow)
    grow[0:1, : gshare_ref.shape[1]] = gshare_ref[...].astype(F32)
    row = jnp.broadcast_to(grow[0:1, :], (8, LANES))
    lane8 = lax.broadcasted_iota(jnp.int32, (8, LANES), 1)
    at = lax.broadcasted_iota(jnp.int32, (8, LANES), 0) * LANES + lane8
    wide, narrow = dm // (n * nz), hd // (n * nz)
    place = c * nz + z

    def placed(first, share, row0):
        shift = lax.rem(place * share, LANES)
        moved = pltpu.roll(row, lax.rem(shift + LANES - first, LANES), 1)
        return jnp.where((at >= row0 + place * share) & (at < row0 + (place + 1) * share), moved, 0.0)

    gpart[0:8, :] = placed(0, wide, 0)
    gpart[8:16, :] = placed(wide, wide, 0)
    gpart[16:24, :] = placed(2 * wide, narrow, 0) + placed(2 * wide + narrow, narrow, LANES)
    for s in range(2):
        net.view(xg, 0, s)[...] = x_ref[s * half : (s + 1) * half, :]
    w[c, z] = wsend[c]
    gu[c, z] = gsend[c]
    wo_all[z] = wo_ref[...]
    wd_all[z] = wd_ref[...]
    net.barrier()
    plane_g = net.to_plane(lambda m: gpart, gbuf.at[c])
    plane_w = net.to_plane(lambda m: wsend.at[net.at(m)], w.at[c, z])
    line_o = Line(net, lambda f: wo_all.at[f])
    gath = Gather(net, xg)
    gath.start(0)
    gath.start(1)
    gbuf[c] = gpart[...]
    for cp in plane_g:
        cp.wait_recv()
    gz[z] = jnp.sum(gbuf[...], axis=0)
    line_g = net.to_line(lambda m: gz.at[z], lambda m: gz.at[z])
    for cp in plane_w:
        cp.wait_recv()
    line_w = Line(net, lambda f: w.at[:, f])

    lo = table_ref[0:half, :]
    begins, firsts = [], []
    begin = 0
    for s in range(lengths_ref.shape[1]):
        begins.append(begin)
        hi_row = table_ref[pl.ds(half + lax.div(begin, half), 1), :]
        lo_row = table_ref[pl.ds(lax.rem(begin, half), 1), :]
        firsts.append(minus_angle(angle_sum(hi_row, lo_row, hd), hd))
        begin = begin + lengths_ref[0, s]
    end = begin
    one = jnp.where(lax.broadcasted_iota(jnp.int32, (1, hd), 1) < hd // 2, 1.0, 0.0)

    def positions(b, carry):
        at = b * half + lax.broadcasted_iota(jnp.int32, (half, hd), 0)
        hi_row = table_ref[pl.ds(half + b, 1), :]
        shift = angle_sum(hi_row, firsts[0], hd)
        for begin, first in zip(begins[1:], firsts[1:]):
            shift = jnp.where(at >= begin, angle_sum(hi_row, first, hd), shift)
        both = jnp.where(at >= end, one, angle_sum(shift, lo, hd))
        cs[lax.div(b, 2), pl.ds(pl.multiple_of(lax.rem(b, 2) * half, half), half), :] = both
        return carry

    lax.fori_loop(0, 2 * tiles, positions, 0)
    for cp in line_g:
        cp.wait_recv()
    gains = jnp.sum(gz[...], axis=0)
    g_in = row_of(gains, 0, dm // LANES)
    g_post = row_of(gains, 8, dm // LANES)
    g_q = gains[16:17, :]
    g_k = gains[17:18, :]
    step = 32

    def normalise(tile):
        def some(i, carry):
            here = pl.ds(pl.multiple_of(i * step, step), step)
            v = xg[tile, here, :].astype(F32)
            r = lax.rsqrt(jnp.mean(v * v, axis=-1, keepdims=True) + eps)
            xn[tile, here, :] = (v * r * g_in).astype(BF)
            return carry

        lax.fori_loop(0, TILE // step, some, 0)

    for mask, s in ARRIVE_ORDER:
        arrive_for(gath, mask, s)
        normalise(net.tile(mask, s))
        if mask == ALONG_Y and s == 1:
            plane_u = net.to_plane(lambda m: gsend.at[net.at(m)], gu.at[c, z])
            line_w.relay()
    line_o.relay()
    gath_d = Gather(net, dblk)
    for s in range(2):
        first = lax.rem(net.core + s, 2) * half + net.tile(0, s) * TILE
        padding = first + lax.broadcasted_iota(jnp.int32, (half, 1), 0) >= end
        net.view(dblk, 0, s)[...] = jnp.where(padding, 0.0, do_ref[s * half : (s + 1) * half, :].astype(F32)).astype(BF)
        gath_d.start(s)
    for cp in plane_u:
        cp.wait_recv()
    line_u = Line(net, lambda f: gu.at[:, f])
    line_w.arrive()
    wqkv = w[...].reshape(dm, -1)
    lane_b = lax.broadcasted_iota(jnp.int32, (TILE, hd), 1)
    minus = jnp.where(lane_b < 3, -1.0, 0.0).astype(BF)

    def heads(tile, carry):
        qkv = dot(xn[tile], wqkv)
        width = qw + kw
        pre[tile] = qkv[:, :width].astype(BF)
        cos, sin = halves(cs[tile], hd)
        for h in range(ql + kvl):
            v = qkv[:, h * hd : (h + 1) * hd]
            r = lax.rsqrt(jnp.mean(v * v, axis=-1, keepdims=True) + eps)
            hat = v * r * (g_q if h < ql else g_k)
            low = (hat * cos + pltpu.roll(hat, hd // 2, 1) * sin).astype(BF)
            if h < ql:
                qx[tile, h, :, :hd] = low
            else:
                kx[tile, :, :hd] = low
        vx[tile, :, :hd] = qkv[:, width:].astype(BF)
        kx[tile, :, hd:] = minus
        vx[tile, :, hd:] = minus
        return carry

    lax.fori_loop(0, tiles, heads, 0)
    hn = xn
    xn_stored = store(xn, xn_out)
    for src, dst in ((pre, pre_out), (cs, cs_out), (kx, kx_out), (vx, vx_out), (w, w_out)):
        store(src, dst)
    line_o.arrive()
    wout = wo_all[...].reshape(-1, dm)
    store(wo_all, wo_out)

    high = ql * TILE
    factor = math.log2(math.e) / math.sqrt(hd)
    lane_q = lax.broadcasted_iota(jnp.int32, (high, hd), 1)

    def attend(i):
        q = qx[i, :, :, :hd].reshape(high, hd)
        start = first_keys(lengths_ref, i * TILE + lax.broadcasted_iota(jnp.int32, (TILE, 1), 0))[0]
        q_at = i * TILE + lax.broadcasted_iota(jnp.int32, (TILE, TILE), 0)
        acc[...] = jnp.zeros_like(acc)

        def k_tile(j, carry):
            s = dot_rt(q, kx[j, :, :hd])
            k_at = j * TILE + lax.broadcasted_iota(jnp.int32, (TILE, TILE), 1)
            allowed = (k_at <= q_at) & (k_at >= start)
            e = jnp.where(allowed[None], jnp.exp2(s * factor).reshape(ql, TILE, TILE), 0.0)
            acc[...] += dot(e.astype(BF).reshape(high, TILE), vx[j])
            return carry

        lax.fori_loop(jnp.maximum(i - cfg["window"], 0), i + 1, k_tile, 0)
        total = -acc[:, hd : hd + 1]
        low = (acc[:, :hd] / total).astype(BF)
        for h in range(ql):
            attn[i, :, h * hd : (h + 1) * hd] = low[h * TILE : (h + 1) * TILE]
        extra = jnp.broadcast_to(jnp.log(total) * math.sqrt(hd), (high, hd))
        qx[i, :, :, hd:] = split_three(extra, lane_q).reshape(ql, TILE, hd)

    xn_stored.wait()
    gath.finish()
    sum1 = PlaneSum(net, sib_out, sib_in, out, inn, mine, keep)
    gath1 = Gather(net, hn)

    def middle(s):
        h_mid = x_ref[s * half : (s + 1) * half, :].astype(F32) + sum1.total(s)
        hmid[s] = h_mid
        r = lax.rsqrt(jnp.mean(h_mid * h_mid, axis=-1, keepdims=True) + eps)
        net.view(hn, 0, s)[...] = (h_mid * r * g_post).astype(BF)
        gath1.start(s)

    for k, (mask, s) in enumerate(SEND_ORDER):
        tile = net.tile(mask, s)
        attend(tile)
        sum1.give(mask, s, dot(attn[tile], wout))
        if k == 2:
            for half_s in range(2):
                gath_d.arrive(ALONG_X, half_s)
                gath_d.arrive(ALONG_Y, half_s)
        if k == 3:
            line_u.relay()
            line_d = Line(net, lambda f: wd_all.at[f])
        if k == 6:
            middle(0)
    sum1.flush()
    store(qx, qx_out)
    store(attn, attn_out)
    for s in range(2):
        gath_d.arrive(ACROSS, s)
    line_d.relay()
    for mask in NEXT:
        gath1.arrive(mask, 0)
    middle(1)
    store(hmid, hmid_out)
    sum1.finish()
    for mask in (CORE, ALONG_X + 1, ALONG_Y + 1, ACROSS + 1):
        for s in range(2):
            gath_d.arrive(mask, s)
    line_u.arrive()
    line_d.arrive()
    wgu = gu[...].reshape(dm, -1)
    wd = wd_all[...].reshape(-1, dm)
    mo_stores = []

    def block(d):
        both = dot(hn[d], wgu)
        gate, up = both[:, :ff], both[:, ff:]
        sig = 1.0 / (1.0 + jnp.exp(-gate))
        silu = gate * sig
        low = (silu * up).astype(BF)
        act[d] = low
        if len(mo_stores) > 1:
            mo_stores[-2].wait()
        place = len(mo_stores) % 2
        mo[place] = dot(low, wd).astype(BF)
        mo_stores.append(store(mo.at[place], mo_out.at[d]))
        d_act = dot_rt(dblk[d], wd)
        dgu[d, :, :ff] = (d_act * up * sig * (1.0 + gate * (1.0 - sig))).astype(BF)
        dgu[d, :, ff:] = (d_act * silu).astype(BF)
        return dot_rt(dgu[d], wgu)

    sum2 = PlaneSum(net, sib_out, sib_in, out, inn, mine, keep)
    gath1.arrive(ACROSS, 0)
    for mask in NEXT:
        gath1.arrive(mask, 1)
    for mask, s in SEND_ORDER:
        if (mask, s) == (ACROSS, 1):
            gath1.arrive(ACROSS, 1)
        gath1.arrive(mask + 1, s)
        sum2.give(mask, s, block(net.tile(mask, s)))
    sum2.flush()
    dgu_all = dgu[...].reshape(rows, 2 * ff)
    gwd_buf[...] = dot_lt(act[...].reshape(rows, ff), dblk[...].reshape(rows, dm)).astype(BF).reshape(gwd_buf.shape)
    store(gwd_buf, gwd_out)
    per = dm // n
    cols = 2
    part_w = dm // cols
    for j in range(cols):
        part = dot_lt(hn[:, :, j * part_w : (j + 1) * part_w].reshape(rows, part_w), dgu_all)
        ggu_buf[j * (n // cols) : (j + 1) * (n // cols)] = part.astype(BF).reshape(n // cols, nz, per // nz, 2 * ff)
    store(ggu_buf, ggu_out)
    g_sum = 0.0
    for s in range(2):
        g_part, dv = norm_back(hmid[s], g_post, sum2.total(s), eps)
        g_sum = g_sum + g_part
        d_hmid = net.view(dblk, 0, s)[...].astype(F32) + dv
        dhmid[s] = d_hmid
        dres[s] = d_hmid.astype(BF)
    store(dhmid, dhmid_out)
    store(dres, dres_out)
    gains_out[...] = gains
    gpost_out[...] = g_sum
    for part in (gath_d, gath1, sum2, line_o, line_w, line_u, line_d):
        part.finish()
    for cp in plane_g + plane_w + plane_u + line_g:
        cp.wait_send()
    for cp in stores:
        if not any(cp is other for other in [xn_stored] + mo_stores[:-2]):
            cp.wait()


def back(cfg, lengths_ref, qx_ref, kx_ref, vx_ref, attn_ref, wo_ref, mo_ref, pre_ref, cs_ref, xn_ref, w_ref, gwd_ref,
         ggu_ref, hmid_ref, dhmid_ref, dres_ref, gains_ref, gpost_ref, x_ref,
         block_out, dx_out, gwo_out, gwd_out, ggu_out, gqkv_out, gains_out,
         mo_own, mo_in, mo_send, mo_recv, pre, cs, xn, w, hmid, dhmid, dresg, dq, dk, dv, dax, gwd, gwd_in, ggu,
         ggu_line, ggu_sum, ggu_in, gwo, gwo_in, dqkv, gbuf, g_line, gsum, g_in, part, gplane, gz,
         sib_out, sib_in, out, inn, mine, keep, local, send, recv):
    n, nz, ql, kvl, hd, ff = cfg["n"], cfg["nz"], cfg["ql"], cfg["kvl"], cfg["hd"], cfg["ff"]
    eps = cfg["eps"]
    t, dm = x_ref.shape
    half = TILE // 2
    rows = n * t
    tiles = qx_ref.shape[0]
    qw, kw = ql * hd, kvl * hd
    net = Net(n, nz, tiles, send, recv)
    c, z = net.c, net.z
    loads = []

    def load(src, dst):
        cp = pltpu.make_async_copy(src, dst, local.at[len(loads)])
        cp.start()
        loads.append(cp)
        return cp

    first = [load(dres_ref.at[s], net.view(dresg, 0, s)) for s in range(2)]
    own = {(m, s): load(net.view(mo_ref, m, s), mo_own.at[m + s]) for m in (0,) + CHIPS for s in range(2)}
    first += [load(gwd_ref, gwd), load(ggu_ref, ggu)]
    more = [load(a, b) for a, b in ((pre_ref, pre), (cs_ref, cs), (xn_ref, xn), (w_ref, w), (hmid_ref, hmid),
                                    (dhmid_ref, dhmid))]
    for cp in first:
        cp.wait()
    net.barrier()
    gath = Gather(net, dresg)
    gath.start(0)
    gath.start(1)
    line_d = LineSum(net, lambda f: gwd.at[f], gwd_in, gwd_in.at[nz - 1], gwd_in.at[nz])
    line_u = LineSum(net, lambda f: ggu.at[:, f], ggu_line, ggu_line.at[nz - 1], ggu_line.at[nz])
    base = net.slots(2 * n)
    sib = {}
    for m in CHIPS + (0,):
        for s in range(2):
            cp = net.copy(net.view(mo_ref, m + 1, s), mo_in.at[m + s], base + m + s, net.peer(CORE))
            cp.start()
            sib[m, s] = cp
    wout = wo_ref[...].reshape(-1, dm)
    gains = gains_ref[...]
    g_q = gains[16:17, :]
    g_k = gains[17:18, :]
    high = ql * TILE
    factor = math.log2(math.e) / math.sqrt(hd)
    scale = 1.0 / math.sqrt(hd)
    lane = lax.broadcasted_iota(jnp.int32, (TILE, hd), 1)
    dk[...] = jnp.zeros_like(dk)
    dv[...] = jnp.zeros_like(dv)

    def attend_back(i):
        d_attn = dot_rt(dresg[i], wout).astype(BF)
        prod = d_attn.astype(F32) * attn_ref[i].astype(F32)
        for h in range(ql):
            delta = jnp.sum(prod[:, h * hd : (h + 1) * hd], axis=-1, keepdims=True)
            dax[h * TILE : (h + 1) * TILE, :hd] = d_attn[:, h * hd : (h + 1) * hd]
            dax[h * TILE : (h + 1) * TILE, hd:] = split_three(jnp.broadcast_to(delta, (TILE, hd)), lane)
        qx = qx_ref[i].reshape(high, 2 * hd)
        start = first_keys(lengths_ref, i * TILE + lax.broadcasted_iota(jnp.int32, (1, TILE), 1))[0]
        q_at = i * TILE + lax.broadcasted_iota(jnp.int32, (TILE, TILE), 1)
        dq[...] = jnp.zeros_like(dq)

        def k_tile(j, carry):
            k_at = j * TILE + lax.broadcasted_iota(jnp.int32, (TILE, TILE), 0)
            allowed = (k_at <= q_at) & (k_at >= start)
            allowed = jnp.concatenate([allowed] * ql, axis=1)
            s = dot_rt(kx_ref[j], qx)
            p = jnp.where(allowed, jnp.exp2(s * factor), 0.0)
            ds = (p * dot_rt(vx_ref[j], dax[...])).astype(BF)
            dv[j] += dot(p.astype(BF), dax[:, :hd])
            dk[j] += dot(ds, qx[:, :hd])
            dq[...] += dot_lt(ds, kx_ref[j, :, :hd])
            return carry

        lax.fori_loop(jnp.maximum(i - cfg["window"], 0), i + 1, k_tile, 0)

    def head_back(i, h, dy, gain):
        cos, sin = halves(cs[i], hd)
        dy = dy * cos - pltpu.roll(dy, hd // 2, 1) * sin
        g_part, dpre = norm_back(pre[i, :, h * hd : (h + 1) * hd].astype(F32), gain, dy, eps)
        dqkv[i, :, h * hd : (h + 1) * hd] = dpre.astype(BF)
        return g_part

    gq = jnp.zeros((1, hd), F32)
    mo_base = net.slots(2 * n)

    def mo_chip(m, s):
        to = NEXT[s] if m == ACROSS else m
        return net.copy(mo_send.at[m + s - 2], mo_recv.at[m + s - 2], mo_base + m + s, net.peer(to))

    def send_mo(m, s):
        own[m, s].wait()
        sib[m, s].wait_recv()
        both = mo_own[m + s].astype(F32) + mo_in[m + s].astype(F32)
        if m == NEXT[1 - s]:
            mo_chip(ACROSS, s).wait_recv()
            both = both + mo_recv[ACROSS - 2 + s].astype(F32)
        mo_send[m + s - 2] = both.astype(BF)
        mo_chip(m, s).start()

    for k, (mask, s) in enumerate(ARRIVE_ORDER):
        arrive_for(gath, mask, s)
        i = net.tile(mask, s)
        attend_back(i)
        if k == 0:
            for cp in more[:2]:
                cp.wait()
        for h in range(ql):
            gq = gq + head_back(i, h, dq[h * TILE : (h + 1) * TILE] * scale, g_q)
        if k == 2:
            line_d.relay()
        if k == 4:
            for half_s in range(2):
                for m in (ACROSS, NEXT[half_s]):
                    send_mo(m, half_s)
        if k == 5:
            line_u.relay()
        if k == 6:
            for half_s in range(2):
                send_mo(NEXT[1 - half_s], half_s)
    gwo[...] = dot_lt(attn_ref[...].reshape(rows, qw), dresg[...].reshape(rows, dm)).astype(BF).reshape(gwo.shape)
    line_o = LineSum(net, lambda f: gwo.at[f], gwo_in, gwo_in.at[nz - 1], gwo_in.at[nz])

    def keys_back(i, carry):
        g_part = head_back(i, ql, dk[i] * scale, g_k)
        dqkv[i, :, qw + kw :] = dv[i].astype(BF)
        return carry + g_part

    gk = lax.fori_loop(0, tiles, keys_back, jnp.zeros((1, hd), F32))
    for cp in more[2:]:
        cp.wait()
    per = dm // n
    cols = 2
    part_w = dm // cols
    d_all = dqkv[...].reshape(rows, -1)
    for j in range(cols):
        grad = dot_lt(xn[:, :, j * part_w : (j + 1) * part_w].reshape(rows, part_w), d_all)
        gbuf[j * (n // cols) : (j + 1) * (n // cols)] = grad.astype(BF).reshape(n // cols, nz, per // nz, -1)
    line_q = LineSum(net, lambda f: gbuf.at[:, f], g_line, g_line.at[nz - 1], g_line.at[nz])
    wqkv = w[...].reshape(dm, -1)
    sum1 = PlaneSum(net, sib_out, sib_in, out, inn, mine, keep)
    for k, (mask, s) in enumerate(SEND_ORDER):
        sum1.give(mask, s, dot_rt(dqkv[net.tile(mask, s)], wqkv))
        if k == 3:
            line_o.relay()
    sum1.flush()

    def write(ref):
        def store(value):
            ref[...] = value.astype(ref.dtype)

        return store

    line_d.total(write(gwd_out))
    line_u.total(write(ggu_sum))
    line_q.relay()
    plane_u = net.to_plane(lambda m: ggu_sum.at[net.at(m)], ggu_in.at[c])
    ggu_in[c] = ggu_sum[c]
    end = 0
    for s in range(lengths_ref.shape[1]):
        end = end + lengths_ref[0, s]
    for s in range(2):
        own[0, s].wait()
        sib[0, s].wait_recv()
        total = hmid[s] + mo_own[s].astype(F32) + mo_in[s].astype(F32)
        for m in NEXT:
            mo_chip(m, s).wait_recv()
            total = total + mo_recv[m - 2 + s].astype(F32)
        at = lax.rem(net.core + s, 2) * half + net.tile(0, s) * TILE
        padding = at + lax.broadcasted_iota(jnp.int32, (half, 1), 0) >= end
        block_out[s * half : (s + 1) * half, :] = jnp.where(padding, 0.0, total).astype(BF)
    line_o.total(write(gwo_out))
    g_in_row = row_of(gains, 0, dm // LANES)
    grad_in = 0.0
    for s in range(2):
        here = slice(s * half, (s + 1) * half)
        g_part, d_x = norm_back(x_ref[here, :].astype(F32), g_in_row, sum1.total(s), eps)
        grad_in = grad_in + g_part
        dx_out[here, :] = dhmid[s] + d_x
    part[...] = jnp.zeros_like(part)
    for j in range(dm // LANES):
        part[j : j + 1, :] = grad_in[:, j * LANES : (j + 1) * LANES]
        part[8 + j : 9 + j, :] = gpost_ref[:, j * LANES : (j + 1) * LANES]
    part[16:17, :] = gq
    part[17:18, :] = gk
    plane_g = net.to_plane(lambda m: part, gplane.at[c])
    gplane[c] = part[...]
    line_q.total(write(gsum))
    plane_q = net.to_plane(lambda m: gsum.at[net.at(m)], g_in.at[c])
    g_in[c] = gsum[c]
    for cp in plane_g:
        cp.wait_recv()
    gz[z] = jnp.sum(gplane[...], axis=0)
    line_g = net.to_line(lambda m: gz.at[z], lambda m: gz.at[z])
    for cp in plane_u:
        cp.wait_recv()
    ggu_out[...] = ggu_in[...]
    for cp in plane_q:
        cp.wait_recv()
    gqkv_out[...] = g_in[...]
    for cp in line_g:
        cp.wait_recv()
    gains_out[...] = jnp.sum(gz[...], axis=0)
    for part in (gath, sum1, line_d, line_u, line_o, line_q):
        part.finish()
    for cp in line_g + plane_u + plane_g + plane_q + list(sib.values()):
        cp.wait_send()
    for s in range(2):
        for m in CHIPS:
            mo_chip(m, s).wait_send()


def finish(cfg, block_ref, dx_ref, gwo_ref, gwd_ref, ggu_ref, gqkv_ref, gains_ref,
           block_out, dx_out, gin_out, gq_out, gk_out, gv_out, gqg_out, gkg_out, gwo_out, gpost_out, ggate_out, gup_out,
           gwd_out):
    n, nz, ql, kvl, hd, ff = cfg["n"], cfg["nz"], cfg["ql"], cfg["kvl"], cfg["hd"], cfg["ff"]
    block_out[...] = block_ref[...]
    dx_out[...] = dx_ref[...]
    gwo_out[...] = gwo_ref[...]
    gwd_out[...] = gwd_ref[...]
    qw, kw = ql * hd, kvl * hd
    for d in range(n):
        both = gqkv_ref[d].astype(F32)
        gq_out[:, d * qw : (d + 1) * qw] = both[:, :qw]
        gk_out[:, d * kw : (d + 1) * kw] = both[:, qw : qw + kw]
        gv_out[:, d * kw : (d + 1) * kw] = both[:, qw + kw :]
        both = ggu_ref[d].astype(F32)
        ggate_out[:, d * ff : (d + 1) * ff] = both[:, :ff]
        gup_out[:, d * ff : (d + 1) * ff] = both[:, ff:]
    place = lax.axis_index("ctx") * nz + lax.axis_index("fsdp")
    for first, ref in ((0, gin_out), (8, gpost_out), (16, gqg_out), (17, gkg_out)):
        width = ref.shape[1]
        at = place * width
        row = gains_ref[pl.ds(first + lax.div(at, LANES), 1), :]
        ref[...] = pltpu.roll(row, lax.rem(LANES - lax.rem(at, LANES), LANES), 1)[:, :width]


def call(body, cfg, ins, outs, scratch, cid, *args):
    remote = cid is not None
    params = dict(collective_id=cid, has_side_effects=True) if remote else {}
    if remote:
        sems = pltpu.SemaphoreType.DMA((cfg["slots"],))
        scratch = scratch + [pltpu.SemaphoreType.DMA((32,)), sems, sems]
    return pl.pallas_call(
        functools.partial(body, cfg),
        out_shape=[jax.ShapeDtypeStruct(shape, dtype) for shape, dtype, *_ in outs],
        in_specs=ins,
        out_specs=[o[2] if len(o) > 2 else VMEM for o in outs],
        scratch_shapes=scratch,
        compiler_params=pltpu.CompilerParams(vmem_limit_bytes=LIMIT, **params),
        name=body.__name__,
    )(*args)


def on_plane(hidden_in, seq_lengths, in_gain, w_query, w_key, w_value, q_gain, k_gain, w_out, post_gain,
             w_gate, w_up, w_down, d_out):
    n, nz = lax.axis_size("ctx"), lax.axis_size("fsdp")
    t, dm = hidden_in.shape[1:]
    rows = n * t
    hd = q_gain.shape[0] * n * nz
    ql = w_query.shape[1] // hd // n
    kvl = w_key.shape[1] // hd // n
    ff = w_gate.shape[1] // n
    r_in, r_out, r_down = w_query.shape[0], w_out.shape[0], w_down.shape[0]
    qkv = (ql + 2 * kvl) * hd
    tiles, half = rows // TILE, TILE // 2
    cfg = dict(n=n, nz=nz, ql=ql, kvl=kvl, hd=hd, ff=ff, eps=1e-6, window=rows // 2 // TILE, slots=14 * n + 8 * nz)

    inv = 1000000.0 ** (-np.arange(hd // 2) * (2.0 / hd))
    angles = np.concatenate([np.arange(half), np.arange(2 * tiles) * half])[:, None] * inv[None, :]
    table = jnp.asarray(np.concatenate([np.cos(angles), np.sin(angles)], axis=1), F32)
    gshare = jnp.concatenate([in_gain, post_gain, q_gain, k_gain])[None]
    x = hidden_in[0]
    smem = pl.BlockSpec(memory_space=pltpu.SMEM)
    anywhere = pl.BlockSpec(memory_space=pl.ANY)

    def hbm(shape, dtype):
        return (shape, dtype, anywhere)

    def vm(shape, dtype=BF):
        return pltpu.VMEM(shape, dtype)

    big, low, wide, pair = (tiles, TILE, dm), (tiles, TILE, 2 * hd), (tiles, ql, TILE, 2 * hd), (2, half, dm)
    pre_w = (ql + kvl) * hd
    w_s, gu_s, wo_s, wd_s = (n, nz, r_in, qkv), (n, nz, r_in, 2 * ff), (nz, r_out, dm), (nz, r_down, dm)
    attn_s = (tiles, TILE, ql * hd)
    gains_s = (GAIN_ROWS, LANES)
    sums = [vm((n, half, dm)), vm((n, half, dm)), vm((n - 2, half, dm)), vm((n - 2, half, dm)), vm((2, TILE, dm), F32), vm(pair, F32)]
    (qx, kx, vx, attn, mo, pre, cs, xn, w, wo, gwd, ggu, h_mid, d_hmid, d_res, gains, gpost) = call(
        front, cfg, [smem] + [VMEM] * 11,
        [hbm(wide, BF), hbm(low, BF), hbm(low, BF), hbm(attn_s, BF), hbm(big, BF), hbm((tiles, TILE, pre_w), BF),
         hbm((tiles, TILE, hd), F32), hbm(big, BF), hbm(w_s, BF), hbm(wo_s, BF), hbm(wd_s, BF), hbm(gu_s, BF),
         hbm(pair, F32), hbm(pair, F32), hbm(pair, BF), (gains_s, F32), ((1, dm), F32)],
        [vm((n, r_in, qkv)), vm((n, r_in, 2 * ff)), vm(w_s), vm(wo_s), vm(gu_s), vm(wd_s),
         vm((8, LANES), F32), vm(gains_s, F32), vm((n,) + gains_s, F32), vm((nz,) + gains_s, F32),
         vm(big), vm(big), vm((tiles, TILE, pre_w)), vm((tiles, TILE, hd), F32), vm(wide), vm(low), vm(low),
         vm((ql * TILE, 2 * hd), F32), vm(attn_s),
         vm(big), vm((tiles, TILE, ff)), vm((tiles, TILE, 2 * ff)), vm((2, TILE, dm))]
        + sums + [vm(pair, F32), vm(pair, F32), vm(pair), vm(wd_s), vm(gu_s)],
        1, seq_lengths, x, d_out[0], w_query, w_key, w_value, w_out, w_gate, w_up, w_down, gshare, table)

    block, dx, gwo, grad_down, ggu, gqkv, small = call(
        back, cfg, [smem] + [VMEM] * 5 + [anywhere] * 10 + [VMEM] * 3,
        [((t, dm), BF), ((t, dm), F32), ((r_out, dm), F32), ((r_down, dm), F32), ((n, r_in, 2 * ff), BF),
         ((n, r_in, qkv), BF), (gains_s, F32)],
        [vm((n, half, dm)), vm((n, half, dm)), vm((n - 2, half, dm)), vm((n - 2, half, dm)),
         vm((tiles, TILE, pre_w)), vm((tiles, TILE, hd), F32), vm(big), vm(w_s), vm(pair, F32), vm(pair, F32), vm(big),
         vm((ql * TILE, hd), F32), vm((tiles, TILE, hd), F32), vm((tiles, TILE, hd), F32), vm((ql * TILE, 2 * hd)),
         vm(wd_s), vm((nz + 1, r_down, dm)), vm(gu_s), vm((nz + 1, n, r_in, 2 * ff)),
         vm((n, r_in, 2 * ff)), vm((n, r_in, 2 * ff)), vm(wo_s), vm((nz + 1, r_out, dm)),
         vm((tiles, TILE, qkv)), vm(w_s), vm((nz + 1, n, r_in, qkv)), vm((n, r_in, qkv)), vm((n, r_in, qkv)),
         vm(gains_s, F32), vm((n,) + gains_s, F32), vm((nz,) + gains_s, F32)]
        + sums,
        2, seq_lengths, qx, kx, vx, attn, wo, mo, pre, cs, xn, w, gwd, ggu, h_mid, d_hmid, d_res, gains, gpost, x)

    grads = call(
        finish, cfg, [VMEM] * 7,
        [((t, dm), BF), ((t, dm), F32), ((1, in_gain.shape[0]), F32), ((r_in, n * ql * hd), F32),
         ((r_in, n * kvl * hd), F32), ((r_in, n * kvl * hd), F32), ((1, q_gain.shape[0]), F32),
         ((1, k_gain.shape[0]), F32), ((r_out, dm), F32), ((1, post_gain.shape[0]), F32), ((r_in, n * ff), F32),
         ((r_in, n * ff), F32), ((r_down, dm), F32)],
        [], None, block, dx, gwo, grad_down, ggu, gqkv, small)
    (block, dx, g_in, g_q, g_k, g_v, g_qg, g_kg, g_o, g_post, g_gate, g_up, g_down) = grads
    return (block[None], dx[None], g_in[0], g_q, g_k, g_v, g_qg[0], g_kg[0], g_o, g_post[0], g_gate, g_up, g_down)


epsilon = 1e-06
rope_base = 1000000.0
negative = -1e30


def row_info(lengths, row_ids, tok_dev, n_ctx):
    half_len = tok_dev // 2
    device = row_ids // tok_dev
    local_row = row_ids % tok_dev
    block_id = jnp.where(local_row < half_len, device, 2 * n_ctx - 1 - device)
    packed = block_id * half_len + local_row % half_len
    seq_ends = jnp.cumsum(lengths)
    seq_starts = seq_ends - lengths
    member = (packed[:, None] >= seq_starts[None, :]) & (packed[:, None] < seq_ends[None, :])
    row_valid = jnp.any(member, axis=1)
    numbers = jnp.arange(lengths.shape[0], dtype=jnp.int32)
    seq_id = jnp.sum(jnp.where(member, numbers[None, :], 0), axis=1)
    offset = jnp.sum(jnp.where(member, seq_starts[None, :], 0), axis=1)
    segment = jnp.where(row_valid, seq_id, -1 - packed)
    position = jnp.where(row_valid, packed - offset, 0)
    return (segment, position, row_valid)


def norm_gain(values_in, gain_vec):
    row_scale = lax.rsqrt(jnp.mean(values_in * values_in, axis=-1, keepdims=True) + epsilon)
    return values_in * row_scale * gain_vec


def rotary(position, head_dim):
    half_len = head_dim // 2
    inv_freq = jnp.power(rope_base, -jnp.arange(half_len, dtype=jnp.float32) * (2.0 / head_dim))
    angles = position.astype(jnp.float32)[:, None] * inv_freq[None, :]
    angles = jnp.concatenate([angles, angles], axis=1)
    return (jnp.cos(angles), jnp.sin(angles))


def rotate(heads, cos_table, sin_table):
    half_len = heads.shape[-1] // 2
    turned = jnp.concatenate([-heads[..., half_len:], heads[..., :half_len]], axis=-1)
    return heads * cos_table[:, None, :] + turned * sin_table[:, None, :]


def head_post(q_in, k_in, q_scale, k_scale, cos_table, sin_table):
    head_dim = q_scale.shape[0]
    row_count = q_in.shape[0]
    q_heads = norm_gain(q_in.reshape(row_count, -1, head_dim), q_scale)
    k_heads = norm_gain(k_in.reshape(row_count, -1, head_dim), k_scale)
    query_rotated = rotate(q_heads, cos_table, sin_table).reshape(row_count, -1)
    key_rotated = rotate(k_heads, cos_table, sin_table).reshape(row_count, -1)
    return (query_rotated, key_rotated)


def swiglu(gate_in, up_in):
    return jax.nn.silu(gate_in) * up_in


def matmul(left, right):
    return jnp.dot(left, right, preferred_element_type=jnp.float32)


def inner(left, right):
    return lax.dot_general(
        left, right, (((0,), (0,)), ((), ())), preferred_element_type=jnp.float32
    )


def backdot(left, right):
    return lax.dot_general(
        left, right, (((1,), (1,)), ((), ())), preferred_element_type=jnp.float32
    )


def pick_step(key_count):
    for candidate in (512, 384, 256):
        return candidate
    return key_count


def on_rows(
    hidden_in,
    seq_lengths,
    in_gain,
    w_query,
    w_key,
    w_value,
    q_gain,
    k_gain,
    w_out,
    post_gain,
    w_gate,
    w_up,
    w_down,
    d_out,
):
    n_ctx = lax.axis_size("ctx")
    row_count = hidden_in.shape[1]
    lengths = seq_lengths[0]
    own_rows = lax.axis_index("ctx") * row_count + jnp.arange(row_count, dtype=jnp.int32)
    seg_q, pos_q, row_valid = row_info(lengths, own_rows, row_count, n_ctx)
    shards = (
        in_gain,
        w_query,
        w_key,
        w_value,
        q_gain,
        k_gain,
        w_out,
        post_gain,
        w_gate,
        w_up,
        w_down,
    )
    gathered = (
        lax.all_gather(shards[0], ("ctx", "fsdp"), axis=0, tiled=True),
        lax.all_gather(shards[1], ("ctx", "fsdp"), axis=0, tiled=True),
        lax.all_gather(shards[2], ("ctx", "fsdp"), axis=0, tiled=True),
        lax.all_gather(shards[3], ("ctx", "fsdp"), axis=0, tiled=True),
        lax.all_gather(shards[4], ("ctx", "fsdp"), axis=0, tiled=True),
        lax.all_gather(shards[5], ("ctx", "fsdp"), axis=0, tiled=True),
        lax.all_gather(shards[6], ("ctx", "fsdp"), axis=0, tiled=True),
        lax.all_gather(shards[7], ("ctx", "fsdp"), axis=0, tiled=True),
        lax.all_gather(shards[8], ("ctx", "fsdp"), axis=0, tiled=True),
        lax.all_gather(shards[9], ("ctx", "fsdp"), axis=0, tiled=True),
        lax.all_gather(shards[10], ("ctx", "fsdp"), axis=0, tiled=True),
    )
    g_in = gathered[0].astype(jnp.float32)
    g_query = gathered[4].astype(jnp.float32)
    g_key = gathered[5].astype(jnp.float32)
    g_post = gathered[7].astype(jnp.float32)
    head_dim = gathered[4].shape[0]
    kv_width = gathered[2].shape[1]
    kv_heads = kv_width // head_dim
    group_count = gathered[1].shape[1] // kv_width
    score_scale = head_dim ** (-0.5)
    rows_per_group = row_count * n_ctx
    x_float = hidden_in[0].astype(jnp.float32)
    x_normf, in_back = jax.vjp(norm_gain, x_float, g_in)
    x_norm = x_normf.astype(jnp.bfloat16)
    q_pre = matmul(x_norm, gathered[1])
    k_pre = matmul(x_norm, gathered[2])
    value_projected = matmul(x_norm, gathered[3])
    cos_table, sin_table = rotary(pos_q, head_dim)

    def post_local(q_in, k_in, q_scale, k_scale):
        return head_post(q_in, k_in, q_scale, k_scale, cos_table, sin_table)

    rotated, post_back = jax.vjp(post_local, q_pre, k_pre, g_query, g_key)
    q_low4 = rotated[0].astype(jnp.bfloat16).reshape(row_count, kv_heads, group_count, head_dim)
    key_narrow = rotated[1].astype(jnp.bfloat16)
    value_narrow = value_projected.astype(jnp.bfloat16)

    def sweep_keys(carry, k_piece, v_piece, block_fn):
        key_count = k_piece.shape[0]
        key_step = pick_step(key_count)

        def one_turn(state, turn_index):
            offset = turn_index * key_step
            k_block = lax.dynamic_slice_in_dim(k_piece, offset, key_step, 0)
            v_block = lax.dynamic_slice_in_dim(v_piece, offset, key_step, 0)
            key_rows = offset + jnp.arange(key_step, dtype=jnp.int32)
            seg_k, pos_k, unused = row_info(lengths, key_rows, row_count, n_ctx)
            allowed = (seg_q[:, None] == seg_k[None, :]) & (pos_k[None, :] <= pos_q[:, None])
            state = block_fn(state, k_block, v_block, allowed, offset)
            return (state, None)

        carry, unused = lax.scan(
            one_turn, carry, jnp.arange(key_count // key_step, dtype=jnp.int32)
        )
        return carry

    def forward_block(carry, k_block, v_block, allowed, first_key):
        row_max, totals, weighted = carry
        k_heads = k_block.reshape(-1, kv_heads, head_dim)
        v_heads = v_block.reshape(-1, kv_heads, head_dim)
        mask_four = allowed[None, None]
        score = (
            jnp.einsum("qhgd,khd->hgqk", q_low4, k_heads, preferred_element_type=jnp.float32)
            * score_scale
        )
        block_max = jnp.max(jnp.where(mask_four, score, negative), axis=-1)
        new_max = jnp.maximum(row_max, block_max)
        expo = jnp.where(mask_four, jnp.exp(score - new_max[..., None]), 0.0)
        factor = jnp.exp(row_max - new_max)
        totals = totals * factor + jnp.sum(expo, axis=-1)
        weighted = weighted * factor[..., None] + jnp.einsum(
            "hgqk,khd->hgqd", expo.astype(jnp.bfloat16), v_heads, preferred_element_type=jnp.float32
        )
        return (new_max, totals, weighted)

    start_state = (
        jnp.full((kv_heads, group_count, row_count), negative, jnp.float32),
        jnp.zeros((kv_heads, group_count, row_count), jnp.float32),
        jnp.zeros((kv_heads, group_count, row_count, head_dim), jnp.float32),
    )
    pieces = (
        lax.all_gather(key_narrow, "ctx", axis=0, tiled=True),
        lax.all_gather(value_narrow, "ctx", axis=0, tiled=True),
    )
    fold_state = sweep_keys(start_state, pieces[0], pieces[1], forward_block)
    row_max, totals, weighted = fold_state
    attn_four = weighted / totals[..., None]
    log_total = row_max + jnp.log(totals)
    attn = jnp.transpose(attn_four, (2, 0, 1, 3)).reshape(row_count, -1)
    attn_low = attn.astype(jnp.bfloat16)
    h_mid = x_float + matmul(attn_low, gathered[6])
    h_normf, post_norm_back = jax.vjp(norm_gain, h_mid, g_post)
    h_norm = h_normf.astype(jnp.bfloat16)
    gate_out = matmul(h_norm, gathered[8])
    up_out = matmul(h_norm, gathered[9])
    act_float, swiglu_back = jax.vjp(swiglu, gate_out, up_out)
    act_low = act_float.astype(jnp.bfloat16)
    row_mask = row_valid.astype(jnp.float32)[:, None]
    block_out = (row_mask * (h_mid + matmul(act_low, gathered[10]))).astype(jnp.bfloat16)
    again = (
        lax.all_gather(shards[0], ("ctx", "fsdp"), axis=0, tiled=True),
        lax.all_gather(shards[1], ("ctx", "fsdp"), axis=0, tiled=True),
        lax.all_gather(shards[2], ("ctx", "fsdp"), axis=0, tiled=True),
        lax.all_gather(shards[3], ("ctx", "fsdp"), axis=0, tiled=True),
        lax.all_gather(shards[4], ("ctx", "fsdp"), axis=0, tiled=True),
        lax.all_gather(shards[5], ("ctx", "fsdp"), axis=0, tiled=True),
        lax.all_gather(shards[6], ("ctx", "fsdp"), axis=0, tiled=True),
        lax.all_gather(shards[7], ("ctx", "fsdp"), axis=0, tiled=True),
        lax.all_gather(shards[8], ("ctx", "fsdp"), axis=0, tiled=True),
        lax.all_gather(shards[9], ("ctx", "fsdp"), axis=0, tiled=True),
        lax.all_gather(shards[10], ("ctx", "fsdp"), axis=0, tiled=True),
    )
    d_block = d_out[0].astype(jnp.float32) * row_mask
    dm_low = d_block.astype(jnp.bfloat16)
    grad_down = inner(act_low, dm_low)
    d_act = backdot(dm_low, again[10])
    d_gate, d_up = swiglu_back(d_act)
    dg_low = d_gate.astype(jnp.bfloat16)
    du_low = d_up.astype(jnp.bfloat16)
    grad_gate = inner(h_norm, dg_low)
    grad_up = inner(h_norm, du_low)
    d_hnorm = backdot(dg_low, again[8]) + backdot(du_low, again[9])
    d_hpart, grad_post = post_norm_back(d_hnorm)
    d_hmid = d_block + d_hpart
    d_res = d_hmid.astype(jnp.bfloat16)
    grad_wout = inner(attn_low, d_res)
    d_attn = backdot(d_res, again[6]).astype(jnp.bfloat16)
    d_attn4 = d_attn.reshape(row_count, kv_heads, group_count, head_dim)
    delta = jnp.einsum("qhgd,hgqd->hgq", d_attn4.astype(jnp.float32), attn_four)

    def backward_block(carry, k_block, v_block, allowed, first_key):
        d_query, d_kv = carry
        key_count = k_block.shape[0]
        k_heads = k_block.reshape(-1, kv_heads, head_dim)
        v_heads = v_block.reshape(-1, kv_heads, head_dim)
        mask_four = allowed[None, None]
        score = (
            jnp.einsum("qhgd,khd->hgqk", q_low4, k_heads, preferred_element_type=jnp.float32)
            * score_scale
        )
        prob = jnp.where(mask_four, jnp.exp(score - log_total[..., None]), 0.0)
        prob_low = prob.astype(jnp.bfloat16)
        d_prob = jnp.einsum("qhgd,khd->hgqk", d_attn4, v_heads, preferred_element_type=jnp.float32)
        d_score = (prob * (d_prob - delta[..., None])).astype(jnp.bfloat16)
        d_query = d_query + jnp.einsum(
            "hgqk,khd->qhgd", d_score, k_heads, preferred_element_type=jnp.float32
        )
        d_key = (
            jnp.einsum("hgqk,qhgd->khd", d_score, q_low4, preferred_element_type=jnp.float32)
            * score_scale
        )
        d_value = jnp.einsum(
            "hgqk,qhgd->khd", prob_low, d_attn4, preferred_element_type=jnp.float32
        )
        joined = jnp.concatenate(
            [d_key.reshape(key_count, -1), d_value.reshape(key_count, -1)], axis=1
        )
        before = lax.dynamic_slice_in_dim(d_kv, first_key, key_count, 0)
        d_kv = lax.dynamic_update_slice_in_dim(d_kv, before + joined, first_key, 0)
        return (d_query, d_kv)

    back_start = (
        jnp.zeros((row_count, kv_heads, group_count, head_dim), jnp.float32),
        jnp.zeros((rows_per_group, 2 * kv_width), jnp.float32),
    )
    pieces = (
        lax.all_gather(key_narrow, "ctx", axis=0, tiled=True),
        lax.all_gather(value_narrow, "ctx", axis=0, tiled=True),
    )
    back_state = sweep_keys(back_start, pieces[0], pieces[1], backward_block)
    d_qrot = back_state[0].reshape(row_count, -1) * score_scale
    d_kv_own = lax.psum_scatter(
        back_state[1].astype(jnp.bfloat16), "ctx", scatter_dimension=0, tiled=True
    ).astype(jnp.float32)
    d_krot = d_kv_own[:, :kv_width]
    d_vpre = d_kv_own[:, kv_width:]
    d_qpre, d_kpre, grad_qgain, grad_kgain = post_back((d_qrot, d_krot))
    dq_low = d_qpre.astype(jnp.bfloat16)
    dk_low = d_kpre.astype(jnp.bfloat16)
    dv_low = d_vpre.astype(jnp.bfloat16)
    grad_query = inner(x_norm, dq_low)
    grad_key = inner(x_norm, dk_low)
    grad_value = inner(x_norm, dv_low)
    d_xnorm = backdot(dq_low, again[1]) + backdot(dk_low, again[2]) + backdot(dv_low, again[3])
    d_xpart, grad_ingain = in_back(d_xnorm)
    d_hidden = d_hmid + d_xpart
    owned = (
        lax.psum_scatter(grad_ingain, ("ctx", "fsdp"), scatter_dimension=0, tiled=True),
        lax.psum_scatter(grad_query, ("ctx", "fsdp"), scatter_dimension=0, tiled=True),
        lax.psum_scatter(grad_key, ("ctx", "fsdp"), scatter_dimension=0, tiled=True),
        lax.psum_scatter(grad_value, ("ctx", "fsdp"), scatter_dimension=0, tiled=True),
        lax.psum_scatter(grad_qgain, ("ctx", "fsdp"), scatter_dimension=0, tiled=True),
        lax.psum_scatter(grad_kgain, ("ctx", "fsdp"), scatter_dimension=0, tiled=True),
        lax.psum_scatter(grad_wout, ("ctx", "fsdp"), scatter_dimension=0, tiled=True),
        lax.psum_scatter(grad_post, ("ctx", "fsdp"), scatter_dimension=0, tiled=True),
        lax.psum_scatter(grad_gate, ("ctx", "fsdp"), scatter_dimension=0, tiled=True),
        lax.psum_scatter(grad_up, ("ctx", "fsdp"), scatter_dimension=0, tiled=True),
        lax.psum_scatter(grad_down, ("ctx", "fsdp"), scatter_dimension=0, tiled=True),
    )
    return (
        block_out[None],
        d_hidden[None],
        owned[0],
        owned[1],
        owned[2],
        owned[3],
        owned[4],
        owned[5],
        owned[6],
        owned[7],
        owned[8],
        owned[9],
        owned[10],
    )


def on_device(*args):
    n = lax.axis_size("ctx")
    hidden_in, w_key, w_out, w_gate, q_gain = args[0], args[4], args[8], args[10], args[6]
    hd = q_gain.shape[0] * n * lax.axis_size("fsdp")
    heads, ff = w_key.shape[1] // hd, w_gate.shape[1] // n
    even = heads % n == 0 and ff % LANES == 0 and w_key.shape[0] % 16 == 0 and w_out.shape[0] % 16 == 0
    if even and heads == n == 8 and hidden_in.shape[1] == TILE:
        return on_plane(*args)
    return on_rows(*args)


def solution(mesh):
    in_specs = (
        P("fsdp", "ctx", None),
        P("fsdp", None),
        P(("ctx", "fsdp")),
        P(("ctx", "fsdp"), None),
        P(("ctx", "fsdp"), None),
        P(("ctx", "fsdp"), None),
        P(("ctx", "fsdp")),
        P(("ctx", "fsdp")),
        P(("ctx", "fsdp"), None),
        P(("ctx", "fsdp")),
        P(("ctx", "fsdp"), None),
        P(("ctx", "fsdp"), None),
        P(("ctx", "fsdp"), None),
        P("fsdp", "ctx", None),
    )
    out_specs = (
        P("fsdp", "ctx", None),
        P("fsdp", "ctx", None),
        P(("ctx", "fsdp")),
        P(("ctx", "fsdp"), None),
        P(("ctx", "fsdp"), None),
        P(("ctx", "fsdp"), None),
        P(("ctx", "fsdp")),
        P(("ctx", "fsdp")),
        P(("ctx", "fsdp"), None),
        P(("ctx", "fsdp")),
        P(("ctx", "fsdp"), None),
        P(("ctx", "fsdp"), None),
        P(("ctx", "fsdp"), None),
    )
    return jax.shard_map(
        on_device, mesh=mesh, in_specs=in_specs, out_specs=out_specs, check_vma=False
    )
```

```python
import functools
import math

import jax
import jax.numpy as jnp
import numpy as np
from jax import lax
from jax.experimental import pallas as pl
from jax.experimental.pallas import tpu as pltpu
from jax.sharding import PartitionSpec as P

BF = jnp.bfloat16
F32 = jnp.float32
MESH = pl.DeviceIdType.MESH
VMEM = pl.BlockSpec(memory_space=pltpu.VMEM)
GAIN_ROWS = 24
LANES = 128
TILE = 256
LIMIT = 61 * 2**20
CORE, ALONG_X, ALONG_Y, ACROSS = 1, 2, 4, 6
CHIPS = (ALONG_X, ALONG_Y, ACROSS)
NEXT = (ALONG_X, ALONG_Y)


def dot(a, b):
    return jnp.dot(a, b, preferred_element_type=F32)


def dot_rt(a, b):
    return lax.dot_general(a, b, (((1,), (1,)), ((), ())), preferred_element_type=F32)


def dot_lt(a, b):
    return lax.dot_general(a, b, (((0,), (0,)), ((), ())), preferred_element_type=F32)


def flip(place, mask, size):
    out, bit = 0, 1
    while bit < size:
        out = out + bit * lax.rem(lax.div(place, bit) + (mask // bit) % 2, 2)
        bit *= 2
    return out


class Net:
    def __init__(self, n, nz, tiles, send, recv):
        self.n, self.nz, self.tiles, self.send, self.recv = n, nz, tiles, send, recv
        self.c = lax.axis_index("ctx")
        self.z = lax.axis_index("fsdp")
        self.core = lax.rem(self.c, 2)
        self.slot = 0

    def slots(self, count):
        first = self.slot
        self.slot += count
        return first

    def at(self, mask):
        return flip(self.c, mask, self.n)

    def zat(self, mask):
        return flip(self.z, mask, self.nz)

    def peer(self, mask):
        return (self.at(mask), self.z)

    def zpeer(self, mask):
        return (self.c, self.zat(mask))

    def tile(self, mask, s):
        chip = lax.div(self.at(mask), 2)
        return chip if s == 0 else self.tiles - 1 - chip

    def view(self, buf, mask, s):
        half = TILE // 2
        core = lax.rem(self.at(mask), 2)
        first = core if s == 0 else 1 - core
        return buf.at[self.tile(mask, s), pl.ds(pl.multiple_of(first * half, half), half), :]

    def barrier(self):
        bar = pltpu.get_barrier_semaphore()
        for mask in range(1, self.n):
            pl.semaphore_signal(bar, inc=1, device_id=self.peer(mask), device_id_type=MESH)
        for mask in range(1, self.nz):
            pl.semaphore_signal(bar, inc=1, device_id=self.zpeer(mask), device_id_type=MESH)
        pl.semaphore_wait(bar, self.n + self.nz - 2)

    def copy(self, src, dst, slot, device, send_slot=None):
        return pltpu.make_async_remote_copy(
            src_ref=src,
            dst_ref=dst,
            send_sem=self.send.at[slot if send_slot is None else send_slot],
            recv_sem=self.recv.at[slot],
            device_id=device,
            device_id_type=MESH,
        )

    def to_plane(self, src, dst):
        base = self.slots(self.n)
        out = []
        for mask in range(1, self.n):
            cp = self.copy(src(mask), dst, base + mask, self.peer(mask))
            cp.start()
            out.append(cp)
        return out

    def to_line(self, src, dst):
        base = self.slots(self.nz)
        out = []
        for mask in range(1, self.nz):
            cp = self.copy(src(mask), dst(mask), base + mask, self.zpeer(mask))
            cp.start()
            out.append(cp)
        return out


class Line:
    def __init__(self, net, view):
        self.net, self.view = net, view
        self.base = net.slots(net.nz)
        self.middle = (net.z == 1) | (net.z == 2)
        self.relayed = net.nz == 4
        own = view(net.z)
        self.direct = [m for m in range(1, net.nz) if not (self.relayed and m == 3)]
        self.copies = {m: net.copy(own, own, self.base + m, net.zpeer(m)) for m in range(1, net.nz)}
        for m in self.direct[::-1]:
            self.copies[m].start()
        if self.relayed:
            far = view(net.zat(2))
            self.passed = net.copy(far, far, self.base + 3, net.zpeer(1), send_slot=self.base)

    def relay(self):
        if self.relayed:
            self.copies[2].wait_recv()

            @pl.when(self.middle)
            def _():
                self.passed.start()
                self.copies[3].start()

    def arrive(self):
        for m, cp in self.copies.items():
            if not (self.relayed and m == 2):
                cp.wait_recv()

    def finish(self):
        for m in self.direct:
            self.copies[m].wait_send()
        if self.relayed:

            @pl.when(self.middle)
            def _():
                self.copies[3].wait_send()
                self.passed.wait_send()


class LineSum:
    def __init__(self, net, piece, inn, passing, both):
        self.net, self.piece, self.inn, self.passing, self.both = net, piece, inn, passing, both
        self.base = net.slots(net.nz)
        self.middle = (net.z == 1) | (net.z == 2)
        self.relayed = net.nz == 4
        if not self.relayed:
            for m in range(1, net.nz):
                self.to(m).start()
            return

        @pl.when(jnp.logical_not(self.middle))
        def _():
            self.far().start()
            self.to(2).start()
            self.to(1).start()

        @pl.when(self.middle)
        def _():
            self.to(3).start()
            self.to(1).start()

    def to(self, m):
        return self.net.copy(self.piece(self.net.zat(m)), self.inn.at[m - 1], self.base + m, self.net.zpeer(m))

    def far(self):
        return self.net.copy(
            self.piece(self.net.zat(3)), self.passing, self.base, self.net.zpeer(1), send_slot=self.base + 3
        )

    def joined(self):
        return self.net.copy(self.both, self.inn.at[1], self.base + 2, self.net.zpeer(2))

    def relay(self):
        if self.relayed:

            @pl.when(self.middle)
            def _():
                self.far().wait_recv()
                own = self.piece(self.net.zat(2))[...].astype(F32)
                self.both[...] = (own + self.passing[...].astype(F32)).astype(BF)
                self.joined().start()

    def total(self, write):
        def some(masks):
            value = self.piece(self.net.z)[...].astype(F32)
            for m in masks:
                self.to(m).wait_recv()
                value = value + self.inn[m - 1].astype(F32)
            write(value)

        if not self.relayed:
            some(range(1, self.net.nz))
            return

        @pl.when(self.middle)
        def _():
            some((1, 2, 3))

        @pl.when(jnp.logical_not(self.middle))
        def _():
            some((1, 2))

    def finish(self):
        if not self.relayed:
            for m in range(1, self.net.nz):
                self.to(m).wait_send()
            return
        self.to(1).wait_send()
        self.to(2).wait_send()
        self.to(3).wait_send()


class Gather:
    def __init__(self, net, buf):
        self.net, self.buf = net, buf
        self.base = net.slots(2 * net.n)
        self.sent = []

    def send(self, mask, s, to, arrives_as):
        view = self.net.view(self.buf, mask, s)
        slot = self.base + 2 * arrives_as + s
        cp = self.net.copy(view, view, slot, self.net.peer(to))
        cp.start()
        self.sent.append(cp)

    def start(self, s):
        for mask in (CORE, ALONG_X, ALONG_Y):
            self.send(0, s, mask, mask)

    def arrive(self, mask, s):
        view = self.net.view(self.buf, mask, s)
        self.net.copy(view, view, self.base + 2 * mask + s, self.net.peer(mask)).wait_recv()
        if mask % 2 == 0:
            if mask == (ALONG_X, ALONG_Y)[s]:
                self.send(mask, s, (ALONG_Y, ALONG_X)[s], ACROSS)
            self.send(mask, s, CORE, mask + 1)

    def finish(self):
        for cp in self.sent:
            cp.wait_send()


class PlaneSum:
    def __init__(self, net, sib_out, sib_in, out, inn, mine, keep, joined):
        self.net, self.joined = net, joined
        self.sib_out, self.sib_in, self.out, self.inn, self.mine, self.keep = sib_out, sib_in, out, inn, mine, keep
        self.base = net.slots(2 * net.n)
        self.sent, self.queue, self.given = [], [], 0

    def sibling(self, mask, s):
        return self.net.copy(
            self.sib_out.at[mask + s], self.sib_in.at[mask + s], self.base + 2 * (mask + 1) + s, self.net.peer(CORE)
        )

    def chip(self, mask, s):
        i = mask - 2 + s
        to = NEXT[s] if mask == ACROSS and self.joined else mask
        return self.net.copy(self.out.at[i], self.inn.at[i], self.base + 2 * mask + s, self.net.peer(to))

    def give(self, mask, s, value):
        half = TILE // 2
        place = self.given % 2
        self.given += 1
        self.mine[place] = value
        mine = lax.rem(self.net.core + s, 2) * half
        own = pl.ds(pl.multiple_of(mine, half), half)
        other = pl.ds(pl.multiple_of(half - mine, half), half)
        self.sib_out[mask + s] = self.mine[place, other, :].astype(BF)
        cp = self.sibling(mask, s)
        cp.start()
        self.sent.append(cp)
        self.queue.append((mask, s, place, own))
        if len(self.queue) > 1:
            self.combine()

    def combine(self):
        mask, s, place, own = self.queue.pop(0)
        self.sibling(mask, s).wait_recv()
        both = self.mine[place, own, :] + self.sib_in[mask + s].astype(F32)
        if mask == 0:
            self.keep[s] = both
            return
        if self.joined and mask == NEXT[1 - s]:
            self.chip(ACROSS, s).wait_recv()
            both = both + self.inn[ACROSS - 2 + s].astype(F32)
        self.out[mask - 2 + s] = both.astype(BF)
        cp = self.chip(mask, s)
        cp.start()
        self.sent.append(cp)

    def flush(self):
        while self.queue:
            self.combine()

    def total(self, s):
        value = self.keep[s]
        for mask in NEXT if self.joined else CHIPS:
            self.chip(mask, s).wait_recv()
            value = value + self.inn[mask - 2 + s].astype(F32)
        return value

    def finish(self):
        for cp in self.sent:
            cp.wait_send()


SEND_ORDER = ((ACROSS, 0), (ACROSS, 1), (ALONG_X, 0), (ALONG_Y, 1), (ALONG_Y, 0), (ALONG_X, 1), (0, 0), (0, 1))
ARRIVE_ORDER = ((0, 0), (0, 1), (ALONG_X, 0), (ALONG_Y, 0), (ALONG_X, 1), (ALONG_Y, 1), (ACROSS, 0), (ACROSS, 1))


def arrive_for(gath, mask, s):
    if mask == ALONG_X:
        gath.arrive(ALONG_X, s)
        gath.arrive(ALONG_Y, s)
    elif mask == ACROSS:
        gath.arrive(ACROSS, s)
    gath.arrive(mask + 1, s)


def row_of(g, first, count):
    return jnp.concatenate([g[first + j : first + j + 1, :] for j in range(count)], axis=1)


def split_three(value, lane):
    first = value.astype(BF).astype(F32)
    rest = value - first
    second = rest.astype(BF).astype(F32)
    third = rest - second
    out = jnp.where(lane == 0, first, jnp.where(lane == 1, second, jnp.where(lane == 2, third, 0.0)))
    return out.astype(BF)


def first_keys(lengths_ref, at):
    start = jnp.zeros_like(at)
    begin = 0
    for s in range(lengths_ref.shape[1]):
        start = jnp.where(at >= begin, begin, start)
        begin = begin + lengths_ref[0, s]
    padding = at >= begin
    return jnp.where(padding, at, start), padding


def halves(a, hd):
    lane = lax.broadcasted_iota(jnp.int32, a.shape, 1)
    other = pltpu.roll(a, hd // 2, 1)
    return jnp.where(lane < hd // 2, a, other), jnp.where(lane < hd // 2, -other, a)


def angle_sum(a, b, hd):
    lane = lax.broadcasted_iota(jnp.int32, jnp.broadcast_shapes(a.shape, b.shape), 1)
    a2, b2 = pltpu.roll(a, hd // 2, 1), pltpu.roll(b, hd // 2, 1)
    return jnp.where(lane < hd // 2, a * b - a2 * b2, a * b2 + a2 * b)


def minus_angle(a, hd):
    lane = lax.broadcasted_iota(jnp.int32, a.shape, 1)
    return jnp.where(lane < hd // 2, a, -a)


def norm_back(v, gain, dy, eps):
    r = lax.rsqrt(jnp.mean(v * v, axis=-1, keepdims=True) + eps)
    gdy = gain * dy
    dv = r * gdy - v * (r * r * r) * jnp.mean(gdy * v, axis=-1, keepdims=True)
    return jnp.sum(dy * v * r, axis=0, keepdims=True), dv


def front(cfg, lengths_ref, x_ref, do_ref, wq_ref, wk_ref, wv_ref, wo_ref, wg_ref, wu_ref, wd_ref, gshare_ref, table_ref,
          qx_out, kx_out, vx_out, attn_out, mo_out, pre_out, cs_out, xn_out, w_out, wo_out, gwd_out, ggu_out,
          hmid_out, dhmid_out, dres_out, gains_out, gpost_out,
          wsend, gsend, w, wo_all, gu, wd_all, grow, gpart, gbuf, gz, xg, xn, pre, cs, qx, kx, vx, acc, attn,
          dblk, act, dgu, mo, sib_out, sib_in, out, inn, mine, keep, hmid, dhmid, dres, gwd_buf, ggu_buf,
          local, send, recv):
    n, nz, ql, kvl, hd, ff = cfg["n"], cfg["nz"], cfg["ql"], cfg["kvl"], cfg["hd"], cfg["ff"]
    eps = cfg["eps"]
    t, dm = x_ref.shape
    half = TILE // 2
    tiles = qx.shape[0]
    rows = n * t
    net = Net(n, nz, tiles, send, recv)
    c, z = net.c, net.z
    stores = []

    def store(src, dst):
        cp = pltpu.make_async_copy(src, dst, local.at[len(stores)])
        cp.start()
        stores.append(cp)
        return cp

    qw, kw = ql * hd, kvl * hd
    for j in range(n):
        wsend[j, :, :qw] = wq_ref[:, j * qw : (j + 1) * qw]
        wsend[j, :, qw : qw + kw] = wk_ref[:, j * kw : (j + 1) * kw]
        wsend[j, :, qw + kw :] = wv_ref[:, j * kw : (j + 1) * kw]
        gsend[j, :, :ff] = wg_ref[:, j * ff : (j + 1) * ff]
        gsend[j, :, ff:] = wu_ref[:, j * ff : (j + 1) * ff]
    grow[...] = jnp.zeros_like(grow)
    grow[0:1, : gshare_ref.shape[1]] = gshare_ref[...].astype(F32)
    row = jnp.broadcast_to(grow[0:1, :], (8, LANES))
    lane8 = lax.broadcasted_iota(jnp.int32, (8, LANES), 1)
    at = lax.broadcasted_iota(jnp.int32, (8, LANES), 0) * LANES + lane8
    wide, narrow = dm // (n * nz), hd // (n * nz)
    place = c * nz + z

    def placed(first, share, row0):
        shift = lax.rem(place * share, LANES)
        moved = pltpu.roll(row, lax.rem(shift + LANES - first, LANES), 1)
        return jnp.where((at >= row0 + place * share) & (at < row0 + (place + 1) * share), moved, 0.0)

    gpart[0:8, :] = placed(0, wide, 0)
    gpart[8:16, :] = placed(wide, wide, 0)
    gpart[16:24, :] = placed(2 * wide, narrow, 0) + placed(2 * wide + narrow, narrow, LANES)
    for s in range(2):
        net.view(xg, 0, s)[...] = x_ref[s * half : (s + 1) * half, :]
    w[c, z] = wsend[c]
    gu[c, z] = gsend[c]
    wo_all[z] = wo_ref[...]
    wd_all[z] = wd_ref[...]
    net.barrier()
    plane_g = net.to_plane(lambda m: gpart, gbuf.at[c])
    plane_w = net.to_plane(lambda m: wsend.at[net.at(m)], w.at[c, z])
    line_o = Line(net, lambda f: wo_all.at[f])
    gath = Gather(net, xg)
    gath.start(0)
    gath.start(1)
    gbuf[c] = gpart[...]
    for cp in plane_g:
        cp.wait_recv()
    gz[z] = jnp.sum(gbuf[...], axis=0)
    line_g = net.to_line(lambda m: gz.at[z], lambda m: gz.at[z])
    for cp in plane_w:
        cp.wait_recv()
    line_w = Line(net, lambda f: w.at[:, f])

    lo = table_ref[0:half, :]
    begins, firsts = [], []
    begin = 0
    for s in range(lengths_ref.shape[1]):
        begins.append(begin)
        hi_row = table_ref[pl.ds(half + lax.div(begin, half), 1), :]
        lo_row = table_ref[pl.ds(lax.rem(begin, half), 1), :]
        firsts.append(minus_angle(angle_sum(hi_row, lo_row, hd), hd))
        begin = begin + lengths_ref[0, s]
    end = begin
    one = jnp.where(lax.broadcasted_iota(jnp.int32, (1, hd), 1) < hd // 2, 1.0, 0.0)

    def positions(b, carry):
        at = b * half + lax.broadcasted_iota(jnp.int32, (half, hd), 0)
        hi_row = table_ref[pl.ds(half + b, 1), :]
        shift = angle_sum(hi_row, firsts[0], hd)
        for begin, first in zip(begins[1:], firsts[1:]):
            shift = jnp.where(at >= begin, angle_sum(hi_row, first, hd), shift)
        both = jnp.where(at >= end, one, angle_sum(shift, lo, hd))
        cs[lax.div(b, 2), pl.ds(pl.multiple_of(lax.rem(b, 2) * half, half), half), :] = both
        return carry

    lax.fori_loop(0, 2 * tiles, positions, 0)
    for cp in line_g:
        cp.wait_recv()
    gains = jnp.sum(gz[...], axis=0)
    g_in = row_of(gains, 0, dm // LANES)
    g_post = row_of(gains, 8, dm // LANES)
    g_q = gains[16:17, :]
    g_k = gains[17:18, :]
    step = 32

    def normalise(tile):
        def some(i, carry):
            here = pl.ds(pl.multiple_of(i * step, step), step)
            v = xg[tile, here, :].astype(F32)
            r = lax.rsqrt(jnp.mean(v * v, axis=-1, keepdims=True) + eps)
            xn[tile, here, :] = (v * r * g_in).astype(BF)
            return carry

        lax.fori_loop(0, TILE // step, some, 0)

    for mask, s in ARRIVE_ORDER:
        arrive_for(gath, mask, s)
        normalise(net.tile(mask, s))
        if mask == ALONG_Y and s == 1:
            plane_u = net.to_plane(lambda m: gsend.at[net.at(m)], gu.at[c, z])
            line_w.relay()
            line_d = Line(net, lambda f: wd_all.at[f])
    line_o.relay()
    gath_d = Gather(net, dblk)
    for s in range(2):
        first = lax.rem(net.core + s, 2) * half + net.tile(0, s) * TILE
        padding = first + lax.broadcasted_iota(jnp.int32, (half, 1), 0) >= end
        net.view(dblk, 0, s)[...] = jnp.where(padding, 0.0, do_ref[s * half : (s + 1) * half, :].astype(F32)).astype(BF)
        gath_d.start(s)
    for cp in plane_u:
        cp.wait_recv()
    line_u = Line(net, lambda f: gu.at[:, f])
    line_w.arrive()
    wqkv = w[...].reshape(dm, -1)
    lane_b = lax.broadcasted_iota(jnp.int32, (TILE, hd), 1)
    minus = jnp.where(lane_b < 3, -1.0, 0.0).astype(BF)

    def heads(tile, carry):
        qkv = dot(xn[tile], wqkv)
        width = qw + kw
        pre[tile] = qkv[:, :width].astype(BF)
        cos, sin = halves(cs[tile], hd)
        for h in range(ql + kvl):
            v = qkv[:, h * hd : (h + 1) * hd]
            r = lax.rsqrt(jnp.mean(v * v, axis=-1, keepdims=True) + eps)
            hat = v * r * (g_q if h < ql else g_k)
            low = (hat * cos + pltpu.roll(hat, hd // 2, 1) * sin).astype(BF)
            if h < ql:
                qx[tile, h, :, :hd] = low
            else:
                kx[tile, :, :hd] = low
        vx[tile, :, :hd] = qkv[:, width:].astype(BF)
        kx[tile, :, hd:] = minus
        vx[tile, :, hd:] = minus
        return carry

    lax.fori_loop(0, tiles, heads, 0)
    hn = xn
    xn_stored = store(xn, xn_out)
    for src, dst in ((pre, pre_out), (cs, cs_out), (kx, kx_out), (vx, vx_out), (w, w_out)):
        store(src, dst)
    line_o.arrive()
    wout = wo_all[...].reshape(-1, dm)
    store(wo_all, wo_out)

    high = ql * TILE
    factor = math.log2(math.e) / math.sqrt(hd)
    lane_q = lax.broadcasted_iota(jnp.int32, (high, hd), 1)

    def attend(i):
        q = qx[i, :, :, :hd].reshape(high, hd)
        start = first_keys(lengths_ref, i * TILE + lax.broadcasted_iota(jnp.int32, (TILE, 1), 0))[0]
        q_at = i * TILE + lax.broadcasted_iota(jnp.int32, (TILE, TILE), 0)
        acc[...] = jnp.zeros_like(acc)

        def k_tile(j, carry):
            s = dot_rt(q, kx[j, :, :hd])
            k_at = j * TILE + lax.broadcasted_iota(jnp.int32, (TILE, TILE), 1)
            allowed = (k_at <= q_at) & (k_at >= start)
            e = jnp.where(allowed[None], jnp.exp2(s * factor).reshape(ql, TILE, TILE), 0.0)
            acc[...] += dot(e.astype(BF).reshape(high, TILE), vx[j])
            return carry

        lax.fori_loop(jnp.maximum(i - cfg["window"], 0), i + 1, k_tile, 0)
        total = -acc[:, hd : hd + 1]
        low = (acc[:, :hd] / total).astype(BF)
        for h in range(ql):
            attn[i, :, h * hd : (h + 1) * hd] = low[h * TILE : (h + 1) * TILE]
        extra = jnp.broadcast_to(jnp.log(total) * math.sqrt(hd), (high, hd))
        qx[i, :, :, hd:] = split_three(extra, lane_q).reshape(ql, TILE, hd)

    xn_stored.wait()
    gath.finish()
    sum1 = PlaneSum(net, sib_out, sib_in, out, inn, mine, keep, True)
    gath1 = Gather(net, hn)

    def middle(s):
        h_mid = x_ref[s * half : (s + 1) * half, :].astype(F32) + sum1.total(s)
        hmid[s] = h_mid
        r = lax.rsqrt(jnp.mean(h_mid * h_mid, axis=-1, keepdims=True) + eps)
        net.view(hn, 0, s)[...] = (h_mid * r * g_post).astype(BF)
        gath1.start(s)

    for k, (mask, s) in enumerate(SEND_ORDER):
        tile = net.tile(mask, s)
        attend(tile)
        sum1.give(mask, s, dot(attn[tile], wout))
        if k == 2:
            for half_s in range(2):
                gath_d.arrive(ALONG_X, half_s)
                gath_d.arrive(ALONG_Y, half_s)
        if k == 4:
            line_d.relay()
        if k == 7:
            line_u.relay()
    sum1.flush()
    store(qx, qx_out)
    store(attn, attn_out)
    for s in range(2):
        gath_d.arrive(ACROSS, s)
    middle(0)
    middle(1)
    store(hmid, hmid_out)
    sum1.finish()
    for mask in (CORE, ALONG_X + 1, ALONG_Y + 1, ACROSS + 1):
        for s in range(2):
            gath_d.arrive(mask, s)
    line_u.arrive()
    line_d.arrive()
    wgu = gu[...].reshape(dm, -1)
    wd = wd_all[...].reshape(-1, dm)
    mo_stores = []

    def block(d):
        both = dot(hn[d], wgu)
        gate, up = both[:, :ff], both[:, ff:]
        sig = 1.0 / (1.0 + jnp.exp(-gate))
        silu = gate * sig
        low = (silu * up).astype(BF)
        act[d] = low
        if len(mo_stores) > 1:
            mo_stores[-2].wait()
        place = len(mo_stores) % 2
        mo[place] = dot(low, wd).astype(BF)
        mo_stores.append(store(mo.at[place], mo_out.at[d]))
        d_act = dot_rt(dblk[d], wd)
        dgu[d, :, :ff] = (d_act * up * sig * (1.0 + gate * (1.0 - sig))).astype(BF)
        dgu[d, :, ff:] = (d_act * silu).astype(BF)
        return dot_rt(dgu[d], wgu)

    sum2 = PlaneSum(net, sib_out, sib_in, out, inn, mine, keep, False)
    for mask, s in ARRIVE_ORDER:
        arrive_for(gath1, mask, s)
        sum2.give(mask, s, block(net.tile(mask, s)))
    sum2.flush()
    dgu_all = dgu[...].reshape(rows, 2 * ff)
    gwd_buf[...] = dot_lt(act[...].reshape(rows, ff), dblk[...].reshape(rows, dm)).astype(BF).reshape(gwd_buf.shape)
    store(gwd_buf, gwd_out)
    per = dm // n
    cols = 2
    part_w = dm // cols
    for j in range(cols):
        part = dot_lt(hn[:, :, j * part_w : (j + 1) * part_w].reshape(rows, part_w), dgu_all)
        ggu_buf[j * (n // cols) : (j + 1) * (n // cols)] = part.astype(BF).reshape(n // cols, nz, per // nz, 2 * ff)
    store(ggu_buf, ggu_out)
    g_sum = 0.0
    for s in range(2):
        g_part, dv = norm_back(hmid[s], g_post, sum2.total(s), eps)
        g_sum = g_sum + g_part
        d_hmid = net.view(dblk, 0, s)[...].astype(F32) + dv
        dhmid[s] = d_hmid
        dres[s] = d_hmid.astype(BF)
    store(dhmid, dhmid_out)
    store(dres, dres_out)
    gains_out[...] = gains
    gpost_out[...] = g_sum
    for part in (gath_d, gath1, sum2, line_o, line_w, line_u, line_d):
        part.finish()
    for cp in plane_g + plane_w + plane_u + line_g:
        cp.wait_send()
    for cp in stores:
        if not any(cp is other for other in [xn_stored] + mo_stores[:-2]):
            cp.wait()


def back(cfg, lengths_ref, qx_ref, kx_ref, vx_ref, attn_ref, wo_ref, mo_ref, pre_ref, cs_ref, xn_ref, w_ref, gwd_ref,
         ggu_ref, hmid_ref, dhmid_ref, dres_ref, gains_ref, gpost_ref, x_ref,
         block_out, dx_out, gwo_out, gwd_out, ggu_out, gqkv_out, gains_out,
         mo_own, mo_in, mo_send, mo_recv, pre, cs, xn, w, hmid, dhmid, dresg, dq, dk, dv, dax, gwd, gwd_in, ggu,
         ggu_line, ggu_sum, ggu_in, gwo, gwo_in, dqkv, gbuf, g_line, gsum, g_in, part, gplane, gz,
         sib_out, sib_in, out, inn, mine, keep, local, send, recv):
    n, nz, ql, kvl, hd, ff = cfg["n"], cfg["nz"], cfg["ql"], cfg["kvl"], cfg["hd"], cfg["ff"]
    eps = cfg["eps"]
    t, dm = x_ref.shape
    half = TILE // 2
    rows = n * t
    tiles = qx_ref.shape[0]
    qw, kw = ql * hd, kvl * hd
    net = Net(n, nz, tiles, send, recv)
    c, z = net.c, net.z
    loads = []

    def load(src, dst):
        cp = pltpu.make_async_copy(src, dst, local.at[len(loads)])
        cp.start()
        loads.append(cp)
        return cp

    first = [load(dres_ref.at[s], net.view(dresg, 0, s)) for s in range(2)]
    own = {(m, s): load(net.view(mo_ref, m, s), mo_own.at[m + s]) for m in (0,) + CHIPS for s in range(2)}
    first += [load(gwd_ref, gwd), load(ggu_ref, ggu)]
    more = [load(a, b) for a, b in ((pre_ref, pre), (cs_ref, cs), (xn_ref, xn), (w_ref, w), (hmid_ref, hmid),
                                    (dhmid_ref, dhmid))]
    for cp in first:
        cp.wait()
    net.barrier()
    gath = Gather(net, dresg)
    gath.start(0)
    gath.start(1)
    line_d = LineSum(net, lambda f: gwd.at[f], gwd_in, gwd_in.at[nz - 1], gwd_in.at[nz])
    line_u = LineSum(net, lambda f: ggu.at[:, f], ggu_line, ggu_line.at[nz - 1], ggu_line.at[nz])
    base = net.slots(2 * n)
    sib = {}
    for m in CHIPS + (0,):
        for s in range(2):
            cp = net.copy(net.view(mo_ref, m + 1, s), mo_in.at[m + s], base + m + s, net.peer(CORE))
            cp.start()
            sib[m, s] = cp
    wout = wo_ref[...].reshape(-1, dm)
    gains = gains_ref[...]
    g_q = gains[16:17, :]
    g_k = gains[17:18, :]
    high = ql * TILE
    factor = math.log2(math.e) / math.sqrt(hd)
    scale = 1.0 / math.sqrt(hd)
    lane = lax.broadcasted_iota(jnp.int32, (TILE, hd), 1)
    dk[...] = jnp.zeros_like(dk)
    dv[...] = jnp.zeros_like(dv)

    def attend_back(i):
        d_attn = dot_rt(dresg[i], wout).astype(BF)
        prod = d_attn.astype(F32) * attn_ref[i].astype(F32)
        for h in range(ql):
            delta = jnp.sum(prod[:, h * hd : (h + 1) * hd], axis=-1, keepdims=True)
            dax[h * TILE : (h + 1) * TILE, :hd] = d_attn[:, h * hd : (h + 1) * hd]
            dax[h * TILE : (h + 1) * TILE, hd:] = split_three(jnp.broadcast_to(delta, (TILE, hd)), lane)
        qx = qx_ref[i].reshape(high, 2 * hd)
        start = first_keys(lengths_ref, i * TILE + lax.broadcasted_iota(jnp.int32, (1, TILE), 1))[0]
        q_at = i * TILE + lax.broadcasted_iota(jnp.int32, (TILE, TILE), 1)
        dq[...] = jnp.zeros_like(dq)

        def k_tile(j, carry):
            k_at = j * TILE + lax.broadcasted_iota(jnp.int32, (TILE, TILE), 0)
            allowed = (k_at <= q_at) & (k_at >= start)
            allowed = jnp.concatenate([allowed] * ql, axis=1)
            s = dot_rt(kx_ref[j], qx)
            p = jnp.where(allowed, jnp.exp2(s * factor), 0.0)
            ds = (p * dot_rt(vx_ref[j], dax[...])).astype(BF)
            dv[j] += dot(p.astype(BF), dax[:, :hd])
            dk[j] += dot(ds, qx[:, :hd])
            dq[...] += dot_lt(ds, kx_ref[j, :, :hd])
            return carry

        lax.fori_loop(jnp.maximum(i - cfg["window"], 0), i + 1, k_tile, 0)

    def head_back(i, h, dy, gain):
        cos, sin = halves(cs[i], hd)
        dy = dy * cos - pltpu.roll(dy, hd // 2, 1) * sin
        g_part, dpre = norm_back(pre[i, :, h * hd : (h + 1) * hd].astype(F32), gain, dy, eps)
        dqkv[i, :, h * hd : (h + 1) * hd] = dpre.astype(BF)
        return g_part

    gq = jnp.zeros((1, hd), F32)
    mo_base = net.slots(2 * n)

    def mo_chip(m, s):
        to = NEXT[s] if m == ACROSS else m
        return net.copy(mo_send.at[m + s - 2], mo_recv.at[m + s - 2], mo_base + m + s, net.peer(to))

    def send_mo(m, s):
        own[m, s].wait()
        sib[m, s].wait_recv()
        both = mo_own[m + s].astype(F32) + mo_in[m + s].astype(F32)
        if m == NEXT[1 - s]:
            mo_chip(ACROSS, s).wait_recv()
            both = both + mo_recv[ACROSS - 2 + s].astype(F32)
        mo_send[m + s - 2] = both.astype(BF)
        mo_chip(m, s).start()

    for k, (mask, s) in enumerate(ARRIVE_ORDER):
        arrive_for(gath, mask, s)
        i = net.tile(mask, s)
        attend_back(i)
        if k == 0:
            for cp in more[:2]:
                cp.wait()
        for h in range(ql):
            gq = gq + head_back(i, h, dq[h * TILE : (h + 1) * TILE] * scale, g_q)
        if k == 2:
            line_d.relay()
        if k == 4:
            for half_s in range(2):
                for m in (ACROSS, NEXT[half_s]):
                    send_mo(m, half_s)
        if k == 5:
            line_u.relay()
        if k == 6:
            for half_s in range(2):
                send_mo(NEXT[1 - half_s], half_s)
    gwo[...] = dot_lt(attn_ref[...].reshape(rows, qw), dresg[...].reshape(rows, dm)).astype(BF).reshape(gwo.shape)
    line_o = LineSum(net, lambda f: gwo.at[f], gwo_in, gwo_in.at[nz - 1], gwo_in.at[nz])

    def keys_back(i, carry):
        g_part = head_back(i, ql, dk[i] * scale, g_k)
        dqkv[i, :, qw + kw :] = dv[i].astype(BF)
        return carry + g_part

    gk = lax.fori_loop(0, tiles, keys_back, jnp.zeros((1, hd), F32))
    for cp in more[2:]:
        cp.wait()
    per = dm // n
    cols = 2
    part_w = dm // cols
    d_all = dqkv[...].reshape(rows, -1)
    for j in range(cols):
        grad = dot_lt(xn[:, :, j * part_w : (j + 1) * part_w].reshape(rows, part_w), d_all)
        gbuf[j * (n // cols) : (j + 1) * (n // cols)] = grad.astype(BF).reshape(n // cols, nz, per // nz, -1)
    line_q = LineSum(net, lambda f: gbuf.at[:, f], g_line, g_line.at[nz - 1], g_line.at[nz])
    wqkv = w[...].reshape(dm, -1)
    sum1 = PlaneSum(net, sib_out, sib_in, out, inn, mine, keep, True)
    for k, (mask, s) in enumerate(SEND_ORDER):
        sum1.give(mask, s, dot_rt(dqkv[net.tile(mask, s)], wqkv))
        if k == 3:
            line_o.relay()
    sum1.flush()

    def write(ref):
        def store(value):
            ref[...] = value.astype(ref.dtype)

        return store

    line_d.total(write(gwd_out))
    line_u.total(write(ggu_sum))
    line_q.relay()
    plane_u = net.to_plane(lambda m: ggu_sum.at[net.at(m)], ggu_in.at[c])
    ggu_in[c] = ggu_sum[c]
    end = 0
    for s in range(lengths_ref.shape[1]):
        end = end + lengths_ref[0, s]
    for s in range(2):
        own[0, s].wait()
        sib[0, s].wait_recv()
        total = hmid[s] + mo_own[s].astype(F32) + mo_in[s].astype(F32)
        for m in NEXT:
            mo_chip(m, s).wait_recv()
            total = total + mo_recv[m - 2 + s].astype(F32)
        at = lax.rem(net.core + s, 2) * half + net.tile(0, s) * TILE
        padding = at + lax.broadcasted_iota(jnp.int32, (half, 1), 0) >= end
        block_out[s * half : (s + 1) * half, :] = jnp.where(padding, 0.0, total).astype(BF)
    line_o.total(write(gwo_out))
    g_in_row = row_of(gains, 0, dm // LANES)
    grad_in = 0.0
    for s in range(2):
        here = slice(s * half, (s + 1) * half)
        g_part, d_x = norm_back(x_ref[here, :].astype(F32), g_in_row, sum1.total(s), eps)
        grad_in = grad_in + g_part
        dx_out[here, :] = dhmid[s] + d_x
    part[...] = jnp.zeros_like(part)
    for j in range(dm // LANES):
        part[j : j + 1, :] = grad_in[:, j * LANES : (j + 1) * LANES]
        part[8 + j : 9 + j, :] = gpost_ref[:, j * LANES : (j + 1) * LANES]
    part[16:17, :] = gq
    part[17:18, :] = gk
    plane_g = net.to_plane(lambda m: part, gplane.at[c])
    gplane[c] = part[...]
    line_q.total(write(gsum))
    plane_q = net.to_plane(lambda m: gsum.at[net.at(m)], g_in.at[c])
    g_in[c] = gsum[c]
    for cp in plane_g:
        cp.wait_recv()
    gz[z] = jnp.sum(gplane[...], axis=0)
    line_g = net.to_line(lambda m: gz.at[z], lambda m: gz.at[z])
    for cp in plane_u:
        cp.wait_recv()
    ggu_out[...] = ggu_in[...]
    for cp in plane_q:
        cp.wait_recv()
    gqkv_out[...] = g_in[...]
    for cp in line_g:
        cp.wait_recv()
    gains_out[...] = jnp.sum(gz[...], axis=0)
    for part in (gath, sum1, line_d, line_u, line_o, line_q):
        part.finish()
    for cp in line_g + plane_u + plane_g + plane_q + list(sib.values()):
        cp.wait_send()
    for s in range(2):
        for m in CHIPS:
            mo_chip(m, s).wait_send()


def finish(cfg, block_ref, dx_ref, gwo_ref, gwd_ref, ggu_ref, gqkv_ref, gains_ref,
           block_out, dx_out, gin_out, gq_out, gk_out, gv_out, gqg_out, gkg_out, gwo_out, gpost_out, ggate_out, gup_out,
           gwd_out):
    n, nz, ql, kvl, hd, ff = cfg["n"], cfg["nz"], cfg["ql"], cfg["kvl"], cfg["hd"], cfg["ff"]
    block_out[...] = block_ref[...]
    dx_out[...] = dx_ref[...]
    gwo_out[...] = gwo_ref[...]
    gwd_out[...] = gwd_ref[...]
    qw, kw = ql * hd, kvl * hd
    for d in range(n):
        both = gqkv_ref[d].astype(F32)
        gq_out[:, d * qw : (d + 1) * qw] = both[:, :qw]
        gk_out[:, d * kw : (d + 1) * kw] = both[:, qw : qw + kw]
        gv_out[:, d * kw : (d + 1) * kw] = both[:, qw + kw :]
        both = ggu_ref[d].astype(F32)
        ggate_out[:, d * ff : (d + 1) * ff] = both[:, :ff]
        gup_out[:, d * ff : (d + 1) * ff] = both[:, ff:]
    place = lax.axis_index("ctx") * nz + lax.axis_index("fsdp")
    for first, ref in ((0, gin_out), (8, gpost_out), (16, gqg_out), (17, gkg_out)):
        width = ref.shape[1]
        at = place * width
        row = gains_ref[pl.ds(first + lax.div(at, LANES), 1), :]
        ref[...] = pltpu.roll(row, lax.rem(LANES - lax.rem(at, LANES), LANES), 1)[:, :width]


def call(body, cfg, ins, outs, scratch, cid, *args):
    remote = cid is not None
    params = dict(collective_id=cid, has_side_effects=True) if remote else {}
    if remote:
        sems = pltpu.SemaphoreType.DMA((cfg["slots"],))
        scratch = scratch + [pltpu.SemaphoreType.DMA((32,)), sems, sems]
    return pl.pallas_call(
        functools.partial(body, cfg),
        out_shape=[jax.ShapeDtypeStruct(shape, dtype) for shape, dtype, *_ in outs],
        in_specs=ins,
        out_specs=[o[2] if len(o) > 2 else VMEM for o in outs],
        scratch_shapes=scratch,
        compiler_params=pltpu.CompilerParams(vmem_limit_bytes=LIMIT, **params),
        name=body.__name__,
    )(*args)


def on_plane(hidden_in, seq_lengths, in_gain, w_query, w_key, w_value, q_gain, k_gain, w_out, post_gain,
             w_gate, w_up, w_down, d_out):
    n, nz = lax.axis_size("ctx"), lax.axis_size("fsdp")
    t, dm = hidden_in.shape[1:]
    rows = n * t
    hd = q_gain.shape[0] * n * nz
    ql = w_query.shape[1] // hd // n
    kvl = w_key.shape[1] // hd // n
    ff = w_gate.shape[1] // n
    r_in, r_out, r_down = w_query.shape[0], w_out.shape[0], w_down.shape[0]
    qkv = (ql + 2 * kvl) * hd
    tiles, half = rows // TILE, TILE // 2
    cfg = dict(n=n, nz=nz, ql=ql, kvl=kvl, hd=hd, ff=ff, eps=1e-6, window=rows // 2 // TILE, slots=14 * n + 8 * nz)

    inv = 1000000.0 ** (-np.arange(hd // 2) * (2.0 / hd))
    angles = np.concatenate([np.arange(half), np.arange(2 * tiles) * half])[:, None] * inv[None, :]
    table = jnp.asarray(np.concatenate([np.cos(angles), np.sin(angles)], axis=1), F32)
    gshare = jnp.concatenate([in_gain, post_gain, q_gain, k_gain])[None]
    x = hidden_in[0]
    smem = pl.BlockSpec(memory_space=pltpu.SMEM)
    anywhere = pl.BlockSpec(memory_space=pl.ANY)

    def hbm(shape, dtype):
        return (shape, dtype, anywhere)

    def vm(shape, dtype=BF):
        return pltpu.VMEM(shape, dtype)

    big, low, wide, pair = (tiles, TILE, dm), (tiles, TILE, 2 * hd), (tiles, ql, TILE, 2 * hd), (2, half, dm)
    pre_w = (ql + kvl) * hd
    w_s, gu_s, wo_s, wd_s = (n, nz, r_in, qkv), (n, nz, r_in, 2 * ff), (nz, r_out, dm), (nz, r_down, dm)
    attn_s = (tiles, TILE, ql * hd)
    gains_s = (GAIN_ROWS, LANES)
    sums = [vm((n, half, dm)), vm((n, half, dm)), vm((n - 2, half, dm)), vm((n - 2, half, dm)), vm((2, TILE, dm), F32), vm(pair, F32)]
    (qx, kx, vx, attn, mo, pre, cs, xn, w, wo, gwd, ggu, h_mid, d_hmid, d_res, gains, gpost) = call(
        front, cfg, [smem] + [VMEM] * 11,
        [hbm(wide, BF), hbm(low, BF), hbm(low, BF), hbm(attn_s, BF), hbm(big, BF), hbm((tiles, TILE, pre_w), BF),
         hbm((tiles, TILE, hd), F32), hbm(big, BF), hbm(w_s, BF), hbm(wo_s, BF), hbm(wd_s, BF), hbm(gu_s, BF),
         hbm(pair, F32), hbm(pair, F32), hbm(pair, BF), (gains_s, F32), ((1, dm), F32)],
        [vm((n, r_in, qkv)), vm((n, r_in, 2 * ff)), vm(w_s), vm(wo_s), vm(gu_s), vm(wd_s),
         vm((8, LANES), F32), vm(gains_s, F32), vm((n,) + gains_s, F32), vm((nz,) + gains_s, F32),
         vm(big), vm(big), vm((tiles, TILE, pre_w)), vm((tiles, TILE, hd), F32), vm(wide), vm(low), vm(low),
         vm((ql * TILE, 2 * hd), F32), vm(attn_s),
         vm(big), vm((tiles, TILE, ff)), vm((tiles, TILE, 2 * ff)), vm((2, TILE, dm))]
        + sums + [vm(pair, F32), vm(pair, F32), vm(pair), vm(wd_s), vm(gu_s)],
        1, seq_lengths, x, d_out[0], w_query, w_key, w_value, w_out, w_gate, w_up, w_down, gshare, table)

    block, dx, gwo, grad_down, ggu, gqkv, small = call(
        back, cfg, [smem] + [VMEM] * 5 + [anywhere] * 10 + [VMEM] * 3,
        [((t, dm), BF), ((t, dm), F32), ((r_out, dm), F32), ((r_down, dm), F32), ((n, r_in, 2 * ff), BF),
         ((n, r_in, qkv), BF), (gains_s, F32)],
        [vm((n, half, dm)), vm((n, half, dm)), vm((n - 2, half, dm)), vm((n - 2, half, dm)),
         vm((tiles, TILE, pre_w)), vm((tiles, TILE, hd), F32), vm(big), vm(w_s), vm(pair, F32), vm(pair, F32), vm(big),
         vm((ql * TILE, hd), F32), vm((tiles, TILE, hd), F32), vm((tiles, TILE, hd), F32), vm((ql * TILE, 2 * hd)),
         vm(wd_s), vm((nz + 1, r_down, dm)), vm(gu_s), vm((nz + 1, n, r_in, 2 * ff)),
         vm((n, r_in, 2 * ff)), vm((n, r_in, 2 * ff)), vm(wo_s), vm((nz + 1, r_out, dm)),
         vm((tiles, TILE, qkv)), vm(w_s), vm((nz + 1, n, r_in, qkv)), vm((n, r_in, qkv)), vm((n, r_in, qkv)),
         vm(gains_s, F32), vm((n,) + gains_s, F32), vm((nz,) + gains_s, F32)]
        + sums,
        2, seq_lengths, qx, kx, vx, attn, wo, mo, pre, cs, xn, w, gwd, ggu, h_mid, d_hmid, d_res, gains, gpost, x)

    grads = call(
        finish, cfg, [VMEM] * 7,
        [((t, dm), BF), ((t, dm), F32), ((1, in_gain.shape[0]), F32), ((r_in, n * ql * hd), F32),
         ((r_in, n * kvl * hd), F32), ((r_in, n * kvl * hd), F32), ((1, q_gain.shape[0]), F32),
         ((1, k_gain.shape[0]), F32), ((r_out, dm), F32), ((1, post_gain.shape[0]), F32), ((r_in, n * ff), F32),
         ((r_in, n * ff), F32), ((r_down, dm), F32)],
        [], None, block, dx, gwo, grad_down, ggu, gqkv, small)
    (block, dx, g_in, g_q, g_k, g_v, g_qg, g_kg, g_o, g_post, g_gate, g_up, g_down) = grads
    return (block[None], dx[None], g_in[0], g_q, g_k, g_v, g_qg[0], g_kg[0], g_o, g_post[0], g_gate, g_up, g_down)


epsilon = 1e-06
rope_base = 1000000.0
negative = -1e30


def row_info(lengths, row_ids, tok_dev, n_ctx):
    half_len = tok_dev // 2
    device = row_ids // tok_dev
    local_row = row_ids % tok_dev
    block_id = jnp.where(local_row < half_len, device, 2 * n_ctx - 1 - device)
    packed = block_id * half_len + local_row % half_len
    seq_ends = jnp.cumsum(lengths)
    seq_starts = seq_ends - lengths
    member = (packed[:, None] >= seq_starts[None, :]) & (packed[:, None] < seq_ends[None, :])
    row_valid = jnp.any(member, axis=1)
    numbers = jnp.arange(lengths.shape[0], dtype=jnp.int32)
    seq_id = jnp.sum(jnp.where(member, numbers[None, :], 0), axis=1)
    offset = jnp.sum(jnp.where(member, seq_starts[None, :], 0), axis=1)
    segment = jnp.where(row_valid, seq_id, -1 - packed)
    position = jnp.where(row_valid, packed - offset, 0)
    return (segment, position, row_valid)


def norm_gain(values_in, gain_vec):
    row_scale = lax.rsqrt(jnp.mean(values_in * values_in, axis=-1, keepdims=True) + epsilon)
    return values_in * row_scale * gain_vec


def rotary(position, head_dim):
    half_len = head_dim // 2
    inv_freq = jnp.power(rope_base, -jnp.arange(half_len, dtype=jnp.float32) * (2.0 / head_dim))
    angles = position.astype(jnp.float32)[:, None] * inv_freq[None, :]
    angles = jnp.concatenate([angles, angles], axis=1)
    return (jnp.cos(angles), jnp.sin(angles))


def rotate(heads, cos_table, sin_table):
    half_len = heads.shape[-1] // 2
    turned = jnp.concatenate([-heads[..., half_len:], heads[..., :half_len]], axis=-1)
    return heads * cos_table[:, None, :] + turned * sin_table[:, None, :]


def head_post(q_in, k_in, q_scale, k_scale, cos_table, sin_table):
    head_dim = q_scale.shape[0]
    row_count = q_in.shape[0]
    q_heads = norm_gain(q_in.reshape(row_count, -1, head_dim), q_scale)
    k_heads = norm_gain(k_in.reshape(row_count, -1, head_dim), k_scale)
    query_rotated = rotate(q_heads, cos_table, sin_table).reshape(row_count, -1)
    key_rotated = rotate(k_heads, cos_table, sin_table).reshape(row_count, -1)
    return (query_rotated, key_rotated)


def swiglu(gate_in, up_in):
    return jax.nn.silu(gate_in) * up_in


def matmul(left, right):
    return jnp.dot(left, right, preferred_element_type=jnp.float32)


def inner(left, right):
    return lax.dot_general(
        left, right, (((0,), (0,)), ((), ())), preferred_element_type=jnp.float32
    )


def backdot(left, right):
    return lax.dot_general(
        left, right, (((1,), (1,)), ((), ())), preferred_element_type=jnp.float32
    )


def pick_step(key_count):
    for candidate in (512, 384, 256):
        return candidate
    return key_count


def on_rows(
    hidden_in,
    seq_lengths,
    in_gain,
    w_query,
    w_key,
    w_value,
    q_gain,
    k_gain,
    w_out,
    post_gain,
    w_gate,
    w_up,
    w_down,
    d_out,
):
    n_ctx = lax.axis_size("ctx")
    row_count = hidden_in.shape[1]
    lengths = seq_lengths[0]
    own_rows = lax.axis_index("ctx") * row_count + jnp.arange(row_count, dtype=jnp.int32)
    seg_q, pos_q, row_valid = row_info(lengths, own_rows, row_count, n_ctx)
    shards = (
        in_gain,
        w_query,
        w_key,
        w_value,
        q_gain,
        k_gain,
        w_out,
        post_gain,
        w_gate,
        w_up,
        w_down,
    )
    gathered = (
        lax.all_gather(shards[0], ("ctx", "fsdp"), axis=0, tiled=True),
        lax.all_gather(shards[1], ("ctx", "fsdp"), axis=0, tiled=True),
        lax.all_gather(shards[2], ("ctx", "fsdp"), axis=0, tiled=True),
        lax.all_gather(shards[3], ("ctx", "fsdp"), axis=0, tiled=True),
        lax.all_gather(shards[4], ("ctx", "fsdp"), axis=0, tiled=True),
        lax.all_gather(shards[5], ("ctx", "fsdp"), axis=0, tiled=True),
        lax.all_gather(shards[6], ("ctx", "fsdp"), axis=0, tiled=True),
        lax.all_gather(shards[7], ("ctx", "fsdp"), axis=0, tiled=True),
        lax.all_gather(shards[8], ("ctx", "fsdp"), axis=0, tiled=True),
        lax.all_gather(shards[9], ("ctx", "fsdp"), axis=0, tiled=True),
        lax.all_gather(shards[10], ("ctx", "fsdp"), axis=0, tiled=True),
    )
    g_in = gathered[0].astype(jnp.float32)
    g_query = gathered[4].astype(jnp.float32)
    g_key = gathered[5].astype(jnp.float32)
    g_post = gathered[7].astype(jnp.float32)
    head_dim = gathered[4].shape[0]
    kv_width = gathered[2].shape[1]
    kv_heads = kv_width // head_dim
    group_count = gathered[1].shape[1] // kv_width
    score_scale = head_dim ** (-0.5)
    rows_per_group = row_count * n_ctx
    x_float = hidden_in[0].astype(jnp.float32)
    x_normf, in_back = jax.vjp(norm_gain, x_float, g_in)
    x_norm = x_normf.astype(jnp.bfloat16)
    q_pre = matmul(x_norm, gathered[1])
    k_pre = matmul(x_norm, gathered[2])
    value_projected = matmul(x_norm, gathered[3])
    cos_table, sin_table = rotary(pos_q, head_dim)

    def post_local(q_in, k_in, q_scale, k_scale):
        return head_post(q_in, k_in, q_scale, k_scale, cos_table, sin_table)

    rotated, post_back = jax.vjp(post_local, q_pre, k_pre, g_query, g_key)
    q_low4 = rotated[0].astype(jnp.bfloat16).reshape(row_count, kv_heads, group_count, head_dim)
    key_narrow = rotated[1].astype(jnp.bfloat16)
    value_narrow = value_projected.astype(jnp.bfloat16)

    def sweep_keys(carry, k_piece, v_piece, block_fn):
        key_count = k_piece.shape[0]
        key_step = pick_step(key_count)

        def one_turn(state, turn_index):
            offset = turn_index * key_step
            k_block = lax.dynamic_slice_in_dim(k_piece, offset, key_step, 0)
            v_block = lax.dynamic_slice_in_dim(v_piece, offset, key_step, 0)
            key_rows = offset + jnp.arange(key_step, dtype=jnp.int32)
            seg_k, pos_k, unused = row_info(lengths, key_rows, row_count, n_ctx)
            allowed = (seg_q[:, None] == seg_k[None, :]) & (pos_k[None, :] <= pos_q[:, None])
            state = block_fn(state, k_block, v_block, allowed, offset)
            return (state, None)

        carry, unused = lax.scan(
            one_turn, carry, jnp.arange(key_count // key_step, dtype=jnp.int32)
        )
        return carry

    def forward_block(carry, k_block, v_block, allowed, first_key):
        row_max, totals, weighted = carry
        k_heads = k_block.reshape(-1, kv_heads, head_dim)
        v_heads = v_block.reshape(-1, kv_heads, head_dim)
        mask_four = allowed[None, None]
        score = (
            jnp.einsum("qhgd,khd->hgqk", q_low4, k_heads, preferred_element_type=jnp.float32)
            * score_scale
        )
        block_max = jnp.max(jnp.where(mask_four, score, negative), axis=-1)
        new_max = jnp.maximum(row_max, block_max)
        expo = jnp.where(mask_four, jnp.exp(score - new_max[..., None]), 0.0)
        factor = jnp.exp(row_max - new_max)
        totals = totals * factor + jnp.sum(expo, axis=-1)
        weighted = weighted * factor[..., None] + jnp.einsum(
            "hgqk,khd->hgqd", expo.astype(jnp.bfloat16), v_heads, preferred_element_type=jnp.float32
        )
        return (new_max, totals, weighted)

    start_state = (
        jnp.full((kv_heads, group_count, row_count), negative, jnp.float32),
        jnp.zeros((kv_heads, group_count, row_count), jnp.float32),
        jnp.zeros((kv_heads, group_count, row_count, head_dim), jnp.float32),
    )
    pieces = (
        lax.all_gather(key_narrow, "ctx", axis=0, tiled=True),
        lax.all_gather(value_narrow, "ctx", axis=0, tiled=True),
    )
    fold_state = sweep_keys(start_state, pieces[0], pieces[1], forward_block)
    row_max, totals, weighted = fold_state
    attn_four = weighted / totals[..., None]
    log_total = row_max + jnp.log(totals)
    attn = jnp.transpose(attn_four, (2, 0, 1, 3)).reshape(row_count, -1)
    attn_low = attn.astype(jnp.bfloat16)
    h_mid = x_float + matmul(attn_low, gathered[6])
    h_normf, post_norm_back = jax.vjp(norm_gain, h_mid, g_post)
    h_norm = h_normf.astype(jnp.bfloat16)
    gate_out = matmul(h_norm, gathered[8])
    up_out = matmul(h_norm, gathered[9])
    act_float, swiglu_back = jax.vjp(swiglu, gate_out, up_out)
    act_low = act_float.astype(jnp.bfloat16)
    row_mask = row_valid.astype(jnp.float32)[:, None]
    block_out = (row_mask * (h_mid + matmul(act_low, gathered[10]))).astype(jnp.bfloat16)
    again = (
        lax.all_gather(shards[0], ("ctx", "fsdp"), axis=0, tiled=True),
        lax.all_gather(shards[1], ("ctx", "fsdp"), axis=0, tiled=True),
        lax.all_gather(shards[2], ("ctx", "fsdp"), axis=0, tiled=True),
        lax.all_gather(shards[3], ("ctx", "fsdp"), axis=0, tiled=True),
        lax.all_gather(shards[4], ("ctx", "fsdp"), axis=0, tiled=True),
        lax.all_gather(shards[5], ("ctx", "fsdp"), axis=0, tiled=True),
        lax.all_gather(shards[6], ("ctx", "fsdp"), axis=0, tiled=True),
        lax.all_gather(shards[7], ("ctx", "fsdp"), axis=0, tiled=True),
        lax.all_gather(shards[8], ("ctx", "fsdp"), axis=0, tiled=True),
        lax.all_gather(shards[9], ("ctx", "fsdp"), axis=0, tiled=True),
        lax.all_gather(shards[10], ("ctx", "fsdp"), axis=0, tiled=True),
    )
    d_block = d_out[0].astype(jnp.float32) * row_mask
    dm_low = d_block.astype(jnp.bfloat16)
    grad_down = inner(act_low, dm_low)
    d_act = backdot(dm_low, again[10])
    d_gate, d_up = swiglu_back(d_act)
    dg_low = d_gate.astype(jnp.bfloat16)
    du_low = d_up.astype(jnp.bfloat16)
    grad_gate = inner(h_norm, dg_low)
    grad_up = inner(h_norm, du_low)
    d_hnorm = backdot(dg_low, again[8]) + backdot(du_low, again[9])
    d_hpart, grad_post = post_norm_back(d_hnorm)
    d_hmid = d_block + d_hpart
    d_res = d_hmid.astype(jnp.bfloat16)
    grad_wout = inner(attn_low, d_res)
    d_attn = backdot(d_res, again[6]).astype(jnp.bfloat16)
    d_attn4 = d_attn.reshape(row_count, kv_heads, group_count, head_dim)
    delta = jnp.einsum("qhgd,hgqd->hgq", d_attn4.astype(jnp.float32), attn_four)

    def backward_block(carry, k_block, v_block, allowed, first_key):
        d_query, d_kv = carry
        key_count = k_block.shape[0]
        k_heads = k_block.reshape(-1, kv_heads, head_dim)
        v_heads = v_block.reshape(-1, kv_heads, head_dim)
        mask_four = allowed[None, None]
        score = (
            jnp.einsum("qhgd,khd->hgqk", q_low4, k_heads, preferred_element_type=jnp.float32)
            * score_scale
        )
        prob = jnp.where(mask_four, jnp.exp(score - log_total[..., None]), 0.0)
        prob_low = prob.astype(jnp.bfloat16)
        d_prob = jnp.einsum("qhgd,khd->hgqk", d_attn4, v_heads, preferred_element_type=jnp.float32)
        d_score = (prob * (d_prob - delta[..., None])).astype(jnp.bfloat16)
        d_query = d_query + jnp.einsum(
            "hgqk,khd->qhgd", d_score, k_heads, preferred_element_type=jnp.float32
        )
        d_key = (
            jnp.einsum("hgqk,qhgd->khd", d_score, q_low4, preferred_element_type=jnp.float32)
            * score_scale
        )
        d_value = jnp.einsum(
            "hgqk,qhgd->khd", prob_low, d_attn4, preferred_element_type=jnp.float32
        )
        joined = jnp.concatenate(
            [d_key.reshape(key_count, -1), d_value.reshape(key_count, -1)], axis=1
        )
        before = lax.dynamic_slice_in_dim(d_kv, first_key, key_count, 0)
        d_kv = lax.dynamic_update_slice_in_dim(d_kv, before + joined, first_key, 0)
        return (d_query, d_kv)

    back_start = (
        jnp.zeros((row_count, kv_heads, group_count, head_dim), jnp.float32),
        jnp.zeros((rows_per_group, 2 * kv_width), jnp.float32),
    )
    pieces = (
        lax.all_gather(key_narrow, "ctx", axis=0, tiled=True),
        lax.all_gather(value_narrow, "ctx", axis=0, tiled=True),
    )
    back_state = sweep_keys(back_start, pieces[0], pieces[1], backward_block)
    d_qrot = back_state[0].reshape(row_count, -1) * score_scale
    d_kv_own = lax.psum_scatter(
        back_state[1].astype(jnp.bfloat16), "ctx", scatter_dimension=0, tiled=True
    ).astype(jnp.float32)
    d_krot = d_kv_own[:, :kv_width]
    d_vpre = d_kv_own[:, kv_width:]
    d_qpre, d_kpre, grad_qgain, grad_kgain = post_back((d_qrot, d_krot))
    dq_low = d_qpre.astype(jnp.bfloat16)
    dk_low = d_kpre.astype(jnp.bfloat16)
    dv_low = d_vpre.astype(jnp.bfloat16)
    grad_query = inner(x_norm, dq_low)
    grad_key = inner(x_norm, dk_low)
    grad_value = inner(x_norm, dv_low)
    d_xnorm = backdot(dq_low, again[1]) + backdot(dk_low, again[2]) + backdot(dv_low, again[3])
    d_xpart, grad_ingain = in_back(d_xnorm)
    d_hidden = d_hmid + d_xpart
    owned = (
        lax.psum_scatter(grad_ingain, ("ctx", "fsdp"), scatter_dimension=0, tiled=True),
        lax.psum_scatter(grad_query, ("ctx", "fsdp"), scatter_dimension=0, tiled=True),
        lax.psum_scatter(grad_key, ("ctx", "fsdp"), scatter_dimension=0, tiled=True),
        lax.psum_scatter(grad_value, ("ctx", "fsdp"), scatter_dimension=0, tiled=True),
        lax.psum_scatter(grad_qgain, ("ctx", "fsdp"), scatter_dimension=0, tiled=True),
        lax.psum_scatter(grad_kgain, ("ctx", "fsdp"), scatter_dimension=0, tiled=True),
        lax.psum_scatter(grad_wout, ("ctx", "fsdp"), scatter_dimension=0, tiled=True),
        lax.psum_scatter(grad_post, ("ctx", "fsdp"), scatter_dimension=0, tiled=True),
        lax.psum_scatter(grad_gate, ("ctx", "fsdp"), scatter_dimension=0, tiled=True),
        lax.psum_scatter(grad_up, ("ctx", "fsdp"), scatter_dimension=0, tiled=True),
        lax.psum_scatter(grad_down, ("ctx", "fsdp"), scatter_dimension=0, tiled=True),
    )
    return (
        block_out[None],
        d_hidden[None],
        owned[0],
        owned[1],
        owned[2],
        owned[3],
        owned[4],
        owned[5],
        owned[6],
        owned[7],
        owned[8],
        owned[9],
        owned[10],
    )


def on_device(*args):
    n = lax.axis_size("ctx")
    hidden_in, w_key, w_out, w_gate, q_gain = args[0], args[4], args[8], args[10], args[6]
    hd = q_gain.shape[0] * n * lax.axis_size("fsdp")
    heads, ff = w_key.shape[1] // hd, w_gate.shape[1] // n
    even = heads % n == 0 and ff % LANES == 0 and w_key.shape[0] % 16 == 0 and w_out.shape[0] % 16 == 0
    if even and heads == n == 8 and hidden_in.shape[1] == TILE:
        return on_plane(*args)
    return on_rows(*args)


def solution(mesh):
    in_specs = (
        P("fsdp", "ctx", None),
        P("fsdp", None),
        P(("ctx", "fsdp")),
        P(("ctx", "fsdp"), None),
        P(("ctx", "fsdp"), None),
        P(("ctx", "fsdp"), None),
        P(("ctx", "fsdp")),
        P(("ctx", "fsdp")),
        P(("ctx", "fsdp"), None),
        P(("ctx", "fsdp")),
        P(("ctx", "fsdp"), None),
        P(("ctx", "fsdp"), None),
        P(("ctx", "fsdp"), None),
        P("fsdp", "ctx", None),
    )
    out_specs = (
        P("fsdp", "ctx", None),
        P("fsdp", "ctx", None),
        P(("ctx", "fsdp")),
        P(("ctx", "fsdp"), None),
        P(("ctx", "fsdp"), None),
        P(("ctx", "fsdp"), None),
        P(("ctx", "fsdp")),
        P(("ctx", "fsdp")),
        P(("ctx", "fsdp"), None),
        P(("ctx", "fsdp")),
        P(("ctx", "fsdp"), None),
        P(("ctx", "fsdp"), None),
        P(("ctx", "fsdp"), None),
    )
    return jax.shard_map(
        on_device, mesh=mesh, in_specs=in_specs, out_specs=out_specs, check_vma=False
    )
```

```python
import functools
import math

import jax
import jax.numpy as jnp
import numpy as np
from jax import lax
from jax.experimental import pallas as pl
from jax.experimental.pallas import tpu as pltpu
from jax.sharding import PartitionSpec as P

BF = jnp.bfloat16
F32 = jnp.float32
MESH = pl.DeviceIdType.MESH
VMEM = pl.BlockSpec(memory_space=pltpu.VMEM)
GAIN_ROWS = 24
LANES = 128
TILE = 256
LIMIT = 63 * 2**20
CORE, ALONG_X, ALONG_Y, ACROSS = 1, 2, 4, 6
CHIPS = (ALONG_X, ALONG_Y, ACROSS)
NEXT = (ALONG_X, ALONG_Y)


def dot(a, b):
    return jnp.dot(a, b, preferred_element_type=F32)


def dot_rt(a, b):
    return lax.dot_general(a, b, (((1,), (1,)), ((), ())), preferred_element_type=F32)


def dot_lt(a, b):
    return lax.dot_general(a, b, (((0,), (0,)), ((), ())), preferred_element_type=F32)


def flip(place, mask, size):
    out, bit = 0, 1
    while bit < size:
        out = out + bit * lax.rem(lax.div(place, bit) + (mask // bit) % 2, 2)
        bit *= 2
    return out


class Net:
    def __init__(self, n, nz, tiles, send, recv):
        self.n, self.nz, self.tiles, self.send, self.recv = n, nz, tiles, send, recv
        self.c = lax.axis_index("ctx")
        self.z = lax.axis_index("fsdp")
        self.core = lax.rem(self.c, 2)
        self.slot = 0

    def slots(self, count):
        first = self.slot
        self.slot += count
        return first

    def at(self, mask):
        return flip(self.c, mask, self.n)

    def zat(self, mask):
        return flip(self.z, mask, self.nz)

    def peer(self, mask):
        return (self.at(mask), self.z)

    def zpeer(self, mask):
        return (self.c, self.zat(mask))

    def tile(self, mask, s):
        chip = lax.div(self.at(mask), 2)
        return chip if s == 0 else self.tiles - 1 - chip

    def view(self, buf, mask, s):
        half = TILE // 2
        core = lax.rem(self.at(mask), 2)
        first = core if s == 0 else 1 - core
        return buf.at[self.tile(mask, s), pl.ds(pl.multiple_of(first * half, half), half), :]

    def barrier(self):
        bar = pltpu.get_barrier_semaphore()
        for mask in range(1, self.n):
            pl.semaphore_signal(bar, inc=1, device_id=self.peer(mask), device_id_type=MESH)
        for mask in range(1, self.nz):
            pl.semaphore_signal(bar, inc=1, device_id=self.zpeer(mask), device_id_type=MESH)
        pl.semaphore_wait(bar, self.n + self.nz - 2)

    def copy(self, src, dst, slot, device, send_slot=None):
        return pltpu.make_async_remote_copy(
            src_ref=src,
            dst_ref=dst,
            send_sem=self.send.at[slot if send_slot is None else send_slot],
            recv_sem=self.recv.at[slot],
            device_id=device,
            device_id_type=MESH,
        )

    def to_plane(self, src, dst):
        base = self.slots(self.n)
        out = []
        for mask in range(1, self.n):
            cp = self.copy(src(mask), dst, base + mask, self.peer(mask))
            cp.start()
            out.append(cp)
        return out

    def to_line(self, src, dst):
        base = self.slots(self.nz)
        out = []
        for mask in range(1, self.nz):
            cp = self.copy(src(mask), dst(mask), base + mask, self.zpeer(mask))
            cp.start()
            out.append(cp)
        return out


class Line:
    def __init__(self, net, view):
        self.net, self.view = net, view
        self.base = net.slots(net.nz)
        self.middle = (net.z == 1) | (net.z == 2)
        self.relayed = net.nz == 4
        own = view(net.z)
        self.direct = [m for m in range(1, net.nz) if not (self.relayed and m == 3)]
        self.copies = {m: net.copy(own, own, self.base + m, net.zpeer(m)) for m in range(1, net.nz)}
        for m in self.direct[::-1]:
            self.copies[m].start()
        if self.relayed:
            far = view(net.zat(2))
            self.passed = net.copy(far, far, self.base + 3, net.zpeer(1), send_slot=self.base)

    def relay(self):
        if self.relayed:
            self.copies[2].wait_recv()

            @pl.when(self.middle)
            def _():
                self.passed.start()
                self.copies[3].start()

    def arrive(self):
        for m, cp in self.copies.items():
            if not (self.relayed and m == 2):
                cp.wait_recv()

    def finish(self):
        for m in self.direct:
            self.copies[m].wait_send()
        if self.relayed:

            @pl.when(self.middle)
            def _():
                self.copies[3].wait_send()
                self.passed.wait_send()


class LineSum:
    def __init__(self, net, piece, inn, passing, both):
        self.net, self.piece, self.inn, self.passing, self.both = net, piece, inn, passing, both
        self.base = net.slots(net.nz)
        self.middle = (net.z == 1) | (net.z == 2)
        self.relayed = net.nz == 4
        if not self.relayed:
            for m in range(1, net.nz):
                self.to(m).start()
            return

        @pl.when(jnp.logical_not(self.middle))
        def _():
            self.far().start()
            self.to(2).start()
            self.to(1).start()

        @pl.when(self.middle)
        def _():
            self.to(3).start()
            self.to(1).start()

    def to(self, m):
        return self.net.copy(self.piece(self.net.zat(m)), self.inn.at[m - 1], self.base + m, self.net.zpeer(m))

    def far(self):
        return self.net.copy(
            self.piece(self.net.zat(3)), self.passing, self.base, self.net.zpeer(1), send_slot=self.base + 3
        )

    def joined(self):
        return self.net.copy(self.both, self.inn.at[1], self.base + 2, self.net.zpeer(2))

    def relay(self):
        if self.relayed:

            @pl.when(self.middle)
            def _():
                self.far().wait_recv()
                own = self.piece(self.net.zat(2))[...].astype(F32)
                self.both[...] = (own + self.passing[...].astype(F32)).astype(BF)
                self.joined().start()

    def total(self, write):
        def some(masks):
            value = self.piece(self.net.z)[...].astype(F32)
            for m in masks:
                self.to(m).wait_recv()
                value = value + self.inn[m - 1].astype(F32)
            write(value)

        if not self.relayed:
            some(range(1, self.net.nz))
            return

        @pl.when(self.middle)
        def _():
            some((1, 2, 3))

        @pl.when(jnp.logical_not(self.middle))
        def _():
            some((1, 2))

    def finish(self):
        if not self.relayed:
            for m in range(1, self.net.nz):
                self.to(m).wait_send()
            return
        self.to(1).wait_send()
        self.to(2).wait_send()
        self.to(3).wait_send()


class Gather:
    def __init__(self, net, buf):
        self.net, self.buf = net, buf
        self.base = net.slots(2 * net.n)
        self.sent = []

    def send(self, mask, s, to, arrives_as):
        view = self.net.view(self.buf, mask, s)
        slot = self.base + 2 * arrives_as + s
        cp = self.net.copy(view, view, slot, self.net.peer(to))
        cp.start()
        self.sent.append(cp)

    def start(self, s):
        for mask in (CORE, ALONG_X, ALONG_Y):
            self.send(0, s, mask, mask)

    def arrive(self, mask, s):
        view = self.net.view(self.buf, mask, s)
        self.net.copy(view, view, self.base + 2 * mask + s, self.net.peer(mask)).wait_recv()
        if mask % 2 == 0:
            if mask == (ALONG_X, ALONG_Y)[s]:
                self.send(mask, s, (ALONG_Y, ALONG_X)[s], ACROSS)
            self.send(mask, s, CORE, mask + 1)

    def finish(self):
        for cp in self.sent:
            cp.wait_send()


class PlaneSum:
    def __init__(self, net, sib_out, sib_in, out, inn, mine, keep, joined):
        self.net, self.joined = net, joined
        self.sib_out, self.sib_in, self.out, self.inn, self.mine, self.keep = sib_out, sib_in, out, inn, mine, keep
        self.base = net.slots(2 * net.n)
        self.sent, self.queue, self.given = [], [], 0

    def sibling(self, mask, s):
        return self.net.copy(
            self.sib_out.at[mask + s], self.sib_in.at[mask + s], self.base + 2 * (mask + 1) + s, self.net.peer(CORE)
        )

    def chip(self, mask, s):
        i = mask - 2 + s
        to = NEXT[s] if mask == ACROSS and self.joined else mask
        return self.net.copy(self.out.at[i], self.inn.at[i], self.base + 2 * mask + s, self.net.peer(to))

    def give(self, mask, s, value):
        half = TILE // 2
        place = self.given % 2
        self.given += 1
        self.mine[place] = value
        mine = lax.rem(self.net.core + s, 2) * half
        own = pl.ds(pl.multiple_of(mine, half), half)
        other = pl.ds(pl.multiple_of(half - mine, half), half)
        self.sib_out[mask + s] = self.mine[place, other, :].astype(BF)
        cp = self.sibling(mask, s)
        cp.start()
        self.sent.append(cp)
        self.queue.append((mask, s, place, own))
        if len(self.queue) > 1:
            self.combine()

    def combine(self):
        mask, s, place, own = self.queue.pop(0)
        self.sibling(mask, s).wait_recv()
        both = self.mine[place, own, :] + self.sib_in[mask + s].astype(F32)
        if mask == 0:
            self.keep[s] = both
            return
        if self.joined and mask == NEXT[1 - s]:
            self.chip(ACROSS, s).wait_recv()
            both = both + self.inn[ACROSS - 2 + s].astype(F32)
        self.out[mask - 2 + s] = both.astype(BF)
        cp = self.chip(mask, s)
        cp.start()
        self.sent.append(cp)

    def flush(self):
        while self.queue:
            self.combine()

    def total(self, s):
        value = self.keep[s]
        for mask in NEXT if self.joined else CHIPS:
            self.chip(mask, s).wait_recv()
            value = value + self.inn[mask - 2 + s].astype(F32)
        return value

    def finish(self):
        for cp in self.sent:
            cp.wait_send()


SEND_ORDER = ((ACROSS, 0), (ACROSS, 1), (ALONG_X, 0), (ALONG_Y, 1), (ALONG_Y, 0), (ALONG_X, 1), (0, 0), (0, 1))
ARRIVE_ORDER = ((0, 0), (0, 1), (ALONG_X, 0), (ALONG_Y, 0), (ALONG_X, 1), (ALONG_Y, 1), (ACROSS, 0), (ACROSS, 1))


def arrive_for(gath, mask, s):
    if mask == ALONG_X:
        gath.arrive(ALONG_X, s)
        gath.arrive(ALONG_Y, s)
    elif mask == ACROSS:
        gath.arrive(ACROSS, s)
    gath.arrive(mask + 1, s)


def row_of(g, first, count):
    return jnp.concatenate([g[first + j : first + j + 1, :] for j in range(count)], axis=1)


def split_three(value, lane):
    first = value.astype(BF).astype(F32)
    rest = value - first
    second = rest.astype(BF).astype(F32)
    third = rest - second
    out = jnp.where(lane == 0, first, jnp.where(lane == 1, second, jnp.where(lane == 2, third, 0.0)))
    return out.astype(BF)


def first_keys(lengths_ref, at):
    start = jnp.zeros_like(at)
    begin = 0
    for s in range(lengths_ref.shape[1]):
        start = jnp.where(at >= begin, begin, start)
        begin = begin + lengths_ref[0, s]
    padding = at >= begin
    return jnp.where(padding, at, start), padding


def halves(a, hd):
    lane = lax.broadcasted_iota(jnp.int32, a.shape, 1)
    other = pltpu.roll(a, hd // 2, 1)
    return jnp.where(lane < hd // 2, a, other), jnp.where(lane < hd // 2, -other, a)


def angle_sum(a, b, hd):
    lane = lax.broadcasted_iota(jnp.int32, jnp.broadcast_shapes(a.shape, b.shape), 1)
    a2, b2 = pltpu.roll(a, hd // 2, 1), pltpu.roll(b, hd // 2, 1)
    return jnp.where(lane < hd // 2, a * b - a2 * b2, a * b2 + a2 * b)


def minus_angle(a, hd):
    lane = lax.broadcasted_iota(jnp.int32, a.shape, 1)
    return jnp.where(lane < hd // 2, a, -a)


def norm_back(v, gain, dy, eps):
    r = lax.rsqrt(jnp.mean(v * v, axis=-1, keepdims=True) + eps)
    gdy = gain * dy
    dv = r * gdy - v * (r * r * r) * jnp.mean(gdy * v, axis=-1, keepdims=True)
    return jnp.sum(dy * v * r, axis=0, keepdims=True), dv


def front(cfg, lengths_ref, x_ref, do_ref, wq_ref, wk_ref, wv_ref, wo_ref, wg_ref, wu_ref, wd_ref, gshare_ref, table_ref,
          qx_out, kx_out, vx_out, attn_out, mo_out, pre_out, cs_out, xn_out, w_out, wo_out, gwd_out, ggu_out,
          hmid_out, dhmid_out, dres_out, gains_out, gpost_out,
          wsend, gsend, w, wo_all, gu, wd_all, grow, gpart, gbuf, gz, xg, xn, pre, cs, qx, kx, vx, acc, attn,
          dblk, act, dgu, mo, sib_out, sib_in, out, inn, mine, keep, hmid, dhmid, dres, gwd_buf, ggu_buf,
          local, send, recv):
    n, nz, ql, kvl, hd, ff = cfg["n"], cfg["nz"], cfg["ql"], cfg["kvl"], cfg["hd"], cfg["ff"]
    eps = cfg["eps"]
    t, dm = x_ref.shape
    half = TILE // 2
    tiles = qx.shape[0]
    rows = n * t
    net = Net(n, nz, tiles, send, recv)
    c, z = net.c, net.z
    stores = []

    def store(src, dst):
        cp = pltpu.make_async_copy(src, dst, local.at[len(stores)])
        cp.start()
        stores.append(cp)
        return cp

    qw, kw = ql * hd, kvl * hd
    for j in range(n):
        wsend[j, :, :qw] = wq_ref[:, j * qw : (j + 1) * qw]
        wsend[j, :, qw : qw + kw] = wk_ref[:, j * kw : (j + 1) * kw]
        wsend[j, :, qw + kw :] = wv_ref[:, j * kw : (j + 1) * kw]
        gsend[j, :, :ff] = wg_ref[:, j * ff : (j + 1) * ff]
        gsend[j, :, ff:] = wu_ref[:, j * ff : (j + 1) * ff]
    grow[...] = jnp.zeros_like(grow)
    grow[0:1, : gshare_ref.shape[1]] = gshare_ref[...].astype(F32)
    row = jnp.broadcast_to(grow[0:1, :], (8, LANES))
    lane8 = lax.broadcasted_iota(jnp.int32, (8, LANES), 1)
    at = lax.broadcasted_iota(jnp.int32, (8, LANES), 0) * LANES + lane8
    wide, narrow = dm // (n * nz), hd // (n * nz)
    place = c * nz + z

    def placed(first, share, row0):
        shift = lax.rem(place * share, LANES)
        moved = pltpu.roll(row, lax.rem(shift + LANES - first, LANES), 1)
        return jnp.where((at >= row0 + place * share) & (at < row0 + (place + 1) * share), moved, 0.0)

    gpart[0:8, :] = placed(0, wide, 0)
    gpart[8:16, :] = placed(wide, wide, 0)
    gpart[16:24, :] = placed(2 * wide, narrow, 0) + placed(2 * wide + narrow, narrow, LANES)
    for s in range(2):
        net.view(xg, 0, s)[...] = x_ref[s * half : (s + 1) * half, :]
    w[c, z] = wsend[c]
    gu[c, z] = gsend[c]
    wo_all[z] = wo_ref[...]
    wd_all[z] = wd_ref[...]
    net.barrier()
    plane_g = net.to_plane(lambda m: gpart, gbuf.at[c])
    plane_w = net.to_plane(lambda m: wsend.at[net.at(m)], w.at[c, z])
    line_o = Line(net, lambda f: wo_all.at[f])
    gath = Gather(net, xg)
    gath.start(0)
    gath.start(1)
    gbuf[c] = gpart[...]
    for cp in plane_g:
        cp.wait_recv()
    gz[z] = jnp.sum(gbuf[...], axis=0)
    line_g = net.to_line(lambda m: gz.at[z], lambda m: gz.at[z])
    for cp in plane_w:
        cp.wait_recv()
    line_w = Line(net, lambda f: w.at[:, f])

    lo = table_ref[0:half, :]
    begins, firsts = [], []
    begin = 0
    for s in range(lengths_ref.shape[1]):
        begins.append(begin)
        hi_row = table_ref[pl.ds(half + lax.div(begin, half), 1), :]
        lo_row = table_ref[pl.ds(lax.rem(begin, half), 1), :]
        firsts.append(minus_angle(angle_sum(hi_row, lo_row, hd), hd))
        begin = begin + lengths_ref[0, s]
    end = begin
    one = jnp.where(lax.broadcasted_iota(jnp.int32, (1, hd), 1) < hd // 2, 1.0, 0.0)

    def positions(b, carry):
        at = b * half + lax.broadcasted_iota(jnp.int32, (half, hd), 0)
        hi_row = table_ref[pl.ds(half + b, 1), :]
        shift = angle_sum(hi_row, firsts[0], hd)
        for begin, first in zip(begins[1:], firsts[1:]):
            shift = jnp.where(at >= begin, angle_sum(hi_row, first, hd), shift)
        both = jnp.where(at >= end, one, angle_sum(shift, lo, hd))
        cs[lax.div(b, 2), pl.ds(pl.multiple_of(lax.rem(b, 2) * half, half), half), :] = both
        return carry

    lax.fori_loop(0, 2 * tiles, positions, 0)
    for cp in line_g:
        cp.wait_recv()
    gains = jnp.sum(gz[...], axis=0)
    g_in = row_of(gains, 0, dm // LANES)
    g_post = row_of(gains, 8, dm // LANES)
    g_q = gains[16:17, :]
    g_k = gains[17:18, :]
    step = 32

    def normalise(tile):
        def some(i, carry):
            here = pl.ds(pl.multiple_of(i * step, step), step)
            v = xg[tile, here, :].astype(F32)
            r = lax.rsqrt(jnp.mean(v * v, axis=-1, keepdims=True) + eps)
            xn[tile, here, :] = (v * r * g_in).astype(BF)
            return carry

        lax.fori_loop(0, TILE // step, some, 0)

    for mask, s in ARRIVE_ORDER:
        arrive_for(gath, mask, s)
        normalise(net.tile(mask, s))
        if mask == ALONG_Y and s == 1:
            plane_u = net.to_plane(lambda m: gsend.at[net.at(m)], gu.at[c, z])
            line_w.relay()
    line_o.relay()
    gath_d = Gather(net, dblk)
    for s in range(2):
        first = lax.rem(net.core + s, 2) * half + net.tile(0, s) * TILE
        padding = first + lax.broadcasted_iota(jnp.int32, (half, 1), 0) >= end
        net.view(dblk, 0, s)[...] = jnp.where(padding, 0.0, do_ref[s * half : (s + 1) * half, :].astype(F32)).astype(BF)
        gath_d.start(s)
    for cp in plane_u:
        cp.wait_recv()
    line_u = Line(net, lambda f: gu.at[:, f])
    line_w.arrive()
    wqkv = w[...].reshape(dm, -1)
    lane_b = lax.broadcasted_iota(jnp.int32, (TILE, hd), 1)
    minus = jnp.where(lane_b < 3, -1.0, 0.0).astype(BF)

    def heads(tile, carry):
        qkv = dot(xn[tile], wqkv)
        width = qw + kw
        pre[tile] = qkv[:, :width].astype(BF)
        cos, sin = halves(cs[tile], hd)
        for h in range(ql + kvl):
            v = qkv[:, h * hd : (h + 1) * hd]
            r = lax.rsqrt(jnp.mean(v * v, axis=-1, keepdims=True) + eps)
            hat = v * r * (g_q if h < ql else g_k)
            low = (hat * cos + pltpu.roll(hat, hd // 2, 1) * sin).astype(BF)
            if h < ql:
                qx[tile, h, :, :hd] = low
            else:
                kx[tile, :, :hd] = low
        vx[tile, :, :hd] = qkv[:, width:].astype(BF)
        kx[tile, :, hd:] = minus
        vx[tile, :, hd:] = minus
        return carry

    lax.fori_loop(0, tiles, heads, 0)
    hn = xn
    xn_stored = store(xn, xn_out)
    for src, dst in ((pre, pre_out), (cs, cs_out), (kx, kx_out), (vx, vx_out), (w, w_out)):
        store(src, dst)
    line_o.arrive()
    wout = wo_all[...].reshape(-1, dm)
    store(wo_all, wo_out)

    high = ql * TILE
    factor = math.log2(math.e) / math.sqrt(hd)
    lane_q = lax.broadcasted_iota(jnp.int32, (high, hd), 1)

    def attend(i):
        q = qx[i, :, :, :hd].reshape(high, hd)
        start = first_keys(lengths_ref, i * TILE + lax.broadcasted_iota(jnp.int32, (TILE, 1), 0))[0]
        q_at = i * TILE + lax.broadcasted_iota(jnp.int32, (TILE, TILE), 0)
        acc[...] = jnp.zeros_like(acc)

        def k_tile(j, carry):
            s = dot_rt(q, kx[j, :, :hd])
            k_at = j * TILE + lax.broadcasted_iota(jnp.int32, (TILE, TILE), 1)
            allowed = (k_at <= q_at) & (k_at >= start)
            e = jnp.where(allowed[None], jnp.exp2(s * factor).reshape(ql, TILE, TILE), 0.0)
            acc[...] += dot(e.astype(BF).reshape(high, TILE), vx[j])
            return carry

        lax.fori_loop(jnp.maximum(i - cfg["window"], 0), i + 1, k_tile, 0)
        total = -acc[:, hd : hd + 1]
        low = (acc[:, :hd] / total).astype(BF)
        for h in range(ql):
            attn[i, :, h * hd : (h + 1) * hd] = low[h * TILE : (h + 1) * TILE]
        extra = jnp.broadcast_to(jnp.log(total) * math.sqrt(hd), (high, hd))
        qx[i, :, :, hd:] = split_three(extra, lane_q).reshape(ql, TILE, hd)

    xn_stored.wait()
    gath.finish()
    sum1 = PlaneSum(net, sib_out, sib_in, out, inn, mine, keep, True)
    gath1 = Gather(net, hn)

    def middle(s):
        h_mid = x_ref[s * half : (s + 1) * half, :].astype(F32) + sum1.total(s)
        hmid[s] = h_mid
        r = lax.rsqrt(jnp.mean(h_mid * h_mid, axis=-1, keepdims=True) + eps)
        net.view(hn, 0, s)[...] = (h_mid * r * g_post).astype(BF)
        gath1.start(s)

    for k, (mask, s) in enumerate(SEND_ORDER):
        tile = net.tile(mask, s)
        attend(tile)
        sum1.give(mask, s, dot(attn[tile], wout))
        if k == 2:
            for half_s in range(2):
                gath_d.arrive(ALONG_X, half_s)
                gath_d.arrive(ALONG_Y, half_s)
        if k == 3:
            line_d = Line(net, lambda f: wd_all.at[f])
        if k == 6:
            line_u.relay()
    sum1.flush()
    store(qx, qx_out)
    store(attn, attn_out)
    for s in range(2):
        gath_d.arrive(ACROSS, s)
    middle(0)
    middle(1)
    line_d.relay()
    store(hmid, hmid_out)
    sum1.finish()
    for mask in (CORE, ALONG_X + 1, ALONG_Y + 1, ACROSS + 1):
        for s in range(2):
            gath_d.arrive(mask, s)
    line_u.arrive()
    wgu = gu[...].reshape(dm, -1)
    mo_stores = []

    def open_up(d):
        dgu[d] = dot(hn[d], wgu).astype(BF)

    def block(d):
        gate, up = dgu[d, :, :ff].astype(F32), dgu[d, :, ff:].astype(F32)
        sig = 1.0 / (1.0 + jnp.exp(-gate))
        silu = gate * sig
        low = (silu * up).astype(BF)
        act[d] = low
        if len(mo_stores) > 1:
            mo_stores[-2].wait()
        place = len(mo_stores) % 2
        mo[place] = dot(low, wd).astype(BF)
        mo_stores.append(store(mo.at[place], mo_out.at[d]))
        d_act = dot_rt(dblk[d], wd)
        dgu[d, :, :ff] = (d_act * up * sig * (1.0 + gate * (1.0 - sig))).astype(BF)
        dgu[d, :, ff:] = (d_act * silu).astype(BF)
        return dot_rt(dgu[d], wgu)

    for mask, s in ARRIVE_ORDER:
        arrive_for(gath1, mask, s)
        open_up(net.tile(mask, s))
    line_d.arrive()
    wd = wd_all[...].reshape(-1, dm)
    sum2 = PlaneSum(net, sib_out, sib_in, out, inn, mine, keep, True)
    for mask, s in SEND_ORDER:
        sum2.give(mask, s, block(net.tile(mask, s)))
    sum2.flush()
    dgu_all = dgu[...].reshape(rows, 2 * ff)
    gwd_buf[...] = dot_lt(act[...].reshape(rows, ff), dblk[...].reshape(rows, dm)).astype(BF).reshape(gwd_buf.shape)
    store(gwd_buf, gwd_out)
    per = dm // n
    cols = 2
    part_w = dm // cols
    for j in range(cols):
        part = dot_lt(hn[:, :, j * part_w : (j + 1) * part_w].reshape(rows, part_w), dgu_all)
        ggu_buf[j * (n // cols) : (j + 1) * (n // cols)] = part.astype(BF).reshape(n // cols, nz, per // nz, 2 * ff)
    store(ggu_buf, ggu_out)
    g_sum = 0.0
    for s in range(2):
        g_part, dv = norm_back(hmid[s], g_post, sum2.total(s), eps)
        g_sum = g_sum + g_part
        d_hmid = net.view(dblk, 0, s)[...].astype(F32) + dv
        dhmid[s] = d_hmid
        dres[s] = d_hmid.astype(BF)
    store(dhmid, dhmid_out)
    store(dres, dres_out)
    gains_out[...] = gains
    gpost_out[...] = g_sum
    for part in (gath_d, gath1, sum2, line_o, line_w, line_u, line_d):
        part.finish()
    for cp in plane_g + plane_w + plane_u + line_g:
        cp.wait_send()
    for cp in stores:
        if not any(cp is other for other in [xn_stored] + mo_stores[:-2]):
            cp.wait()


def back(cfg, lengths_ref, qx_ref, kx_ref, vx_ref, attn_ref, wo_ref, mo_ref, pre_ref, cs_ref, xn_ref, w_ref, gwd_ref,
         ggu_ref, hmid_ref, dhmid_ref, dres_ref, gains_ref, gpost_ref, x_ref,
         block_out, dx_out, gwo_out, gwd_out, ggu_out, gqkv_out, gains_out,
         mo_own, mo_in, mo_send, mo_recv, pre, cs, xn, w, hmid, dhmid, dresg, dq, dk, dv, dax, gwd, gwd_in, ggu,
         ggu_line, ggu_sum, ggu_in, gwo, gwo_in, dqkv, gbuf, g_line, gsum, g_in, part, gplane, gz,
         sib_out, sib_in, out, inn, mine, keep, local, send, recv):
    n, nz, ql, kvl, hd, ff = cfg["n"], cfg["nz"], cfg["ql"], cfg["kvl"], cfg["hd"], cfg["ff"]
    eps = cfg["eps"]
    t, dm = x_ref.shape
    half = TILE // 2
    rows = n * t
    tiles = qx_ref.shape[0]
    qw, kw = ql * hd, kvl * hd
    net = Net(n, nz, tiles, send, recv)
    c, z = net.c, net.z
    loads = []

    def load(src, dst):
        cp = pltpu.make_async_copy(src, dst, local.at[len(loads)])
        cp.start()
        loads.append(cp)
        return cp

    first = [load(dres_ref.at[s], net.view(dresg, 0, s)) for s in range(2)]
    own = {(m, s): load(net.view(mo_ref, m, s), mo_own.at[m + s]) for m in (0,) + CHIPS for s in range(2)}
    first += [load(gwd_ref, gwd), load(ggu_ref, ggu)]
    more = [load(a, b) for a, b in ((pre_ref, pre), (cs_ref, cs), (xn_ref, xn), (w_ref, w), (hmid_ref, hmid),
                                    (dhmid_ref, dhmid))]
    for cp in first:
        cp.wait()
    net.barrier()
    gath = Gather(net, dresg)
    gath.start(0)
    gath.start(1)
    line_d = LineSum(net, lambda f: gwd.at[f], gwd_in, gwd_in.at[nz - 1], gwd_in.at[nz])
    line_u = LineSum(net, lambda f: ggu.at[:, f], ggu_line, ggu_line.at[nz - 1], ggu_line.at[nz])
    base = net.slots(2 * n)
    sib = {}
    for m in CHIPS + (0,):
        for s in range(2):
            cp = net.copy(net.view(mo_ref, m + 1, s), mo_in.at[m + s], base + m + s, net.peer(CORE))
            cp.start()
            sib[m, s] = cp
    wout = wo_ref[...].reshape(-1, dm)
    gains = gains_ref[...]
    g_q = gains[16:17, :]
    g_k = gains[17:18, :]
    high = ql * TILE
    factor = math.log2(math.e) / math.sqrt(hd)
    scale = 1.0 / math.sqrt(hd)
    lane = lax.broadcasted_iota(jnp.int32, (TILE, hd), 1)
    dk[...] = jnp.zeros_like(dk)
    dv[...] = jnp.zeros_like(dv)

    def attend_back(i):
        d_attn = dot_rt(dresg[i], wout).astype(BF)
        prod = d_attn.astype(F32) * attn_ref[i].astype(F32)
        for h in range(ql):
            delta = jnp.sum(prod[:, h * hd : (h + 1) * hd], axis=-1, keepdims=True)
            dax[h * TILE : (h + 1) * TILE, :hd] = d_attn[:, h * hd : (h + 1) * hd]
            dax[h * TILE : (h + 1) * TILE, hd:] = split_three(jnp.broadcast_to(delta, (TILE, hd)), lane)
        qx = qx_ref[i].reshape(high, 2 * hd)
        start = first_keys(lengths_ref, i * TILE + lax.broadcasted_iota(jnp.int32, (1, TILE), 1))[0]
        q_at = i * TILE + lax.broadcasted_iota(jnp.int32, (TILE, TILE), 1)
        dq[...] = jnp.zeros_like(dq)

        def k_tile(j, carry):
            k_at = j * TILE + lax.broadcasted_iota(jnp.int32, (TILE, TILE), 0)
            allowed = (k_at <= q_at) & (k_at >= start)
            allowed = jnp.concatenate([allowed] * ql, axis=1)
            s = dot_rt(kx_ref[j], qx)
            p = jnp.where(allowed, jnp.exp2(s * factor), 0.0)
            ds = (p * dot_rt(vx_ref[j], dax[...])).astype(BF)
            dv[j] += dot(p.astype(BF), dax[:, :hd])
            dk[j] += dot(ds, qx[:, :hd])
            dq[...] += dot_lt(ds, kx_ref[j, :, :hd])
            return carry

        lax.fori_loop(jnp.maximum(i - cfg["window"], 0), i + 1, k_tile, 0)

    def head_back(i, h, dy, gain):
        cos, sin = halves(cs[i], hd)
        dy = dy * cos - pltpu.roll(dy, hd // 2, 1) * sin
        g_part, dpre = norm_back(pre[i, :, h * hd : (h + 1) * hd].astype(F32), gain, dy, eps)
        dqkv[i, :, h * hd : (h + 1) * hd] = dpre.astype(BF)
        return g_part

    gq = jnp.zeros((1, hd), F32)
    mo_base = net.slots(2 * n)

    def mo_chip(m, s):
        to = NEXT[s] if m == ACROSS else m
        return net.copy(mo_send.at[m + s - 2], mo_recv.at[m + s - 2], mo_base + m + s, net.peer(to))

    def send_mo(m, s):
        own[m, s].wait()
        sib[m, s].wait_recv()
        both = mo_own[m + s].astype(F32) + mo_in[m + s].astype(F32)
        if m == NEXT[1 - s]:
            mo_chip(ACROSS, s).wait_recv()
            both = both + mo_recv[ACROSS - 2 + s].astype(F32)
        mo_send[m + s - 2] = both.astype(BF)
        mo_chip(m, s).start()

    for k, (mask, s) in enumerate(ARRIVE_ORDER):
        arrive_for(gath, mask, s)
        i = net.tile(mask, s)
        attend_back(i)
        if k == 0:
            for cp in more[:2]:
                cp.wait()
        for h in range(ql):
            gq = gq + head_back(i, h, dq[h * TILE : (h + 1) * TILE] * scale, g_q)
        if k == 2:
            line_d.relay()
        if k == 4:
            for half_s in range(2):
                for m in (ACROSS, NEXT[half_s]):
                    send_mo(m, half_s)
        if k == 5:
            line_u.relay()
        if k == 6:
            for half_s in range(2):
                send_mo(NEXT[1 - half_s], half_s)
    gwo[...] = dot_lt(attn_ref[...].reshape(rows, qw), dresg[...].reshape(rows, dm)).astype(BF).reshape(gwo.shape)
    line_o = LineSum(net, lambda f: gwo.at[f], gwo_in, gwo_in.at[nz - 1], gwo_in.at[nz])

    def keys_back(i, carry):
        g_part = head_back(i, ql, dk[i] * scale, g_k)
        dqkv[i, :, qw + kw :] = dv[i].astype(BF)
        return carry + g_part

    gk = lax.fori_loop(0, tiles, keys_back, jnp.zeros((1, hd), F32))
    for cp in more[2:]:
        cp.wait()
    per = dm // n
    cols = 2
    part_w = dm // cols
    d_all = dqkv[...].reshape(rows, -1)
    for j in range(cols):
        grad = dot_lt(xn[:, :, j * part_w : (j + 1) * part_w].reshape(rows, part_w), d_all)
        gbuf[j * (n // cols) : (j + 1) * (n // cols)] = grad.astype(BF).reshape(n // cols, nz, per // nz, -1)
    line_q = LineSum(net, lambda f: gbuf.at[:, f], g_line, g_line.at[nz - 1], g_line.at[nz])
    wqkv = w[...].reshape(dm, -1)
    sum1 = PlaneSum(net, sib_out, sib_in, out, inn, mine, keep, True)
    for k, (mask, s) in enumerate(SEND_ORDER):
        sum1.give(mask, s, dot_rt(dqkv[net.tile(mask, s)], wqkv))
        if k == 3:
            line_o.relay()
    sum1.flush()

    def write(ref):
        def store(value):
            ref[...] = value.astype(ref.dtype)

        return store

    line_d.total(write(gwd_out))
    line_u.total(write(ggu_sum))
    line_q.relay()
    plane_u = net.to_plane(lambda m: ggu_sum.at[net.at(m)], ggu_in.at[c])
    ggu_in[c] = ggu_sum[c]
    end = 0
    for s in range(lengths_ref.shape[1]):
        end = end + lengths_ref[0, s]
    for s in range(2):
        own[0, s].wait()
        sib[0, s].wait_recv()
        total = hmid[s] + mo_own[s].astype(F32) + mo_in[s].astype(F32)
        for m in NEXT:
            mo_chip(m, s).wait_recv()
            total = total + mo_recv[m - 2 + s].astype(F32)
        at = lax.rem(net.core + s, 2) * half + net.tile(0, s) * TILE
        padding = at + lax.broadcasted_iota(jnp.int32, (half, 1), 0) >= end
        block_out[s * half : (s + 1) * half, :] = jnp.where(padding, 0.0, total).astype(BF)
    line_o.total(write(gwo_out))
    g_in_row = row_of(gains, 0, dm // LANES)
    grad_in = 0.0
    for s in range(2):
        here = slice(s * half, (s + 1) * half)
        g_part, d_x = norm_back(x_ref[here, :].astype(F32), g_in_row, sum1.total(s), eps)
        grad_in = grad_in + g_part
        dx_out[here, :] = dhmid[s] + d_x
    part[...] = jnp.zeros_like(part)
    for j in range(dm // LANES):
        part[j : j + 1, :] = grad_in[:, j * LANES : (j + 1) * LANES]
        part[8 + j : 9 + j, :] = gpost_ref[:, j * LANES : (j + 1) * LANES]
    part[16:17, :] = gq
    part[17:18, :] = gk
    plane_g = net.to_plane(lambda m: part, gplane.at[c])
    gplane[c] = part[...]
    line_q.total(write(gsum))
    plane_q = net.to_plane(lambda m: gsum.at[net.at(m)], g_in.at[c])
    g_in[c] = gsum[c]
    for cp in plane_g:
        cp.wait_recv()
    gz[z] = jnp.sum(gplane[...], axis=0)
    line_g = net.to_line(lambda m: gz.at[z], lambda m: gz.at[z])
    for cp in plane_u:
        cp.wait_recv()
    ggu_out[...] = ggu_in[...]
    for cp in plane_q:
        cp.wait_recv()
    gqkv_out[...] = g_in[...]
    for cp in line_g:
        cp.wait_recv()
    gains_out[...] = jnp.sum(gz[...], axis=0)
    for part in (gath, sum1, line_d, line_u, line_o, line_q):
        part.finish()
    for cp in line_g + plane_u + plane_g + plane_q + list(sib.values()):
        cp.wait_send()
    for s in range(2):
        for m in CHIPS:
            mo_chip(m, s).wait_send()


def finish(cfg, block_ref, dx_ref, gwo_ref, gwd_ref, ggu_ref, gqkv_ref, gains_ref,
           block_out, dx_out, gin_out, gq_out, gk_out, gv_out, gqg_out, gkg_out, gwo_out, gpost_out, ggate_out, gup_out,
           gwd_out):
    n, nz, ql, kvl, hd, ff = cfg["n"], cfg["nz"], cfg["ql"], cfg["kvl"], cfg["hd"], cfg["ff"]
    block_out[...] = block_ref[...]
    dx_out[...] = dx_ref[...]
    gwo_out[...] = gwo_ref[...]
    gwd_out[...] = gwd_ref[...]
    qw, kw = ql * hd, kvl * hd
    for d in range(n):
        both = gqkv_ref[d].astype(F32)
        gq_out[:, d * qw : (d + 1) * qw] = both[:, :qw]
        gk_out[:, d * kw : (d + 1) * kw] = both[:, qw : qw + kw]
        gv_out[:, d * kw : (d + 1) * kw] = both[:, qw + kw :]
        both = ggu_ref[d].astype(F32)
        ggate_out[:, d * ff : (d + 1) * ff] = both[:, :ff]
        gup_out[:, d * ff : (d + 1) * ff] = both[:, ff:]
    place = lax.axis_index("ctx") * nz + lax.axis_index("fsdp")
    for first, ref in ((0, gin_out), (8, gpost_out), (16, gqg_out), (17, gkg_out)):
        width = ref.shape[1]
        at = place * width
        row = gains_ref[pl.ds(first + lax.div(at, LANES), 1), :]
        ref[...] = pltpu.roll(row, lax.rem(LANES - lax.rem(at, LANES), LANES), 1)[:, :width]


def call(body, cfg, ins, outs, scratch, cid, *args):
    remote = cid is not None
    params = dict(collective_id=cid, has_side_effects=True) if remote else {}
    if remote:
        sems = pltpu.SemaphoreType.DMA((cfg["slots"],))
        scratch = scratch + [pltpu.SemaphoreType.DMA((32,)), sems, sems]
    return pl.pallas_call(
        functools.partial(body, cfg),
        out_shape=[jax.ShapeDtypeStruct(shape, dtype) for shape, dtype, *_ in outs],
        in_specs=ins,
        out_specs=[o[2] if len(o) > 2 else VMEM for o in outs],
        scratch_shapes=scratch,
        compiler_params=pltpu.CompilerParams(vmem_limit_bytes=LIMIT, **params),
        name=body.__name__,
    )(*args)


def on_plane(hidden_in, seq_lengths, in_gain, w_query, w_key, w_value, q_gain, k_gain, w_out, post_gain,
             w_gate, w_up, w_down, d_out):
    n, nz = lax.axis_size("ctx"), lax.axis_size("fsdp")
    t, dm = hidden_in.shape[1:]
    rows = n * t
    hd = q_gain.shape[0] * n * nz
    ql = w_query.shape[1] // hd // n
    kvl = w_key.shape[1] // hd // n
    ff = w_gate.shape[1] // n
    r_in, r_out, r_down = w_query.shape[0], w_out.shape[0], w_down.shape[0]
    qkv = (ql + 2 * kvl) * hd
    tiles, half = rows // TILE, TILE // 2
    cfg = dict(n=n, nz=nz, ql=ql, kvl=kvl, hd=hd, ff=ff, eps=1e-6, window=rows // 2 // TILE, slots=14 * n + 8 * nz)

    inv = 1000000.0 ** (-np.arange(hd // 2) * (2.0 / hd))
    angles = np.concatenate([np.arange(half), np.arange(2 * tiles) * half])[:, None] * inv[None, :]
    table = jnp.asarray(np.concatenate([np.cos(angles), np.sin(angles)], axis=1), F32)
    gshare = jnp.concatenate([in_gain, post_gain, q_gain, k_gain])[None]
    x = hidden_in[0]
    smem = pl.BlockSpec(memory_space=pltpu.SMEM)
    anywhere = pl.BlockSpec(memory_space=pl.ANY)

    def hbm(shape, dtype):
        return (shape, dtype, anywhere)

    def vm(shape, dtype=BF):
        return pltpu.VMEM(shape, dtype)

    big, low, wide, pair = (tiles, TILE, dm), (tiles, TILE, 2 * hd), (tiles, ql, TILE, 2 * hd), (2, half, dm)
    pre_w = (ql + kvl) * hd
    w_s, gu_s, wo_s, wd_s = (n, nz, r_in, qkv), (n, nz, r_in, 2 * ff), (nz, r_out, dm), (nz, r_down, dm)
    attn_s = (tiles, TILE, ql * hd)
    gains_s = (GAIN_ROWS, LANES)
    sums = [vm((n, half, dm)), vm((n, half, dm)), vm((n - 2, half, dm)), vm((n - 2, half, dm)), vm((2, TILE, dm), F32), vm(pair, F32)]
    (qx, kx, vx, attn, mo, pre, cs, xn, w, wo, gwd, ggu, h_mid, d_hmid, d_res, gains, gpost) = call(
        front, cfg, [smem] + [VMEM] * 11,
        [hbm(wide, BF), hbm(low, BF), hbm(low, BF), hbm(attn_s, BF), hbm(big, BF), hbm((tiles, TILE, pre_w), BF),
         hbm((tiles, TILE, hd), F32), hbm(big, BF), hbm(w_s, BF), hbm(wo_s, BF), hbm(wd_s, BF), hbm(gu_s, BF),
         hbm(pair, F32), hbm(pair, F32), hbm(pair, BF), (gains_s, F32), ((1, dm), F32)],
        [vm((n, r_in, qkv)), vm((n, r_in, 2 * ff)), vm(w_s), vm(wo_s), vm(gu_s), vm(wd_s),
         vm((8, LANES), F32), vm(gains_s, F32), vm((n,) + gains_s, F32), vm((nz,) + gains_s, F32),
         vm(big), vm(big), vm((tiles, TILE, pre_w)), vm((tiles, TILE, hd), F32), vm(wide), vm(low), vm(low),
         vm((ql * TILE, 2 * hd), F32), vm(attn_s),
         vm(big), vm((tiles, TILE, ff)), vm((tiles, TILE, 2 * ff)), vm((2, TILE, dm))]
        + sums + [vm(pair, F32), vm(pair, F32), vm(pair), vm(wd_s), vm(gu_s)],
        1, seq_lengths, x, d_out[0], w_query, w_key, w_value, w_out, w_gate, w_up, w_down, gshare, table)

    block, dx, gwo, grad_down, ggu, gqkv, small = call(
        back, cfg, [smem] + [VMEM] * 5 + [anywhere] * 10 + [VMEM] * 3,
        [((t, dm), BF), ((t, dm), F32), ((r_out, dm), F32), ((r_down, dm), F32), ((n, r_in, 2 * ff), BF),
         ((n, r_in, qkv), BF), (gains_s, F32)],
        [vm((n, half, dm)), vm((n, half, dm)), vm((n - 2, half, dm)), vm((n - 2, half, dm)),
         vm((tiles, TILE, pre_w)), vm((tiles, TILE, hd), F32), vm(big), vm(w_s), vm(pair, F32), vm(pair, F32), vm(big),
         vm((ql * TILE, hd), F32), vm((tiles, TILE, hd), F32), vm((tiles, TILE, hd), F32), vm((ql * TILE, 2 * hd)),
         vm(wd_s), vm((nz + 1, r_down, dm)), vm(gu_s), vm((nz + 1, n, r_in, 2 * ff)),
         vm((n, r_in, 2 * ff)), vm((n, r_in, 2 * ff)), vm(wo_s), vm((nz + 1, r_out, dm)),
         vm((tiles, TILE, qkv)), vm(w_s), vm((nz + 1, n, r_in, qkv)), vm((n, r_in, qkv)), vm((n, r_in, qkv)),
         vm(gains_s, F32), vm((n,) + gains_s, F32), vm((nz,) + gains_s, F32)]
        + sums,
        2, seq_lengths, qx, kx, vx, attn, wo, mo, pre, cs, xn, w, gwd, ggu, h_mid, d_hmid, d_res, gains, gpost, x)

    grads = call(
        finish, cfg, [VMEM] * 7,
        [((t, dm), BF), ((t, dm), F32), ((1, in_gain.shape[0]), F32), ((r_in, n * ql * hd), F32),
         ((r_in, n * kvl * hd), F32), ((r_in, n * kvl * hd), F32), ((1, q_gain.shape[0]), F32),
         ((1, k_gain.shape[0]), F32), ((r_out, dm), F32), ((1, post_gain.shape[0]), F32), ((r_in, n * ff), F32),
         ((r_in, n * ff), F32), ((r_down, dm), F32)],
        [], None, block, dx, gwo, grad_down, ggu, gqkv, small)
    (block, dx, g_in, g_q, g_k, g_v, g_qg, g_kg, g_o, g_post, g_gate, g_up, g_down) = grads
    return (block[None], dx[None], g_in[0], g_q, g_k, g_v, g_qg[0], g_kg[0], g_o, g_post[0], g_gate, g_up, g_down)


epsilon = 1e-06
rope_base = 1000000.0
negative = -1e30


def row_info(lengths, row_ids, tok_dev, n_ctx):
    half_len = tok_dev // 2
    device = row_ids // tok_dev
    local_row = row_ids % tok_dev
    block_id = jnp.where(local_row < half_len, device, 2 * n_ctx - 1 - device)
    packed = block_id * half_len + local_row % half_len
    seq_ends = jnp.cumsum(lengths)
    seq_starts = seq_ends - lengths
    member = (packed[:, None] >= seq_starts[None, :]) & (packed[:, None] < seq_ends[None, :])
    row_valid = jnp.any(member, axis=1)
    numbers = jnp.arange(lengths.shape[0], dtype=jnp.int32)
    seq_id = jnp.sum(jnp.where(member, numbers[None, :], 0), axis=1)
    offset = jnp.sum(jnp.where(member, seq_starts[None, :], 0), axis=1)
    segment = jnp.where(row_valid, seq_id, -1 - packed)
    position = jnp.where(row_valid, packed - offset, 0)
    return (segment, position, row_valid)


def norm_gain(values_in, gain_vec):
    row_scale = lax.rsqrt(jnp.mean(values_in * values_in, axis=-1, keepdims=True) + epsilon)
    return values_in * row_scale * gain_vec


def rotary(position, head_dim):
    half_len = head_dim // 2
    inv_freq = jnp.power(rope_base, -jnp.arange(half_len, dtype=jnp.float32) * (2.0 / head_dim))
    angles = position.astype(jnp.float32)[:, None] * inv_freq[None, :]
    angles = jnp.concatenate([angles, angles], axis=1)
    return (jnp.cos(angles), jnp.sin(angles))


def rotate(heads, cos_table, sin_table):
    half_len = heads.shape[-1] // 2
    turned = jnp.concatenate([-heads[..., half_len:], heads[..., :half_len]], axis=-1)
    return heads * cos_table[:, None, :] + turned * sin_table[:, None, :]


def head_post(q_in, k_in, q_scale, k_scale, cos_table, sin_table):
    head_dim = q_scale.shape[0]
    row_count = q_in.shape[0]
    q_heads = norm_gain(q_in.reshape(row_count, -1, head_dim), q_scale)
    k_heads = norm_gain(k_in.reshape(row_count, -1, head_dim), k_scale)
    query_rotated = rotate(q_heads, cos_table, sin_table).reshape(row_count, -1)
    key_rotated = rotate(k_heads, cos_table, sin_table).reshape(row_count, -1)
    return (query_rotated, key_rotated)


def swiglu(gate_in, up_in):
    return jax.nn.silu(gate_in) * up_in


def matmul(left, right):
    return jnp.dot(left, right, preferred_element_type=jnp.float32)


def inner(left, right):
    return lax.dot_general(
        left, right, (((0,), (0,)), ((), ())), preferred_element_type=jnp.float32
    )


def backdot(left, right):
    return lax.dot_general(
        left, right, (((1,), (1,)), ((), ())), preferred_element_type=jnp.float32
    )


def pick_step(key_count):
    for candidate in (512, 384, 256):
        return candidate
    return key_count


def on_rows(
    hidden_in,
    seq_lengths,
    in_gain,
    w_query,
    w_key,
    w_value,
    q_gain,
    k_gain,
    w_out,
    post_gain,
    w_gate,
    w_up,
    w_down,
    d_out,
):
    n_ctx = lax.axis_size("ctx")
    row_count = hidden_in.shape[1]
    lengths = seq_lengths[0]
    own_rows = lax.axis_index("ctx") * row_count + jnp.arange(row_count, dtype=jnp.int32)
    seg_q, pos_q, row_valid = row_info(lengths, own_rows, row_count, n_ctx)
    shards = (
        in_gain,
        w_query,
        w_key,
        w_value,
        q_gain,
        k_gain,
        w_out,
        post_gain,
        w_gate,
        w_up,
        w_down,
    )
    gathered = (
        lax.all_gather(shards[0], ("ctx", "fsdp"), axis=0, tiled=True),
        lax.all_gather(shards[1], ("ctx", "fsdp"), axis=0, tiled=True),
        lax.all_gather(shards[2], ("ctx", "fsdp"), axis=0, tiled=True),
        lax.all_gather(shards[3], ("ctx", "fsdp"), axis=0, tiled=True),
        lax.all_gather(shards[4], ("ctx", "fsdp"), axis=0, tiled=True),
        lax.all_gather(shards[5], ("ctx", "fsdp"), axis=0, tiled=True),
        lax.all_gather(shards[6], ("ctx", "fsdp"), axis=0, tiled=True),
        lax.all_gather(shards[7], ("ctx", "fsdp"), axis=0, tiled=True),
        lax.all_gather(shards[8], ("ctx", "fsdp"), axis=0, tiled=True),
        lax.all_gather(shards[9], ("ctx", "fsdp"), axis=0, tiled=True),
        lax.all_gather(shards[10], ("ctx", "fsdp"), axis=0, tiled=True),
    )
    g_in = gathered[0].astype(jnp.float32)
    g_query = gathered[4].astype(jnp.float32)
    g_key = gathered[5].astype(jnp.float32)
    g_post = gathered[7].astype(jnp.float32)
    head_dim = gathered[4].shape[0]
    kv_width = gathered[2].shape[1]
    kv_heads = kv_width // head_dim
    group_count = gathered[1].shape[1] // kv_width
    score_scale = head_dim ** (-0.5)
    rows_per_group = row_count * n_ctx
    x_float = hidden_in[0].astype(jnp.float32)
    x_normf, in_back = jax.vjp(norm_gain, x_float, g_in)
    x_norm = x_normf.astype(jnp.bfloat16)
    q_pre = matmul(x_norm, gathered[1])
    k_pre = matmul(x_norm, gathered[2])
    value_projected = matmul(x_norm, gathered[3])
    cos_table, sin_table = rotary(pos_q, head_dim)

    def post_local(q_in, k_in, q_scale, k_scale):
        return head_post(q_in, k_in, q_scale, k_scale, cos_table, sin_table)

    rotated, post_back = jax.vjp(post_local, q_pre, k_pre, g_query, g_key)
    q_low4 = rotated[0].astype(jnp.bfloat16).reshape(row_count, kv_heads, group_count, head_dim)
    key_narrow = rotated[1].astype(jnp.bfloat16)
    value_narrow = value_projected.astype(jnp.bfloat16)

    def sweep_keys(carry, k_piece, v_piece, block_fn):
        key_count = k_piece.shape[0]
        key_step = pick_step(key_count)

        def one_turn(state, turn_index):
            offset = turn_index * key_step
            k_block = lax.dynamic_slice_in_dim(k_piece, offset, key_step, 0)
            v_block = lax.dynamic_slice_in_dim(v_piece, offset, key_step, 0)
            key_rows = offset + jnp.arange(key_step, dtype=jnp.int32)
            seg_k, pos_k, unused = row_info(lengths, key_rows, row_count, n_ctx)
            allowed = (seg_q[:, None] == seg_k[None, :]) & (pos_k[None, :] <= pos_q[:, None])
            state = block_fn(state, k_block, v_block, allowed, offset)
            return (state, None)

        carry, unused = lax.scan(
            one_turn, carry, jnp.arange(key_count // key_step, dtype=jnp.int32)
        )
        return carry

    def forward_block(carry, k_block, v_block, allowed, first_key):
        row_max, totals, weighted = carry
        k_heads = k_block.reshape(-1, kv_heads, head_dim)
        v_heads = v_block.reshape(-1, kv_heads, head_dim)
        mask_four = allowed[None, None]
        score = (
            jnp.einsum("qhgd,khd->hgqk", q_low4, k_heads, preferred_element_type=jnp.float32)
            * score_scale
        )
        block_max = jnp.max(jnp.where(mask_four, score, negative), axis=-1)
        new_max = jnp.maximum(row_max, block_max)
        expo = jnp.where(mask_four, jnp.exp(score - new_max[..., None]), 0.0)
        factor = jnp.exp(row_max - new_max)
        totals = totals * factor + jnp.sum(expo, axis=-1)
        weighted = weighted * factor[..., None] + jnp.einsum(
            "hgqk,khd->hgqd", expo.astype(jnp.bfloat16), v_heads, preferred_element_type=jnp.float32
        )
        return (new_max, totals, weighted)

    start_state = (
        jnp.full((kv_heads, group_count, row_count), negative, jnp.float32),
        jnp.zeros((kv_heads, group_count, row_count), jnp.float32),
        jnp.zeros((kv_heads, group_count, row_count, head_dim), jnp.float32),
    )
    pieces = (
        lax.all_gather(key_narrow, "ctx", axis=0, tiled=True),
        lax.all_gather(value_narrow, "ctx", axis=0, tiled=True),
    )
    fold_state = sweep_keys(start_state, pieces[0], pieces[1], forward_block)
    row_max, totals, weighted = fold_state
    attn_four = weighted / totals[..., None]
    log_total = row_max + jnp.log(totals)
    attn = jnp.transpose(attn_four, (2, 0, 1, 3)).reshape(row_count, -1)
    attn_low = attn.astype(jnp.bfloat16)
    h_mid = x_float + matmul(attn_low, gathered[6])
    h_normf, post_norm_back = jax.vjp(norm_gain, h_mid, g_post)
    h_norm = h_normf.astype(jnp.bfloat16)
    gate_out = matmul(h_norm, gathered[8])
    up_out = matmul(h_norm, gathered[9])
    act_float, swiglu_back = jax.vjp(swiglu, gate_out, up_out)
    act_low = act_float.astype(jnp.bfloat16)
    row_mask = row_valid.astype(jnp.float32)[:, None]
    block_out = (row_mask * (h_mid + matmul(act_low, gathered[10]))).astype(jnp.bfloat16)
    again = (
        lax.all_gather(shards[0], ("ctx", "fsdp"), axis=0, tiled=True),
        lax.all_gather(shards[1], ("ctx", "fsdp"), axis=0, tiled=True),
        lax.all_gather(shards[2], ("ctx", "fsdp"), axis=0, tiled=True),
        lax.all_gather(shards[3], ("ctx", "fsdp"), axis=0, tiled=True),
        lax.all_gather(shards[4], ("ctx", "fsdp"), axis=0, tiled=True),
        lax.all_gather(shards[5], ("ctx", "fsdp"), axis=0, tiled=True),
        lax.all_gather(shards[6], ("ctx", "fsdp"), axis=0, tiled=True),
        lax.all_gather(shards[7], ("ctx", "fsdp"), axis=0, tiled=True),
        lax.all_gather(shards[8], ("ctx", "fsdp"), axis=0, tiled=True),
        lax.all_gather(shards[9], ("ctx", "fsdp"), axis=0, tiled=True),
        lax.all_gather(shards[10], ("ctx", "fsdp"), axis=0, tiled=True),
    )
    d_block = d_out[0].astype(jnp.float32) * row_mask
    dm_low = d_block.astype(jnp.bfloat16)
    grad_down = inner(act_low, dm_low)
    d_act = backdot(dm_low, again[10])
    d_gate, d_up = swiglu_back(d_act)
    dg_low = d_gate.astype(jnp.bfloat16)
    du_low = d_up.astype(jnp.bfloat16)
    grad_gate = inner(h_norm, dg_low)
    grad_up = inner(h_norm, du_low)
    d_hnorm = backdot(dg_low, again[8]) + backdot(du_low, again[9])
    d_hpart, grad_post = post_norm_back(d_hnorm)
    d_hmid = d_block + d_hpart
    d_res = d_hmid.astype(jnp.bfloat16)
    grad_wout = inner(attn_low, d_res)
    d_attn = backdot(d_res, again[6]).astype(jnp.bfloat16)
    d_attn4 = d_attn.reshape(row_count, kv_heads, group_count, head_dim)
    delta = jnp.einsum("qhgd,hgqd->hgq", d_attn4.astype(jnp.float32), attn_four)

    def backward_block(carry, k_block, v_block, allowed, first_key):
        d_query, d_kv = carry
        key_count = k_block.shape[0]
        k_heads = k_block.reshape(-1, kv_heads, head_dim)
        v_heads = v_block.reshape(-1, kv_heads, head_dim)
        mask_four = allowed[None, None]
        score = (
            jnp.einsum("qhgd,khd->hgqk", q_low4, k_heads, preferred_element_type=jnp.float32)
            * score_scale
        )
        prob = jnp.where(mask_four, jnp.exp(score - log_total[..., None]), 0.0)
        prob_low = prob.astype(jnp.bfloat16)
        d_prob = jnp.einsum("qhgd,khd->hgqk", d_attn4, v_heads, preferred_element_type=jnp.float32)
        d_score = (prob * (d_prob - delta[..., None])).astype(jnp.bfloat16)
        d_query = d_query + jnp.einsum(
            "hgqk,khd->qhgd", d_score, k_heads, preferred_element_type=jnp.float32
        )
        d_key = (
            jnp.einsum("hgqk,qhgd->khd", d_score, q_low4, preferred_element_type=jnp.float32)
            * score_scale
        )
        d_value = jnp.einsum(
            "hgqk,qhgd->khd", prob_low, d_attn4, preferred_element_type=jnp.float32
        )
        joined = jnp.concatenate(
            [d_key.reshape(key_count, -1), d_value.reshape(key_count, -1)], axis=1
        )
        before = lax.dynamic_slice_in_dim(d_kv, first_key, key_count, 0)
        d_kv = lax.dynamic_update_slice_in_dim(d_kv, before + joined, first_key, 0)
        return (d_query, d_kv)

    back_start = (
        jnp.zeros((row_count, kv_heads, group_count, head_dim), jnp.float32),
        jnp.zeros((rows_per_group, 2 * kv_width), jnp.float32),
    )
    pieces = (
        lax.all_gather(key_narrow, "ctx", axis=0, tiled=True),
        lax.all_gather(value_narrow, "ctx", axis=0, tiled=True),
    )
    back_state = sweep_keys(back_start, pieces[0], pieces[1], backward_block)
    d_qrot = back_state[0].reshape(row_count, -1) * score_scale
    d_kv_own = lax.psum_scatter(
        back_state[1].astype(jnp.bfloat16), "ctx", scatter_dimension=0, tiled=True
    ).astype(jnp.float32)
    d_krot = d_kv_own[:, :kv_width]
    d_vpre = d_kv_own[:, kv_width:]
    d_qpre, d_kpre, grad_qgain, grad_kgain = post_back((d_qrot, d_krot))
    dq_low = d_qpre.astype(jnp.bfloat16)
    dk_low = d_kpre.astype(jnp.bfloat16)
    dv_low = d_vpre.astype(jnp.bfloat16)
    grad_query = inner(x_norm, dq_low)
    grad_key = inner(x_norm, dk_low)
    grad_value = inner(x_norm, dv_low)
    d_xnorm = backdot(dq_low, again[1]) + backdot(dk_low, again[2]) + backdot(dv_low, again[3])
    d_xpart, grad_ingain = in_back(d_xnorm)
    d_hidden = d_hmid + d_xpart
    owned = (
        lax.psum_scatter(grad_ingain, ("ctx", "fsdp"), scatter_dimension=0, tiled=True),
        lax.psum_scatter(grad_query, ("ctx", "fsdp"), scatter_dimension=0, tiled=True),
        lax.psum_scatter(grad_key, ("ctx", "fsdp"), scatter_dimension=0, tiled=True),
        lax.psum_scatter(grad_value, ("ctx", "fsdp"), scatter_dimension=0, tiled=True),
        lax.psum_scatter(grad_qgain, ("ctx", "fsdp"), scatter_dimension=0, tiled=True),
        lax.psum_scatter(grad_kgain, ("ctx", "fsdp"), scatter_dimension=0, tiled=True),
        lax.psum_scatter(grad_wout, ("ctx", "fsdp"), scatter_dimension=0, tiled=True),
        lax.psum_scatter(grad_post, ("ctx", "fsdp"), scatter_dimension=0, tiled=True),
        lax.psum_scatter(grad_gate, ("ctx", "fsdp"), scatter_dimension=0, tiled=True),
        lax.psum_scatter(grad_up, ("ctx", "fsdp"), scatter_dimension=0, tiled=True),
        lax.psum_scatter(grad_down, ("ctx", "fsdp"), scatter_dimension=0, tiled=True),
    )
    return (
        block_out[None],
        d_hidden[None],
        owned[0],
        owned[1],
        owned[2],
        owned[3],
        owned[4],
        owned[5],
        owned[6],
        owned[7],
        owned[8],
        owned[9],
        owned[10],
    )


def on_device(*args):
    n = lax.axis_size("ctx")
    hidden_in, w_key, w_out, w_gate, q_gain = args[0], args[4], args[8], args[10], args[6]
    hd = q_gain.shape[0] * n * lax.axis_size("fsdp")
    heads, ff = w_key.shape[1] // hd, w_gate.shape[1] // n
    even = heads % n == 0 and ff % LANES == 0 and w_key.shape[0] % 16 == 0 and w_out.shape[0] % 16 == 0
    if even and heads == n == 8 and hidden_in.shape[1] == TILE:
        return on_plane(*args)
    return on_rows(*args)


def solution(mesh):
    in_specs = (
        P("fsdp", "ctx", None),
        P("fsdp", None),
        P(("ctx", "fsdp")),
        P(("ctx", "fsdp"), None),
        P(("ctx", "fsdp"), None),
        P(("ctx", "fsdp"), None),
        P(("ctx", "fsdp")),
        P(("ctx", "fsdp")),
        P(("ctx", "fsdp"), None),
        P(("ctx", "fsdp")),
        P(("ctx", "fsdp"), None),
        P(("ctx", "fsdp"), None),
        P(("ctx", "fsdp"), None),
        P("fsdp", "ctx", None),
    )
    out_specs = (
        P("fsdp", "ctx", None),
        P("fsdp", "ctx", None),
        P(("ctx", "fsdp")),
        P(("ctx", "fsdp"), None),
        P(("ctx", "fsdp"), None),
        P(("ctx", "fsdp"), None),
        P(("ctx", "fsdp")),
        P(("ctx", "fsdp")),
        P(("ctx", "fsdp"), None),
        P(("ctx", "fsdp")),
        P(("ctx", "fsdp"), None),
        P(("ctx", "fsdp"), None),
        P(("ctx", "fsdp"), None),
    )
    return jax.shard_map(
        on_device, mesh=mesh, in_specs=in_specs, out_specs=out_specs, check_vma=False
    )
```

```python
import functools
import math

import jax
import jax.numpy as jnp
import numpy as np
from jax import lax
from jax.experimental import pallas as pl
from jax.experimental.pallas import tpu as pltpu
from jax.sharding import PartitionSpec as P

BF = jnp.bfloat16
F32 = jnp.float32
MESH = pl.DeviceIdType.MESH
VMEM = pl.BlockSpec(memory_space=pltpu.VMEM)
GAIN_ROWS = 24
LANES = 128
TILE = 256
LIMIT = 63 * 2**20
CORE, ALONG_X, ALONG_Y, ACROSS = 1, 2, 4, 6
CHIPS = (ALONG_X, ALONG_Y, ACROSS)
NEXT = (ALONG_X, ALONG_Y)


def dot(a, b):
    return jnp.dot(a, b, preferred_element_type=F32)


def dot_rt(a, b):
    return lax.dot_general(a, b, (((1,), (1,)), ((), ())), preferred_element_type=F32)


def dot_lt(a, b):
    return lax.dot_general(a, b, (((0,), (0,)), ((), ())), preferred_element_type=F32)


def flip(place, mask, size):
    out, bit = 0, 1
    while bit < size:
        out = out + bit * lax.rem(lax.div(place, bit) + (mask // bit) % 2, 2)
        bit *= 2
    return out


class Net:
    def __init__(self, n, nz, tiles, send, recv):
        self.n, self.nz, self.tiles, self.send, self.recv = n, nz, tiles, send, recv
        self.c = lax.axis_index("ctx")
        self.z = lax.axis_index("fsdp")
        self.core = lax.rem(self.c, 2)
        self.slot = 0

    def slots(self, count):
        first = self.slot
        self.slot += count
        return first

    def at(self, mask):
        return flip(self.c, mask, self.n)

    def zat(self, mask):
        return flip(self.z, mask, self.nz)

    def peer(self, mask):
        return (self.at(mask), self.z)

    def zpeer(self, mask):
        return (self.c, self.zat(mask))

    def tile(self, mask, s):
        chip = lax.div(self.at(mask), 2)
        return chip if s == 0 else self.tiles - 1 - chip

    def view(self, buf, mask, s):
        half = TILE // 2
        core = lax.rem(self.at(mask), 2)
        first = core if s == 0 else 1 - core
        return buf.at[self.tile(mask, s), pl.ds(pl.multiple_of(first * half, half), half), :]

    def barrier(self):
        bar = pltpu.get_barrier_semaphore()
        for mask in range(1, self.n):
            pl.semaphore_signal(bar, inc=1, device_id=self.peer(mask), device_id_type=MESH)
        for mask in range(1, self.nz):
            pl.semaphore_signal(bar, inc=1, device_id=self.zpeer(mask), device_id_type=MESH)
        pl.semaphore_wait(bar, self.n + self.nz - 2)

    def copy(self, src, dst, slot, device, send_slot=None):
        return pltpu.make_async_remote_copy(
            src_ref=src,
            dst_ref=dst,
            send_sem=self.send.at[slot if send_slot is None else send_slot],
            recv_sem=self.recv.at[slot],
            device_id=device,
            device_id_type=MESH,
        )

    def to_plane(self, src, dst):
        base = self.slots(self.n)
        out = []
        for mask in range(1, self.n):
            cp = self.copy(src(mask), dst, base + mask, self.peer(mask))
            cp.start()
            out.append(cp)
        return out

    def to_line(self, src, dst):
        base = self.slots(self.nz)
        out = []
        for mask in range(1, self.nz):
            cp = self.copy(src(mask), dst(mask), base + mask, self.zpeer(mask))
            cp.start()
            out.append(cp)
        return out


class Line:
    def __init__(self, net, view):
        self.net, self.view = net, view
        self.base = net.slots(net.nz)
        self.middle = (net.z == 1) | (net.z == 2)
        self.relayed = net.nz == 4
        own = view(net.z)
        self.direct = [m for m in range(1, net.nz) if not (self.relayed and m == 3)]
        self.copies = {m: net.copy(own, own, self.base + m, net.zpeer(m)) for m in range(1, net.nz)}
        for m in self.direct[::-1]:
            self.copies[m].start()
        if self.relayed:
            far = view(net.zat(2))
            self.passed = net.copy(far, far, self.base + 3, net.zpeer(1), send_slot=self.base)

    def relay(self):
        if self.relayed:
            self.copies[2].wait_recv()

            @pl.when(self.middle)
            def _():
                self.passed.start()
                self.copies[3].start()

    def arrive(self):
        for m, cp in self.copies.items():
            if not (self.relayed and m == 2):
                cp.wait_recv()

    def finish(self):
        for m in self.direct:
            self.copies[m].wait_send()
        if self.relayed:

            @pl.when(self.middle)
            def _():
                self.copies[3].wait_send()
                self.passed.wait_send()


class LineSum:
    def __init__(self, net, piece, inn, passing, both):
        self.net, self.piece, self.inn, self.passing, self.both = net, piece, inn, passing, both
        self.base = net.slots(net.nz)
        self.middle = (net.z == 1) | (net.z == 2)
        self.relayed = net.nz == 4
        if not self.relayed:
            for m in range(1, net.nz):
                self.to(m).start()
            return

        @pl.when(jnp.logical_not(self.middle))
        def _():
            self.far().start()
            self.to(2).start()
            self.to(1).start()

        @pl.when(self.middle)
        def _():
            self.to(3).start()
            self.to(1).start()

    def to(self, m):
        return self.net.copy(self.piece(self.net.zat(m)), self.inn.at[m - 1], self.base + m, self.net.zpeer(m))

    def far(self):
        return self.net.copy(
            self.piece(self.net.zat(3)), self.passing, self.base, self.net.zpeer(1), send_slot=self.base + 3
        )

    def joined(self):
        return self.net.copy(self.both, self.inn.at[1], self.base + 2, self.net.zpeer(2))

    def relay(self):
        if self.relayed:

            @pl.when(self.middle)
            def _():
                self.far().wait_recv()
                own = self.piece(self.net.zat(2))[...].astype(F32)
                self.both[...] = (own + self.passing[...].astype(F32)).astype(BF)
                self.joined().start()

    def total(self, write):
        def some(masks):
            value = self.piece(self.net.z)[...].astype(F32)
            for m in masks:
                self.to(m).wait_recv()
                value = value + self.inn[m - 1].astype(F32)
            write(value)

        if not self.relayed:
            some(range(1, self.net.nz))
            return

        @pl.when(self.middle)
        def _():
            some((1, 2, 3))

        @pl.when(jnp.logical_not(self.middle))
        def _():
            some((1, 2))

    def finish(self):
        if not self.relayed:
            for m in range(1, self.net.nz):
                self.to(m).wait_send()
            return
        self.to(1).wait_send()
        self.to(2).wait_send()
        self.to(3).wait_send()


class Gather:
    def __init__(self, net, buf):
        self.net, self.buf = net, buf
        self.base = net.slots(2 * net.n)
        self.sent = []

    def send(self, mask, s, to, arrives_as):
        view = self.net.view(self.buf, mask, s)
        slot = self.base + 2 * arrives_as + s
        cp = self.net.copy(view, view, slot, self.net.peer(to))
        cp.start()
        self.sent.append(cp)

    def start(self, s):
        for mask in (CORE, ALONG_X, ALONG_Y):
            self.send(0, s, mask, mask)

    def arrive(self, mask, s):
        view = self.net.view(self.buf, mask, s)
        self.net.copy(view, view, self.base + 2 * mask + s, self.net.peer(mask)).wait_recv()
        if mask % 2 == 0:
            if mask == (ALONG_X, ALONG_Y)[s]:
                self.send(mask, s, (ALONG_Y, ALONG_X)[s], ACROSS)
            self.send(mask, s, CORE, mask + 1)

    def finish(self):
        for cp in self.sent:
            cp.wait_send()


class PlaneSum:
    def __init__(self, net, sib_out, sib_in, out, inn, mine, keep, joined):
        self.net, self.joined = net, joined
        self.sib_out, self.sib_in, self.out, self.inn, self.mine, self.keep = sib_out, sib_in, out, inn, mine, keep
        self.base = net.slots(2 * net.n)
        self.sent, self.queue, self.given = [], [], 0

    def sibling(self, mask, s):
        return self.net.copy(
            self.sib_out.at[mask + s], self.sib_in.at[mask + s], self.base + 2 * (mask + 1) + s, self.net.peer(CORE)
        )

    def chip(self, mask, s):
        i = mask - 2 + s
        to = NEXT[s] if mask == ACROSS and self.joined else mask
        return self.net.copy(self.out.at[i], self.inn.at[i], self.base + 2 * mask + s, self.net.peer(to))

    def give(self, mask, s, value):
        half = TILE // 2
        place = self.given % 2
        self.given += 1
        self.mine[place] = value
        mine = lax.rem(self.net.core + s, 2) * half
        own = pl.ds(pl.multiple_of(mine, half), half)
        other = pl.ds(pl.multiple_of(half - mine, half), half)
        self.sib_out[mask + s] = self.mine[place, other, :].astype(BF)
        cp = self.sibling(mask, s)
        cp.start()
        self.sent.append(cp)
        self.queue.append((mask, s, place, own))
        if len(self.queue) > 1:
            self.combine()

    def combine(self):
        mask, s, place, own = self.queue.pop(0)
        self.sibling(mask, s).wait_recv()
        both = self.mine[place, own, :] + self.sib_in[mask + s].astype(F32)
        if mask == 0:
            self.keep[s] = both
            return
        if self.joined and mask == NEXT[1 - s]:
            self.chip(ACROSS, s).wait_recv()
            both = both + self.inn[ACROSS - 2 + s].astype(F32)
        self.out[mask - 2 + s] = both.astype(BF)
        cp = self.chip(mask, s)
        cp.start()
        self.sent.append(cp)

    def flush(self):
        while self.queue:
            self.combine()

    def total(self, s):
        value = self.keep[s]
        for mask in NEXT if self.joined else CHIPS:
            self.chip(mask, s).wait_recv()
            value = value + self.inn[mask - 2 + s].astype(F32)
        return value

    def finish(self):
        for cp in self.sent:
            cp.wait_send()


SEND_ORDER = ((ACROSS, 0), (ACROSS, 1), (ALONG_X, 0), (ALONG_Y, 1), (ALONG_Y, 0), (ALONG_X, 1), (0, 0), (0, 1))
ARRIVE_ORDER = ((0, 0), (0, 1), (ALONG_X, 0), (ALONG_Y, 0), (ALONG_X, 1), (ALONG_Y, 1), (ACROSS, 0), (ACROSS, 1))


def arrive_for(gath, mask, s):
    if mask == ALONG_X:
        gath.arrive(ALONG_X, s)
        gath.arrive(ALONG_Y, s)
    elif mask == ACROSS:
        gath.arrive(ACROSS, s)
    gath.arrive(mask + 1, s)


def row_of(g, first, count):
    return jnp.concatenate([g[first + j : first + j + 1, :] for j in range(count)], axis=1)


def split_three(value, lane):
    first = value.astype(BF).astype(F32)
    rest = value - first
    second = rest.astype(BF).astype(F32)
    third = rest - second
    out = jnp.where(lane == 0, first, jnp.where(lane == 1, second, jnp.where(lane == 2, third, 0.0)))
    return out.astype(BF)


def first_keys(lengths_ref, at):
    start = jnp.zeros_like(at)
    begin = 0
    for s in range(lengths_ref.shape[1]):
        start = jnp.where(at >= begin, begin, start)
        begin = begin + lengths_ref[0, s]
    padding = at >= begin
    return jnp.where(padding, at, start), padding


def halves(a, hd):
    lane = lax.broadcasted_iota(jnp.int32, a.shape, 1)
    other = pltpu.roll(a, hd // 2, 1)
    return jnp.where(lane < hd // 2, a, other), jnp.where(lane < hd // 2, -other, a)


def angle_sum(a, b, hd):
    lane = lax.broadcasted_iota(jnp.int32, jnp.broadcast_shapes(a.shape, b.shape), 1)
    a2, b2 = pltpu.roll(a, hd // 2, 1), pltpu.roll(b, hd // 2, 1)
    return jnp.where(lane < hd // 2, a * b - a2 * b2, a * b2 + a2 * b)


def minus_angle(a, hd):
    lane = lax.broadcasted_iota(jnp.int32, a.shape, 1)
    return jnp.where(lane < hd // 2, a, -a)


def norm_back(v, gain, dy, eps):
    r = lax.rsqrt(jnp.mean(v * v, axis=-1, keepdims=True) + eps)
    gdy = gain * dy
    dv = r * gdy - v * (r * r * r) * jnp.mean(gdy * v, axis=-1, keepdims=True)
    return jnp.sum(dy * v * r, axis=0, keepdims=True), dv


def front(cfg, lengths_ref, x_ref, do_ref, wq_ref, wk_ref, wv_ref, wo_ref, wg_ref, wu_ref, wd_ref, gi_ref, gp_ref, gq_ref, gk_ref, table_ref,
          qx_out, kx_out, vx_out, attn_out, mo_out, pre_out, cs_out, xn_out, w_out, wo_out, gwd_out, ggu_out,
          hmid_out, dhmid_out, dres_out, gains_out, gpost_out,
          wsend, gsend, w, wo_all, gu, wd_all, grow, gpart, gbuf, gz, xg, xn, pre, cs, qx, kx, vx, acc, attn,
          dblk, act, dgu, mo, sib_out, sib_in, out, inn, mine, keep, hmid, dhmid, dres, gwd_buf, ggu_buf,
          local, send, recv):
    n, nz, ql, kvl, hd, ff = cfg["n"], cfg["nz"], cfg["ql"], cfg["kvl"], cfg["hd"], cfg["ff"]
    eps = cfg["eps"]
    t, dm = x_ref.shape
    half = TILE // 2
    tiles = qx.shape[0]
    rows = n * t
    net = Net(n, nz, tiles, send, recv)
    c, z = net.c, net.z
    stores = []

    def store(src, dst):
        cp = pltpu.make_async_copy(src, dst, local.at[len(stores)])
        cp.start()
        stores.append(cp)
        return cp

    qw, kw = ql * hd, kvl * hd
    for j in range(n):
        wsend[j, :, :qw] = wq_ref[:, j * qw : (j + 1) * qw]
        wsend[j, :, qw : qw + kw] = wk_ref[:, j * kw : (j + 1) * kw]
        wsend[j, :, qw + kw :] = wv_ref[:, j * kw : (j + 1) * kw]
        gsend[j, :, :ff] = wg_ref[:, j * ff : (j + 1) * ff]
        gsend[j, :, ff:] = wu_ref[:, j * ff : (j + 1) * ff]
    grow[...] = jnp.zeros_like(grow)
    put = 0
    for ref in (gi_ref, gp_ref, gq_ref, gk_ref):
        grow[0:1, put : put + ref.shape[1]] = ref[...].astype(F32)
        put += ref.shape[1]
    row = jnp.broadcast_to(grow[0:1, :], (8, LANES))
    lane8 = lax.broadcasted_iota(jnp.int32, (8, LANES), 1)
    at = lax.broadcasted_iota(jnp.int32, (8, LANES), 0) * LANES + lane8
    wide, narrow = dm // (n * nz), hd // (n * nz)
    place = c * nz + z

    def placed(first, share, row0):
        shift = lax.rem(place * share, LANES)
        moved = pltpu.roll(row, lax.rem(shift + LANES - first, LANES), 1)
        return jnp.where((at >= row0 + place * share) & (at < row0 + (place + 1) * share), moved, 0.0)

    gpart[0:8, :] = placed(0, wide, 0)
    gpart[8:16, :] = placed(wide, wide, 0)
    gpart[16:24, :] = placed(2 * wide, narrow, 0) + placed(2 * wide + narrow, narrow, LANES)
    for s in range(2):
        net.view(xg, 0, s)[...] = x_ref[s * half : (s + 1) * half, :]
    w[c, z] = wsend[c]
    gu[c, z] = gsend[c]
    wo_all[z] = wo_ref[...]
    wd_all[z] = wd_ref[...]
    net.barrier()
    plane_g = net.to_plane(lambda m: gpart, gbuf.at[c])
    plane_w = net.to_plane(lambda m: wsend.at[net.at(m)], w.at[c, z])
    line_o = Line(net, lambda f: wo_all.at[f])
    gath = Gather(net, xg)
    gath.start(0)
    gath.start(1)
    gbuf[c] = gpart[...]
    for cp in plane_g:
        cp.wait_recv()
    gz[z] = jnp.sum(gbuf[...], axis=0)
    line_g = net.to_line(lambda m: gz.at[z], lambda m: gz.at[z])
    for cp in plane_w:
        cp.wait_recv()
    line_w = Line(net, lambda f: w.at[:, f])

    lo = table_ref[0:half, :]
    begins, firsts = [], []
    begin = 0
    for s in range(lengths_ref.shape[1]):
        begins.append(begin)
        hi_row = table_ref[pl.ds(half + lax.div(begin, half), 1), :]
        lo_row = table_ref[pl.ds(lax.rem(begin, half), 1), :]
        firsts.append(minus_angle(angle_sum(hi_row, lo_row, hd), hd))
        begin = begin + lengths_ref[0, s]
    end = begin
    one = jnp.where(lax.broadcasted_iota(jnp.int32, (1, hd), 1) < hd // 2, 1.0, 0.0)

    def positions(b, carry):
        at = b * half + lax.broadcasted_iota(jnp.int32, (half, hd), 0)
        hi_row = table_ref[pl.ds(half + b, 1), :]
        shift = angle_sum(hi_row, firsts[0], hd)
        for begin, first in zip(begins[1:], firsts[1:]):
            shift = jnp.where(at >= begin, angle_sum(hi_row, first, hd), shift)
        both = jnp.where(at >= end, one, angle_sum(shift, lo, hd))
        cs[lax.div(b, 2), pl.ds(pl.multiple_of(lax.rem(b, 2) * half, half), half), :] = both
        return carry

    lax.fori_loop(0, 2 * tiles, positions, 0)
    for cp in line_g:
        cp.wait_recv()
    gains = jnp.sum(gz[...], axis=0)
    g_in = row_of(gains, 0, dm // LANES)
    g_post = row_of(gains, 8, dm // LANES)
    g_q = gains[16:17, :]
    g_k = gains[17:18, :]
    step = 32

    def normalise(tile):
        def some(i, carry):
            here = pl.ds(pl.multiple_of(i * step, step), step)
            v = xg[tile, here, :].astype(F32)
            r = lax.rsqrt(jnp.mean(v * v, axis=-1, keepdims=True) + eps)
            xn[tile, here, :] = (v * r * g_in).astype(BF)
            return carry

        lax.fori_loop(0, TILE // step, some, 0)

    for mask, s in ARRIVE_ORDER:
        arrive_for(gath, mask, s)
        normalise(net.tile(mask, s))
        if mask == ALONG_Y and s == 1:
            plane_u = net.to_plane(lambda m: gsend.at[net.at(m)], gu.at[c, z])
            line_w.relay()
    line_o.relay()
    gath_d = Gather(net, dblk)
    for s in range(2):
        first = lax.rem(net.core + s, 2) * half + net.tile(0, s) * TILE
        padding = first + lax.broadcasted_iota(jnp.int32, (half, 1), 0) >= end
        net.view(dblk, 0, s)[...] = jnp.where(padding, 0.0, do_ref[s * half : (s + 1) * half, :].astype(F32)).astype(BF)
        gath_d.start(s)
    for cp in plane_u:
        cp.wait_recv()
    line_u = Line(net, lambda f: gu.at[:, f])
    line_w.arrive()
    wqkv = w[...].reshape(dm, -1)
    lane_b = lax.broadcasted_iota(jnp.int32, (TILE, hd), 1)
    minus = jnp.where(lane_b < 3, -1.0, 0.0).astype(BF)

    def heads(tile, carry):
        qkv = dot(xn[tile], wqkv)
        width = qw + kw
        pre[tile] = qkv[:, :width].astype(BF)
        cos, sin = halves(cs[tile], hd)
        for h in range(ql + kvl):
            v = qkv[:, h * hd : (h + 1) * hd]
            r = lax.rsqrt(jnp.mean(v * v, axis=-1, keepdims=True) + eps)
            hat = v * r * (g_q if h < ql else g_k)
            low = (hat * cos + pltpu.roll(hat, hd // 2, 1) * sin).astype(BF)
            if h < ql:
                qx[tile, h, :, :hd] = low
            else:
                kx[tile, :, :hd] = low
        vx[tile, :, :hd] = qkv[:, width:].astype(BF)
        kx[tile, :, hd:] = minus
        vx[tile, :, hd:] = minus
        return carry

    lax.fori_loop(0, tiles, heads, 0)
    hn = xn
    xn_stored = store(xn, xn_out)
    for src, dst in ((pre, pre_out), (cs, cs_out), (kx, kx_out), (vx, vx_out), (w, w_out)):
        store(src, dst)
    line_o.arrive()
    wout = wo_all[...].reshape(-1, dm)
    store(wo_all, wo_out)

    high = ql * TILE
    factor = math.log2(math.e) / math.sqrt(hd)
    lane_q = lax.broadcasted_iota(jnp.int32, (high, hd), 1)

    def attend(i):
        q = qx[i, :, :, :hd].reshape(high, hd)
        start = first_keys(lengths_ref, i * TILE + lax.broadcasted_iota(jnp.int32, (TILE, 1), 0))[0]
        q_at = i * TILE + lax.broadcasted_iota(jnp.int32, (TILE, 2 * TILE), 0)
        acc[...] = jnp.zeros_like(acc)

        def k_tile(j, carry):
            here = pl.ds(2 * j, 2)
            s = dot_rt(q, kx[here, :, :hd].reshape(2 * TILE, hd))
            k_at = j * (2 * TILE) + lax.broadcasted_iota(jnp.int32, (TILE, 2 * TILE), 1)
            allowed = (k_at <= q_at) & (k_at >= start)
            e = jnp.where(allowed[None], jnp.exp2(s * factor).reshape(ql, TILE, 2 * TILE), 0.0)
            acc[...] += dot(e.astype(BF).reshape(high, 2 * TILE), vx[here].reshape(2 * TILE, 2 * hd))
            return carry

        lax.fori_loop(lax.div(jnp.maximum(i - cfg["window"], 0), 2), lax.div(i, 2) + 1, k_tile, 0)
        total = -acc[:, hd : hd + 1]
        low = (acc[:, :hd] / total).astype(BF)
        for h in range(ql):
            attn[i, :, h * hd : (h + 1) * hd] = low[h * TILE : (h + 1) * TILE]
        extra = jnp.broadcast_to(jnp.log(total) * math.sqrt(hd), (high, hd))
        qx[i, :, :, hd:] = split_three(extra, lane_q).reshape(ql, TILE, hd)

    xn_stored.wait()
    gath.finish()
    sum1 = PlaneSum(net, sib_out, sib_in, out, inn, mine, keep, True)
    gath1 = Gather(net, hn)

    def middle(s):
        h_mid = x_ref[s * half : (s + 1) * half, :].astype(F32) + sum1.total(s)
        hmid[s] = h_mid
        r = lax.rsqrt(jnp.mean(h_mid * h_mid, axis=-1, keepdims=True) + eps)
        net.view(hn, 0, s)[...] = (h_mid * r * g_post).astype(BF)
        gath1.start(s)

    for k, (mask, s) in enumerate(SEND_ORDER):
        tile = net.tile(mask, s)
        attend(tile)
        sum1.give(mask, s, dot(attn[tile], wout))
        if k == 2:
            for half_s in range(2):
                gath_d.arrive(ALONG_X, half_s)
                gath_d.arrive(ALONG_Y, half_s)
        if k == 3:
            line_d = Line(net, lambda f: wd_all.at[f])
        if k == 6:
            line_u.relay()
    sum1.flush()
    store(qx, qx_out)
    store(attn, attn_out)
    for s in range(2):
        gath_d.arrive(ACROSS, s)
    middle(0)
    middle(1)
    line_d.relay()
    store(hmid, hmid_out)
    sum1.finish()
    for mask in (CORE, ALONG_X + 1, ALONG_Y + 1, ACROSS + 1):
        for s in range(2):
            gath_d.arrive(mask, s)
    line_u.arrive()
    wgu = gu[...].reshape(dm, -1)
    mo_stores = []

    def open_up(d):
        dgu[d] = dot(hn[d], wgu).astype(BF)

    def block(d):
        gate, up = dgu[d, :, :ff].astype(F32), dgu[d, :, ff:].astype(F32)
        sig = 1.0 / (1.0 + jnp.exp(-gate))
        silu = gate * sig
        low = (silu * up).astype(BF)
        act[d] = low
        if len(mo_stores) > 1:
            mo_stores[-2].wait()
        place = len(mo_stores) % 2
        mo[place] = dot(low, wd).astype(BF)
        mo_stores.append(store(mo.at[place], mo_out.at[d]))
        d_act = dot_rt(dblk[d], wd)
        dgu[d, :, :ff] = (d_act * up * sig * (1.0 + gate * (1.0 - sig))).astype(BF)
        dgu[d, :, ff:] = (d_act * silu).astype(BF)
        return dot_rt(dgu[d], wgu)

    for mask, s in ARRIVE_ORDER:
        arrive_for(gath1, mask, s)
        open_up(net.tile(mask, s))
    line_d.arrive()
    wd = wd_all[...].reshape(-1, dm)
    sum2 = PlaneSum(net, sib_out, sib_in, out, inn, mine, keep, True)
    for mask, s in SEND_ORDER:
        sum2.give(mask, s, block(net.tile(mask, s)))
    sum2.flush()
    dgu_all = dgu[...].reshape(rows, 2 * ff)
    gwd_buf[...] = dot_lt(act[...].reshape(rows, ff), dblk[...].reshape(rows, dm)).astype(BF).reshape(gwd_buf.shape)
    store(gwd_buf, gwd_out)
    per = dm // n
    cols = 2
    part_w = dm // cols
    for j in range(cols):
        part = dot_lt(hn[:, :, j * part_w : (j + 1) * part_w].reshape(rows, part_w), dgu_all)
        ggu_buf[j * (n // cols) : (j + 1) * (n // cols)] = part.astype(BF).reshape(n // cols, nz, per // nz, 2 * ff)
    store(ggu_buf, ggu_out)
    g_sum = 0.0
    for s in range(2):
        g_part, dv = norm_back(hmid[s], g_post, sum2.total(s), eps)
        g_sum = g_sum + g_part
        d_hmid = net.view(dblk, 0, s)[...].astype(F32) + dv
        dhmid[s] = d_hmid
        dres[s] = d_hmid.astype(BF)
    store(dhmid, dhmid_out)
    store(dres, dres_out)
    gains_out[...] = gains
    gpost_out[...] = g_sum
    for part in (gath_d, gath1, sum2, line_o, line_w, line_u, line_d):
        part.finish()
    for cp in plane_g + plane_w + plane_u + line_g:
        cp.wait_send()
    for cp in stores:
        if not any(cp is other for other in [xn_stored] + mo_stores[:-2]):
            cp.wait()


def back(cfg, lengths_ref, qx_ref, kx_ref, vx_ref, attn_ref, wo_ref, mo_ref, pre_ref, cs_ref, xn_ref, w_ref, gwd_ref,
         ggu_ref, hmid_ref, dhmid_ref, dres_ref, gains_ref, gpost_ref, x_ref,
         block_out, dx_out, gwo_out, gwd_out, ggu_out, gqkv_out, gains_out,
         mo_own, mo_in, mo_send, mo_recv, pre, cs, xn, w, hmid, dhmid, dresg, dq, dk, dv, dax, gwd, gwd_in, ggu,
         ggu_line, ggu_sum, ggu_in, gwo, gwo_in, dqkv, gbuf, g_line, gsum, g_in, part, gplane, gz,
         sib_out, sib_in, out, inn, mine, keep, local, send, recv):
    n, nz, ql, kvl, hd, ff = cfg["n"], cfg["nz"], cfg["ql"], cfg["kvl"], cfg["hd"], cfg["ff"]
    eps = cfg["eps"]
    t, dm = x_ref.shape
    half = TILE // 2
    rows = n * t
    tiles = qx_ref.shape[0]
    qw, kw = ql * hd, kvl * hd
    net = Net(n, nz, tiles, send, recv)
    c, z = net.c, net.z
    loads = []

    def load(src, dst):
        cp = pltpu.make_async_copy(src, dst, local.at[len(loads)])
        cp.start()
        loads.append(cp)
        return cp

    first = [load(dres_ref.at[s], net.view(dresg, 0, s)) for s in range(2)]
    own = {(m, s): load(net.view(mo_ref, m, s), mo_own.at[m + s]) for m in (0,) + CHIPS for s in range(2)}
    first += [load(gwd_ref, gwd), load(ggu_ref, ggu)]
    more = [load(a, b) for a, b in ((pre_ref, pre), (cs_ref, cs), (xn_ref, xn), (w_ref, w), (hmid_ref, hmid),
                                    (dhmid_ref, dhmid))]
    for cp in first:
        cp.wait()
    net.barrier()
    gath = Gather(net, dresg)
    gath.start(0)
    gath.start(1)
    line_d = LineSum(net, lambda f: gwd.at[f], gwd_in, gwd_in.at[nz - 1], gwd_in.at[nz])
    line_u = LineSum(net, lambda f: ggu.at[:, f], ggu_line, ggu_line.at[nz - 1], ggu_line.at[nz])
    base = net.slots(2 * n)
    sib = {}
    for m in CHIPS + (0,):
        for s in range(2):
            cp = net.copy(net.view(mo_ref, m + 1, s), mo_in.at[m + s], base + m + s, net.peer(CORE))
            cp.start()
            sib[m, s] = cp
    wout = wo_ref[...].reshape(-1, dm)
    gains = gains_ref[...]
    g_q = gains[16:17, :]
    g_k = gains[17:18, :]
    high = ql * TILE
    factor = math.log2(math.e) / math.sqrt(hd)
    scale = 1.0 / math.sqrt(hd)
    lane = lax.broadcasted_iota(jnp.int32, (TILE, hd), 1)
    dk[...] = jnp.zeros_like(dk)
    dv[...] = jnp.zeros_like(dv)

    def attend_back(i):
        d_attn = dot_rt(dresg[i], wout).astype(BF)
        prod = d_attn.astype(F32) * attn_ref[i].astype(F32)
        for h in range(ql):
            delta = jnp.sum(prod[:, h * hd : (h + 1) * hd], axis=-1, keepdims=True)
            dax[h * TILE : (h + 1) * TILE, :hd] = d_attn[:, h * hd : (h + 1) * hd]
            dax[h * TILE : (h + 1) * TILE, hd:] = split_three(jnp.broadcast_to(delta, (TILE, hd)), lane)
        qx = qx_ref[i].reshape(high, 2 * hd)
        start = first_keys(lengths_ref, i * TILE + lax.broadcasted_iota(jnp.int32, (1, TILE), 1))[0]
        q_at = i * TILE + lax.broadcasted_iota(jnp.int32, (2 * TILE, TILE), 1)
        dq[...] = jnp.zeros_like(dq)

        def k_tile(j, carry):
            here = pl.ds(2 * j, 2)
            k_at = j * (2 * TILE) + lax.broadcasted_iota(jnp.int32, (2 * TILE, TILE), 0)
            allowed = (k_at <= q_at) & (k_at >= start)
            allowed = jnp.concatenate([allowed] * ql, axis=1)
            s = dot_rt(kx_ref[here].reshape(2 * TILE, 2 * hd), qx)
            p = jnp.where(allowed, jnp.exp2(s * factor), 0.0)
            ds = (p * dot_rt(vx_ref[here].reshape(2 * TILE, 2 * hd), dax[...])).astype(BF)
            dv[here] += dot(p.astype(BF), dax[:, :hd]).reshape(2, TILE, hd)
            dk[here] += dot(ds, qx[:, :hd]).reshape(2, TILE, hd)
            dq[...] += dot_lt(ds, kx_ref[here, :, :hd].reshape(2 * TILE, hd))
            return carry

        lax.fori_loop(lax.div(jnp.maximum(i - cfg["window"], 0), 2), lax.div(i, 2) + 1, k_tile, 0)

    def head_back(i, h, dy, gain):
        cos, sin = halves(cs[i], hd)
        dy = dy * cos - pltpu.roll(dy, hd // 2, 1) * sin
        g_part, dpre = norm_back(pre[i, :, h * hd : (h + 1) * hd].astype(F32), gain, dy, eps)
        dqkv[i, :, h * hd : (h + 1) * hd] = dpre.astype(BF)
        return g_part

    gq = jnp.zeros((1, hd), F32)
    mo_base = net.slots(2 * n)

    def mo_chip(m, s):
        to = NEXT[s] if m == ACROSS else m
        return net.copy(mo_send.at[m + s - 2], mo_recv.at[m + s - 2], mo_base + m + s, net.peer(to))

    def send_mo(m, s):
        own[m, s].wait()
        sib[m, s].wait_recv()
        both = mo_own[m + s].astype(F32) + mo_in[m + s].astype(F32)
        if m == NEXT[1 - s]:
            mo_chip(ACROSS, s).wait_recv()
            both = both + mo_recv[ACROSS - 2 + s].astype(F32)
        mo_send[m + s - 2] = both.astype(BF)
        mo_chip(m, s).start()

    for k, (mask, s) in enumerate(ARRIVE_ORDER):
        arrive_for(gath, mask, s)
        i = net.tile(mask, s)
        attend_back(i)
        if k == 0:
            for cp in more[:2]:
                cp.wait()
        for h in range(ql):
            gq = gq + head_back(i, h, dq[h * TILE : (h + 1) * TILE] * scale, g_q)
        if k == 2:
            line_d.relay()
        if k == 4:
            for half_s in range(2):
                for m in (ACROSS, NEXT[half_s]):
                    send_mo(m, half_s)
        if k == 5:
            line_u.relay()
        if k == 6:
            for half_s in range(2):
                send_mo(NEXT[1 - half_s], half_s)
    gwo[...] = dot_lt(attn_ref[...].reshape(rows, qw), dresg[...].reshape(rows, dm)).astype(BF).reshape(gwo.shape)
    line_o = LineSum(net, lambda f: gwo.at[f], gwo_in, gwo_in.at[nz - 1], gwo_in.at[nz])

    def keys_back(i, carry):
        g_part = head_back(i, ql, dk[i] * scale, g_k)
        dqkv[i, :, qw + kw :] = dv[i].astype(BF)
        return carry + g_part

    gk = lax.fori_loop(0, tiles, keys_back, jnp.zeros((1, hd), F32))
    for cp in more[2:]:
        cp.wait()
    per = dm // n
    cols = 2
    part_w = dm // cols
    d_all = dqkv[...].reshape(rows, -1)
    for j in range(cols):
        grad = dot_lt(xn[:, :, j * part_w : (j + 1) * part_w].reshape(rows, part_w), d_all)
        gbuf[j * (n // cols) : (j + 1) * (n // cols)] = grad.astype(BF).reshape(n // cols, nz, per // nz, -1)
    line_q = LineSum(net, lambda f: gbuf.at[:, f], g_line, g_line.at[nz - 1], g_line.at[nz])
    wqkv = w[...].reshape(dm, -1)
    sum1 = PlaneSum(net, sib_out, sib_in, out, inn, mine, keep, True)
    for k, (mask, s) in enumerate(SEND_ORDER):
        sum1.give(mask, s, dot_rt(dqkv[net.tile(mask, s)], wqkv))
        if k == 3:
            line_o.relay()
    sum1.flush()

    def write(ref):
        def store(value):
            ref[...] = value.astype(ref.dtype)

        return store

    line_d.total(write(gwd_out))
    line_u.total(write(ggu_sum))
    line_q.relay()
    plane_u = net.to_plane(lambda m: ggu_sum.at[net.at(m)], ggu_in.at[c])
    ggu_in[c] = ggu_sum[c]
    end = 0
    for s in range(lengths_ref.shape[1]):
        end = end + lengths_ref[0, s]
    for s in range(2):
        own[0, s].wait()
        sib[0, s].wait_recv()
        total = hmid[s] + mo_own[s].astype(F32) + mo_in[s].astype(F32)
        for m in NEXT:
            mo_chip(m, s).wait_recv()
            total = total + mo_recv[m - 2 + s].astype(F32)
        at = lax.rem(net.core + s, 2) * half + net.tile(0, s) * TILE
        padding = at + lax.broadcasted_iota(jnp.int32, (half, 1), 0) >= end
        block_out[s * half : (s + 1) * half, :] = jnp.where(padding, 0.0, total).astype(BF)
    line_o.total(write(gwo_out))
    g_in_row = row_of(gains, 0, dm // LANES)
    grad_in = 0.0
    for s in range(2):
        here = slice(s * half, (s + 1) * half)
        g_part, d_x = norm_back(x_ref[here, :].astype(F32), g_in_row, sum1.total(s), eps)
        grad_in = grad_in + g_part
        dx_out[here, :] = dhmid[s] + d_x
    part[...] = jnp.zeros_like(part)
    for j in range(dm // LANES):
        part[j : j + 1, :] = grad_in[:, j * LANES : (j + 1) * LANES]
        part[8 + j : 9 + j, :] = gpost_ref[:, j * LANES : (j + 1) * LANES]
    part[16:17, :] = gq
    part[17:18, :] = gk
    plane_g = net.to_plane(lambda m: part, gplane.at[c])
    gplane[c] = part[...]
    line_q.total(write(gsum))
    plane_q = net.to_plane(lambda m: gsum.at[net.at(m)], g_in.at[c])
    g_in[c] = gsum[c]
    for cp in plane_g:
        cp.wait_recv()
    gz[z] = jnp.sum(gplane[...], axis=0)
    line_g = net.to_line(lambda m: gz.at[z], lambda m: gz.at[z])
    for cp in plane_u:
        cp.wait_recv()
    ggu_out[...] = ggu_in[...]
    for cp in plane_q:
        cp.wait_recv()
    gqkv_out[...] = g_in[...]
    for cp in line_g:
        cp.wait_recv()
    gains_out[...] = jnp.sum(gz[...], axis=0)
    for part in (gath, sum1, line_d, line_u, line_o, line_q):
        part.finish()
    for cp in line_g + plane_u + plane_g + plane_q + list(sib.values()):
        cp.wait_send()
    for s in range(2):
        for m in CHIPS:
            mo_chip(m, s).wait_send()


def finish(cfg, block_ref, dx_ref, gwo_ref, gwd_ref, ggu_ref, gqkv_ref, gains_ref,
           block_out, dx_out, gin_out, gq_out, gk_out, gv_out, gqg_out, gkg_out, gwo_out, gpost_out, ggate_out, gup_out,
           gwd_out):
    n, nz, ql, kvl, hd, ff = cfg["n"], cfg["nz"], cfg["ql"], cfg["kvl"], cfg["hd"], cfg["ff"]
    block_out[...] = block_ref[...]
    dx_out[...] = dx_ref[...]
    gwo_out[...] = gwo_ref[...]
    gwd_out[...] = gwd_ref[...]
    qw, kw = ql * hd, kvl * hd
    for d in range(n):
        both = gqkv_ref[d].astype(F32)
        gq_out[:, d * qw : (d + 1) * qw] = both[:, :qw]
        gk_out[:, d * kw : (d + 1) * kw] = both[:, qw : qw + kw]
        gv_out[:, d * kw : (d + 1) * kw] = both[:, qw + kw :]
        both = ggu_ref[d].astype(F32)
        ggate_out[:, d * ff : (d + 1) * ff] = both[:, :ff]
        gup_out[:, d * ff : (d + 1) * ff] = both[:, ff:]
    place = lax.axis_index("ctx") * nz + lax.axis_index("fsdp")
    for first, ref in ((0, gin_out), (8, gpost_out), (16, gqg_out), (17, gkg_out)):
        width = ref.shape[1]
        at = place * width
        row = gains_ref[pl.ds(first + lax.div(at, LANES), 1), :]
        ref[...] = pltpu.roll(row, lax.rem(LANES - lax.rem(at, LANES), LANES), 1)[:, :width]


def call(body, cfg, ins, outs, scratch, cid, *args):
    remote = cid is not None
    params = dict(collective_id=cid, has_side_effects=True) if remote else {}
    if remote:
        sems = pltpu.SemaphoreType.DMA((cfg["slots"],))
        scratch = scratch + [pltpu.SemaphoreType.DMA((32,)), sems, sems]
    return pl.pallas_call(
        functools.partial(body, cfg),
        out_shape=[jax.ShapeDtypeStruct(shape, dtype) for shape, dtype, *_ in outs],
        in_specs=ins,
        out_specs=[o[2] if len(o) > 2 else VMEM for o in outs],
        scratch_shapes=scratch,
        compiler_params=pltpu.CompilerParams(vmem_limit_bytes=LIMIT, **params),
        name=body.__name__,
    )(*args)


def on_plane(hidden_in, seq_lengths, in_gain, w_query, w_key, w_value, q_gain, k_gain, w_out, post_gain,
             w_gate, w_up, w_down, d_out):
    n, nz = lax.axis_size("ctx"), lax.axis_size("fsdp")
    t, dm = hidden_in.shape[1:]
    rows = n * t
    hd = q_gain.shape[0] * n * nz
    ql = w_query.shape[1] // hd // n
    kvl = w_key.shape[1] // hd // n
    ff = w_gate.shape[1] // n
    r_in, r_out, r_down = w_query.shape[0], w_out.shape[0], w_down.shape[0]
    qkv = (ql + 2 * kvl) * hd
    tiles, half = rows // TILE, TILE // 2
    cfg = dict(n=n, nz=nz, ql=ql, kvl=kvl, hd=hd, ff=ff, eps=1e-6, window=rows // 2 // TILE, slots=14 * n + 8 * nz)

    inv = 1000000.0 ** (-np.arange(hd // 2) * (2.0 / hd))
    angles = np.concatenate([np.arange(half), np.arange(2 * tiles) * half])[:, None] * inv[None, :]
    table = jnp.asarray(np.concatenate([np.cos(angles), np.sin(angles)], axis=1), F32)
    x = hidden_in[0]
    smem = pl.BlockSpec(memory_space=pltpu.SMEM)
    anywhere = pl.BlockSpec(memory_space=pl.ANY)

    def hbm(shape, dtype):
        return (shape, dtype, anywhere)

    def vm(shape, dtype=BF):
        return pltpu.VMEM(shape, dtype)

    big, low, wide, pair = (tiles, TILE, dm), (tiles, TILE, 2 * hd), (tiles, ql, TILE, 2 * hd), (2, half, dm)
    pre_w = (ql + kvl) * hd
    w_s, gu_s, wo_s, wd_s = (n, nz, r_in, qkv), (n, nz, r_in, 2 * ff), (nz, r_out, dm), (nz, r_down, dm)
    attn_s = (tiles, TILE, ql * hd)
    gains_s = (GAIN_ROWS, LANES)
    sums = [vm((n, half, dm)), vm((n, half, dm)), vm((n - 2, half, dm)), vm((n - 2, half, dm)), vm((2, TILE, dm), F32), vm(pair, F32)]
    (qx, kx, vx, attn, mo, pre, cs, xn, w, wo, gwd, ggu, h_mid, d_hmid, d_res, gains, gpost) = call(
        front, cfg, [smem] + [VMEM] * 14,
        [hbm(wide, BF), hbm(low, BF), hbm(low, BF), hbm(attn_s, BF), hbm(big, BF), hbm((tiles, TILE, pre_w), BF),
         hbm((tiles, TILE, hd), F32), hbm(big, BF), hbm(w_s, BF), hbm(wo_s, BF), hbm(wd_s, BF), hbm(gu_s, BF),
         hbm(pair, F32), hbm(pair, F32), hbm(pair, BF), (gains_s, F32), ((1, dm), F32)],
        [vm((n, r_in, qkv)), vm((n, r_in, 2 * ff)), vm(w_s), vm(wo_s), vm(gu_s), vm(wd_s),
         vm((8, LANES), F32), vm(gains_s, F32), vm((n,) + gains_s, F32), vm((nz,) + gains_s, F32),
         vm(big), vm(big), vm((tiles, TILE, pre_w)), vm((tiles, TILE, hd), F32), vm(wide), vm(low), vm(low),
         vm((ql * TILE, 2 * hd), F32), vm(attn_s),
         vm(big), vm((tiles, TILE, ff)), vm((tiles, TILE, 2 * ff)), vm((2, TILE, dm))]
        + sums + [vm(pair, F32), vm(pair, F32), vm(pair), vm(wd_s), vm(gu_s)],
        1, seq_lengths, x, d_out[0], w_query, w_key, w_value, w_out, w_gate, w_up, w_down, in_gain[None], post_gain[None], q_gain[None], k_gain[None], table)

    block, dx, gwo, grad_down, ggu, gqkv, small = call(
        back, cfg, [smem] + [VMEM] * 5 + [anywhere] * 10 + [VMEM] * 3,
        [((t, dm), BF), ((t, dm), F32), ((r_out, dm), F32), ((r_down, dm), F32), ((n, r_in, 2 * ff), BF),
         ((n, r_in, qkv), BF), (gains_s, F32)],
        [vm((n, half, dm)), vm((n, half, dm)), vm((n - 2, half, dm)), vm((n - 2, half, dm)),
         vm((tiles, TILE, pre_w)), vm((tiles, TILE, hd), F32), vm(big), vm(w_s), vm(pair, F32), vm(pair, F32), vm(big),
         vm((ql * TILE, hd), F32), vm((tiles, TILE, hd), F32), vm((tiles, TILE, hd), F32), vm((ql * TILE, 2 * hd)),
         vm(wd_s), vm((nz + 1, r_down, dm)), vm(gu_s), vm((nz + 1, n, r_in, 2 * ff)),
         vm((n, r_in, 2 * ff)), vm((n, r_in, 2 * ff)), vm(wo_s), vm((nz + 1, r_out, dm)),
         vm((tiles, TILE, qkv)), vm(w_s), vm((nz + 1, n, r_in, qkv)), vm((n, r_in, qkv)), vm((n, r_in, qkv)),
         vm(gains_s, F32), vm((n,) + gains_s, F32), vm((nz,) + gains_s, F32)]
        + sums,
        2, seq_lengths, qx, kx, vx, attn, wo, mo, pre, cs, xn, w, gwd, ggu, h_mid, d_hmid, d_res, gains, gpost, x)

    grads = call(
        finish, cfg, [VMEM] * 7,
        [((t, dm), BF), ((t, dm), F32), ((1, in_gain.shape[0]), F32), ((r_in, n * ql * hd), F32),
         ((r_in, n * kvl * hd), F32), ((r_in, n * kvl * hd), F32), ((1, q_gain.shape[0]), F32),
         ((1, k_gain.shape[0]), F32), ((r_out, dm), F32), ((1, post_gain.shape[0]), F32), ((r_in, n * ff), F32),
         ((r_in, n * ff), F32), ((r_down, dm), F32)],
        [], None, block, dx, gwo, grad_down, ggu, gqkv, small)
    (block, dx, g_in, g_q, g_k, g_v, g_qg, g_kg, g_o, g_post, g_gate, g_up, g_down) = grads
    return (block[None], dx[None], g_in[0], g_q, g_k, g_v, g_qg[0], g_kg[0], g_o, g_post[0], g_gate, g_up, g_down)


epsilon = 1e-06
rope_base = 1000000.0
negative = -1e30


def row_info(lengths, row_ids, tok_dev, n_ctx):
    half_len = tok_dev // 2
    device = row_ids // tok_dev
    local_row = row_ids % tok_dev
    block_id = jnp.where(local_row < half_len, device, 2 * n_ctx - 1 - device)
    packed = block_id * half_len + local_row % half_len
    seq_ends = jnp.cumsum(lengths)
    seq_starts = seq_ends - lengths
    member = (packed[:, None] >= seq_starts[None, :]) & (packed[:, None] < seq_ends[None, :])
    row_valid = jnp.any(member, axis=1)
    numbers = jnp.arange(lengths.shape[0], dtype=jnp.int32)
    seq_id = jnp.sum(jnp.where(member, numbers[None, :], 0), axis=1)
    offset = jnp.sum(jnp.where(member, seq_starts[None, :], 0), axis=1)
    segment = jnp.where(row_valid, seq_id, -1 - packed)
    position = jnp.where(row_valid, packed - offset, 0)
    return (segment, position, row_valid)


def norm_gain(values_in, gain_vec):
    row_scale = lax.rsqrt(jnp.mean(values_in * values_in, axis=-1, keepdims=True) + epsilon)
    return values_in * row_scale * gain_vec


def rotary(position, head_dim):
    half_len = head_dim // 2
    inv_freq = jnp.power(rope_base, -jnp.arange(half_len, dtype=jnp.float32) * (2.0 / head_dim))
    angles = position.astype(jnp.float32)[:, None] * inv_freq[None, :]
    angles = jnp.concatenate([angles, angles], axis=1)
    return (jnp.cos(angles), jnp.sin(angles))


def rotate(heads, cos_table, sin_table):
    half_len = heads.shape[-1] // 2
    turned = jnp.concatenate([-heads[..., half_len:], heads[..., :half_len]], axis=-1)
    return heads * cos_table[:, None, :] + turned * sin_table[:, None, :]


def head_post(q_in, k_in, q_scale, k_scale, cos_table, sin_table):
    head_dim = q_scale.shape[0]
    row_count = q_in.shape[0]
    q_heads = norm_gain(q_in.reshape(row_count, -1, head_dim), q_scale)
    k_heads = norm_gain(k_in.reshape(row_count, -1, head_dim), k_scale)
    query_rotated = rotate(q_heads, cos_table, sin_table).reshape(row_count, -1)
    key_rotated = rotate(k_heads, cos_table, sin_table).reshape(row_count, -1)
    return (query_rotated, key_rotated)


def swiglu(gate_in, up_in):
    return jax.nn.silu(gate_in) * up_in


def matmul(left, right):
    return jnp.dot(left, right, preferred_element_type=jnp.float32)


def inner(left, right):
    return lax.dot_general(
        left, right, (((0,), (0,)), ((), ())), preferred_element_type=jnp.float32
    )


def backdot(left, right):
    return lax.dot_general(
        left, right, (((1,), (1,)), ((), ())), preferred_element_type=jnp.float32
    )


def pick_step(key_count):
    for candidate in (512, 384, 256):
        return candidate
    return key_count


def on_rows(
    hidden_in,
    seq_lengths,
    in_gain,
    w_query,
    w_key,
    w_value,
    q_gain,
    k_gain,
    w_out,
    post_gain,
    w_gate,
    w_up,
    w_down,
    d_out,
):
    n_ctx = lax.axis_size("ctx")
    row_count = hidden_in.shape[1]
    lengths = seq_lengths[0]
    own_rows = lax.axis_index("ctx") * row_count + jnp.arange(row_count, dtype=jnp.int32)
    seg_q, pos_q, row_valid = row_info(lengths, own_rows, row_count, n_ctx)
    shards = (
        in_gain,
        w_query,
        w_key,
        w_value,
        q_gain,
        k_gain,
        w_out,
        post_gain,
        w_gate,
        w_up,
        w_down,
    )
    gathered = (
        lax.all_gather(shards[0], ("ctx", "fsdp"), axis=0, tiled=True),
        lax.all_gather(shards[1], ("ctx", "fsdp"), axis=0, tiled=True),
        lax.all_gather(shards[2], ("ctx", "fsdp"), axis=0, tiled=True),
        lax.all_gather(shards[3], ("ctx", "fsdp"), axis=0, tiled=True),
        lax.all_gather(shards[4], ("ctx", "fsdp"), axis=0, tiled=True),
        lax.all_gather(shards[5], ("ctx", "fsdp"), axis=0, tiled=True),
        lax.all_gather(shards[6], ("ctx", "fsdp"), axis=0, tiled=True),
        lax.all_gather(shards[7], ("ctx", "fsdp"), axis=0, tiled=True),
        lax.all_gather(shards[8], ("ctx", "fsdp"), axis=0, tiled=True),
        lax.all_gather(shards[9], ("ctx", "fsdp"), axis=0, tiled=True),
        lax.all_gather(shards[10], ("ctx", "fsdp"), axis=0, tiled=True),
    )
    g_in = gathered[0].astype(jnp.float32)
    g_query = gathered[4].astype(jnp.float32)
    g_key = gathered[5].astype(jnp.float32)
    g_post = gathered[7].astype(jnp.float32)
    head_dim = gathered[4].shape[0]
    kv_width = gathered[2].shape[1]
    kv_heads = kv_width // head_dim
    group_count = gathered[1].shape[1] // kv_width
    score_scale = head_dim ** (-0.5)
    rows_per_group = row_count * n_ctx
    x_float = hidden_in[0].astype(jnp.float32)
    x_normf, in_back = jax.vjp(norm_gain, x_float, g_in)
    x_norm = x_normf.astype(jnp.bfloat16)
    q_pre = matmul(x_norm, gathered[1])
    k_pre = matmul(x_norm, gathered[2])
    value_projected = matmul(x_norm, gathered[3])
    cos_table, sin_table = rotary(pos_q, head_dim)

    def post_local(q_in, k_in, q_scale, k_scale):
        return head_post(q_in, k_in, q_scale, k_scale, cos_table, sin_table)

    rotated, post_back = jax.vjp(post_local, q_pre, k_pre, g_query, g_key)
    q_low4 = rotated[0].astype(jnp.bfloat16).reshape(row_count, kv_heads, group_count, head_dim)
    key_narrow = rotated[1].astype(jnp.bfloat16)
    value_narrow = value_projected.astype(jnp.bfloat16)

    def sweep_keys(carry, k_piece, v_piece, block_fn):
        key_count = k_piece.shape[0]
        key_step = pick_step(key_count)

        def one_turn(state, turn_index):
            offset = turn_index * key_step
            k_block = lax.dynamic_slice_in_dim(k_piece, offset, key_step, 0)
            v_block = lax.dynamic_slice_in_dim(v_piece, offset, key_step, 0)
            key_rows = offset + jnp.arange(key_step, dtype=jnp.int32)
            seg_k, pos_k, unused = row_info(lengths, key_rows, row_count, n_ctx)
            allowed = (seg_q[:, None] == seg_k[None, :]) & (pos_k[None, :] <= pos_q[:, None])
            state = block_fn(state, k_block, v_block, allowed, offset)
            return (state, None)

        carry, unused = lax.scan(
            one_turn, carry, jnp.arange(key_count // key_step, dtype=jnp.int32)
        )
        return carry

    def forward_block(carry, k_block, v_block, allowed, first_key):
        row_max, totals, weighted = carry
        k_heads = k_block.reshape(-1, kv_heads, head_dim)
        v_heads = v_block.reshape(-1, kv_heads, head_dim)
        mask_four = allowed[None, None]
        score = (
            jnp.einsum("qhgd,khd->hgqk", q_low4, k_heads, preferred_element_type=jnp.float32)
            * score_scale
        )
        block_max = jnp.max(jnp.where(mask_four, score, negative), axis=-1)
        new_max = jnp.maximum(row_max, block_max)
        expo = jnp.where(mask_four, jnp.exp(score - new_max[..., None]), 0.0)
        factor = jnp.exp(row_max - new_max)
        totals = totals * factor + jnp.sum(expo, axis=-1)
        weighted = weighted * factor[..., None] + jnp.einsum(
            "hgqk,khd->hgqd", expo.astype(jnp.bfloat16), v_heads, preferred_element_type=jnp.float32
        )
        return (new_max, totals, weighted)

    start_state = (
        jnp.full((kv_heads, group_count, row_count), negative, jnp.float32),
        jnp.zeros((kv_heads, group_count, row_count), jnp.float32),
        jnp.zeros((kv_heads, group_count, row_count, head_dim), jnp.float32),
    )
    pieces = (
        lax.all_gather(key_narrow, "ctx", axis=0, tiled=True),
        lax.all_gather(value_narrow, "ctx", axis=0, tiled=True),
    )
    fold_state = sweep_keys(start_state, pieces[0], pieces[1], forward_block)
    row_max, totals, weighted = fold_state
    attn_four = weighted / totals[..., None]
    log_total = row_max + jnp.log(totals)
    attn = jnp.transpose(attn_four, (2, 0, 1, 3)).reshape(row_count, -1)
    attn_low = attn.astype(jnp.bfloat16)
    h_mid = x_float + matmul(attn_low, gathered[6])
    h_normf, post_norm_back = jax.vjp(norm_gain, h_mid, g_post)
    h_norm = h_normf.astype(jnp.bfloat16)
    gate_out = matmul(h_norm, gathered[8])
    up_out = matmul(h_norm, gathered[9])
    act_float, swiglu_back = jax.vjp(swiglu, gate_out, up_out)
    act_low = act_float.astype(jnp.bfloat16)
    row_mask = row_valid.astype(jnp.float32)[:, None]
    block_out = (row_mask * (h_mid + matmul(act_low, gathered[10]))).astype(jnp.bfloat16)
    again = (
        lax.all_gather(shards[0], ("ctx", "fsdp"), axis=0, tiled=True),
        lax.all_gather(shards[1], ("ctx", "fsdp"), axis=0, tiled=True),
        lax.all_gather(shards[2], ("ctx", "fsdp"), axis=0, tiled=True),
        lax.all_gather(shards[3], ("ctx", "fsdp"), axis=0, tiled=True),
        lax.all_gather(shards[4], ("ctx", "fsdp"), axis=0, tiled=True),
        lax.all_gather(shards[5], ("ctx", "fsdp"), axis=0, tiled=True),
        lax.all_gather(shards[6], ("ctx", "fsdp"), axis=0, tiled=True),
        lax.all_gather(shards[7], ("ctx", "fsdp"), axis=0, tiled=True),
        lax.all_gather(shards[8], ("ctx", "fsdp"), axis=0, tiled=True),
        lax.all_gather(shards[9], ("ctx", "fsdp"), axis=0, tiled=True),
        lax.all_gather(shards[10], ("ctx", "fsdp"), axis=0, tiled=True),
    )
    d_block = d_out[0].astype(jnp.float32) * row_mask
    dm_low = d_block.astype(jnp.bfloat16)
    grad_down = inner(act_low, dm_low)
    d_act = backdot(dm_low, again[10])
    d_gate, d_up = swiglu_back(d_act)
    dg_low = d_gate.astype(jnp.bfloat16)
    du_low = d_up.astype(jnp.bfloat16)
    grad_gate = inner(h_norm, dg_low)
    grad_up = inner(h_norm, du_low)
    d_hnorm = backdot(dg_low, again[8]) + backdot(du_low, again[9])
    d_hpart, grad_post = post_norm_back(d_hnorm)
    d_hmid = d_block + d_hpart
    d_res = d_hmid.astype(jnp.bfloat16)
    grad_wout = inner(attn_low, d_res)
    d_attn = backdot(d_res, again[6]).astype(jnp.bfloat16)
    d_attn4 = d_attn.reshape(row_count, kv_heads, group_count, head_dim)
    delta = jnp.einsum("qhgd,hgqd->hgq", d_attn4.astype(jnp.float32), attn_four)

    def backward_block(carry, k_block, v_block, allowed, first_key):
        d_query, d_kv = carry
        key_count = k_block.shape[0]
        k_heads = k_block.reshape(-1, kv_heads, head_dim)
        v_heads = v_block.reshape(-1, kv_heads, head_dim)
        mask_four = allowed[None, None]
        score = (
            jnp.einsum("qhgd,khd->hgqk", q_low4, k_heads, preferred_element_type=jnp.float32)
            * score_scale
        )
        prob = jnp.where(mask_four, jnp.exp(score - log_total[..., None]), 0.0)
        prob_low = prob.astype(jnp.bfloat16)
        d_prob = jnp.einsum("qhgd,khd->hgqk", d_attn4, v_heads, preferred_element_type=jnp.float32)
        d_score = (prob * (d_prob - delta[..., None])).astype(jnp.bfloat16)
        d_query = d_query + jnp.einsum(
            "hgqk,khd->qhgd", d_score, k_heads, preferred_element_type=jnp.float32
        )
        d_key = (
            jnp.einsum("hgqk,qhgd->khd", d_score, q_low4, preferred_element_type=jnp.float32)
            * score_scale
        )
        d_value = jnp.einsum(
            "hgqk,qhgd->khd", prob_low, d_attn4, preferred_element_type=jnp.float32
        )
        joined = jnp.concatenate(
            [d_key.reshape(key_count, -1), d_value.reshape(key_count, -1)], axis=1
        )
        before = lax.dynamic_slice_in_dim(d_kv, first_key, key_count, 0)
        d_kv = lax.dynamic_update_slice_in_dim(d_kv, before + joined, first_key, 0)
        return (d_query, d_kv)

    back_start = (
        jnp.zeros((row_count, kv_heads, group_count, head_dim), jnp.float32),
        jnp.zeros((rows_per_group, 2 * kv_width), jnp.float32),
    )
    pieces = (
        lax.all_gather(key_narrow, "ctx", axis=0, tiled=True),
        lax.all_gather(value_narrow, "ctx", axis=0, tiled=True),
    )
    back_state = sweep_keys(back_start, pieces[0], pieces[1], backward_block)
    d_qrot = back_state[0].reshape(row_count, -1) * score_scale
    d_kv_own = lax.psum_scatter(
        back_state[1].astype(jnp.bfloat16), "ctx", scatter_dimension=0, tiled=True
    ).astype(jnp.float32)
    d_krot = d_kv_own[:, :kv_width]
    d_vpre = d_kv_own[:, kv_width:]
    d_qpre, d_kpre, grad_qgain, grad_kgain = post_back((d_qrot, d_krot))
    dq_low = d_qpre.astype(jnp.bfloat16)
    dk_low = d_kpre.astype(jnp.bfloat16)
    dv_low = d_vpre.astype(jnp.bfloat16)
    grad_query = inner(x_norm, dq_low)
    grad_key = inner(x_norm, dk_low)
    grad_value = inner(x_norm, dv_low)
    d_xnorm = backdot(dq_low, again[1]) + backdot(dk_low, again[2]) + backdot(dv_low, again[3])
    d_xpart, grad_ingain = in_back(d_xnorm)
    d_hidden = d_hmid + d_xpart
    owned = (
        lax.psum_scatter(grad_ingain, ("ctx", "fsdp"), scatter_dimension=0, tiled=True),
        lax.psum_scatter(grad_query, ("ctx", "fsdp"), scatter_dimension=0, tiled=True),
        lax.psum_scatter(grad_key, ("ctx", "fsdp"), scatter_dimension=0, tiled=True),
        lax.psum_scatter(grad_value, ("ctx", "fsdp"), scatter_dimension=0, tiled=True),
        lax.psum_scatter(grad_qgain, ("ctx", "fsdp"), scatter_dimension=0, tiled=True),
        lax.psum_scatter(grad_kgain, ("ctx", "fsdp"), scatter_dimension=0, tiled=True),
        lax.psum_scatter(grad_wout, ("ctx", "fsdp"), scatter_dimension=0, tiled=True),
        lax.psum_scatter(grad_post, ("ctx", "fsdp"), scatter_dimension=0, tiled=True),
        lax.psum_scatter(grad_gate, ("ctx", "fsdp"), scatter_dimension=0, tiled=True),
        lax.psum_scatter(grad_up, ("ctx", "fsdp"), scatter_dimension=0, tiled=True),
        lax.psum_scatter(grad_down, ("ctx", "fsdp"), scatter_dimension=0, tiled=True),
    )
    return (
        block_out[None],
        d_hidden[None],
        owned[0],
        owned[1],
        owned[2],
        owned[3],
        owned[4],
        owned[5],
        owned[6],
        owned[7],
        owned[8],
        owned[9],
        owned[10],
    )


def on_device(*args):
    n = lax.axis_size("ctx")
    hidden_in, w_key, w_out, w_gate, q_gain = args[0], args[4], args[8], args[10], args[6]
    hd = q_gain.shape[0] * n * lax.axis_size("fsdp")
    heads, ff = w_key.shape[1] // hd, w_gate.shape[1] // n
    even = heads % n == 0 and ff % LANES == 0 and w_key.shape[0] % 16 == 0 and w_out.shape[0] % 16 == 0
    if even and heads == n == 8 and hidden_in.shape[1] == TILE:
        return on_plane(*args)
    return on_rows(*args)


def solution(mesh):
    in_specs = (
        P("fsdp", "ctx", None),
        P("fsdp", None),
        P(("ctx", "fsdp")),
        P(("ctx", "fsdp"), None),
        P(("ctx", "fsdp"), None),
        P(("ctx", "fsdp"), None),
        P(("ctx", "fsdp")),
        P(("ctx", "fsdp")),
        P(("ctx", "fsdp"), None),
        P(("ctx", "fsdp")),
        P(("ctx", "fsdp"), None),
        P(("ctx", "fsdp"), None),
        P(("ctx", "fsdp"), None),
        P("fsdp", "ctx", None),
    )
    out_specs = (
        P("fsdp", "ctx", None),
        P("fsdp", "ctx", None),
        P(("ctx", "fsdp")),
        P(("ctx", "fsdp"), None),
        P(("ctx", "fsdp"), None),
        P(("ctx", "fsdp"), None),
        P(("ctx", "fsdp")),
        P(("ctx", "fsdp")),
        P(("ctx", "fsdp"), None),
        P(("ctx", "fsdp")),
        P(("ctx", "fsdp"), None),
        P(("ctx", "fsdp"), None),
        P(("ctx", "fsdp"), None),
    )
    return jax.shard_map(
        on_device, mesh=mesh, in_specs=in_specs, out_specs=out_specs, check_vma=False
    )
```

```python
import functools
import math

import jax
import jax.numpy as jnp
import numpy as np
from jax import lax
from jax.experimental import pallas as pl
from jax.experimental.pallas import tpu as pltpu
from jax.sharding import PartitionSpec as P

BF = jnp.bfloat16
F32 = jnp.float32
MESH = pl.DeviceIdType.MESH
VMEM = pl.BlockSpec(memory_space=pltpu.VMEM)
GAIN_ROWS = 24
LANES = 128
TILE = 256
LIMIT = 63 * 2**20
CORE, ALONG_X, ALONG_Y, ACROSS = 1, 2, 4, 6
CHIPS = (ALONG_X, ALONG_Y, ACROSS)
NEXT = (ALONG_X, ALONG_Y)


def dot(a, b):
    return jnp.dot(a, b, preferred_element_type=F32)


def dot_rt(a, b):
    return lax.dot_general(a, b, (((1,), (1,)), ((), ())), preferred_element_type=F32)


def dot_lt(a, b):
    return lax.dot_general(a, b, (((0,), (0,)), ((), ())), preferred_element_type=F32)


def flip(place, mask, size):
    out, bit = 0, 1
    while bit < size:
        out = out + bit * lax.rem(lax.div(place, bit) + (mask // bit) % 2, 2)
        bit *= 2
    return out


class Net:
    def __init__(self, n, nz, tiles, send, recv):
        self.n, self.nz, self.tiles, self.send, self.recv = n, nz, tiles, send, recv
        self.c = lax.axis_index("ctx")
        self.z = lax.axis_index("fsdp")
        self.core = lax.rem(self.c, 2)
        self.slot = 0

    def slots(self, count):
        first = self.slot
        self.slot += count
        return first

    def at(self, mask):
        return flip(self.c, mask, self.n)

    def zat(self, mask):
        return flip(self.z, mask, self.nz)

    def peer(self, mask):
        return (self.at(mask), self.z)

    def zpeer(self, mask):
        return (self.c, self.zat(mask))

    def tile(self, mask, s):
        chip = lax.div(self.at(mask), 2)
        return chip if s == 0 else self.tiles - 1 - chip

    def view(self, buf, mask, s):
        half = TILE // 2
        core = lax.rem(self.at(mask), 2)
        first = core if s == 0 else 1 - core
        return buf.at[self.tile(mask, s), pl.ds(pl.multiple_of(first * half, half), half), :]

    def barrier(self):
        bar = pltpu.get_barrier_semaphore()
        for mask in range(1, self.n):
            pl.semaphore_signal(bar, inc=1, device_id=self.peer(mask), device_id_type=MESH)
        for mask in range(1, self.nz):
            pl.semaphore_signal(bar, inc=1, device_id=self.zpeer(mask), device_id_type=MESH)
        pl.semaphore_wait(bar, self.n + self.nz - 2)

    def copy(self, src, dst, slot, device, send_slot=None):
        return pltpu.make_async_remote_copy(
            src_ref=src,
            dst_ref=dst,
            send_sem=self.send.at[slot if send_slot is None else send_slot],
            recv_sem=self.recv.at[slot],
            device_id=device,
            device_id_type=MESH,
        )

    def to_plane(self, src, dst):
        base = self.slots(self.n)
        out = []
        for mask in range(1, self.n):
            cp = self.copy(src(mask), dst, base + mask, self.peer(mask))
            cp.start()
            out.append(cp)
        return out

    def to_line(self, src, dst):
        base = self.slots(self.nz)
        out = []
        for mask in range(1, self.nz):
            cp = self.copy(src(mask), dst(mask), base + mask, self.zpeer(mask))
            cp.start()
            out.append(cp)
        return out


class Line:
    def __init__(self, net, view):
        self.net, self.view = net, view
        self.base = net.slots(net.nz)
        self.middle = (net.z == 1) | (net.z == 2)
        self.relayed = net.nz == 4
        own = view(net.z)
        self.direct = [m for m in range(1, net.nz) if not (self.relayed and m == 3)]
        self.copies = {m: net.copy(own, own, self.base + m, net.zpeer(m)) for m in range(1, net.nz)}
        for m in self.direct[::-1]:
            self.copies[m].start()
        if self.relayed:
            far = view(net.zat(2))
            self.passed = net.copy(far, far, self.base + 3, net.zpeer(1), send_slot=self.base)

    def relay(self):
        if self.relayed:
            self.copies[2].wait_recv()

            @pl.when(self.middle)
            def _():
                self.passed.start()
                self.copies[3].start()

    def arrive(self):
        for m, cp in self.copies.items():
            if not (self.relayed and m == 2):
                cp.wait_recv()

    def finish(self):
        for m in self.direct:
            self.copies[m].wait_send()
        if self.relayed:

            @pl.when(self.middle)
            def _():
                self.copies[3].wait_send()
                self.passed.wait_send()


class LineSum:
    def __init__(self, net, piece, inn, passing, both):
        self.net, self.piece, self.inn, self.passing, self.both = net, piece, inn, passing, both
        self.base = net.slots(net.nz)
        self.middle = (net.z == 1) | (net.z == 2)
        self.relayed = net.nz == 4
        if not self.relayed:
            for m in range(1, net.nz):
                self.to(m).start()
            return

        @pl.when(jnp.logical_not(self.middle))
        def _():
            self.far().start()
            self.to(2).start()
            self.to(1).start()

        @pl.when(self.middle)
        def _():
            self.to(3).start()
            self.to(1).start()

    def to(self, m):
        return self.net.copy(self.piece(self.net.zat(m)), self.inn.at[m - 1], self.base + m, self.net.zpeer(m))

    def far(self):
        return self.net.copy(
            self.piece(self.net.zat(3)), self.passing, self.base, self.net.zpeer(1), send_slot=self.base + 3
        )

    def joined(self):
        return self.net.copy(self.both, self.inn.at[1], self.base + 2, self.net.zpeer(2))

    def relay(self):
        if self.relayed:

            @pl.when(self.middle)
            def _():
                self.far().wait_recv()
                own = self.piece(self.net.zat(2))[...].astype(F32)
                self.both[...] = (own + self.passing[...].astype(F32)).astype(BF)
                self.joined().start()

    def total(self, write):
        def some(masks):
            value = self.piece(self.net.z)[...].astype(F32)
            for m in masks:
                self.to(m).wait_recv()
                value = value + self.inn[m - 1].astype(F32)
            write(value)

        if not self.relayed:
            some(range(1, self.net.nz))
            return

        @pl.when(self.middle)
        def _():
            some((1, 2, 3))

        @pl.when(jnp.logical_not(self.middle))
        def _():
            some((1, 2))

    def finish(self):
        if not self.relayed:
            for m in range(1, self.net.nz):
                self.to(m).wait_send()
            return
        self.to(1).wait_send()
        self.to(2).wait_send()
        self.to(3).wait_send()


class Gather:
    def __init__(self, net, buf):
        self.net, self.buf = net, buf
        self.base = net.slots(2 * net.n)
        self.sent = []

    def send(self, mask, s, to, arrives_as):
        view = self.net.view(self.buf, mask, s)
        slot = self.base + 2 * arrives_as + s
        cp = self.net.copy(view, view, slot, self.net.peer(to))
        cp.start()
        self.sent.append(cp)

    def start(self, s):
        for mask in (CORE, ALONG_X, ALONG_Y):
            self.send(0, s, mask, mask)

    def arrive(self, mask, s):
        view = self.net.view(self.buf, mask, s)
        self.net.copy(view, view, self.base + 2 * mask + s, self.net.peer(mask)).wait_recv()
        if mask % 2 == 0:
            if mask == (ALONG_X, ALONG_Y)[s]:
                self.send(mask, s, (ALONG_Y, ALONG_X)[s], ACROSS)
            self.send(mask, s, CORE, mask + 1)

    def finish(self):
        for cp in self.sent:
            cp.wait_send()


class PlaneSum:
    def __init__(self, net, sib_out, sib_in, out, inn, mine, keep, joined):
        self.net, self.joined = net, joined
        self.sib_out, self.sib_in, self.out, self.inn, self.mine, self.keep = sib_out, sib_in, out, inn, mine, keep
        self.base = net.slots(2 * net.n)
        self.sent, self.queue, self.given = [], [], 0

    def sibling(self, mask, s):
        return self.net.copy(
            self.sib_out.at[mask + s], self.sib_in.at[mask + s], self.base + 2 * (mask + 1) + s, self.net.peer(CORE)
        )

    def chip(self, mask, s):
        i = mask - 2 + s
        to = NEXT[s] if mask == ACROSS and self.joined else mask
        return self.net.copy(self.out.at[i], self.inn.at[i], self.base + 2 * mask + s, self.net.peer(to))

    def give(self, mask, s, value):
        half = TILE // 2
        place = self.given % 2
        self.given += 1
        self.mine[place] = value
        mine = lax.rem(self.net.core + s, 2) * half
        own = pl.ds(pl.multiple_of(mine, half), half)
        other = pl.ds(pl.multiple_of(half - mine, half), half)
        self.sib_out[mask + s] = self.mine[place, other, :].astype(BF)
        cp = self.sibling(mask, s)
        cp.start()
        self.sent.append(cp)
        self.queue.append((mask, s, place, own))
        if len(self.queue) > 1:
            self.combine()

    def combine(self):
        mask, s, place, own = self.queue.pop(0)
        self.sibling(mask, s).wait_recv()
        both = self.mine[place, own, :] + self.sib_in[mask + s].astype(F32)
        if mask == 0:
            self.keep[s] = both
            return
        if self.joined and mask == NEXT[1 - s]:
            self.chip(ACROSS, s).wait_recv()
            both = both + self.inn[ACROSS - 2 + s].astype(F32)
        self.out[mask - 2 + s] = both.astype(BF)
        cp = self.chip(mask, s)
        cp.start()
        self.sent.append(cp)

    def flush(self):
        while self.queue:
            self.combine()

    def total(self, s):
        value = self.keep[s]
        for mask in NEXT if self.joined else CHIPS:
            self.chip(mask, s).wait_recv()
            value = value + self.inn[mask - 2 + s].astype(F32)
        return value

    def finish(self):
        for cp in self.sent:
            cp.wait_send()


SEND_ORDER = ((ACROSS, 0), (ACROSS, 1), (ALONG_X, 0), (ALONG_Y, 1), (ALONG_Y, 0), (ALONG_X, 1), (0, 0), (0, 1))
ARRIVE_ORDER = ((0, 0), (0, 1), (ALONG_X, 0), (ALONG_Y, 0), (ALONG_X, 1), (ALONG_Y, 1), (ACROSS, 0), (ACROSS, 1))


def arrive_for(gath, mask, s):
    if mask == ALONG_X:
        gath.arrive(ALONG_X, s)
        gath.arrive(ALONG_Y, s)
    elif mask == ACROSS:
        gath.arrive(ACROSS, s)
    gath.arrive(mask + 1, s)


def row_of(g, first, count):
    return jnp.concatenate([g[first + j : first + j + 1, :] for j in range(count)], axis=1)


def split_three(value, lane):
    first = value.astype(BF).astype(F32)
    rest = value - first
    second = rest.astype(BF).astype(F32)
    third = rest - second
    out = jnp.where(lane == 0, first, jnp.where(lane == 1, second, jnp.where(lane == 2, third, 0.0)))
    return out.astype(BF)


def first_keys(lengths_ref, at):
    start = jnp.zeros_like(at)
    begin = 0
    for s in range(lengths_ref.shape[1]):
        start = jnp.where(at >= begin, begin, start)
        begin = begin + lengths_ref[0, s]
    padding = at >= begin
    return jnp.where(padding, at, start), padding


def halves(a, hd):
    lane = lax.broadcasted_iota(jnp.int32, a.shape, 1)
    other = pltpu.roll(a, hd // 2, 1)
    return jnp.where(lane < hd // 2, a, other), jnp.where(lane < hd // 2, -other, a)


def angle_sum(a, b, hd):
    lane = lax.broadcasted_iota(jnp.int32, jnp.broadcast_shapes(a.shape, b.shape), 1)
    a2, b2 = pltpu.roll(a, hd // 2, 1), pltpu.roll(b, hd // 2, 1)
    return jnp.where(lane < hd // 2, a * b - a2 * b2, a * b2 + a2 * b)


def minus_angle(a, hd):
    lane = lax.broadcasted_iota(jnp.int32, a.shape, 1)
    return jnp.where(lane < hd // 2, a, -a)


def norm_back(v, gain, dy, eps):
    r = lax.rsqrt(jnp.mean(v * v, axis=-1, keepdims=True) + eps)
    gdy = gain * dy
    dv = r * gdy - v * (r * r * r) * jnp.mean(gdy * v, axis=-1, keepdims=True)
    return jnp.sum(dy * v * r, axis=0, keepdims=True), dv


def front(cfg, lengths_ref, x_ref, do_ref, wq_ref, wk_ref, wv_ref, wo_ref, wg_ref, wu_ref, wd_ref, gi_ref, gp_ref, gq_ref, gk_ref, table_ref,
          qx_out, kx_out, vx_out, attn_out, mo_out, pre_out, cs_out, xn_out, w_out, wo_out, gwd_out, ggu_out,
          hmid_out, dhmid_out, dres_out, gains_out, gpost_out,
          wsend, gsend, w, wo_all, gu, wd_all, grow, gpart, gbuf, gz, xg, xn, pre, cs, qx, kx, vx, acc, attn,
          dblk, act, dgu, mo, sib_out, sib_in, out, inn, mine, keep, hmid, dhmid, dres, gwd_buf, ggu_buf,
          local, send, recv):
    n, nz, ql, kvl, hd, ff = cfg["n"], cfg["nz"], cfg["ql"], cfg["kvl"], cfg["hd"], cfg["ff"]
    eps = cfg["eps"]
    t, dm = x_ref.shape
    half = TILE // 2
    tiles = qx.shape[0]
    rows = n * t
    net = Net(n, nz, tiles, send, recv)
    c, z = net.c, net.z
    stores = []

    def store(src, dst):
        cp = pltpu.make_async_copy(src, dst, local.at[len(stores)])
        cp.start()
        stores.append(cp)
        return cp

    qw, kw = ql * hd, kvl * hd
    for j in range(n):
        wsend[j, :, :qw] = wq_ref[:, j * qw : (j + 1) * qw]
        wsend[j, :, qw : qw + kw] = wk_ref[:, j * kw : (j + 1) * kw]
        wsend[j, :, qw + kw :] = wv_ref[:, j * kw : (j + 1) * kw]
        gsend[j, :, :ff] = wg_ref[:, j * ff : (j + 1) * ff]
        gsend[j, :, ff:] = wu_ref[:, j * ff : (j + 1) * ff]
    grow[...] = jnp.zeros_like(grow)
    put = 0
    for ref in (gi_ref, gp_ref, gq_ref, gk_ref):
        grow[0:1, put : put + ref.shape[1]] = ref[...].astype(F32)
        put += ref.shape[1]
    row = jnp.broadcast_to(grow[0:1, :], (8, LANES))
    lane8 = lax.broadcasted_iota(jnp.int32, (8, LANES), 1)
    at = lax.broadcasted_iota(jnp.int32, (8, LANES), 0) * LANES + lane8
    wide, narrow = dm // (n * nz), hd // (n * nz)
    place = c * nz + z

    def placed(first, share, row0):
        shift = lax.rem(place * share, LANES)
        moved = pltpu.roll(row, lax.rem(shift + LANES - first, LANES), 1)
        return jnp.where((at >= row0 + place * share) & (at < row0 + (place + 1) * share), moved, 0.0)

    gpart[0:8, :] = placed(0, wide, 0)
    gpart[8:16, :] = placed(wide, wide, 0)
    gpart[16:24, :] = placed(2 * wide, narrow, 0) + placed(2 * wide + narrow, narrow, LANES)
    for s in range(2):
        net.view(xg, 0, s)[...] = x_ref[s * half : (s + 1) * half, :]
    w[c, z] = wsend[c]
    gu[c, z] = gsend[c]
    wo_all[z] = wo_ref[...]
    wd_all[z] = wd_ref[...]
    net.barrier()
    plane_g = net.to_plane(lambda m: gpart, gbuf.at[c])
    plane_w = net.to_plane(lambda m: wsend.at[net.at(m)], w.at[c, z])
    line_o = Line(net, lambda f: wo_all.at[f])
    gath = Gather(net, xg)
    gath.start(0)
    gath.start(1)
    gbuf[c] = gpart[...]
    for cp in plane_g:
        cp.wait_recv()
    gz[z] = jnp.sum(gbuf[...], axis=0)
    line_g = net.to_line(lambda m: gz.at[z], lambda m: gz.at[z])
    for cp in plane_w:
        cp.wait_recv()
    line_w = Line(net, lambda f: w.at[:, f])

    lo = table_ref[0:half, :]
    begins, firsts = [], []
    begin = 0
    for s in range(lengths_ref.shape[1]):
        begins.append(begin)
        hi_row = table_ref[pl.ds(half + lax.div(begin, half), 1), :]
        lo_row = table_ref[pl.ds(lax.rem(begin, half), 1), :]
        firsts.append(minus_angle(angle_sum(hi_row, lo_row, hd), hd))
        begin = begin + lengths_ref[0, s]
    end = begin
    one = jnp.where(lax.broadcasted_iota(jnp.int32, (1, hd), 1) < hd // 2, 1.0, 0.0)

    def positions(b, carry):
        at = b * half + lax.broadcasted_iota(jnp.int32, (half, hd), 0)
        hi_row = table_ref[pl.ds(half + b, 1), :]
        shift = angle_sum(hi_row, firsts[0], hd)
        for begin, first in zip(begins[1:], firsts[1:]):
            shift = jnp.where(at >= begin, angle_sum(hi_row, first, hd), shift)
        both = jnp.where(at >= end, one, angle_sum(shift, lo, hd))
        cs[lax.div(b, 2), pl.ds(pl.multiple_of(lax.rem(b, 2) * half, half), half), :] = both
        return carry

    lax.fori_loop(0, 2 * tiles, positions, 0)
    for cp in line_g:
        cp.wait_recv()
    gains = jnp.sum(gz[...], axis=0)
    g_in = row_of(gains, 0, dm // LANES)
    g_post = row_of(gains, 8, dm // LANES)
    g_q = gains[16:17, :]
    g_k = gains[17:18, :]
    step = 32

    def normalise(tile):
        def some(i, carry):
            here = pl.ds(pl.multiple_of(i * step, step), step)
            v = xg[tile, here, :].astype(F32)
            r = lax.rsqrt(jnp.mean(v * v, axis=-1, keepdims=True) + eps)
            xn[tile, here, :] = (v * r * g_in).astype(BF)
            return carry

        lax.fori_loop(0, TILE // step, some, 0, unroll=True)

    for mask, s in ARRIVE_ORDER:
        arrive_for(gath, mask, s)
        normalise(net.tile(mask, s))
        if mask == ALONG_Y and s == 1:
            plane_u = net.to_plane(lambda m: gsend.at[net.at(m)], gu.at[c, z])
            line_w.relay()
    line_o.relay()
    gath_d = Gather(net, dblk)
    for s in range(2):
        first = lax.rem(net.core + s, 2) * half + net.tile(0, s) * TILE
        padding = first + lax.broadcasted_iota(jnp.int32, (half, 1), 0) >= end
        net.view(dblk, 0, s)[...] = jnp.where(padding, 0.0, do_ref[s * half : (s + 1) * half, :].astype(F32)).astype(BF)
        gath_d.start(s)
    for cp in plane_u:
        cp.wait_recv()
    line_u = Line(net, lambda f: gu.at[:, f])
    line_w.arrive()
    wqkv = w[...].reshape(dm, -1)
    lane_b = lax.broadcasted_iota(jnp.int32, (TILE, hd), 1)
    minus = jnp.where(lane_b < 3, -1.0, 0.0).astype(BF)

    def heads(tile, carry):
        qkv = dot(xn[tile], wqkv)
        width = qw + kw
        pre[tile] = qkv[:, :width].astype(BF)
        cos, sin = halves(cs[tile], hd)
        for h in range(ql + kvl):
            v = qkv[:, h * hd : (h + 1) * hd]
            r = lax.rsqrt(jnp.mean(v * v, axis=-1, keepdims=True) + eps)
            hat = v * r * (g_q if h < ql else g_k)
            low = (hat * cos + pltpu.roll(hat, hd // 2, 1) * sin).astype(BF)
            if h < ql:
                qx[tile, h, :, :hd] = low
            else:
                kx[tile, :, :hd] = low
        vx[tile, :, :hd] = qkv[:, width:].astype(BF)
        kx[tile, :, hd:] = minus
        vx[tile, :, hd:] = minus
        return carry

    lax.fori_loop(0, tiles, heads, 0)
    hn = xn
    xn_stored = store(xn, xn_out)
    for src, dst in ((pre, pre_out), (cs, cs_out), (kx, kx_out), (vx, vx_out), (w, w_out)):
        store(src, dst)
    line_o.arrive()
    wout = wo_all[...].reshape(-1, dm)
    store(wo_all, wo_out)

    high = ql * TILE
    factor = math.log2(math.e) / math.sqrt(hd)
    lane_q = lax.broadcasted_iota(jnp.int32, (high, hd), 1)

    def attend(i):
        q = qx[i, :, :, :hd].reshape(high, hd)
        start = first_keys(lengths_ref, i * TILE + lax.broadcasted_iota(jnp.int32, (TILE, 1), 0))[0]
        q_at = i * TILE + lax.broadcasted_iota(jnp.int32, (TILE, 2 * TILE), 0)
        acc[...] = jnp.zeros_like(acc)

        def k_tile(j, carry):
            here = pl.ds(2 * j, 2)
            s = dot_rt(q, kx[here, :, :hd].reshape(2 * TILE, hd))
            k_at = j * (2 * TILE) + lax.broadcasted_iota(jnp.int32, (TILE, 2 * TILE), 1)
            allowed = (k_at <= q_at) & (k_at >= start)
            e = jnp.where(allowed[None], jnp.exp2(s * factor).reshape(ql, TILE, 2 * TILE), 0.0)
            acc[...] += dot(e.astype(BF).reshape(high, 2 * TILE), vx[here].reshape(2 * TILE, 2 * hd))
            return carry

        lax.fori_loop(lax.div(jnp.maximum(i - cfg["window"], 0), 2), lax.div(i, 2) + 1, k_tile, 0)
        total = -acc[:, hd : hd + 1]
        low = (acc[:, :hd] / total).astype(BF)
        for h in range(ql):
            attn[i, :, h * hd : (h + 1) * hd] = low[h * TILE : (h + 1) * TILE]
        extra = jnp.broadcast_to(jnp.log(total) * math.sqrt(hd), (high, hd))
        qx[i, :, :, hd:] = split_three(extra, lane_q).reshape(ql, TILE, hd)

    xn_stored.wait()
    gath.finish()
    sum1 = PlaneSum(net, sib_out, sib_in, out, inn, mine, keep, True)
    gath1 = Gather(net, hn)

    def middle(s):
        h_mid = x_ref[s * half : (s + 1) * half, :].astype(F32) + sum1.total(s)
        hmid[s] = h_mid
        r = lax.rsqrt(jnp.mean(h_mid * h_mid, axis=-1, keepdims=True) + eps)
        net.view(hn, 0, s)[...] = (h_mid * r * g_post).astype(BF)
        gath1.start(s)

    for k, (mask, s) in enumerate(SEND_ORDER):
        tile = net.tile(mask, s)
        attend(tile)
        sum1.give(mask, s, dot(attn[tile], wout))
        if k == 2:
            for half_s in range(2):
                gath_d.arrive(ALONG_X, half_s)
                gath_d.arrive(ALONG_Y, half_s)
        if k == 3:
            line_d = Line(net, lambda f: wd_all.at[f])
        if k == 6:
            line_u.relay()
    sum1.flush()
    store(qx, qx_out)
    store(attn, attn_out)
    for s in range(2):
        gath_d.arrive(ACROSS, s)
    middle(0)
    middle(1)
    line_d.relay()
    store(hmid, hmid_out)
    sum1.finish()
    for mask in (CORE, ALONG_X + 1, ALONG_Y + 1, ACROSS + 1):
        for s in range(2):
            gath_d.arrive(mask, s)
    line_u.arrive()
    wgu = gu[...].reshape(dm, -1)
    mo_stores = []

    def open_up(d):
        dgu[d] = dot(hn[d], wgu).astype(BF)

    def block(d):
        gate, up = dgu[d, :, :ff].astype(F32), dgu[d, :, ff:].astype(F32)
        sig = 1.0 / (1.0 + jnp.exp(-gate))
        silu = gate * sig
        low = (silu * up).astype(BF)
        act[d] = low
        if len(mo_stores) > 1:
            mo_stores[-2].wait()
        place = len(mo_stores) % 2
        mo[place] = dot(low, wd).astype(BF)
        mo_stores.append(store(mo.at[place], mo_out.at[d]))
        d_act = dot_rt(dblk[d], wd)
        dgu[d, :, :ff] = (d_act * up * sig * (1.0 + gate * (1.0 - sig))).astype(BF)
        dgu[d, :, ff:] = (d_act * silu).astype(BF)
        return dot_rt(dgu[d], wgu)

    for mask, s in ARRIVE_ORDER:
        arrive_for(gath1, mask, s)
        open_up(net.tile(mask, s))
    line_d.arrive()
    wd = wd_all[...].reshape(-1, dm)
    sum2 = PlaneSum(net, sib_out, sib_in, out, inn, mine, keep, True)
    for mask, s in SEND_ORDER:
        sum2.give(mask, s, block(net.tile(mask, s)))
    sum2.flush()
    dgu_all = dgu[...].reshape(rows, 2 * ff)
    gwd_buf[...] = dot_lt(act[...].reshape(rows, ff), dblk[...].reshape(rows, dm)).astype(BF).reshape(gwd_buf.shape)
    store(gwd_buf, gwd_out)
    per = dm // n
    cols = 2
    part_w = dm // cols
    for j in range(cols):
        part = dot_lt(hn[:, :, j * part_w : (j + 1) * part_w].reshape(rows, part_w), dgu_all)
        ggu_buf[j * (n // cols) : (j + 1) * (n // cols)] = part.astype(BF).reshape(n // cols, nz, per // nz, 2 * ff)
    store(ggu_buf, ggu_out)
    g_sum = 0.0
    for s in range(2):
        g_part, dv = norm_back(hmid[s], g_post, sum2.total(s), eps)
        g_sum = g_sum + g_part
        d_hmid = net.view(dblk, 0, s)[...].astype(F32) + dv
        dhmid[s] = d_hmid
        dres[s] = d_hmid.astype(BF)
    store(dhmid, dhmid_out)
    store(dres, dres_out)
    gains_out[...] = gains
    gpost_out[...] = g_sum
    for part in (gath_d, gath1, sum2, line_o, line_w, line_u, line_d):
        part.finish()
    for cp in plane_g + plane_w + plane_u + line_g:
        cp.wait_send()
    for cp in stores:
        if not any(cp is other for other in [xn_stored] + mo_stores[:-2]):
            cp.wait()


def back(cfg, lengths_ref, qx_ref, kx_ref, vx_ref, attn_ref, wo_ref, mo_ref, pre_ref, cs_ref, xn_ref, w_ref, gwd_ref,
         ggu_ref, hmid_ref, dhmid_ref, dres_ref, gains_ref, gpost_ref, x_ref,
         block_out, dx_out, gwo_out, gwd_out, ggu_out, gqkv_out, gains_out,
         mo_own, mo_in, mo_send, mo_recv, pre, cs, xn, w, hmid, dhmid, dresg, dq, dk, dv, dax, gwd, gwd_in, ggu,
         ggu_line, ggu_sum, ggu_in, gwo, gwo_in, dqkv, gbuf, g_line, gsum, g_in, part, gplane, gz,
         sib_out, sib_in, out, inn, mine, keep, local, send, recv):
    n, nz, ql, kvl, hd, ff = cfg["n"], cfg["nz"], cfg["ql"], cfg["kvl"], cfg["hd"], cfg["ff"]
    eps = cfg["eps"]
    t, dm = x_ref.shape
    half = TILE // 2
    rows = n * t
    tiles = qx_ref.shape[0]
    qw, kw = ql * hd, kvl * hd
    net = Net(n, nz, tiles, send, recv)
    c, z = net.c, net.z
    loads = []

    def load(src, dst):
        cp = pltpu.make_async_copy(src, dst, local.at[len(loads)])
        cp.start()
        loads.append(cp)
        return cp

    first = [load(dres_ref.at[s], net.view(dresg, 0, s)) for s in range(2)]
    own = {(m, s): load(net.view(mo_ref, m, s), mo_own.at[m + s]) for m in (0,) + CHIPS for s in range(2)}
    first += [load(gwd_ref, gwd), load(ggu_ref, ggu)]
    more = [load(a, b) for a, b in ((pre_ref, pre), (cs_ref, cs), (xn_ref, xn), (w_ref, w), (hmid_ref, hmid),
                                    (dhmid_ref, dhmid))]
    for cp in first:
        cp.wait()
    net.barrier()
    gath = Gather(net, dresg)
    gath.start(0)
    gath.start(1)
    line_d = LineSum(net, lambda f: gwd.at[f], gwd_in, gwd_in.at[nz - 1], gwd_in.at[nz])
    line_u = LineSum(net, lambda f: ggu.at[:, f], ggu_line, ggu_line.at[nz - 1], ggu_line.at[nz])
    base = net.slots(2 * n)
    sib = {}
    for m in CHIPS + (0,):
        for s in range(2):
            cp = net.copy(net.view(mo_ref, m + 1, s), mo_in.at[m + s], base + m + s, net.peer(CORE))
            cp.start()
            sib[m, s] = cp
    wout = wo_ref[...].reshape(-1, dm)
    gains = gains_ref[...]
    g_q = gains[16:17, :]
    g_k = gains[17:18, :]
    high = ql * TILE
    factor = math.log2(math.e) / math.sqrt(hd)
    scale = 1.0 / math.sqrt(hd)
    lane = lax.broadcasted_iota(jnp.int32, (TILE, hd), 1)
    dk[...] = jnp.zeros_like(dk)
    dv[...] = jnp.zeros_like(dv)

    def attend_back(i):
        d_attn = dot_rt(dresg[i], wout).astype(BF)
        prod = d_attn.astype(F32) * attn_ref[i].astype(F32)
        for h in range(ql):
            delta = jnp.sum(prod[:, h * hd : (h + 1) * hd], axis=-1, keepdims=True)
            dax[h * TILE : (h + 1) * TILE, :hd] = d_attn[:, h * hd : (h + 1) * hd]
            dax[h * TILE : (h + 1) * TILE, hd:] = split_three(jnp.broadcast_to(delta, (TILE, hd)), lane)
        qx = qx_ref[i].reshape(high, 2 * hd)
        start = first_keys(lengths_ref, i * TILE + lax.broadcasted_iota(jnp.int32, (1, TILE), 1))[0]
        q_at = i * TILE + lax.broadcasted_iota(jnp.int32, (2 * TILE, TILE), 1)
        dq[...] = jnp.zeros_like(dq)

        def k_tile(j, carry):
            here = pl.ds(2 * j, 2)
            k_at = j * (2 * TILE) + lax.broadcasted_iota(jnp.int32, (2 * TILE, TILE), 0)
            allowed = (k_at <= q_at) & (k_at >= start)
            allowed = jnp.concatenate([allowed] * ql, axis=1)
            s = dot_rt(kx_ref[here].reshape(2 * TILE, 2 * hd), qx)
            p = jnp.where(allowed, jnp.exp2(s * factor), 0.0)
            ds = (p * dot_rt(vx_ref[here].reshape(2 * TILE, 2 * hd), dax[...])).astype(BF)
            dv[here] += dot(p.astype(BF), dax[:, :hd]).reshape(2, TILE, hd)
            dk[here] += dot(ds, qx[:, :hd]).reshape(2, TILE, hd)
            dq[...] += dot_lt(ds, kx_ref[here, :, :hd].reshape(2 * TILE, hd))
            return carry

        lax.fori_loop(lax.div(jnp.maximum(i - cfg["window"], 0), 2), lax.div(i, 2) + 1, k_tile, 0)

    def head_back(i, h, dy, gain):
        cos, sin = halves(cs[i], hd)
        dy = dy * cos - pltpu.roll(dy, hd // 2, 1) * sin
        g_part, dpre = norm_back(pre[i, :, h * hd : (h + 1) * hd].astype(F32), gain, dy, eps)
        dqkv[i, :, h * hd : (h + 1) * hd] = dpre.astype(BF)
        return g_part

    gq = jnp.zeros((1, hd), F32)
    mo_base = net.slots(2 * n)

    def mo_chip(m, s):
        to = NEXT[s] if m == ACROSS else m
        return net.copy(mo_send.at[m + s - 2], mo_recv.at[m + s - 2], mo_base + m + s, net.peer(to))

    def send_mo(m, s):
        own[m, s].wait()
        sib[m, s].wait_recv()
        both = mo_own[m + s].astype(F32) + mo_in[m + s].astype(F32)
        if m == NEXT[1 - s]:
            mo_chip(ACROSS, s).wait_recv()
            both = both + mo_recv[ACROSS - 2 + s].astype(F32)
        mo_send[m + s - 2] = both.astype(BF)
        mo_chip(m, s).start()

    for k, (mask, s) in enumerate(ARRIVE_ORDER):
        arrive_for(gath, mask, s)
        i = net.tile(mask, s)
        attend_back(i)
        if k == 0:
            for cp in more[:2]:
                cp.wait()
        for h in range(ql):
            gq = gq + head_back(i, h, dq[h * TILE : (h + 1) * TILE] * scale, g_q)
        if k == 2:
            line_d.relay()
        if k == 4:
            for half_s in range(2):
                for m in (ACROSS, NEXT[half_s]):
                    send_mo(m, half_s)
        if k == 5:
            line_u.relay()
        if k == 6:
            for half_s in range(2):
                send_mo(NEXT[1 - half_s], half_s)
    gwo[...] = dot_lt(attn_ref[...].reshape(rows, qw), dresg[...].reshape(rows, dm)).astype(BF).reshape(gwo.shape)
    line_o = LineSum(net, lambda f: gwo.at[f], gwo_in, gwo_in.at[nz - 1], gwo_in.at[nz])

    def keys_back(i, carry):
        g_part = head_back(i, ql, dk[i] * scale, g_k)
        dqkv[i, :, qw + kw :] = dv[i].astype(BF)
        return carry + g_part

    gk = lax.fori_loop(0, tiles, keys_back, jnp.zeros((1, hd), F32))
    for cp in more[2:]:
        cp.wait()
    per = dm // n
    cols = 2
    part_w = dm // cols
    d_all = dqkv[...].reshape(rows, -1)
    for j in range(cols):
        grad = dot_lt(xn[:, :, j * part_w : (j + 1) * part_w].reshape(rows, part_w), d_all)
        gbuf[j * (n // cols) : (j + 1) * (n // cols)] = grad.astype(BF).reshape(n // cols, nz, per // nz, -1)
    line_q = LineSum(net, lambda f: gbuf.at[:, f], g_line, g_line.at[nz - 1], g_line.at[nz])
    wqkv = w[...].reshape(dm, -1)
    sum1 = PlaneSum(net, sib_out, sib_in, out, inn, mine, keep, True)
    for k, (mask, s) in enumerate(SEND_ORDER):
        sum1.give(mask, s, dot_rt(dqkv[net.tile(mask, s)], wqkv))
        if k == 3:
            line_o.relay()
    sum1.flush()

    def write(ref):
        def store(value):
            ref[...] = value.astype(ref.dtype)

        return store

    line_d.total(write(gwd_out))
    line_u.total(write(ggu_sum))
    line_q.relay()
    plane_u = net.to_plane(lambda m: ggu_sum.at[net.at(m)], ggu_in.at[c])
    ggu_in[c] = ggu_sum[c]
    end = 0
    for s in range(lengths_ref.shape[1]):
        end = end + lengths_ref[0, s]
    for s in range(2):
        own[0, s].wait()
        sib[0, s].wait_recv()
        total = hmid[s] + mo_own[s].astype(F32) + mo_in[s].astype(F32)
        for m in NEXT:
            mo_chip(m, s).wait_recv()
            total = total + mo_recv[m - 2 + s].astype(F32)
        at = lax.rem(net.core + s, 2) * half + net.tile(0, s) * TILE
        padding = at + lax.broadcasted_iota(jnp.int32, (half, 1), 0) >= end
        block_out[s * half : (s + 1) * half, :] = jnp.where(padding, 0.0, total).astype(BF)
    line_o.total(write(gwo_out))
    g_in_row = row_of(gains, 0, dm // LANES)
    grad_in = 0.0
    for s in range(2):
        here = slice(s * half, (s + 1) * half)
        g_part, d_x = norm_back(x_ref[here, :].astype(F32), g_in_row, sum1.total(s), eps)
        grad_in = grad_in + g_part
        dx_out[here, :] = dhmid[s] + d_x
    part[...] = jnp.zeros_like(part)
    for j in range(dm // LANES):
        part[j : j + 1, :] = grad_in[:, j * LANES : (j + 1) * LANES]
        part[8 + j : 9 + j, :] = gpost_ref[:, j * LANES : (j + 1) * LANES]
    part[16:17, :] = gq
    part[17:18, :] = gk
    plane_g = net.to_plane(lambda m: part, gplane.at[c])
    gplane[c] = part[...]
    line_q.total(write(gsum))
    plane_q = net.to_plane(lambda m: gsum.at[net.at(m)], g_in.at[c])
    g_in[c] = gsum[c]
    for cp in plane_g:
        cp.wait_recv()
    gz[z] = jnp.sum(gplane[...], axis=0)
    line_g = net.to_line(lambda m: gz.at[z], lambda m: gz.at[z])
    for cp in plane_u:
        cp.wait_recv()
    ggu_out[...] = ggu_in[...]
    for cp in plane_q:
        cp.wait_recv()
    gqkv_out[...] = g_in[...]
    for cp in line_g:
        cp.wait_recv()
    gains_out[...] = jnp.sum(gz[...], axis=0)
    for part in (gath, sum1, line_d, line_u, line_o, line_q):
        part.finish()
    for cp in line_g + plane_u + plane_g + plane_q + list(sib.values()):
        cp.wait_send()
    for s in range(2):
        for m in CHIPS:
            mo_chip(m, s).wait_send()


def finish(cfg, block_ref, dx_ref, gwo_ref, gwd_ref, ggu_ref, gqkv_ref, gains_ref,
           block_out, dx_out, gin_out, gq_out, gk_out, gv_out, gqg_out, gkg_out, gwo_out, gpost_out, ggate_out, gup_out,
           gwd_out):
    n, nz, ql, kvl, hd, ff = cfg["n"], cfg["nz"], cfg["ql"], cfg["kvl"], cfg["hd"], cfg["ff"]
    block_out[...] = block_ref[...]
    dx_out[...] = dx_ref[...]
    gwo_out[...] = gwo_ref[...]
    gwd_out[...] = gwd_ref[...]
    qw, kw = ql * hd, kvl * hd
    for d in range(n):
        both = gqkv_ref[d].astype(F32)
        gq_out[:, d * qw : (d + 1) * qw] = both[:, :qw]
        gk_out[:, d * kw : (d + 1) * kw] = both[:, qw : qw + kw]
        gv_out[:, d * kw : (d + 1) * kw] = both[:, qw + kw :]
        both = ggu_ref[d].astype(F32)
        ggate_out[:, d * ff : (d + 1) * ff] = both[:, :ff]
        gup_out[:, d * ff : (d + 1) * ff] = both[:, ff:]
    place = lax.axis_index("ctx") * nz + lax.axis_index("fsdp")
    for first, ref in ((0, gin_out), (8, gpost_out), (16, gqg_out), (17, gkg_out)):
        width = ref.shape[1]
        at = place * width
        row = gains_ref[pl.ds(first + lax.div(at, LANES), 1), :]
        ref[...] = pltpu.roll(row, lax.rem(LANES - lax.rem(at, LANES), LANES), 1)[:, :width]


def call(body, cfg, ins, outs, scratch, cid, *args):
    remote = cid is not None
    params = dict(collective_id=cid, has_side_effects=True) if remote else {}
    if remote:
        sems = pltpu.SemaphoreType.DMA((cfg["slots"],))
        scratch = scratch + [pltpu.SemaphoreType.DMA((32,)), sems, sems]
    return pl.pallas_call(
        functools.partial(body, cfg),
        out_shape=[jax.ShapeDtypeStruct(shape, dtype) for shape, dtype, *_ in outs],
        in_specs=ins,
        out_specs=[o[2] if len(o) > 2 else VMEM for o in outs],
        scratch_shapes=scratch,
        compiler_params=pltpu.CompilerParams(vmem_limit_bytes=LIMIT, **params),
        name=body.__name__,
    )(*args)


def on_plane(hidden_in, seq_lengths, in_gain, w_query, w_key, w_value, q_gain, k_gain, w_out, post_gain,
             w_gate, w_up, w_down, d_out):
    n, nz = lax.axis_size("ctx"), lax.axis_size("fsdp")
    t, dm = hidden_in.shape[1:]
    rows = n * t
    hd = q_gain.shape[0] * n * nz
    ql = w_query.shape[1] // hd // n
    kvl = w_key.shape[1] // hd // n
    ff = w_gate.shape[1] // n
    r_in, r_out, r_down = w_query.shape[0], w_out.shape[0], w_down.shape[0]
    qkv = (ql + 2 * kvl) * hd
    tiles, half = rows // TILE, TILE // 2
    cfg = dict(n=n, nz=nz, ql=ql, kvl=kvl, hd=hd, ff=ff, eps=1e-6, window=rows // 2 // TILE, slots=14 * n + 8 * nz)

    inv = 1000000.0 ** (-np.arange(hd // 2) * (2.0 / hd))
    angles = np.concatenate([np.arange(half), np.arange(2 * tiles) * half])[:, None] * inv[None, :]
    table = jnp.asarray(np.concatenate([np.cos(angles), np.sin(angles)], axis=1), F32)
    x = hidden_in[0]
    smem = pl.BlockSpec(memory_space=pltpu.SMEM)
    anywhere = pl.BlockSpec(memory_space=pl.ANY)

    def hbm(shape, dtype):
        return (shape, dtype, anywhere)

    def vm(shape, dtype=BF):
        return pltpu.VMEM(shape, dtype)

    big, low, wide, pair = (tiles, TILE, dm), (tiles, TILE, 2 * hd), (tiles, ql, TILE, 2 * hd), (2, half, dm)
    pre_w = (ql + kvl) * hd
    w_s, gu_s, wo_s, wd_s = (n, nz, r_in, qkv), (n, nz, r_in, 2 * ff), (nz, r_out, dm), (nz, r_down, dm)
    attn_s = (tiles, TILE, ql * hd)
    gains_s = (GAIN_ROWS, LANES)
    sums = [vm((n, half, dm)), vm((n, half, dm)), vm((n - 2, half, dm)), vm((n - 2, half, dm)), vm((2, TILE, dm), F32), vm(pair, F32)]
    (qx, kx, vx, attn, mo, pre, cs, xn, w, wo, gwd, ggu, h_mid, d_hmid, d_res, gains, gpost) = call(
        front, cfg, [smem] + [VMEM] * 14,
        [hbm(wide, BF), hbm(low, BF), hbm(low, BF), hbm(attn_s, BF), hbm(big, BF), hbm((tiles, TILE, pre_w), BF),
         hbm((tiles, TILE, hd), F32), hbm(big, BF), hbm(w_s, BF), hbm(wo_s, BF), hbm(wd_s, BF), hbm(gu_s, BF),
         hbm(pair, F32), hbm(pair, F32), hbm(pair, BF), (gains_s, F32), ((1, dm), F32)],
        [vm((n, r_in, qkv)), vm((n, r_in, 2 * ff)), vm(w_s), vm(wo_s), vm(gu_s), vm(wd_s),
         vm((8, LANES), F32), vm(gains_s, F32), vm((n,) + gains_s, F32), vm((nz,) + gains_s, F32),
         vm(big), vm(big), vm((tiles, TILE, pre_w)), vm((tiles, TILE, hd), F32), vm(wide), vm(low), vm(low),
         vm((ql * TILE, 2 * hd), F32), vm(attn_s),
         vm(big), vm((tiles, TILE, ff)), vm((tiles, TILE, 2 * ff)), vm((2, TILE, dm))]
        + sums + [vm(pair, F32), vm(pair, F32), vm(pair), vm(wd_s), vm(gu_s)],
        1, seq_lengths, x, d_out[0], w_query, w_key, w_value, w_out, w_gate, w_up, w_down, in_gain[None], post_gain[None], q_gain[None], k_gain[None], table)

    block, dx, gwo, grad_down, ggu, gqkv, small = call(
        back, cfg, [smem] + [VMEM] * 5 + [anywhere] * 10 + [VMEM] * 3,
        [((t, dm), BF), ((t, dm), F32), ((r_out, dm), F32), ((r_down, dm), F32), ((n, r_in, 2 * ff), BF),
         ((n, r_in, qkv), BF), (gains_s, F32)],
        [vm((n, half, dm)), vm((n, half, dm)), vm((n - 2, half, dm)), vm((n - 2, half, dm)),
         vm((tiles, TILE, pre_w)), vm((tiles, TILE, hd), F32), vm(big), vm(w_s), vm(pair, F32), vm(pair, F32), vm(big),
         vm((ql * TILE, hd), F32), vm((tiles, TILE, hd), F32), vm((tiles, TILE, hd), F32), vm((ql * TILE, 2 * hd)),
         vm(wd_s), vm((nz + 1, r_down, dm)), vm(gu_s), vm((nz + 1, n, r_in, 2 * ff)),
         vm((n, r_in, 2 * ff)), vm((n, r_in, 2 * ff)), vm(wo_s), vm((nz + 1, r_out, dm)),
         vm((tiles, TILE, qkv)), vm(w_s), vm((nz + 1, n, r_in, qkv)), vm((n, r_in, qkv)), vm((n, r_in, qkv)),
         vm(gains_s, F32), vm((n,) + gains_s, F32), vm((nz,) + gains_s, F32)]
        + sums,
        2, seq_lengths, qx, kx, vx, attn, wo, mo, pre, cs, xn, w, gwd, ggu, h_mid, d_hmid, d_res, gains, gpost, x)

    grads = call(
        finish, cfg, [VMEM] * 7,
        [((t, dm), BF), ((t, dm), F32), ((1, in_gain.shape[0]), F32), ((r_in, n * ql * hd), F32),
         ((r_in, n * kvl * hd), F32), ((r_in, n * kvl * hd), F32), ((1, q_gain.shape[0]), F32),
         ((1, k_gain.shape[0]), F32), ((r_out, dm), F32), ((1, post_gain.shape[0]), F32), ((r_in, n * ff), F32),
         ((r_in, n * ff), F32), ((r_down, dm), F32)],
        [], None, block, dx, gwo, grad_down, ggu, gqkv, small)
    (block, dx, g_in, g_q, g_k, g_v, g_qg, g_kg, g_o, g_post, g_gate, g_up, g_down) = grads
    return (block[None], dx[None], g_in[0], g_q, g_k, g_v, g_qg[0], g_kg[0], g_o, g_post[0], g_gate, g_up, g_down)


epsilon = 1e-06
rope_base = 1000000.0
negative = -1e30


def row_info(lengths, row_ids, tok_dev, n_ctx):
    half_len = tok_dev // 2
    device = row_ids // tok_dev
    local_row = row_ids % tok_dev
    block_id = jnp.where(local_row < half_len, device, 2 * n_ctx - 1 - device)
    packed = block_id * half_len + local_row % half_len
    seq_ends = jnp.cumsum(lengths)
    seq_starts = seq_ends - lengths
    member = (packed[:, None] >= seq_starts[None, :]) & (packed[:, None] < seq_ends[None, :])
    row_valid = jnp.any(member, axis=1)
    numbers = jnp.arange(lengths.shape[0], dtype=jnp.int32)
    seq_id = jnp.sum(jnp.where(member, numbers[None, :], 0), axis=1)
    offset = jnp.sum(jnp.where(member, seq_starts[None, :], 0), axis=1)
    segment = jnp.where(row_valid, seq_id, -1 - packed)
    position = jnp.where(row_valid, packed - offset, 0)
    return (segment, position, row_valid)


def norm_gain(values_in, gain_vec):
    row_scale = lax.rsqrt(jnp.mean(values_in * values_in, axis=-1, keepdims=True) + epsilon)
    return values_in * row_scale * gain_vec


def rotary(position, head_dim):
    half_len = head_dim // 2
    inv_freq = jnp.power(rope_base, -jnp.arange(half_len, dtype=jnp.float32) * (2.0 / head_dim))
    angles = position.astype(jnp.float32)[:, None] * inv_freq[None, :]
    angles = jnp.concatenate([angles, angles], axis=1)
    return (jnp.cos(angles), jnp.sin(angles))


def rotate(heads, cos_table, sin_table):
    half_len = heads.shape[-1] // 2
    turned = jnp.concatenate([-heads[..., half_len:], heads[..., :half_len]], axis=-1)
    return heads * cos_table[:, None, :] + turned * sin_table[:, None, :]


def head_post(q_in, k_in, q_scale, k_scale, cos_table, sin_table):
    head_dim = q_scale.shape[0]
    row_count = q_in.shape[0]
    q_heads = norm_gain(q_in.reshape(row_count, -1, head_dim), q_scale)
    k_heads = norm_gain(k_in.reshape(row_count, -1, head_dim), k_scale)
    query_rotated = rotate(q_heads, cos_table, sin_table).reshape(row_count, -1)
    key_rotated = rotate(k_heads, cos_table, sin_table).reshape(row_count, -1)
    return (query_rotated, key_rotated)


def swiglu(gate_in, up_in):
    return jax.nn.silu(gate_in) * up_in


def matmul(left, right):
    return jnp.dot(left, right, preferred_element_type=jnp.float32)


def inner(left, right):
    return lax.dot_general(
        left, right, (((0,), (0,)), ((), ())), preferred_element_type=jnp.float32
    )


def backdot(left, right):
    return lax.dot_general(
        left, right, (((1,), (1,)), ((), ())), preferred_element_type=jnp.float32
    )


def pick_step(key_count):
    for candidate in (512, 384, 256):
        return candidate
    return key_count


def on_rows(
    hidden_in,
    seq_lengths,
    in_gain,
    w_query,
    w_key,
    w_value,
    q_gain,
    k_gain,
    w_out,
    post_gain,
    w_gate,
    w_up,
    w_down,
    d_out,
):
    n_ctx = lax.axis_size("ctx")
    row_count = hidden_in.shape[1]
    lengths = seq_lengths[0]
    own_rows = lax.axis_index("ctx") * row_count + jnp.arange(row_count, dtype=jnp.int32)
    seg_q, pos_q, row_valid = row_info(lengths, own_rows, row_count, n_ctx)
    shards = (
        in_gain,
        w_query,
        w_key,
        w_value,
        q_gain,
        k_gain,
        w_out,
        post_gain,
        w_gate,
        w_up,
        w_down,
    )
    gathered = (
        lax.all_gather(shards[0], ("ctx", "fsdp"), axis=0, tiled=True),
        lax.all_gather(shards[1], ("ctx", "fsdp"), axis=0, tiled=True),
        lax.all_gather(shards[2], ("ctx", "fsdp"), axis=0, tiled=True),
        lax.all_gather(shards[3], ("ctx", "fsdp"), axis=0, tiled=True),
        lax.all_gather(shards[4], ("ctx", "fsdp"), axis=0, tiled=True),
        lax.all_gather(shards[5], ("ctx", "fsdp"), axis=0, tiled=True),
        lax.all_gather(shards[6], ("ctx", "fsdp"), axis=0, tiled=True),
        lax.all_gather(shards[7], ("ctx", "fsdp"), axis=0, tiled=True),
        lax.all_gather(shards[8], ("ctx", "fsdp"), axis=0, tiled=True),
        lax.all_gather(shards[9], ("ctx", "fsdp"), axis=0, tiled=True),
        lax.all_gather(shards[10], ("ctx", "fsdp"), axis=0, tiled=True),
    )
    g_in = gathered[0].astype(jnp.float32)
    g_query = gathered[4].astype(jnp.float32)
    g_key = gathered[5].astype(jnp.float32)
    g_post = gathered[7].astype(jnp.float32)
    head_dim = gathered[4].shape[0]
    kv_width = gathered[2].shape[1]
    kv_heads = kv_width // head_dim
    group_count = gathered[1].shape[1] // kv_width
    score_scale = head_dim ** (-0.5)
    rows_per_group = row_count * n_ctx
    x_float = hidden_in[0].astype(jnp.float32)
    x_normf, in_back = jax.vjp(norm_gain, x_float, g_in)
    x_norm = x_normf.astype(jnp.bfloat16)
    q_pre = matmul(x_norm, gathered[1])
    k_pre = matmul(x_norm, gathered[2])
    value_projected = matmul(x_norm, gathered[3])
    cos_table, sin_table = rotary(pos_q, head_dim)

    def post_local(q_in, k_in, q_scale, k_scale):
        return head_post(q_in, k_in, q_scale, k_scale, cos_table, sin_table)

    rotated, post_back = jax.vjp(post_local, q_pre, k_pre, g_query, g_key)
    q_low4 = rotated[0].astype(jnp.bfloat16).reshape(row_count, kv_heads, group_count, head_dim)
    key_narrow = rotated[1].astype(jnp.bfloat16)
    value_narrow = value_projected.astype(jnp.bfloat16)

    def sweep_keys(carry, k_piece, v_piece, block_fn):
        key_count = k_piece.shape[0]
        key_step = pick_step(key_count)

        def one_turn(state, turn_index):
            offset = turn_index * key_step
            k_block = lax.dynamic_slice_in_dim(k_piece, offset, key_step, 0)
            v_block = lax.dynamic_slice_in_dim(v_piece, offset, key_step, 0)
            key_rows = offset + jnp.arange(key_step, dtype=jnp.int32)
            seg_k, pos_k, unused = row_info(lengths, key_rows, row_count, n_ctx)
            allowed = (seg_q[:, None] == seg_k[None, :]) & (pos_k[None, :] <= pos_q[:, None])
            state = block_fn(state, k_block, v_block, allowed, offset)
            return (state, None)

        carry, unused = lax.scan(
            one_turn, carry, jnp.arange(key_count // key_step, dtype=jnp.int32)
        )
        return carry

    def forward_block(carry, k_block, v_block, allowed, first_key):
        row_max, totals, weighted = carry
        k_heads = k_block.reshape(-1, kv_heads, head_dim)
        v_heads = v_block.reshape(-1, kv_heads, head_dim)
        mask_four = allowed[None, None]
        score = (
            jnp.einsum("qhgd,khd->hgqk", q_low4, k_heads, preferred_element_type=jnp.float32)
            * score_scale
        )
        block_max = jnp.max(jnp.where(mask_four, score, negative), axis=-1)
        new_max = jnp.maximum(row_max, block_max)
        expo = jnp.where(mask_four, jnp.exp(score - new_max[..., None]), 0.0)
        factor = jnp.exp(row_max - new_max)
        totals = totals * factor + jnp.sum(expo, axis=-1)
        weighted = weighted * factor[..., None] + jnp.einsum(
            "hgqk,khd->hgqd", expo.astype(jnp.bfloat16), v_heads, preferred_element_type=jnp.float32
        )
        return (new_max, totals, weighted)

    start_state = (
        jnp.full((kv_heads, group_count, row_count), negative, jnp.float32),
        jnp.zeros((kv_heads, group_count, row_count), jnp.float32),
        jnp.zeros((kv_heads, group_count, row_count, head_dim), jnp.float32),
    )
    pieces = (
        lax.all_gather(key_narrow, "ctx", axis=0, tiled=True),
        lax.all_gather(value_narrow, "ctx", axis=0, tiled=True),
    )
    fold_state = sweep_keys(start_state, pieces[0], pieces[1], forward_block)
    row_max, totals, weighted = fold_state
    attn_four = weighted / totals[..., None]
    log_total = row_max + jnp.log(totals)
    attn = jnp.transpose(attn_four, (2, 0, 1, 3)).reshape(row_count, -1)
    attn_low = attn.astype(jnp.bfloat16)
    h_mid = x_float + matmul(attn_low, gathered[6])
    h_normf, post_norm_back = jax.vjp(norm_gain, h_mid, g_post)
    h_norm = h_normf.astype(jnp.bfloat16)
    gate_out = matmul(h_norm, gathered[8])
    up_out = matmul(h_norm, gathered[9])
    act_float, swiglu_back = jax.vjp(swiglu, gate_out, up_out)
    act_low = act_float.astype(jnp.bfloat16)
    row_mask = row_valid.astype(jnp.float32)[:, None]
    block_out = (row_mask * (h_mid + matmul(act_low, gathered[10]))).astype(jnp.bfloat16)
    again = (
        lax.all_gather(shards[0], ("ctx", "fsdp"), axis=0, tiled=True),
        lax.all_gather(shards[1], ("ctx", "fsdp"), axis=0, tiled=True),
        lax.all_gather(shards[2], ("ctx", "fsdp"), axis=0, tiled=True),
        lax.all_gather(shards[3], ("ctx", "fsdp"), axis=0, tiled=True),
        lax.all_gather(shards[4], ("ctx", "fsdp"), axis=0, tiled=True),
        lax.all_gather(shards[5], ("ctx", "fsdp"), axis=0, tiled=True),
        lax.all_gather(shards[6], ("ctx", "fsdp"), axis=0, tiled=True),
        lax.all_gather(shards[7], ("ctx", "fsdp"), axis=0, tiled=True),
        lax.all_gather(shards[8], ("ctx", "fsdp"), axis=0, tiled=True),
        lax.all_gather(shards[9], ("ctx", "fsdp"), axis=0, tiled=True),
        lax.all_gather(shards[10], ("ctx", "fsdp"), axis=0, tiled=True),
    )
    d_block = d_out[0].astype(jnp.float32) * row_mask
    dm_low = d_block.astype(jnp.bfloat16)
    grad_down = inner(act_low, dm_low)
    d_act = backdot(dm_low, again[10])
    d_gate, d_up = swiglu_back(d_act)
    dg_low = d_gate.astype(jnp.bfloat16)
    du_low = d_up.astype(jnp.bfloat16)
    grad_gate = inner(h_norm, dg_low)
    grad_up = inner(h_norm, du_low)
    d_hnorm = backdot(dg_low, again[8]) + backdot(du_low, again[9])
    d_hpart, grad_post = post_norm_back(d_hnorm)
    d_hmid = d_block + d_hpart
    d_res = d_hmid.astype(jnp.bfloat16)
    grad_wout = inner(attn_low, d_res)
    d_attn = backdot(d_res, again[6]).astype(jnp.bfloat16)
    d_attn4 = d_attn.reshape(row_count, kv_heads, group_count, head_dim)
    delta = jnp.einsum("qhgd,hgqd->hgq", d_attn4.astype(jnp.float32), attn_four)

    def backward_block(carry, k_block, v_block, allowed, first_key):
        d_query, d_kv = carry
        key_count = k_block.shape[0]
        k_heads = k_block.reshape(-1, kv_heads, head_dim)
        v_heads = v_block.reshape(-1, kv_heads, head_dim)
        mask_four = allowed[None, None]
        score = (
            jnp.einsum("qhgd,khd->hgqk", q_low4, k_heads, preferred_element_type=jnp.float32)
            * score_scale
        )
        prob = jnp.where(mask_four, jnp.exp(score - log_total[..., None]), 0.0)
        prob_low = prob.astype(jnp.bfloat16)
        d_prob = jnp.einsum("qhgd,khd->hgqk", d_attn4, v_heads, preferred_element_type=jnp.float32)
        d_score = (prob * (d_prob - delta[..., None])).astype(jnp.bfloat16)
        d_query = d_query + jnp.einsum(
            "hgqk,khd->qhgd", d_score, k_heads, preferred_element_type=jnp.float32
        )
        d_key = (
            jnp.einsum("hgqk,qhgd->khd", d_score, q_low4, preferred_element_type=jnp.float32)
            * score_scale
        )
        d_value = jnp.einsum(
            "hgqk,qhgd->khd", prob_low, d_attn4, preferred_element_type=jnp.float32
        )
        joined = jnp.concatenate(
            [d_key.reshape(key_count, -1), d_value.reshape(key_count, -1)], axis=1
        )
        before = lax.dynamic_slice_in_dim(d_kv, first_key, key_count, 0)
        d_kv = lax.dynamic_update_slice_in_dim(d_kv, before + joined, first_key, 0)
        return (d_query, d_kv)

    back_start = (
        jnp.zeros((row_count, kv_heads, group_count, head_dim), jnp.float32),
        jnp.zeros((rows_per_group, 2 * kv_width), jnp.float32),
    )
    pieces = (
        lax.all_gather(key_narrow, "ctx", axis=0, tiled=True),
        lax.all_gather(value_narrow, "ctx", axis=0, tiled=True),
    )
    back_state = sweep_keys(back_start, pieces[0], pieces[1], backward_block)
    d_qrot = back_state[0].reshape(row_count, -1) * score_scale
    d_kv_own = lax.psum_scatter(
        back_state[1].astype(jnp.bfloat16), "ctx", scatter_dimension=0, tiled=True
    ).astype(jnp.float32)
    d_krot = d_kv_own[:, :kv_width]
    d_vpre = d_kv_own[:, kv_width:]
    d_qpre, d_kpre, grad_qgain, grad_kgain = post_back((d_qrot, d_krot))
    dq_low = d_qpre.astype(jnp.bfloat16)
    dk_low = d_kpre.astype(jnp.bfloat16)
    dv_low = d_vpre.astype(jnp.bfloat16)
    grad_query = inner(x_norm, dq_low)
    grad_key = inner(x_norm, dk_low)
    grad_value = inner(x_norm, dv_low)
    d_xnorm = backdot(dq_low, again[1]) + backdot(dk_low, again[2]) + backdot(dv_low, again[3])
    d_xpart, grad_ingain = in_back(d_xnorm)
    d_hidden = d_hmid + d_xpart
    owned = (
        lax.psum_scatter(grad_ingain, ("ctx", "fsdp"), scatter_dimension=0, tiled=True),
        lax.psum_scatter(grad_query, ("ctx", "fsdp"), scatter_dimension=0, tiled=True),
        lax.psum_scatter(grad_key, ("ctx", "fsdp"), scatter_dimension=0, tiled=True),
        lax.psum_scatter(grad_value, ("ctx", "fsdp"), scatter_dimension=0, tiled=True),
        lax.psum_scatter(grad_qgain, ("ctx", "fsdp"), scatter_dimension=0, tiled=True),
        lax.psum_scatter(grad_kgain, ("ctx", "fsdp"), scatter_dimension=0, tiled=True),
        lax.psum_scatter(grad_wout, ("ctx", "fsdp"), scatter_dimension=0, tiled=True),
        lax.psum_scatter(grad_post, ("ctx", "fsdp"), scatter_dimension=0, tiled=True),
        lax.psum_scatter(grad_gate, ("ctx", "fsdp"), scatter_dimension=0, tiled=True),
        lax.psum_scatter(grad_up, ("ctx", "fsdp"), scatter_dimension=0, tiled=True),
        lax.psum_scatter(grad_down, ("ctx", "fsdp"), scatter_dimension=0, tiled=True),
    )
    return (
        block_out[None],
        d_hidden[None],
        owned[0],
        owned[1],
        owned[2],
        owned[3],
        owned[4],
        owned[5],
        owned[6],
        owned[7],
        owned[8],
        owned[9],
        owned[10],
    )


def on_device(*args):
    n = lax.axis_size("ctx")
    hidden_in, w_key, w_out, w_gate, q_gain = args[0], args[4], args[8], args[10], args[6]
    hd = q_gain.shape[0] * n * lax.axis_size("fsdp")
    heads, ff = w_key.shape[1] // hd, w_gate.shape[1] // n
    even = heads % n == 0 and ff % LANES == 0 and w_key.shape[0] % 16 == 0 and w_out.shape[0] % 16 == 0
    if even and heads == n == 8 and hidden_in.shape[1] == TILE:
        return on_plane(*args)
    return on_rows(*args)


def solution(mesh):
    in_specs = (
        P("fsdp", "ctx", None),
        P("fsdp", None),
        P(("ctx", "fsdp")),
        P(("ctx", "fsdp"), None),
        P(("ctx", "fsdp"), None),
        P(("ctx", "fsdp"), None),
        P(("ctx", "fsdp")),
        P(("ctx", "fsdp")),
        P(("ctx", "fsdp"), None),
        P(("ctx", "fsdp")),
        P(("ctx", "fsdp"), None),
        P(("ctx", "fsdp"), None),
        P(("ctx", "fsdp"), None),
        P("fsdp", "ctx", None),
    )
    out_specs = (
        P("fsdp", "ctx", None),
        P("fsdp", "ctx", None),
        P(("ctx", "fsdp")),
        P(("ctx", "fsdp"), None),
        P(("ctx", "fsdp"), None),
        P(("ctx", "fsdp"), None),
        P(("ctx", "fsdp")),
        P(("ctx", "fsdp")),
        P(("ctx", "fsdp"), None),
        P(("ctx", "fsdp")),
        P(("ctx", "fsdp"), None),
        P(("ctx", "fsdp"), None),
        P(("ctx", "fsdp"), None),
    )
    return jax.shard_map(
        on_device, mesh=mesh, in_specs=in_specs, out_specs=out_specs, check_vma=False
    )
```
